32 devices in a mesh: dp: 4 (over y, x), row: 4 (over z), col: 2 (over core).
Axes of the slice: x: 2, y: 2, z: 4, core: 2. Of those that a mesh axis runs over, the one named last changes fastest.
Arguments:
- inputs: bfloat16 [2916, 1152], P('dp', ('row', 'col')), may hold values from -11 to 11
- cotangent: bfloat16 [2916, 1152], P('dp', ('row', 'col')), may hold values from -6 to 6
- qkv_master: float32 [288, 4, 3456], P('row', 'dp', 'col'), may hold values from -0.1875 to 0.1875
- out_master: float32 [1152, 288, 4], P('col', 'row', 'dp'), may hold values from -1 to 1
- up_master: float32 [288, 4, 4304], P('row', 'dp', 'col'), may hold values from -0.20623948 to 0.20623948
- down_master: float32 [4304, 288, 4], P('col', 'row', 'dp'), may hold values from -0.09375 to 0.09375
- qkv_first: float32 [288, 4, 3456], P('row', 'dp', 'col'), may hold values from -16 to 16
- out_first: float32 [1152, 288, 4], P('col', 'row', 'dp'), may hold values from -6 to 6
- up_first: float32 [288, 4, 4304], P('row', 'dp', 'col'), may hold values from -6 to 6
- down_first: float32 [4304, 288, 4], P('col', 'row', 'dp'), may hold values from -20 to 20
- qkv_second: float32 [288, 4, 3456], P('row', 'dp', 'col'), may hold values from 0.729 to 2.916
- out_second: float32 [1152, 288, 4], P('col', 'row', 'dp'), may hold values from 0.06561 to 0.26244
- up_second: float32 [288, 4, 4304], P('row', 'dp', 'col'), may hold values from 0.26244 to 1.04976
- down_second: float32 [4304, 288, 4], P('col', 'row', 'dp'), may hold values from 1.04976 to 4.19904
- norm_gains: float32 [2, 1152], replicated, may hold values from 0.5 to 1.5
- gain_first: float32 [2, 1152], replicated, may hold values from -32 to 32
- gain_second: float32 [2, 1152], replicated, may hold values from 2.916 to 11.664
- biases: float32 [11216], replicated, may hold values from -1.5 to 1.5
- bias_first: float32 [11216], replicated, may hold values from -32 to 32
- bias_second: float32 [11216], replicated, may hold values from 2.916 to 11.664
Outputs:
- outputs: bfloat16 [2916, 1152], P('dp', ('row', 'col'))
- input_grad: bfloat16 [2916, 1152], P('dp', ('row', 'col'))
- new_qkv: float32 [288, 4, 3456], P('row', 'dp', 'col')
- new_qkv_first: float32 [288, 4, 3456], P('row', 'dp', 'col')
- new_qkv_second: float32 [288, 4, 3456], P('row', 'dp', 'col')
- new_out: float32 [1152, 288, 4], P('col', 'row', 'dp')
- new_out_first: float32 [1152, 288, 4], P('col', 'row', 'dp')
- new_out_second: float32 [1152, 288, 4], P('col', 'row', 'dp')
- new_up: float32 [288, 4, 4304], P('row', 'dp', 'col')
- new_up_first: float32 [288, 4, 4304], P('row', 'dp', 'col')
- new_up_second: float32 [288, 4, 4304], P('row', 'dp', 'col')
- new_down: float32 [4304, 288, 4], P('col', 'row', 'dp')
- new_down_first: float32 [4304, 288, 4], P('col', 'row', 'dp')
- new_down_second: float32 [4304, 288, 4], P('col', 'row', 'dp')
- new_gains: float32 [2, 1152], replicated
- new_gain_first: float32 [2, 1152], replicated
- new_gain_second: float32 [2, 1152], replicated
- new_biases: float32 [11216], replicated
- new_bias_first: float32 [11216], replicated
- new_bias_second: float32 [11216], replicated
The draws below stay inside these ranges and needn't reach their ends.
All inputs are finite; a program needn't handle non-finite values.
Results may differ from the reference program's by a relative error of at most 0.02.
Values may be sent and summed in bfloat16 or wider, within the bound.
No kernel may reach another device: no remote copies, remote signals or barrier semaphores. Data moves between devices by JAX's collectives and lax.ppermute only.
A program may use at most 128 MiB of HBM per device.

```python
import math
import jax
import jax.numpy as jnp
from jax import lax

D = 1152
FF = 4304
HEADS = 16
HEAD = 72
SEQ = 729
STEP = 10
TOKENS = 2916
BIAS = 11216
N_DP = 4


def draw_inputs(key, part):
    key = jax.random.fold_in(key, 11)
    base_key, rough_key = jax.random.split(key)
    position = jnp.arange(D, dtype=jnp.float32) / (D - 1)
    rising = jnp.exp(jnp.log(3.0) * position)
    base = jnp.clip(jax.random.normal(base_key, (TOKENS, D), jnp.float32), -4.0, 4.0)
    rough = jax.random.uniform(rough_key, (1, D), jnp.float32, 0.7, 1.4)
    return (base * rising[None, :] * rough / 1.6).astype(jnp.bfloat16)


def draw_up_master(key, part):
    key = jax.random.fold_in(key, 13)
    entry_key, column_key = jax.random.split(key)
    entries = jnp.clip(jax.random.normal(entry_key, (D // N_DP, N_DP, FF), jnp.float32), -4.0, 4.0)
    columns = jnp.clip(jax.random.normal(column_key, (FF,), jnp.float32), -3.0, 3.0)
    return (entries + columns[None, None, :]) / jnp.sqrt(jnp.float32(D))


def level_of(rng, shape, shards, smallest, high):
    factor_of = 1.0
    for dim, parts in shards:
        draws = jax.random.uniform(jax.random.fold_in(jax.random.fold_in(rng, 6), dim), (parts,), jnp.float32, smallest / len(shards), high / len(shards))
        factor_of = factor_of * jnp.repeat(jnp.exp(draws), shape[dim] // parts).reshape((-1,) + (1,) * (len(shape) - 1 - dim))
    return factor_of


def centred(key, extent, deviation, reach, shards=(), held_as=jnp.bfloat16):
    array = deviation * jax.random.normal(key, extent, jnp.float32)
    if shards:
        array = array * level_of(key, extent, shards, -0.22, 0.18)
    return jnp.clip(array, -reach, reach).astype(held_as)


def setup_inputs(seed: int = 0) -> dict:
    streams_of = jax.random.split(jax.random.key(seed), 21)
    inputs = draw_inputs(jax.random.fold_in(streams_of[20], 71), 0)
    cotangent = centred(streams_of[1], (TOKENS, D), 1.0, 6.0, ((0, 4), (1, 8)))
    qkv_master = centred(streams_of[2], (D // N_DP, N_DP, 3 * D), D ** -0.5, 0.1875, ((0, 4), (1, 4), (2, 2)), jnp.float32)
    out_master = centred(streams_of[3], (D, D // N_DP, N_DP), (D // 32) ** -0.5, 1.0, ((0, 2), (1, 4), (2, 4)), jnp.float32)
    up_master = draw_up_master(jax.random.fold_in(streams_of[20], 71), 0)
    down_master = centred(streams_of[5], (FF, D // N_DP, N_DP), FF ** -0.5, 0.09375, ((0, 2), (1, 4), (2, 4)), jnp.float32)
    qkv_first = centred(streams_of[6], (D // N_DP, N_DP, 3 * D), (0.11 * 0.5 * TOKENS ** 0.5), 16.0, ((0, 4), (1, 4), (2, 2)), jnp.float32)
    out_first = centred(streams_of[7], (D, D // N_DP, N_DP), (0.11 * 0.15 * TOKENS ** 0.5), 6.0, ((0, 2), (1, 4), (2, 4)), jnp.float32)
    up_first = centred(streams_of[8], (D // N_DP, N_DP, FF), (0.11 * 0.3 * TOKENS ** 0.5), 6.0, ((0, 4), (1, 4), (2, 2)), jnp.float32)
    down_first = centred(streams_of[9], (FF, D // N_DP, N_DP), (0.11 * 0.6 * TOKENS ** 0.5), 20.0, ((0, 2), (1, 4), (2, 4)), jnp.float32)
    qkv_second = jnp.clip(jnp.exp(math.log(2.916) - 1.3862944 * jax.random.uniform(streams_of[10], (D // N_DP, N_DP, 3 * D), jnp.float32) ** level_of(streams_of[10], (D // N_DP, N_DP, 3 * D), ((0, 4), (1, 4), (2, 2)), -0.2, 0.2)), 0.729, 2.916)
    out_second = jnp.clip(jnp.exp(math.log(0.26244) - 1.3862944 * jax.random.uniform(streams_of[11], (D, D // N_DP, N_DP), jnp.float32) ** level_of(streams_of[11], (D, D // N_DP, N_DP), ((0, 2), (1, 4), (2, 4)), -0.2, 0.2)), 0.06561, 0.26244)
    up_second = jnp.clip(jnp.exp(math.log(1.04976) - 1.3862944 * jax.random.uniform(streams_of[12], (D // N_DP, N_DP, FF), jnp.float32) ** level_of(streams_of[12], (D // N_DP, N_DP, FF), ((0, 4), (1, 4), (2, 2)), -0.2, 0.2)), 0.26244, 1.04976)
    down_second = jnp.clip(jnp.exp(math.log(4.19904) - 1.3862944 * jax.random.uniform(streams_of[13], (FF, D // N_DP, N_DP), jnp.float32) ** level_of(streams_of[13], (FF, D // N_DP, N_DP), ((0, 2), (1, 4), (2, 4)), -0.2, 0.2)), 1.04976, 4.19904)
    norm_gains = jnp.clip(1.0 + 0.1 * jax.random.normal(streams_of[14], (2, D), jnp.float32), 0.5, 1.5)
    gain_first = centred(streams_of[15], (2, D), (0.11 * TOKENS ** 0.5), 32.0, (), jnp.float32)
    gain_second = jnp.clip(jnp.exp(jax.random.uniform(streams_of[16], (2, D), jnp.float32, math.log(2.916), math.log(11.664))), 2.916, 11.664)
    biases = centred(streams_of[17], (BIAS,), 0.3, 1.5, (), jnp.float32)
    bias_first = centred(streams_of[18], (BIAS,), (0.11 * TOKENS ** 0.5), 32.0, (), jnp.float32)
    bias_second = jnp.clip(jnp.exp(jax.random.uniform(streams_of[19], (BIAS,), jnp.float32, math.log(2.916), math.log(11.664))), 2.916, 11.664)
    return dict(inputs=inputs, cotangent=cotangent, qkv_master=qkv_master, out_master=out_master, up_master=up_master, down_master=down_master, qkv_first=qkv_first, out_first=out_first, up_first=up_first, down_first=down_first, qkv_second=qkv_second, out_second=out_second, up_second=up_second, down_second=down_second, norm_gains=norm_gains, gain_first=gain_first, gain_second=gain_second, biases=biases, bias_first=bias_first, bias_second=bias_second)


NORM_EPS = 1e-06
ADAM_EPS = 1e-08
BETA_ONE = 0.9
BETA_TWO = 0.999
HIGHEST_PREC = lax.Precision.HIGHEST

@jax.custom_vjp
def low(v):
    return lax.optimization_barrier(v.astype(jnp.bfloat16)).astype(jnp.float32)

@jax.custom_vjp
def low_back(v):
    return v

def low_keep(v):
    return (low(v), None)

def low_pass(kept, grad):
    return (grad,)

def back_keep(v):
    return (v, None)

def back_low(kept, grad):
    return (low(grad),)
low.defvjp(low_keep, low_pass)
low_back.defvjp(back_keep, back_low)

def matmul(left_side, right_side):
    return jnp.dot(left_side, right_side, precision=HIGHEST_PREC, preferred_element_type=jnp.float32)

def layer_norm(operand, norm_gain, norm_shift):
    average = lax.optimization_barrier(jnp.mean(operand, axis=-1, keepdims=True))
    center = operand - average
    spread = lax.optimization_barrier(jnp.mean(center * center, axis=-1, keepdims=True))
    return center * lax.rsqrt(spread + NORM_EPS) * norm_gain + norm_shift

def attend(image_block):
    queries = image_block[:, :, 0]
    key_rows = image_block[:, :, 1]
    values = image_block[:, :, 2]
    scores = low_back(jnp.einsum('qhe,khe->hqk', queries, key_rows, precision=HIGHEST_PREC) * HEAD ** (-0.5))
    attn_probs = jax.nn.softmax(scores, axis=-1)
    return jnp.einsum('hqk,khe->qhe', low(attn_probs), values, precision=HIGHEST_PREC)

def forward(inputs, w_qkv, w_out, w_up, w_down, norm_gains, biases):
    tokens = inputs.shape[0]
    z_one = low(layer_norm(inputs, norm_gains[0], biases[0:D]))
    query_bias = biases[2 * D:3 * D].reshape(HEADS, HEAD)
    value_bias = biases[3 * D:4 * D].reshape(HEADS, HEAD)
    qkv_bias = jnp.stack([query_bias, jnp.zeros_like(query_bias), value_bias], axis=1).reshape(3 * D)
    qkv = low(low_back(matmul(z_one, w_qkv) + qkv_bias))
    image_blocks = qkv.reshape(tokens // SEQ, SEQ, HEADS, 3, HEAD)
    attended = lax.map(jax.checkpoint(attend), image_blocks).reshape(tokens, D)
    attended = low(low_back(attended))
    branch = low_back(matmul(attended, w_out) + biases[4 * D:5 * D])
    middle = inputs + branch
    z_two = low(layer_norm(middle, norm_gains[1], biases[D:2 * D]))
    hidden = low_back(matmul(z_two, w_up) + biases[6 * D:6 * D + FF])
    active = low(jax.nn.gelu(hidden, approximate=True))
    mlp_out = low_back(matmul(active, w_down) + biases[5 * D:6 * D])
    return middle + mlp_out

def adam_update(weights, moment_one, second, gradient, step_rate, weight_decay):
    moment_one = BETA_ONE * moment_one + (1.0 - BETA_ONE) * gradient
    second = BETA_TWO * second + (1.0 - BETA_TWO) * gradient * gradient
    direction = moment_one / (1.0 - BETA_ONE ** STEP) / (jnp.sqrt(second / (1.0 - BETA_TWO ** STEP)) + ADAM_EPS)
    return (weights - step_rate * (direction + weight_decay * weights), moment_one, second)

def as_weight(master, shape):
    return master.astype(jnp.bfloat16).astype(jnp.float32).reshape(shape)

def reference(inputs, cotangent, qkv_master, out_master, up_master, down_master, qkv_first, out_first, up_first, down_first, qkv_second, out_second, up_second, down_second, norm_gains, gain_first, gain_second, biases, bias_first, bias_second):
    w_qkv = as_weight(qkv_master, (D, 3 * D))
    w_out = as_weight(out_master, (D, D))
    w_up = as_weight(up_master, (D, FF))
    w_down = as_weight(down_master, (FF, D))
    result, pullback = jax.vjp(forward, inputs.astype(jnp.float32), w_qkv, w_out, w_up, w_down, norm_gains, biases)
    grads = pullback(cotangent.astype(jnp.float32))
    q_new, q_one, q_two = adam_update(qkv_master, qkv_first, qkv_second, grads[1].reshape(qkv_master.shape), 0.03, 0.1)
    o_new, o_one, o_two = adam_update(out_master, out_first, out_second, grads[2].reshape(out_master.shape), 0.12, 0.1)
    u_new, u_one, u_two = adam_update(up_master, up_first, up_second, grads[3].reshape(up_master.shape), 0.03, 0.1)
    d_new, d_one, d_two = adam_update(down_master, down_first, down_second, grads[4].reshape(down_master.shape), 0.02, 0.1)
    g_new, g_one, g_two = adam_update(norm_gains, gain_first, gain_second, grads[5], 0.5, 0.0)
    b_new, b_one, b_two = adam_update(biases, bias_first, bias_second, grads[6], 0.5, 0.0)
    return (result.astype(jnp.bfloat16), grads[0].astype(jnp.bfloat16), q_new, q_one, q_two, o_new, o_one, o_two, u_new, u_one, u_two, d_new, d_one, d_two, g_new, g_one, g_two, b_new, b_one, b_two)
```

```python
import jax
import jax.numpy as jnp
from jax import lax
from jax.sharding import PartitionSpec as P

D = 1152
FF = 4304
HEAD = 72
SEQ = 729
STEP = 10

NORM_EPS = 1e-06
ADAM_EPS = 1e-08
BETA_ONE = 0.9
BETA_TWO = 0.999
LOW = jnp.bfloat16


def dot(left, right, left_dim, right_dim, out=jnp.float32, precision=None):
    return lax.dot_general(
        left,
        right,
        (((left_dim,), (right_dim,)), ((), ())),
        precision=precision,
        preferred_element_type=out,
    )


def take(array, index, size):
    return lax.dynamic_slice_in_dim(array, index * size, size, axis=0)


def swap_cores(array):
    n_col = lax.axis_size("col")
    return lax.ppermute(array, "col", [(i, (i + 1) % n_col) for i in range(n_col)])


def gather_eight(block):
    rows = lax.all_gather(block, "row", axis=0, tiled=True)
    return lax.all_gather(rows, "col", axis=0, tiled=True)


def sum_over_rows(half):
    n_row = lax.axis_size("row")
    blocks = half.astype(LOW).reshape(n_row, half.shape[0] // n_row, half.shape[1])
    return jnp.sum(lax.all_to_all(blocks, "row", 0, 0).astype(jnp.float32), axis=0)


def reduce_eight(product):
    core = lax.axis_index("col")
    theirs = product(1 - core).astype(LOW)
    got = swap_cores(theirs)
    mine = product(core)
    return sum_over_rows(mine + got.astype(jnp.float32))


def exchange_rows(blocks):
    return lax.all_to_all(blocks, "row", 0, 0)


def all_sum(vector):
    for axis in ("col", "row", "dp"):
        size = lax.axis_size(axis)
        if size & (size - 1) or size > 4:
            vector = lax.psum(vector, axis)
            continue
        step = 1
        while step < size:
            vector = vector + lax.ppermute(vector, axis, [(i, i ^ step) for i in range(size)])
            step *= 2
    return vector


def attend_forward(queries, key_rows, values):
    scores = (
        jnp.einsum("hdq,hdk->hqk", queries, key_rows, preferred_element_type=jnp.float32)
        * HEAD ** (-0.5)
    )
    row_max = jnp.max(scores, axis=2, keepdims=True)
    exponent = jnp.exp(scores - row_max)
    row_total = jnp.sum(exponent, axis=2, keepdims=True)
    probs_low = (exponent / row_total).astype(LOW)
    attended = jnp.einsum("hqk,hdk->hdq", probs_low, values, preferred_element_type=jnp.float32)
    return attended.astype(LOW), row_max + jnp.log(row_total)


def attend_backward(queries, key_rows, values, log_total, attended_grad):
    scale = HEAD ** (-0.5)
    scores = (
        jnp.einsum("hdq,hdk->hqk", queries, key_rows, preferred_element_type=jnp.float32) * scale
    )
    probs = jnp.exp(scores - log_total)
    probs_low = probs.astype(LOW)
    value_grad = jnp.einsum(
        "hqk,hdq->hdk", probs_low, attended_grad, preferred_element_type=jnp.float32
    )
    probs_grad = jnp.einsum(
        "hdq,hdk->hqk", attended_grad, values, preferred_element_type=jnp.float32
    )
    inner = jnp.sum(probs * probs_grad, axis=2, keepdims=True)
    scores_grad = (probs * (probs_grad - inner)).astype(LOW)
    query_grad = (
        jnp.einsum("hqk,hdk->hdq", scores_grad, key_rows, preferred_element_type=jnp.float32)
        * scale
    )
    key_grad = (
        jnp.einsum("hqk,hdq->hdk", scores_grad, queries, preferred_element_type=jnp.float32) * scale
    )
    return jnp.stack([query_grad, key_grad, value_grad], axis=1).astype(LOW)


def adam_update(weights, moment_one, second, gradient, step_rate, weight_decay):
    moment_one = BETA_ONE * moment_one + (1.0 - BETA_ONE) * gradient
    second = BETA_TWO * second + (1.0 - BETA_TWO) * gradient * gradient
    direction = (
        moment_one / (1.0 - BETA_ONE**STEP) / (jnp.sqrt(second / (1.0 - BETA_TWO**STEP)) + ADAM_EPS)
    )
    return (weights - step_rate * (direction + weight_decay * weights), moment_one, second)


def shards(
    inputs,
    cotangent,
    qkv_master,
    out_master,
    up_master,
    down_master,
    qkv_first,
    out_first,
    up_first,
    down_first,
    qkv_second,
    out_second,
    up_second,
    down_second,
    norm_gains,
    gain_first,
    gain_second,
    biases,
    bias_first,
    bias_second,
):
    tokens, width = inputs.shape
    n_row = lax.axis_size("row")
    n_col = lax.axis_size("col")
    n_dp = lax.axis_size("dp")
    row = lax.axis_index("row")
    core = lax.axis_index("col")
    group = n_row * n_col
    heads = width // HEAD
    hidden_width = FF // group
    own = core * n_row + row
    chunk = -(-tokens // (group * 16)) * 16
    padded = chunk * group
    shard_rows = qkv_master.shape[0]

    place = lax.broadcasted_iota(jnp.int32, (D, D), 0)
    source = lax.broadcasted_iota(jnp.int32, (D, D), 1)
    feature = (
        ((place // width) % n_row) * n_col + place // (width * n_row)
    ) * width + place % width
    order = (source == (feature % n_dp) * (D // n_dp) + feature // n_dp).astype(LOW)

    def mixed(vector):
        return vector.reshape(n_row, n_col, width).transpose(1, 0, 2).reshape(D)

    def plain(vector):
        return vector.reshape(n_col, n_row, width).transpose(1, 0, 2).reshape(D)

    def to_owner(rows, parts):
        return rows.reshape(shard_rows, parts, -1).transpose(1, 0, 2)

    def gathered(blocks):
        flat = blocks.reshape(n_row * shard_rows, blocks.shape[2])
        return dot(order, lax.all_gather(flat, "dp", axis=0, tiled=True), 1, 0, LOW)

    def scattered(gradient):
        n = gradient.shape[1]
        rows = dot(order, gradient.astype(LOW), 0, 0, LOW)
        summed = lax.psum_scatter(rows, "dp", scatter_dimension=0, tiled=True)
        blocks = exchange_rows(summed.reshape(n_row, shard_rows, n))
        return blocks.astype(jnp.float32)

    def widened(blocks):
        return blocks.transpose(1, 0, 2).reshape(shard_rows, -1)

    x_all = gather_eight(inputs.T)
    w_qkv = gathered(exchange_rows(to_owner(qkv_master[:, 0].astype(LOW), n_row)))
    rest = jnp.concatenate(
        [
            to_owner(out_master[:, :, 0].T.astype(LOW), n_row),
            to_owner(up_master[:, 0].astype(LOW), n_row),
            to_owner(down_master[:, :, 0].T.astype(LOW), n_row),
        ],
        axis=2,
    )
    w_rest = gathered(exchange_rows(rest))
    w_out = w_rest[:, :width]
    w_up = w_rest[:, width : width + hidden_width]
    w_down = w_rest[:, width + hidden_width :]
    cot_all = gather_eight(cotangent.T)

    gain_one = mixed(norm_gains[0])
    gain_two = mixed(norm_gains[1])
    shift_one = mixed(biases[:D])
    shift_two = mixed(biases[D : 2 * D])
    query_bias = lax.dynamic_slice_in_dim(biases, 2 * D + own * width, width).reshape(heads, HEAD)
    value_bias = lax.dynamic_slice_in_dim(biases, 3 * D + own * width, width).reshape(heads, HEAD)
    out_bias = mixed(biases[4 * D : 5 * D])
    feature_start = (row * n_col + core) * width
    down_bias = lax.dynamic_slice_in_dim(biases, 5 * D + feature_start, width)
    up_bias = lax.dynamic_slice_in_dim(biases, 6 * D + own * hidden_width, hidden_width)
    qkv_bias = jnp.stack([query_bias, jnp.zeros_like(query_bias), value_bias], axis=1).reshape(
        3 * width, 1
    )

    x_full = x_all.astype(jnp.float32)
    center = x_full - jnp.sum(x_full, axis=0, keepdims=True) / D
    inverse_one = lax.rsqrt(jnp.sum(center * center, axis=0, keepdims=True) / D + NORM_EPS)
    za = (center * inverse_one * gain_one[:, None] + shift_one[:, None]).astype(LOW)

    qkv = (dot(w_qkv, za, 0, 0) + qkv_bias).astype(LOW).reshape(heads, 3, HEAD, tokens)
    queries, key_rows, values = qkv[:, 0], qkv[:, 1], qkv[:, 2]
    attended, log_total = attend_forward(queries, key_rows, values)
    attended = jnp.pad(attended.reshape(width, tokens), ((0, 0), (0, padded - tokens)))

    half = padded // n_col
    branch = reduce_eight(
        lambda c: dot(lax.dynamic_slice_in_dim(attended, c * half, half, axis=1), w_out, 0, 1)
    )
    token_start = own * chunk
    mine = (
        lax.broadcasted_iota(jnp.int32, (chunk, tokens), 1)
        == lax.broadcasted_iota(jnp.int32, (chunk, tokens), 0) + token_start
    ).astype(LOW)
    middle = dot(mine, x_all, 1, 1) + branch + out_bias[None, :]
    center = middle - jnp.sum(middle, axis=1, keepdims=True) / D
    inverse_two = lax.rsqrt(jnp.sum(center * center, axis=1, keepdims=True) / D + NORM_EPS)
    normed_two = center * inverse_two
    zb = gather_eight((normed_two * gain_two + shift_two).astype(LOW))

    hidden = dot(zb, w_up, 1, 0) + up_bias
    active_grad = dot(
        jnp.pad(cot_all, ((0, 0), (0, padded - tokens))), w_down, 0, 0
    )
    active, gelu_pullback = jax.vjp(lambda v: jax.nn.gelu(v, approximate=True), hidden)
    active = active.astype(LOW)
    hidden_grad = gelu_pullback(active_grad)[0].astype(LOW)

    two_grad = reduce_eight(lambda c: dot(take(hidden_grad, c, half), w_up, 1, 1))
    cot_mine = dot(mine, cot_all, 1, 1)
    scaled = two_grad * gain_two
    first_sum = jnp.sum(scaled, axis=1, keepdims=True) / D
    second_sum = jnp.sum(scaled * normed_two, axis=1, keepdims=True) / D
    middle_grad = cot_mine + inverse_two * (scaled - first_sum - normed_two * second_sum)
    branch_all = gather_eight(middle_grad.astype(LOW))
    gain_two_grad = jnp.sum(two_grad * normed_two, axis=0)
    shift_two_grad = jnp.sum(two_grad, axis=0)
    out_bias_grad = jnp.sum(middle_grad.astype(LOW), axis=0, dtype=jnp.float32)
    down_bias_grad = jnp.sum(cot_mine, axis=0)
    up_bias_grad = jnp.sum(hidden_grad, axis=0, dtype=jnp.float32)

    attended_grad = dot(w_out, branch_all, 0, 1, LOW)[:, :tokens].reshape(heads, HEAD, tokens)
    qkv_grad = attend_backward(queries, key_rows, values, log_total, attended_grad)
    bias_sums = jnp.sum(qkv_grad, axis=3, dtype=jnp.float32)
    qkv_grad = qkv_grad.reshape(3 * width, tokens)
    qkv_blocks = scattered(dot(za, qkv_grad, 1, 1, LOW))

    one_part = dot(w_qkv, qkv_grad, 1, 0)
    normed_one = (x_full - jnp.sum(x_full, axis=0, keepdims=True) / D) * inverse_one
    gain_one_grad = jnp.sum(one_part * normed_one, axis=1)
    shift_one_grad = jnp.sum(one_part, axis=1)
    scaled_part = one_part * gain_one[:, None]
    sums = jnp.stack(
        [jnp.sum(scaled_part, axis=0), jnp.sum(scaled_part * normed_one, axis=0)], axis=0
    )
    sums = jnp.pad(sums, ((0, 14), (0, 0)))
    one_rows = one_part.reshape(n_col, n_row, width, tokens)
    one_rows = jnp.concatenate(
        [one_rows, jnp.broadcast_to(sums, (n_col, n_row, 16, tokens))], axis=2
    ).astype(LOW).reshape(n_col, n_row * (width + 16), tokens)
    one_grad = reduce_eight(
        lambda c: lax.dynamic_index_in_dim(one_rows, c, 0, keepdims=False).astype(jnp.float32)
    )
    own_gain = lax.dynamic_slice_in_dim(norm_gains[0], feature_start, width)[:, None]
    own_input = inputs.T.astype(jnp.float32)
    own_normed = (own_input - jnp.sum(x_full, axis=0, keepdims=True) / D) * inverse_one
    own_middle = lax.dynamic_slice_in_dim(branch_all, own * width, width, axis=1)[:tokens].T
    input_grad = own_middle.astype(jnp.float32) + inverse_one * (
        one_grad[:width] * own_gain
        - one_grad[width : width + 1] / D
        - own_normed * (one_grad[width + 1 : width + 2] / D)
    )
    input_grad = input_grad.astype(LOW).T

    down_half = lambda c: dot(take(w_down, c, D // n_col), active, 1, 1)[:, :tokens] + dot(
        lax.dynamic_slice_in_dim(middle, c * (D // n_col), D // n_col, axis=1),
        mine.astype(jnp.float32),
        0,
        0,
        precision=lax.Precision.HIGHEST,
    )
    result = (reduce_eight(down_half) + down_bias[:, None]).astype(LOW).T

    down_blocks = scattered(dot(jnp.pad(cot_all, ((0, 0), (0, padded - tokens))), active, 1, 0, LOW))
    up_blocks = scattered(dot(zb, hidden_grad, 0, 0, LOW))
    out_blocks = scattered(dot(branch_all, attended, 0, 1, LOW))

    gain_grad = jnp.stack([plain(gain_one_grad), plain(gain_two_grad)])
    zeros = jnp.zeros(biases.shape, jnp.float32)
    bias_grad = jnp.concatenate(
        [
            plain(shift_one_grad),
            plain(shift_two_grad),
            jnp.zeros((2 * D,), jnp.float32),
            plain(out_bias_grad),
            plain(down_bias_grad),
            jnp.zeros((FF,), jnp.float32),
        ]
    )
    bias_grad = lax.dynamic_update_slice_in_dim(
        bias_grad, bias_sums[:, 0].reshape(width), 2 * D + own * width, 0
    )
    bias_grad = lax.dynamic_update_slice_in_dim(
        bias_grad, bias_sums[:, 2].reshape(width), 3 * D + own * width, 0
    )
    bias_grad = lax.dynamic_update_slice_in_dim(
        bias_grad, up_bias_grad, 6 * D + own * hidden_width, 0
    )
    total = all_sum(jnp.concatenate([gain_grad.reshape(-1), bias_grad]))
    gain_total = total[: 2 * D].reshape(2, D)
    bias_total = total[2 * D :]

    q_new = adam_update(
        qkv_master, qkv_first, qkv_second, widened(qkv_blocks)[:, None], 0.03, 0.1
    )
    o_new = adam_update(
        out_master, out_first, out_second, widened(out_blocks).T[:, :, None], 0.12, 0.1
    )
    u_new = adam_update(up_master, up_first, up_second, widened(up_blocks)[:, None], 0.03, 0.1)
    d_new = adam_update(
        down_master, down_first, down_second, widened(down_blocks).T[:, :, None], 0.02, 0.1
    )
    g_new = adam_update(norm_gains, gain_first, gain_second, gain_total, 0.5, 0.0)
    b_new = adam_update(biases, bias_first, bias_second, bias_total, 0.5, 0.0)
    return (result, input_grad, *q_new, *o_new, *u_new, *d_new, *g_new, *b_new)


def solution(mesh):
    token_spec = P("dp", ("row", "col"))
    wide = P("row", "dp", "col")
    tall = P("col", "row", "dp")
    return jax.shard_map(
        shards,
        mesh=mesh,
        in_specs=(token_spec,) * 2 + (wide, tall, wide, tall) * 3 + (P(),) * 6,
        out_specs=(token_spec,) * 2
        + (wide,) * 3
        + (tall,) * 3
        + (wide,) * 3
        + (tall,) * 3
        + (P(),) * 6,
        check_vma=False,
    )
```

```python
import jax
import jax.numpy as jnp
from jax import lax
from jax.sharding import PartitionSpec as P

D = 1152
FF = 4304
HEAD = 72
SEQ = 729
STEP = 10

NORM_EPS = 1e-06
ADAM_EPS = 1e-08
BETA_ONE = 0.9
BETA_TWO = 0.999
LOW = jnp.bfloat16


def dot(left, right, left_dim, right_dim, out=jnp.float32, precision=None):
    return lax.dot_general(
        left,
        right,
        (((left_dim,), (right_dim,)), ((), ())),
        precision=precision,
        preferred_element_type=out,
    )


def take(array, index, size):
    return lax.dynamic_slice_in_dim(array, index * size, size, axis=0)


def swap_cores(array):
    n_col = lax.axis_size("col")
    return lax.ppermute(array, "col", [(i, (i + 1) % n_col) for i in range(n_col)])


def gather_eight(block):
    rows = lax.all_gather(block, "row", axis=0, tiled=True)
    return lax.all_gather(rows, "col", axis=0, tiled=True)


def send_copies(block, axis):
    copies = jnp.broadcast_to(block, (lax.axis_size(axis),) + block.shape)
    return lax.all_to_all(copies, axis, 0, 0).reshape(-1, block.shape[1])


def zero_of(array):
    first = lax.slice(array, (0,) * array.ndim, (1,) * array.ndim)
    return first.reshape(()).astype(jnp.float32) * 0.0


def sum_over_rows(half):
    n_row = lax.axis_size("row")
    blocks = half.astype(LOW).reshape(n_row, half.shape[0] // n_row, half.shape[1])
    return jnp.sum(lax.all_to_all(blocks, "row", 0, 0).astype(jnp.float32), axis=0)


def reduce_eight(product):
    core = lax.axis_index("col")
    theirs = product(1 - core).astype(LOW)
    got = swap_cores(theirs)
    mine = product(core)
    return sum_over_rows(mine + got.astype(jnp.float32))


def exchange_rows(blocks):
    return lax.all_to_all(blocks, "row", 0, 0)


def all_sum(vector):
    for axis in ("col", "row", "dp"):
        size = lax.axis_size(axis)
        if size & (size - 1) or size > 4:
            vector = lax.psum(vector, axis)
            continue
        step = 1
        while step < size:
            vector = vector + lax.ppermute(vector, axis, [(i, i ^ step) for i in range(size)])
            step *= 2
    return vector


def attend_forward(queries, key_rows, values):
    scores = (
        jnp.einsum("hdq,hdk->hqk", queries, key_rows, preferred_element_type=jnp.float32)
        * HEAD ** (-0.5)
    )
    row_max = jnp.max(scores, axis=2, keepdims=True)
    exponent = jnp.exp(scores - row_max)
    row_total = jnp.sum(exponent, axis=2, keepdims=True)
    probs_low = (exponent / row_total).astype(LOW)
    attended = jnp.einsum("hqk,hdk->hdq", probs_low, values, preferred_element_type=jnp.float32)
    return attended.astype(LOW), row_max + jnp.log(row_total)


def attend_backward(queries, key_rows, values, log_total, attended_grad):
    scale = HEAD ** (-0.5)
    scores = (
        jnp.einsum("hdq,hdk->hqk", queries, key_rows, preferred_element_type=jnp.float32) * scale
    )
    probs = jnp.exp(scores - log_total)
    probs_low = probs.astype(LOW)
    value_grad = jnp.einsum(
        "hqk,hdq->hdk", probs_low, attended_grad, preferred_element_type=jnp.float32
    )
    probs_grad = jnp.einsum(
        "hdq,hdk->hqk", attended_grad, values, preferred_element_type=jnp.float32
    )
    inner = jnp.sum(probs * probs_grad, axis=2, keepdims=True)
    scores_grad = (probs * (probs_grad - inner)).astype(LOW)
    query_grad = (
        jnp.einsum("hqk,hdk->hdq", scores_grad, key_rows, preferred_element_type=jnp.float32)
        * scale
    )
    key_grad = (
        jnp.einsum("hqk,hdq->hdk", scores_grad, queries, preferred_element_type=jnp.float32) * scale
    )
    return jnp.stack([query_grad, key_grad, value_grad], axis=1).astype(LOW)


def adam_update(weights, moment_one, second, gradient, step_rate, weight_decay):
    moment_one = BETA_ONE * moment_one + (1.0 - BETA_ONE) * gradient
    second = BETA_TWO * second + (1.0 - BETA_TWO) * gradient * gradient
    direction = (
        moment_one / (1.0 - BETA_ONE**STEP) / (jnp.sqrt(second / (1.0 - BETA_TWO**STEP)) + ADAM_EPS)
    )
    return (weights - step_rate * (direction + weight_decay * weights), moment_one, second)


def shards(
    inputs,
    cotangent,
    qkv_master,
    out_master,
    up_master,
    down_master,
    qkv_first,
    out_first,
    up_first,
    down_first,
    qkv_second,
    out_second,
    up_second,
    down_second,
    norm_gains,
    gain_first,
    gain_second,
    biases,
    bias_first,
    bias_second,
):
    tokens, width = inputs.shape
    n_row = lax.axis_size("row")
    n_col = lax.axis_size("col")
    n_dp = lax.axis_size("dp")
    row = lax.axis_index("row")
    core = lax.axis_index("col")
    group = n_row * n_col
    heads = width // HEAD
    hidden_width = FF // group
    own = core * n_row + row
    chunk = -(-tokens // (group * 16)) * 16
    padded = chunk * group
    shard_rows = qkv_master.shape[0]

    place = lax.broadcasted_iota(jnp.int32, (D, D), 0)
    source = lax.broadcasted_iota(jnp.int32, (D, D), 1)
    feature = (
        ((place // width) % n_row) * n_col + place // (width * n_row)
    ) * width + place % width
    order = lax.optimization_barrier(
        (source == (feature % n_dp) * (D // n_dp) + feature // n_dp).astype(LOW)
    )

    def mixed(vector):
        return vector.reshape(n_row, n_col, width).transpose(1, 0, 2).reshape(D)

    def plain(vector):
        return vector.reshape(n_col, n_row, width).transpose(1, 0, 2).reshape(D)

    def dealt(vector):
        return vector.reshape(D // n_dp, n_dp).T.reshape(D)

    def undealt(vector):
        return vector.reshape(n_dp, D // n_dp).T.reshape(D)

    def to_owner(rows, parts):
        return rows.reshape(shard_rows, parts, -1).transpose(1, 0, 2)

    def scattered(gradient):
        n = gradient.shape[1]
        blocks = lax.all_to_all(gradient.reshape(n_dp, D // n_dp, n), "dp", 0, 0)
        summed = jnp.sum(blocks.astype(jnp.float32), axis=0).astype(LOW)
        return exchange_rows(summed.reshape(n_row, shard_rows, n)).astype(jnp.float32)

    def widened(blocks):
        return blocks.transpose(1, 0, 2).reshape(shard_rows, -1)

    qkv_rows = exchange_rows(to_owner(qkv_master[:, 0].astype(LOW), n_row))
    x_all = gather_eight(inputs.T)
    w_qkv = send_copies(qkv_rows.reshape(D // n_dp, -1), "dp")
    rest = jnp.concatenate(
        [
            to_owner(out_master[:, :, 0].T.astype(LOW), n_row),
            to_owner(up_master[:, 0].astype(LOW), n_row),
            to_owner(down_master[:, :, 0].T.astype(LOW), n_row),
        ],
        axis=2,
    )
    rest = exchange_rows(rest).reshape(D // n_dp, -1)
    w_out = send_copies(rest[:, :width], "dp")
    cot_rows = send_copies(cotangent.T, "row")
    w_up = send_copies(rest[:, width : width + hidden_width], "dp")
    w_down = send_copies(rest[:, width + hidden_width :], "dp")

    gain_one = mixed(norm_gains[0])
    gain_two = dealt(norm_gains[1])
    shift_one = mixed(biases[:D])
    shift_two = dealt(biases[D : 2 * D])
    query_bias = lax.dynamic_slice_in_dim(biases, 2 * D + own * width, width).reshape(heads, HEAD)
    value_bias = lax.dynamic_slice_in_dim(biases, 3 * D + own * width, width).reshape(heads, HEAD)
    out_bias = dealt(biases[4 * D : 5 * D])
    feature_start = (row * n_col + core) * width
    down_bias = lax.dynamic_slice_in_dim(biases, 5 * D + feature_start, width)
    up_bias = lax.dynamic_slice_in_dim(biases, 6 * D + own * hidden_width, hidden_width)
    qkv_bias = jnp.stack([query_bias, jnp.zeros_like(query_bias), value_bias], axis=1).reshape(
        3 * width, 1
    )

    x_full = x_all.astype(jnp.float32)
    x_mean = jnp.sum(x_full, axis=0, keepdims=True) / D
    center = x_full - x_mean
    inverse_one = lax.rsqrt(jnp.sum(center * center, axis=0, keepdims=True) / D + NORM_EPS)
    za = (center * inverse_one * gain_one[:, None] + shift_one[:, None]).astype(LOW)
    za = dot(order, za, 0, 0, LOW)
    token_start = own * chunk
    mine = (
        lax.broadcasted_iota(jnp.int32, (chunk, tokens), 1)
        == lax.broadcasted_iota(jnp.int32, (chunk, tokens), 0) + token_start
    ).astype(LOW)
    x_mine = dot(dot(mine, x_all, 1, 1, LOW), order, 1, 0)

    qkv = (dot(w_qkv, za, 0, 0) + qkv_bias).astype(LOW).reshape(heads, 3, HEAD, tokens)
    queries, key_rows, values = qkv[:, 0], qkv[:, 1], qkv[:, 2]
    attended, log_total = attend_forward(queries, key_rows, values)
    attended = jnp.pad(attended.reshape(width, tokens), ((0, 0), (0, padded - tokens)))

    half = padded // n_col
    branch = reduce_eight(
        lambda c: dot(lax.dynamic_slice_in_dim(attended, c * half, half, axis=1), w_out, 0, 1)
        + zero_of(cot_rows)
    )

    cot_all = lax.all_gather(cot_rows, "col", axis=0, tiled=True)
    cot_all = jnp.pad(cot_all, ((0, 0), (0, padded - tokens)))
    cot_dealt = dot(order, cot_all, 0, 0, LOW)
    active_grad = dot(cot_dealt, w_down, 0, 0)
    cot_mine = dot(mine, cot_dealt[:, :tokens], 1, 1)
    qkv_mixed = dot(order, w_qkv, 1, 0, LOW)
    down_mixed = dot(order, w_down, 1, 0, LOW)

    middle = x_mine + branch + out_bias[None, :]
    center = middle - jnp.sum(middle, axis=1, keepdims=True) / D
    inverse_two = lax.rsqrt(jnp.sum(center * center, axis=1, keepdims=True) / D + NORM_EPS)
    normed_two = center * inverse_two
    zb = gather_eight((normed_two * gain_two + shift_two).astype(LOW))

    hidden = dot(zb, w_up, 1, 0) + up_bias
    active, gelu_pullback = jax.vjp(lambda v: jax.nn.gelu(v, approximate=True), hidden)
    active = active.astype(LOW)
    hidden_grad = gelu_pullback(active_grad)[0].astype(LOW)

    two_grad = reduce_eight(lambda c: dot(take(hidden_grad, c, half), w_up, 1, 1))
    down_blocks = scattered(dot(cot_dealt, active, 1, 0, LOW))
    up_blocks = scattered(dot(zb, hidden_grad, 0, 0, LOW))

    scaled = two_grad * gain_two
    first_sum = jnp.sum(scaled, axis=1, keepdims=True) / D
    second_sum = jnp.sum(scaled * normed_two, axis=1, keepdims=True) / D
    middle_grad = cot_mine + inverse_two * (scaled - first_sum - normed_two * second_sum)
    branch_all = gather_eight(middle_grad.astype(LOW))

    attended_grad = dot(w_out, branch_all, 0, 1, LOW)[:, :tokens].reshape(heads, HEAD, tokens)
    qkv_grad = attend_backward(queries, key_rows, values, log_total, attended_grad)
    qkv_grad = qkv_grad.reshape(3 * width, tokens)
    qkv_blocks = scattered(dot(za, qkv_grad, 1, 1, LOW))

    one_part = dot(qkv_mixed, qkv_grad, 1, 0)
    normed_one = (x_full - x_mean) * inverse_one
    scaled_part = one_part * gain_one[:, None]
    sums = jnp.stack(
        [jnp.sum(scaled_part, axis=0), jnp.sum(scaled_part * normed_one, axis=0)], axis=0
    )
    sums = jnp.pad(sums, ((0, 14), (0, 0)))
    one_rows = one_part.reshape(n_col, n_row, width, tokens)
    one_rows = jnp.concatenate(
        [one_rows, jnp.broadcast_to(sums, (n_col, n_row, 16, tokens))], axis=2
    ).astype(LOW).reshape(n_col, n_row * (width + 16), tokens)
    one_grad = reduce_eight(
        lambda c: lax.dynamic_index_in_dim(one_rows, c, 0, keepdims=False).astype(jnp.float32)
    )
    own_gain = lax.dynamic_slice_in_dim(norm_gains[0], feature_start, width)[:, None]
    own_normed = (inputs.T.astype(jnp.float32) - x_mean) * inverse_one
    own_order = lax.dynamic_slice_in_dim(order, own * width, width, axis=0)
    own_middle = dot(own_order, branch_all, 1, 1)[:, :tokens]
    input_grad = own_middle + inverse_one * (
        one_grad[:width] * own_gain
        - one_grad[width : width + 1] / D
        - own_normed * (one_grad[width + 1 : width + 2] / D)
    )
    input_grad = input_grad.astype(LOW).T

    later = zero_of(branch_all)
    middle_mixed = dot(middle, order.astype(jnp.float32), 1, 1, precision=lax.Precision.HIGHEST)
    down_half = lambda c: dot(take(down_mixed, c, D // n_col), active, 1, 1)[:, :tokens] + dot(
        lax.dynamic_slice_in_dim(middle_mixed, c * (D // n_col), D // n_col, axis=1) + later,
        mine.astype(jnp.float32),
        0,
        0,
        precision=lax.Precision.HIGHEST,
    )
    result = (reduce_eight(down_half) + down_bias[:, None]).astype(LOW).T

    out_blocks = scattered(dot(branch_all, attended, 0, 1, LOW))

    bias_sums = jnp.sum(qkv_grad, axis=1, dtype=jnp.float32).reshape(heads, 3, HEAD)
    gain_one_grad = jnp.sum(one_part * normed_one, axis=1)
    shift_one_grad = jnp.sum(one_part, axis=1)
    gain_two_grad = jnp.sum(two_grad * normed_two, axis=0)
    shift_two_grad = jnp.sum(two_grad, axis=0)
    out_bias_grad = jnp.sum(middle_grad.astype(LOW), axis=0, dtype=jnp.float32)
    down_bias_grad = jnp.sum(cot_mine, axis=0)
    up_bias_grad = jnp.sum(hidden_grad, axis=0, dtype=jnp.float32)
    bias_grad = jnp.concatenate(
        [
            plain(gain_one_grad),
            undealt(gain_two_grad),
            plain(shift_one_grad),
            undealt(shift_two_grad),
            jnp.zeros((2 * D,), jnp.float32),
            undealt(out_bias_grad),
            undealt(down_bias_grad),
            jnp.zeros((FF,), jnp.float32),
        ]
    )
    for piece, offset in (
        (bias_sums[:, 0].reshape(width), 4 * D + own * width),
        (bias_sums[:, 2].reshape(width), 5 * D + own * width),
        (up_bias_grad, 8 * D + own * hidden_width),
    ):
        bias_grad = lax.dynamic_update_slice_in_dim(bias_grad, piece, offset, 0)
    total = all_sum(bias_grad)
    gain_total = total[: 2 * D].reshape(2, D)
    bias_total = total[2 * D :]

    later = zero_of(qkv_grad)
    q_new = adam_update(
        qkv_master, qkv_first, qkv_second, widened(qkv_blocks)[:, None], 0.03, 0.1
    )
    o_new = adam_update(
        out_master, out_first, out_second, widened(out_blocks + later).T[:, :, None], 0.12, 0.1
    )
    u_new = adam_update(
        up_master, up_first, up_second, widened(up_blocks + later)[:, None], 0.03, 0.1
    )
    d_new = adam_update(
        down_master, down_first, down_second, widened(down_blocks + later).T[:, :, None], 0.02, 0.1
    )
    g_new = adam_update(norm_gains, gain_first, gain_second, gain_total, 0.5, 0.0)
    b_new = adam_update(biases, bias_first, bias_second, bias_total, 0.5, 0.0)
    return (result, input_grad, *q_new, *o_new, *u_new, *d_new, *g_new, *b_new)


def solution(mesh):
    token_spec = P("dp", ("row", "col"))
    wide = P("row", "dp", "col")
    tall = P("col", "row", "dp")
    return jax.shard_map(
        shards,
        mesh=mesh,
        in_specs=(token_spec,) * 2 + (wide, tall, wide, tall) * 3 + (P(),) * 6,
        out_specs=(token_spec,) * 2
        + (wide,) * 3
        + (tall,) * 3
        + (wide,) * 3
        + (tall,) * 3
        + (P(),) * 6,
        check_vma=False,
    )
```

```python
import jax
import jax.numpy as jnp
from jax import lax
from jax.sharding import PartitionSpec as P

D = 1152
FF = 4304
HEAD = 72
SEQ = 729
STEP = 10

NORM_EPS = 1e-06
ADAM_EPS = 1e-08
BETA_ONE = 0.9
BETA_TWO = 0.999
LOW = jnp.bfloat16


def dot(left, right, left_dim, right_dim, out=jnp.float32, precision=None):
    return lax.dot_general(
        left,
        right,
        (((left_dim,), (right_dim,)), ((), ())),
        precision=precision,
        preferred_element_type=out,
    )


def take(array, index, size):
    return lax.dynamic_slice_in_dim(array, index * size, size, axis=0)


def swap_cores(array):
    n_col = lax.axis_size("col")
    return lax.ppermute(array, "col", [(i, (i + 1) % n_col) for i in range(n_col)])


def gather_eight(block):
    rows = lax.all_gather(block, "row", axis=0, tiled=True)
    pieces = [
        lax.all_gather(piece, "col", axis=0) for piece in jnp.split(rows, 2, axis=0)
    ]
    return jnp.concatenate(pieces, axis=1).reshape(-1, block.shape[1])


def send_copies(block, axis):
    copies = jnp.broadcast_to(block, (lax.axis_size(axis),) + block.shape)
    return lax.all_to_all(copies, axis, 0, 0).reshape(-1, block.shape[1])


def zero_of(array):
    first = lax.slice(array, (0,) * array.ndim, (1,) * array.ndim)
    return first.reshape(()).astype(jnp.float32) * 0.0


def sum_over_rows(half):
    summed = lax.psum_scatter(half.astype(LOW), "row", scatter_dimension=0, tiled=True)
    return summed.astype(jnp.float32)


def reduce_eight(product):
    core = lax.axis_index("col")
    theirs = product(1 - core).astype(LOW)
    got = swap_cores(theirs)
    mine = product(core)
    return sum_over_rows(mine + got.astype(jnp.float32))


def exchange_rows(blocks):
    return lax.all_to_all(blocks, "row", 0, 0)


def all_sum(vector):
    for axis in ("col", "row", "dp"):
        size = lax.axis_size(axis)
        if size & (size - 1) or size > 4:
            vector = lax.psum(vector, axis)
            continue
        step = 1
        while step < size:
            vector = vector + lax.ppermute(vector, axis, [(i, i ^ step) for i in range(size)])
            step *= 2
    return vector


def attend_forward(queries, key_rows, values):
    scores = (
        jnp.einsum("hdq,hdk->hqk", queries, key_rows, preferred_element_type=jnp.float32)
        * HEAD ** (-0.5)
    )
    row_max = jnp.max(scores, axis=2, keepdims=True)
    exponent = jnp.exp(scores - row_max)
    row_total = jnp.sum(exponent, axis=2, keepdims=True)
    probs_low = (exponent / row_total).astype(LOW)
    attended = jnp.einsum("hqk,hdk->hdq", probs_low, values, preferred_element_type=jnp.float32)
    return attended.astype(LOW), row_max + jnp.log(row_total)


def attend_backward(queries, key_rows, values, log_total, attended_grad):
    scale = HEAD ** (-0.5)
    scores = (
        jnp.einsum("hdq,hdk->hqk", queries, key_rows, preferred_element_type=jnp.float32) * scale
    )
    probs = jnp.exp(scores - log_total)
    probs_low = probs.astype(LOW)
    value_grad = jnp.einsum(
        "hqk,hdq->hdk", probs_low, attended_grad, preferred_element_type=jnp.float32
    )
    probs_grad = jnp.einsum(
        "hdq,hdk->hqk", attended_grad, values, preferred_element_type=jnp.float32
    )
    inner = jnp.sum(probs * probs_grad, axis=2, keepdims=True)
    scores_grad = (probs * (probs_grad - inner)).astype(LOW)
    query_grad = (
        jnp.einsum("hqk,hdk->hdq", scores_grad, key_rows, preferred_element_type=jnp.float32)
        * scale
    )
    key_grad = (
        jnp.einsum("hqk,hdq->hdk", scores_grad, queries, preferred_element_type=jnp.float32) * scale
    )
    return jnp.stack([query_grad, key_grad, value_grad], axis=1).astype(LOW)


def adam_update(weights, moment_one, second, gradient, step_rate, weight_decay):
    moment_one = BETA_ONE * moment_one + (1.0 - BETA_ONE) * gradient
    second = BETA_TWO * second + (1.0 - BETA_TWO) * gradient * gradient
    direction = (
        moment_one / (1.0 - BETA_ONE**STEP) / (jnp.sqrt(second / (1.0 - BETA_TWO**STEP)) + ADAM_EPS)
    )
    return (weights - step_rate * (direction + weight_decay * weights), moment_one, second)


def shards(
    inputs,
    cotangent,
    qkv_master,
    out_master,
    up_master,
    down_master,
    qkv_first,
    out_first,
    up_first,
    down_first,
    qkv_second,
    out_second,
    up_second,
    down_second,
    norm_gains,
    gain_first,
    gain_second,
    biases,
    bias_first,
    bias_second,
):
    tokens, width = inputs.shape
    n_row = lax.axis_size("row")
    n_col = lax.axis_size("col")
    n_dp = lax.axis_size("dp")
    row = lax.axis_index("row")
    core = lax.axis_index("col")
    group = n_row * n_col
    heads = width // HEAD
    hidden_width = FF // group
    own = core * n_row + row
    chunk = -(-tokens // (group * 16)) * 16
    padded = chunk * group
    shard_rows = qkv_master.shape[0]

    place = lax.broadcasted_iota(jnp.int32, (D, D), 0)
    source = lax.broadcasted_iota(jnp.int32, (D, D), 1)
    feature = (
        ((place // width) % n_row) * n_col + place // (width * n_row)
    ) * width + place % width
    order = lax.optimization_barrier(
        (source == (feature % n_dp) * (D // n_dp) + feature // n_dp).astype(LOW)
    )

    def mixed(vector):
        return vector.reshape(n_row, n_col, width).transpose(1, 0, 2).reshape(D)

    def plain(vector):
        return vector.reshape(n_col, n_row, width).transpose(1, 0, 2).reshape(D)

    def dealt(vector):
        return vector.reshape(D // n_dp, n_dp).T.reshape(D)

    def undealt(vector):
        return vector.reshape(n_dp, D // n_dp).T.reshape(D)

    def to_owner(rows, parts):
        return rows.reshape(shard_rows, parts, -1).transpose(1, 0, 2)

    def scattered(gradient):
        return lax.psum_scatter(gradient, "dp", scatter_dimension=0, tiled=True)

    def scattered_now(gradient):
        blocks = lax.all_to_all(gradient.reshape(n_dp, D // n_dp, -1), "dp", 0, 0)
        return jnp.sum(blocks.astype(jnp.float32), axis=0).astype(LOW)

    def returned(rows):
        blocks = exchange_rows(rows.reshape(n_row, shard_rows, -1))
        return blocks.astype(jnp.float32)

    def widened(blocks):
        return blocks.transpose(1, 0, 2).reshape(shard_rows, -1)

    qkv_rows = exchange_rows(to_owner(qkv_master[:, 0].astype(LOW), n_row))
    x_all = gather_eight(inputs.T)
    w_qkv = send_copies(qkv_rows.reshape(D // n_dp, -1), "dp")
    rest = jnp.concatenate(
        [
            to_owner(out_master[:, :, 0].T.astype(LOW), n_row),
            to_owner(up_master[:, 0].astype(LOW), n_row),
            to_owner(down_master[:, :, 0].T.astype(LOW), n_row),
        ],
        axis=2,
    )
    rest = exchange_rows(rest).reshape(D // n_dp, -1)
    w_out = lax.all_gather(rest[:, :width], "dp", axis=0, tiled=True)
    w_up = lax.all_gather(rest[:, width : width + hidden_width], "dp", axis=0, tiled=True)
    w_down = lax.all_gather(rest[:, width + hidden_width :], "dp", axis=0, tiled=True)
    cot_all = lax.all_gather(cotangent.T, ("row", "col"), axis=0, tiled=True)

    gain_one = mixed(norm_gains[0])
    gain_two = dealt(norm_gains[1])
    shift_one = mixed(biases[:D])
    shift_two = dealt(biases[D : 2 * D])
    query_bias = lax.dynamic_slice_in_dim(biases, 2 * D + own * width, width).reshape(heads, HEAD)
    value_bias = lax.dynamic_slice_in_dim(biases, 3 * D + own * width, width).reshape(heads, HEAD)
    out_bias = dealt(biases[4 * D : 5 * D])
    feature_start = (row * n_col + core) * width
    down_bias = lax.dynamic_slice_in_dim(biases, 5 * D + feature_start, width)
    up_bias = lax.dynamic_slice_in_dim(biases, 6 * D + own * hidden_width, hidden_width)
    qkv_bias = jnp.stack([query_bias, jnp.zeros_like(query_bias), value_bias], axis=1).reshape(
        3 * width, 1
    )

    x_full = x_all.astype(jnp.float32)
    x_mean = jnp.sum(x_full, axis=0, keepdims=True) / D
    center = x_full - x_mean
    inverse_one = lax.rsqrt(jnp.sum(center * center, axis=0, keepdims=True) / D + NORM_EPS)
    za = (center * inverse_one * gain_one[:, None] + shift_one[:, None]).astype(LOW)
    za = dot(order, za, 0, 0, LOW)
    token_start = own * chunk
    mine = (
        lax.broadcasted_iota(jnp.int32, (chunk, tokens), 1)
        == lax.broadcasted_iota(jnp.int32, (chunk, tokens), 0) + token_start
    ).astype(LOW)
    x_mine = dot(dot(mine, x_all, 1, 1, LOW), order, 1, 0)

    qkv = (dot(w_qkv, za, 0, 0) + qkv_bias).astype(LOW).reshape(heads, 3, HEAD, tokens)
    queries, key_rows, values = qkv[:, 0], qkv[:, 1], qkv[:, 2]
    attended, log_total = attend_forward(queries, key_rows, values)
    attended = jnp.pad(attended.reshape(width, tokens), ((0, 0), (0, padded - tokens)))

    half = padded // n_col
    branch = reduce_eight(
        lambda c: dot(lax.dynamic_slice_in_dim(attended, c * half, half, axis=1), w_out, 0, 1)
    )

    cot_all = jnp.pad(cot_all, ((0, 0), (0, padded - tokens)))
    cot_all = cot_all.reshape(n_row, n_col, width, padded).transpose(1, 0, 2, 3).reshape(D, padded)
    cot_dealt = dot(order, cot_all, 0, 0, LOW)
    active_grad = dot(cot_dealt, w_down, 0, 0)
    cot_mine = dot(mine, cot_dealt[:, :tokens], 1, 1)
    qkv_mixed = dot(order, w_qkv, 1, 0, LOW)
    down_mixed = dot(order, w_down, 1, 0, LOW)

    middle = x_mine + branch + out_bias[None, :]
    center = middle - jnp.sum(middle, axis=1, keepdims=True) / D
    inverse_two = lax.rsqrt(jnp.sum(center * center, axis=1, keepdims=True) / D + NORM_EPS)
    normed_two = center * inverse_two
    zb = gather_eight((normed_two * gain_two + shift_two).astype(LOW))

    hidden = dot(zb, w_up, 1, 0) + up_bias
    active, gelu_pullback = jax.vjp(lambda v: jax.nn.gelu(v, approximate=True), hidden)
    active = active.astype(LOW)
    hidden_grad = gelu_pullback(active_grad)[0].astype(LOW)

    two_grad = reduce_eight(lambda c: dot(take(hidden_grad, c, half), w_up, 1, 1))
    down_rows = scattered(dot(cot_dealt, active, 1, 0, LOW))
    up_rows = scattered(dot(zb, hidden_grad, 0, 0, LOW))

    scaled = two_grad * gain_two
    first_sum = jnp.sum(scaled, axis=1, keepdims=True) / D
    second_sum = jnp.sum(scaled * normed_two, axis=1, keepdims=True) / D
    middle_grad = cot_mine + inverse_two * (scaled - first_sum - normed_two * second_sum)
    branch_all = gather_eight(middle_grad.astype(LOW))

    attended_grad = dot(w_out, branch_all, 0, 1, LOW)[:, :tokens].reshape(heads, HEAD, tokens)
    qkv_grad = attend_backward(queries, key_rows, values, log_total, attended_grad)
    qkv_grad = qkv_grad.reshape(3 * width, tokens)
    qkv_rows = scattered_now(dot(za, qkv_grad, 1, 1, LOW))

    one_part = dot(qkv_mixed, qkv_grad, 1, 0)
    normed_one = (x_full - x_mean) * inverse_one
    scaled_part = one_part * gain_one[:, None]
    sums = jnp.stack(
        [jnp.sum(scaled_part, axis=0), jnp.sum(scaled_part * normed_one, axis=0)], axis=0
    )
    sums = jnp.pad(sums, ((0, 14), (0, 0)))
    one_rows = one_part.reshape(n_col, n_row, width, tokens)
    one_rows = jnp.concatenate(
        [one_rows, jnp.broadcast_to(sums, (n_col, n_row, 16, tokens))], axis=2
    ).astype(LOW).reshape(n_col, n_row * (width + 16), tokens)
    one_grad = reduce_eight(
        lambda c: lax.dynamic_index_in_dim(one_rows, c, 0, keepdims=False).astype(jnp.float32)
    )
    own_gain = lax.dynamic_slice_in_dim(norm_gains[0], feature_start, width)[:, None]
    own_normed = (inputs.T.astype(jnp.float32) - x_mean) * inverse_one
    own_order = lax.dynamic_slice_in_dim(order, own * width, width, axis=0)
    own_middle = dot(own_order, branch_all, 1, 1)[:, :tokens]
    input_grad = own_middle + inverse_one * (
        one_grad[:width] * own_gain
        - one_grad[width : width + 1] / D
        - own_normed * (one_grad[width + 1 : width + 2] / D)
    )
    input_grad = input_grad.astype(LOW).T

    later = zero_of(branch_all)
    middle_mixed = dot(middle, order.astype(jnp.float32), 1, 1, precision=lax.Precision.HIGHEST)
    down_half = lambda c: dot(take(down_mixed, c, D // n_col), active, 1, 1)[:, :tokens] + dot(
        lax.dynamic_slice_in_dim(middle_mixed, c * (D // n_col), D // n_col, axis=1) + later,
        mine.astype(jnp.float32),
        0,
        0,
        precision=lax.Precision.HIGHEST,
    )
    result = jnp.concatenate([down_half(c) for c in range(n_col)], axis=0).astype(LOW)
    result = lax.psum_scatter(result, "col", scatter_dimension=0, tiled=True)
    result = (sum_over_rows(result) + down_bias[:, None]).astype(LOW).T

    out_rows = scattered(dot(branch_all, attended, 0, 1, LOW))
    last = returned(jnp.concatenate([out_rows, qkv_rows], axis=1))
    out_blocks = last[:, :, :width]
    qkv_blocks = last[:, :, width:]

    bias_sums = jnp.sum(qkv_grad, axis=1, dtype=jnp.float32).reshape(heads, 3, HEAD)
    gain_one_grad = jnp.sum(one_part * normed_one, axis=1)
    shift_one_grad = jnp.sum(one_part, axis=1)
    gain_two_grad = jnp.sum(two_grad * normed_two, axis=0)
    shift_two_grad = jnp.sum(two_grad, axis=0)
    out_bias_grad = jnp.sum(middle_grad.astype(LOW), axis=0, dtype=jnp.float32)
    down_bias_grad = jnp.sum(cot_mine, axis=0)
    up_bias_grad = jnp.sum(hidden_grad, axis=0, dtype=jnp.float32)
    bias_grad = jnp.concatenate(
        [
            plain(gain_one_grad),
            undealt(gain_two_grad),
            plain(shift_one_grad),
            undealt(shift_two_grad),
            jnp.zeros((2 * D,), jnp.float32),
            undealt(out_bias_grad),
            undealt(down_bias_grad),
            jnp.zeros((FF,), jnp.float32),
        ]
    )
    for piece, offset in (
        (bias_sums[:, 0].reshape(width), 4 * D + own * width),
        (bias_sums[:, 2].reshape(width), 5 * D + own * width),
        (up_bias_grad, 8 * D + own * hidden_width),
    ):
        bias_grad = lax.dynamic_update_slice_in_dim(bias_grad, piece, offset, 0)
    total = all_sum(bias_grad)
    gain_total = total[: 2 * D].reshape(2, D)
    bias_total = total[2 * D :]

    later = zero_of(qkv_grad)
    first = returned(jnp.concatenate([up_rows, down_rows], axis=1))
    up_blocks = first[:, :, :hidden_width]
    down_blocks = first[:, :, hidden_width:]
    q_new = adam_update(
        qkv_master, qkv_first, qkv_second, widened(qkv_blocks)[:, None], 0.03, 0.1
    )
    o_new = adam_update(
        out_master, out_first, out_second, widened(out_blocks).T[:, :, None], 0.12, 0.1
    )
    u_new = adam_update(
        up_master, up_first, up_second, widened(up_blocks + later)[:, None], 0.03, 0.1
    )
    d_new = adam_update(
        down_master, down_first, down_second, widened(down_blocks + later).T[:, :, None], 0.02, 0.1
    )
    g_new = adam_update(norm_gains, gain_first, gain_second, gain_total, 0.5, 0.0)
    b_new = adam_update(biases, bias_first, bias_second, bias_total, 0.5, 0.0)
    return (result, input_grad, *q_new, *o_new, *u_new, *d_new, *g_new, *b_new)


def solution(mesh):
    token_spec = P("dp", ("row", "col"))
    wide = P("row", "dp", "col")
    tall = P("col", "row", "dp")
    return jax.shard_map(
        shards,
        mesh=mesh,
        in_specs=(token_spec,) * 2 + (wide, tall, wide, tall) * 3 + (P(),) * 6,
        out_specs=(token_spec,) * 2
        + (wide,) * 3
        + (tall,) * 3
        + (wide,) * 3
        + (tall,) * 3
        + (P(),) * 6,
        check_vma=False,
    )
```

```python
import jax
import jax.numpy as jnp
from jax import lax
from jax.experimental import pallas as pl
from jax.experimental.pallas import tpu as pltpu
from jax.sharding import PartitionSpec as P

D = 1152
FF = 4304
HEAD = 72
SEQ = 729
STEP = 10

NORM_EPS = 1e-06
ADAM_EPS = 1e-08
BETA_ONE = 0.9
BETA_TWO = 0.999
LOW = jnp.bfloat16


def dot(left, right, left_dim, right_dim, out=jnp.float32, precision=None):
    return lax.dot_general(
        left,
        right,
        (((left_dim,), (right_dim,)), ((), ())),
        precision=precision,
        preferred_element_type=out,
    )


def take(array, index, size):
    return lax.dynamic_slice_in_dim(array, index * size, size, axis=0)


def swap_cores(array):
    n_col = lax.axis_size("col")
    return lax.ppermute(array, "col", [(i, (i + 1) % n_col) for i in range(n_col)])


def both_cores(rows):
    pieces = [
        lax.all_gather(piece, "col", axis=0) for piece in jnp.split(rows, 2, axis=0)
    ]
    return jnp.concatenate(pieces, axis=1).reshape(-1, rows.shape[1])


def send_copies(block, axis):
    copies = jnp.broadcast_to(block, (lax.axis_size(axis),) + block.shape)
    return lax.all_to_all(copies, axis, 0, 0).reshape(-1, block.shape[1])


def zero_of(array):
    first = lax.slice(array, (0,) * array.ndim, (1,) * array.ndim)
    return first.reshape(()).astype(jnp.float32) * 0.0


def exchange_rows(blocks):
    return lax.all_to_all(blocks, "row", 0, 0)


def all_sum(vector):
    for axis in ("col", "row", "dp"):
        size = lax.axis_size(axis)
        if size & (size - 1) or size > 4:
            vector = lax.psum(vector, axis)
            continue
        step = 1
        while step < size:
            vector = vector + lax.ppermute(vector, axis, [(i, i ^ step) for i in range(size)])
            step *= 2
    return vector


VMEM = pl.BlockSpec(memory_space=pltpu.VMEM)
SMEM = pl.BlockSpec(memory_space=pltpu.SMEM)
BIG = pltpu.CompilerParams(vmem_limit_bytes=56 * 1024 * 1024)


def head_probs(queries, key_rows):
    scores = dot(queries, key_rows, 0, 0) * HEAD ** (-0.5)
    scores = jnp.where(lax.broadcasted_iota(jnp.int32, scores.shape, 1) < SEQ, scores, -1e30)
    exponent = jnp.exp(scores - jnp.max(scores, axis=1, keepdims=True))
    return exponent * (1.0 / jnp.sum(exponent, axis=1, keepdims=True))


def split_cores(core, first, second, theirs_ref, mine_ref):
    @pl.when(core == 0)
    def _():
        mine_ref[...] = first
        theirs_ref[...] = second

    @pl.when(core != 0)
    def _():
        mine_ref[...] = second
        theirs_ref[...] = first


def attend_kernel(core_ref, w_ref, za_ref, bias_ref, out_ref, qkv_ref, att_ref, theirs_ref, mine_ref):
    qkv = dot(w_ref[...], za_ref[...], 0, 0) + bias_ref[...]
    heads = qkv_ref.shape[0]
    parts = []
    for head in range(heads):
        for t in range(3):
            start = (head * 3 + t) * HEAD
            qkv_ref[head, t] = qkv[start : start + HEAD].astype(LOW)
        probs = head_probs(qkv_ref[head, 0], qkv_ref[head, 1]).astype(LOW)
        parts.append(dot(qkv_ref[head, 2], probs, 1, 1))
    attended = jnp.concatenate(parts, axis=0).T.astype(LOW)
    att_ref[...] = attended
    branch = dot(attended, out_ref[...], 1, 1).astype(LOW)
    half = branch.shape[0] // 2
    split_cores(core_ref[0], branch[:half], branch[half:], theirs_ref, mine_ref)


def attend(core, w_qkv, za, qkv_bias, w_out):
    tokens = za.shape[1]
    width = w_out.shape[1]
    return pl.pallas_call(
        attend_kernel,
        in_specs=[SMEM, VMEM, VMEM, VMEM, VMEM],
        out_specs=[VMEM] * 4,
        out_shape=(
            jax.ShapeDtypeStruct((width // HEAD, 3, HEAD, tokens), LOW),
            jax.ShapeDtypeStruct((tokens, width), LOW),
            jax.ShapeDtypeStruct((tokens // 2, D), LOW),
            jax.ShapeDtypeStruct((tokens // 2, D), LOW),
        ),
        compiler_params=BIG,
        name="attend",
    )(core, w_qkv, za, qkv_bias, w_out)


def mlp_kernel(core_ref, zb_ref, up_ref, bias_ref, grad_ref, act_ref, hid_ref, two_ref, sum_ref):
    hidden = dot(zb_ref[...], up_ref[...], 1, 0) + bias_ref[...]
    square = hidden * hidden
    slope = 0.7978845608028654 * (1.0 + 0.044715 * square)
    bent = jnp.tanh(hidden * slope)
    gate = 0.5 * (1.0 + bent)
    act_ref[...] = (hidden * gate).astype(LOW)
    steep = gate + 0.5 * hidden * (1.0 - bent * bent) * (
        0.7978845608028654 * (1.0 + 3 * 0.044715 * square)
    )
    hidden_grad = (grad_ref[...] * steep).astype(LOW)
    hid_ref[...] = hidden_grad
    two_ref[...] = dot(hidden_grad, up_ref[...], 1, 1).astype(LOW)

    @pl.when(pl.program_id(0) == 0)
    def _():
        sum_ref[...] = jnp.zeros(sum_ref.shape, jnp.float32)

    sum_ref[...] += jnp.sum(hidden_grad.astype(jnp.float32), axis=0, keepdims=True)


def mlp(core, zb, w_up, up_bias, active_grad):
    tokens = zb.shape[0]
    wide = w_up.shape[1]
    steps = 6
    block = tokens // steps
    turned = lambda i, c: ((i + (steps // 2) * (1 - c[0])) % steps, 0)
    whole = lambda i, c: (0, 0)
    return pl.pallas_call(
        mlp_kernel,
        grid_spec=pltpu.PrefetchScalarGridSpec(
            num_scalar_prefetch=1,
            grid=(steps,),
            in_specs=[
                pl.BlockSpec((block, D), turned),
                pl.BlockSpec((D, wide), whole),
                pl.BlockSpec((1, wide), whole),
                pl.BlockSpec((block, wide), turned),
            ],
            out_specs=[
                pl.BlockSpec((block, wide), turned),
                pl.BlockSpec((block, wide), turned),
                pl.BlockSpec((block, D), lambda i, c: (i, 0)),
                pl.BlockSpec((1, wide), whole),
            ],
        ),
        out_shape=(
            jax.ShapeDtypeStruct((tokens, wide), LOW),
            jax.ShapeDtypeStruct((tokens, wide), LOW),
            jax.ShapeDtypeStruct((tokens, D), LOW),
            jax.ShapeDtypeStruct((1, wide), jnp.float32),
        ),
        compiler_params=BIG,
        name="mlp",
    )(core, zb, w_up, up_bias, active_grad)


def back_kernel(bg_ref, out_ref, qkv_ref, za_ref, att_ref, grad_ref, sum_ref, wq_ref, wo_ref):
    attended_grad = dot(bg_ref[...], out_ref[...], 1, 0).T
    scale = HEAD ** (-0.5)
    parts = []
    for head in range(qkv_ref.shape[0]):
        queries, key_rows, values = qkv_ref[head, 0], qkv_ref[head, 1], qkv_ref[head, 2]
        grad = attended_grad[head * HEAD : (head + 1) * HEAD].astype(LOW)
        probs = head_probs(queries, key_rows)
        probs_grad = dot(grad, values, 0, 0)
        inner = jnp.sum(probs * probs_grad, axis=1, keepdims=True)
        scores_grad = (probs * (probs_grad - inner)).astype(LOW)
        parts.append(dot(key_rows, scores_grad, 1, 1) * scale)
        parts.append(dot(queries, scores_grad, 1, 0) * scale)
        parts.append(dot(grad, probs.astype(LOW), 1, 0))
    qkv_grad = jnp.concatenate(parts, axis=0).astype(LOW)
    grad_ref[...] = qkv_grad
    sum_ref[...] = jnp.sum(qkv_grad.astype(jnp.float32), axis=1, keepdims=True)
    wq_ref[...] = dot(za_ref[...], qkv_grad, 1, 1).astype(LOW)
    wo_ref[...] = dot(bg_ref[...], att_ref[...], 0, 0).astype(LOW)


def attend_back(branch_all, w_out, qkv, za, attended):
    tokens = za.shape[1]
    width = w_out.shape[1]
    return pl.pallas_call(
        back_kernel,
        in_specs=[VMEM] * 5,
        out_specs=[VMEM] * 4,
        out_shape=(
            jax.ShapeDtypeStruct((3 * width, tokens), LOW),
            jax.ShapeDtypeStruct((3 * width, 1), jnp.float32),
            jax.ShapeDtypeStruct((D, 3 * width), LOW),
            jax.ShapeDtypeStruct((D, width), LOW),
        ),
        compiler_params=BIG,
        name="attend_back",
    )(branch_all, w_out, qkv, za, attended)


def first_kernel(core_ref, w_ref, grad_ref, x_ref, mean_ref, inv_ref, gain_ref, theirs_ref, mine_ref, sum_ref):
    n_row, rows, tokens = theirs_ref.shape
    width = rows - 16
    first = jnp.zeros((1, tokens), jnp.float32)
    second = jnp.zeros((1, tokens), jnp.float32)
    blocks = []
    for slot in range(D // width):
        here = slice(slot * width, (slot + 1) * width)
        part = dot(w_ref[here], grad_ref[...], 1, 0)
        normed = (x_ref[here].astype(jnp.float32) - mean_ref[...]) * inv_ref[...]
        product = part * normed
        sum_ref[here, 0:1] = jnp.sum(product, axis=1, keepdims=True)
        sum_ref[here, 1:2] = jnp.sum(part, axis=1, keepdims=True)
        first += jnp.sum(part * gain_ref[here], axis=0, keepdims=True)
        second += jnp.sum(product * gain_ref[here], axis=0, keepdims=True)
        blocks.append(part.astype(LOW))
    line = lax.broadcasted_iota(jnp.int32, (16, tokens), 0)
    sums = jnp.where(line == 0, first, jnp.where(line == 1, second, 0.0)).astype(LOW)
    for near, ref in ((False, theirs_ref), (True, mine_ref)):
        for core in range(2):

            @pl.when((core_ref[0] == core) == near)
            def _(core=core, ref=ref):
                for row in range(n_row):
                    ref[row, :width] = blocks[core * n_row + row]
                    ref[row, width:] = sums


def first_back(core, w_mixed, qkv_grad, x_all, x_mean, inverse, gain, width, n_row):
    tokens = x_all.shape[1]
    return pl.pallas_call(
        first_kernel,
        in_specs=[SMEM] + [VMEM] * 6,
        out_specs=[VMEM] * 3,
        out_shape=(
            jax.ShapeDtypeStruct((n_row, width + 16, tokens), LOW),
            jax.ShapeDtypeStruct((n_row, width + 16, tokens), LOW),
            jax.ShapeDtypeStruct((D, 2), jnp.float32),
        ),
        compiler_params=BIG,
        name="first_back",
    )(core, w_mixed, qkv_grad, x_all, x_mean, inverse, gain)


def adam_update(weights, moment_one, second, gradient, step_rate, weight_decay):
    moment_one = BETA_ONE * moment_one + (1.0 - BETA_ONE) * gradient
    second = BETA_TWO * second + (1.0 - BETA_TWO) * gradient * gradient
    direction = (
        moment_one / (1.0 - BETA_ONE**STEP) / (jnp.sqrt(second / (1.0 - BETA_TWO**STEP)) + ADAM_EPS)
    )
    return (weights - step_rate * (direction + weight_decay * weights), moment_one, second)


def shards(
    inputs,
    cotangent,
    qkv_master,
    out_master,
    up_master,
    down_master,
    qkv_first,
    out_first,
    up_first,
    down_first,
    qkv_second,
    out_second,
    up_second,
    down_second,
    norm_gains,
    gain_first,
    gain_second,
    biases,
    bias_first,
    bias_second,
):
    tokens, width = inputs.shape
    n_row = lax.axis_size("row")
    n_col = lax.axis_size("col")
    n_dp = lax.axis_size("dp")
    row = lax.axis_index("row")
    core = lax.axis_index("col")
    core_of = core.reshape(1).astype(jnp.int32)
    group = n_row * n_col
    heads = width // HEAD
    hidden_width = FF // group
    own = core * n_row + row
    padded = -(-tokens // (group * 16)) * (group * 16)
    half = padded // n_col
    shard_rows = qkv_master.shape[0]

    place = lax.broadcasted_iota(jnp.int32, (D, D), 0)
    source = lax.broadcasted_iota(jnp.int32, (D, D), 1)
    feature = (
        ((place // width) % n_row) * n_col + place // (width * n_row)
    ) * width + place % width
    order = lax.optimization_barrier(
        (source == (feature % n_dp) * (D // n_dp) + feature // n_dp).astype(LOW)
    )

    def mixed(vector):
        return vector.reshape(n_row, n_col, width).transpose(1, 0, 2).reshape(D)

    def plain(vector):
        return vector.reshape(n_col, n_row, width).transpose(1, 0, 2).reshape(D)

    def dealt(vector):
        return vector.reshape(D // n_dp, n_dp).T.reshape(D)

    def undealt(vector):
        return vector.reshape(n_dp, D // n_dp).T.reshape(D)

    def to_owner(rows, parts):
        return rows.reshape(shard_rows, parts, -1).transpose(1, 0, 2)

    def scattered(gradient):
        return lax.psum_scatter(gradient, "dp", scatter_dimension=0, tiled=True)

    def returned(rows):
        blocks = exchange_rows(rows.reshape(n_row, shard_rows, -1))
        return blocks.astype(jnp.float32)

    def widened(blocks):
        return blocks.transpose(1, 0, 2).reshape(shard_rows, -1)

    def long(array):
        return jnp.pad(array, ((0, 0), (0, padded - tokens)))

    qkv_rows = exchange_rows(to_owner(qkv_master[:, 0].astype(LOW), n_row))
    x_own = long(inputs.T)
    x_all = both_cores(lax.all_gather(x_own, "row", axis=0, tiled=True))
    w_qkv = send_copies(qkv_rows.reshape(D // n_dp, -1), "dp")
    rest = jnp.concatenate(
        [
            to_owner(out_master[:, :, 0].T.astype(LOW), n_row),
            to_owner(up_master[:, 0].astype(LOW), n_row),
            to_owner(down_master[:, :, 0].T.astype(LOW), n_row),
        ],
        axis=2,
    )
    rest = exchange_rows(rest).reshape(D // n_dp, -1)
    w_out = lax.all_gather(rest[:, :width], "dp", axis=0, tiled=True)
    w_up = lax.all_gather(rest[:, width : width + hidden_width], "dp", axis=0, tiled=True)
    w_down = lax.all_gather(rest[:, width + hidden_width :], "dp", axis=0, tiled=True)
    cot_all = lax.all_gather(long(cotangent.T), ("row", "col"), axis=0, tiled=True)

    gain_one = mixed(norm_gains[0])
    gain_two = dealt(norm_gains[1])
    shift_one = mixed(biases[:D])
    shift_two = dealt(biases[D : 2 * D])
    query_bias = lax.dynamic_slice_in_dim(biases, 2 * D + own * width, width).reshape(heads, HEAD)
    value_bias = lax.dynamic_slice_in_dim(biases, 3 * D + own * width, width).reshape(heads, HEAD)
    out_bias = dealt(biases[4 * D : 5 * D])
    feature_start = (row * n_col + core) * width
    down_bias = lax.dynamic_slice_in_dim(biases, 5 * D + feature_start, width)
    up_bias = lax.dynamic_slice_in_dim(biases, 6 * D + own * hidden_width, hidden_width)
    qkv_bias = jnp.stack([query_bias, jnp.zeros_like(query_bias), value_bias], axis=1).reshape(
        3 * width, 1
    )

    x_full = x_all.astype(jnp.float32)
    x_mean = jnp.sum(x_full, axis=0, keepdims=True) / D
    center = x_full - x_mean
    inverse_one = lax.rsqrt(jnp.sum(center * center, axis=0, keepdims=True) / D + NORM_EPS)
    za = (center * inverse_one * gain_one[:, None] + shift_one[:, None]).astype(LOW)
    za = dot(order, za, 0, 0, LOW)

    qkv, attended, theirs, mine = attend(core_of, w_qkv, za, qkv_bias, w_out)
    pair = (mine.astype(jnp.float32) + swap_cores(theirs).astype(jnp.float32)).astype(LOW)
    branch = lax.psum(pair, "row").astype(jnp.float32)

    x_half = lax.dynamic_slice_in_dim(x_all, core * half, half, axis=1)
    x_half = dot(x_half, order, 0, 0)
    cot_mixed = cot_all.reshape(n_row, n_col, width, padded).transpose(1, 0, 2, 3)
    cot_tokens = dot(cot_mixed.reshape(D, padded), order, 0, 0, LOW)
    active_grad = dot(cot_tokens, w_down, 1, 0)
    cot_half = take(cot_tokens, core, half).astype(jnp.float32)
    qkv_mixed = dot(order, w_qkv, 1, 0, LOW)
    down_mixed = dot(order, w_down, 1, 0, LOW)

    middle = x_half + branch + out_bias[None, :]
    center = middle - jnp.sum(middle, axis=1, keepdims=True) / D
    inverse_two = lax.rsqrt(jnp.sum(center * center, axis=1, keepdims=True) / D + NORM_EPS)
    normed_two = center * inverse_two
    zb = both_cores((normed_two * gain_two + shift_two).astype(LOW))

    active, hidden_grad, two_parts, up_sums = mlp(core_of, zb, w_up, up_bias[None, :], active_grad)
    pair = two_parts[half:].astype(jnp.float32) + swap_cores(two_parts[:half]).astype(jnp.float32)
    two_grad = lax.psum(pair.astype(LOW), "row").astype(jnp.float32)
    down_rows = scattered(dot(cot_tokens, active, 0, 0, LOW))
    up_rows = scattered(dot(zb, hidden_grad, 0, 0, LOW))

    scaled = two_grad * gain_two
    first_sum = jnp.sum(scaled, axis=1, keepdims=True) / D
    second_sum = jnp.sum(scaled * normed_two, axis=1, keepdims=True) / D
    middle_grad = cot_half + inverse_two * (scaled - first_sum - normed_two * second_sum)
    middle_grad = middle_grad.astype(LOW)
    branch_all = both_cores(middle_grad)

    qkv_grad, bias_sums, qkv_full, out_full = attend_back(branch_all, w_out, qkv, za, attended)
    theirs, mine, one_sums = first_back(
        core_of, qkv_mixed, qkv_grad, x_all, x_mean, inverse_one, gain_one[:, None], width, n_row
    )
    qkv_blocks = lax.all_to_all(qkv_full.reshape(n_dp, D // n_dp, -1), "dp", 0, 0)
    qkv_rows = jnp.sum(qkv_blocks.astype(jnp.float32), axis=0).astype(LOW)
    pair = (mine.astype(jnp.float32) + swap_cores(theirs).astype(jnp.float32)).astype(LOW)
    one_grad = jnp.sum(exchange_rows(pair).astype(jnp.float32), axis=0)
    own_gain = lax.dynamic_slice_in_dim(norm_gains[0], feature_start, width)[:, None]
    own_normed = (x_own.astype(jnp.float32) - x_mean) * inverse_one
    own_order = lax.dynamic_slice_in_dim(order, own * width, width, axis=0)
    own_middle = dot(own_order, branch_all, 1, 1)
    input_grad = own_middle + inverse_one * (
        one_grad[:width] * own_gain
        - one_grad[width : width + 1] / D
        - own_normed * (one_grad[width + 1 : width + 2] / D)
    )
    input_grad = input_grad.astype(LOW)[:, :tokens].T

    middle_mixed = dot(order, middle.astype(LOW), 1, 1)
    at_row = ((jnp.arange(D) // width) % n_row == row)[:, None]
    middle_mixed = jnp.where(at_row, middle_mixed, 0.0)
    middle_mixed = lax.dynamic_update_slice_in_dim(
        jnp.zeros((D, padded), jnp.float32), middle_mixed, core * half, 1
    )
    result = (dot(down_mixed, active, 1, 1) + middle_mixed + zero_of(branch_all)).astype(LOW)
    result = lax.psum_scatter(result, "col", scatter_dimension=0, tiled=True)
    result = exchange_rows(result.reshape(n_row, width, padded))
    result = jnp.sum(result.astype(jnp.float32), axis=0) + down_bias[:, None]
    result = result.astype(LOW)[:, :tokens].T

    out_rows = scattered(out_full)
    last = returned(jnp.concatenate([out_rows, qkv_rows], axis=1))
    out_blocks = last[:, :, :width]
    qkv_blocks = last[:, :, width:]

    bias_sums = bias_sums.reshape(heads, 3, HEAD)
    once = (row == 0).astype(jnp.float32)
    shared = jnp.stack(
        [
            jnp.sum(two_grad * normed_two, axis=0),
            jnp.sum(two_grad, axis=0),
            jnp.sum(middle_grad, axis=0, dtype=jnp.float32),
            jnp.sum(cot_half, axis=0),
        ]
    )
    shared = (shared * once).reshape(4, n_dp, D // n_dp).transpose(0, 2, 1).reshape(4, D)
    bias_grad = jnp.concatenate(
        [
            plain(one_sums[:, 0]),
            shared[0],
            plain(one_sums[:, 1]),
            shared[1],
            jnp.zeros((2 * D,), jnp.float32),
            shared[2],
            shared[3],
            jnp.zeros((FF,), jnp.float32),
        ]
    )
    for piece, offset in (
        (bias_sums[:, 0].reshape(width), 4 * D + own * width),
        (bias_sums[:, 2].reshape(width), 5 * D + own * width),
        (up_sums[0], 8 * D + own * hidden_width),
    ):
        bias_grad = lax.dynamic_update_slice_in_dim(bias_grad, piece, offset, 0)
    total = all_sum(bias_grad)
    gain_total = total[: 2 * D].reshape(2, D)
    bias_total = total[2 * D :]

    later = zero_of(qkv_grad)
    first = returned(jnp.concatenate([up_rows, down_rows], axis=1))
    up_blocks = first[:, :, :hidden_width]
    down_blocks = first[:, :, hidden_width:]
    q_new = adam_update(
        qkv_master, qkv_first, qkv_second, widened(qkv_blocks)[:, None], 0.03, 0.1
    )
    o_new = adam_update(
        out_master, out_first, out_second, widened(out_blocks).T[:, :, None], 0.12, 0.1
    )
    u_new = adam_update(
        up_master, up_first, up_second, widened(up_blocks + later)[:, None], 0.03, 0.1
    )
    d_new = adam_update(
        down_master, down_first, down_second, widened(down_blocks + later).T[:, :, None], 0.02, 0.1
    )
    g_new = adam_update(norm_gains, gain_first, gain_second, gain_total, 0.5, 0.0)
    b_new = adam_update(biases, bias_first, bias_second, bias_total, 0.5, 0.0)
    return (result, input_grad, *q_new, *o_new, *u_new, *d_new, *g_new, *b_new)


def solution(mesh):
    token_spec = P("dp", ("row", "col"))
    wide = P("row", "dp", "col")
    tall = P("col", "row", "dp")
    return jax.shard_map(
        shards,
        mesh=mesh,
        in_specs=(token_spec,) * 2 + (wide, tall, wide, tall) * 3 + (P(),) * 6,
        out_specs=(token_spec,) * 2
        + (wide,) * 3
        + (tall,) * 3
        + (wide,) * 3
        + (tall,) * 3
        + (P(),) * 6,
        check_vma=False,
    )
```

```python
import jax
import jax.numpy as jnp
from jax import lax
from jax.experimental import pallas as pl
from jax.experimental.pallas import tpu as pltpu
from jax.sharding import PartitionSpec as P

D = 1152
FF = 4304
HEAD = 72
SEQ = 729
STEP = 10

NORM_EPS = 1e-06
ADAM_EPS = 1e-08
BETA_ONE = 0.9
BETA_TWO = 0.999
LOW = jnp.bfloat16


def dot(left, right, left_dim, right_dim, out=jnp.float32, precision=None):
    return lax.dot_general(
        left,
        right,
        (((left_dim,), (right_dim,)), ((), ())),
        precision=precision,
        preferred_element_type=out,
    )


def take(array, index, size):
    return lax.dynamic_slice_in_dim(array, index * size, size, axis=0)


def swap_cores(array):
    n_col = lax.axis_size("col")
    return lax.ppermute(array, "col", [(i, (i + 1) % n_col) for i in range(n_col)])


def both_cores(rows):
    pieces = [
        lax.all_gather(piece, "col", axis=0) for piece in jnp.split(rows, 2, axis=0)
    ]
    return jnp.concatenate(pieces, axis=1).reshape(-1, rows.shape[1])


def send_copies(block, axis):
    copies = jnp.broadcast_to(block, (lax.axis_size(axis),) + block.shape)
    return lax.all_to_all(copies, axis, 0, 0).reshape(-1, block.shape[1])


def zero_of(array):
    first = lax.slice(array, (0,) * array.ndim, (1,) * array.ndim)
    return first.reshape(()).astype(jnp.float32) * 0.0


def exchange_rows(blocks):
    return lax.all_to_all(blocks, "row", 0, 0)


def sum_blocks(blocks, axis):
    size = lax.axis_size(axis)
    if size > 4:
        return jnp.sum(lax.all_to_all(blocks, axis, 0, 0).astype(jnp.float32), axis=0)
    me = lax.axis_index(axis)
    got = [
        lax.ppermute(
            lax.dynamic_index_in_dim(blocks, me ^ step, 0, keepdims=False),
            axis,
            [(i, i ^ step) for i in range(size)],
        )
        for step in range(1, size)
    ]
    total = lax.dynamic_index_in_dim(blocks, me, 0, keepdims=False).astype(jnp.float32)
    for block in got:
        total = total + block.astype(jnp.float32)
    return total


def sum_over_rows(half):
    summed = lax.psum_scatter(half.astype(LOW), "row", scatter_dimension=0, tiled=True)
    return summed.astype(jnp.float32)


def all_sum(vector):
    for axis in ("col", "row", "dp"):
        size = lax.axis_size(axis)
        if size & (size - 1) or size > 4:
            vector = lax.psum(vector, axis)
            continue
        step = 1
        while step < size:
            vector = vector + lax.ppermute(vector, axis, [(i, i ^ step) for i in range(size)])
            step *= 2
    return vector


VMEM = pl.BlockSpec(memory_space=pltpu.VMEM)
SMEM = pl.BlockSpec(memory_space=pltpu.SMEM)
BIG = pltpu.CompilerParams(vmem_limit_bytes=56 * 1024 * 1024)


def head_probs(queries, key_rows):
    scores = dot(queries, key_rows, 0, 0) * HEAD ** (-0.5)
    scores = jnp.where(lax.broadcasted_iota(jnp.int32, scores.shape, 1) < SEQ, scores, -1e30)
    exponent = jnp.exp(scores - jnp.max(scores, axis=1, keepdims=True))
    return exponent * (1.0 / jnp.sum(exponent, axis=1, keepdims=True))


def split_cores(core, first, second, theirs_ref, mine_ref):
    @pl.when(core == 0)
    def _():
        mine_ref[...] = first
        theirs_ref[...] = second

    @pl.when(core != 0)
    def _():
        mine_ref[...] = second
        theirs_ref[...] = first


def attend_kernel(core_ref, w_ref, za_ref, bias_ref, out_ref, qkv_ref, att_ref, theirs_ref, mine_ref):
    qkv = dot(w_ref[...], za_ref[...], 0, 0) + bias_ref[...]
    heads = qkv_ref.shape[0]
    parts = []
    for head in range(heads):
        for t in range(3):
            start = (head * 3 + t) * HEAD
            qkv_ref[head, t] = qkv[start : start + HEAD].astype(LOW)
        probs = head_probs(qkv_ref[head, 0], qkv_ref[head, 1]).astype(LOW)
        parts.append(dot(qkv_ref[head, 2], probs, 1, 1))
    attended = jnp.concatenate(parts, axis=0).T.astype(LOW)
    att_ref[...] = attended
    branch = dot(attended, out_ref[...], 1, 1).astype(LOW)
    half = branch.shape[0] // 2
    split_cores(core_ref[0], branch[:half], branch[half:], theirs_ref, mine_ref)


def attend(core, w_qkv, za, qkv_bias, w_out):
    tokens = za.shape[1]
    width = w_out.shape[1]
    return pl.pallas_call(
        attend_kernel,
        in_specs=[SMEM, VMEM, VMEM, VMEM, VMEM],
        out_specs=[VMEM] * 4,
        out_shape=(
            jax.ShapeDtypeStruct((width // HEAD, 3, HEAD, tokens), LOW),
            jax.ShapeDtypeStruct((tokens, width), LOW),
            jax.ShapeDtypeStruct((tokens // 2, D), LOW),
            jax.ShapeDtypeStruct((tokens // 2, D), LOW),
        ),
        compiler_params=BIG,
        name="attend",
    )(core, w_qkv, za, qkv_bias, w_out)


def mlp_kernel(core_ref, zb_ref, up_ref, bias_ref, grad_ref, act_ref, hid_ref, two_ref, sum_ref):
    hidden = dot(zb_ref[...], up_ref[...], 1, 0) + bias_ref[...]
    square = hidden * hidden
    slope = 0.7978845608028654 * (1.0 + 0.044715 * square)
    bent = jnp.tanh(hidden * slope)
    gate = 0.5 * (1.0 + bent)
    act_ref[...] = (hidden * gate).astype(LOW)
    steep = gate + 0.5 * hidden * (1.0 - bent * bent) * (
        0.7978845608028654 * (1.0 + 3 * 0.044715 * square)
    )
    hidden_grad = (grad_ref[...] * steep).astype(LOW)
    hid_ref[...] = hidden_grad
    two_ref[...] = dot(hidden_grad, up_ref[...], 1, 1).astype(LOW)

    @pl.when(pl.program_id(0) == 0)
    def _():
        sum_ref[...] = jnp.zeros(sum_ref.shape, jnp.float32)

    sum_ref[...] += jnp.sum(hidden_grad.astype(jnp.float32), axis=0, keepdims=True)


def mlp(core, zb, w_up, up_bias, active_grad):
    tokens = zb.shape[0]
    wide = w_up.shape[1]
    steps = 6
    block = tokens // steps
    turned = lambda i, c: ((i + (steps // 2) * (1 - c[0])) % steps, 0)
    whole = lambda i, c: (0, 0)
    return pl.pallas_call(
        mlp_kernel,
        grid_spec=pltpu.PrefetchScalarGridSpec(
            num_scalar_prefetch=1,
            grid=(steps,),
            in_specs=[
                pl.BlockSpec((block, D), turned),
                pl.BlockSpec((D, wide), whole),
                pl.BlockSpec((1, wide), whole),
                pl.BlockSpec((block, wide), turned),
            ],
            out_specs=[
                pl.BlockSpec((block, wide), turned),
                pl.BlockSpec((block, wide), turned),
                pl.BlockSpec((block, D), lambda i, c: (i, 0)),
                pl.BlockSpec((1, wide), whole),
            ],
        ),
        out_shape=(
            jax.ShapeDtypeStruct((tokens, wide), LOW),
            jax.ShapeDtypeStruct((tokens, wide), LOW),
            jax.ShapeDtypeStruct((tokens, D), LOW),
            jax.ShapeDtypeStruct((1, wide), jnp.float32),
        ),
        compiler_params=BIG,
        name="mlp",
    )(core, zb, w_up, up_bias, active_grad)


def back_kernel(bg_ref, out_ref, qkv_ref, za_ref, att_ref, grad_ref, sum_ref, wq_ref, wo_ref):
    attended_grad = dot(bg_ref[...], out_ref[...], 1, 0).T
    scale = HEAD ** (-0.5)
    parts = []
    for head in range(qkv_ref.shape[0]):
        queries, key_rows, values = qkv_ref[head, 0], qkv_ref[head, 1], qkv_ref[head, 2]
        grad = attended_grad[head * HEAD : (head + 1) * HEAD].astype(LOW)
        probs = head_probs(queries, key_rows)
        probs_grad = dot(grad, values, 0, 0)
        inner = jnp.sum(probs * probs_grad, axis=1, keepdims=True)
        scores_grad = (probs * (probs_grad - inner)).astype(LOW)
        parts.append(dot(key_rows, scores_grad, 1, 1) * scale)
        parts.append(dot(queries, scores_grad, 1, 0) * scale)
        parts.append(dot(grad, probs.astype(LOW), 1, 0))
    qkv_grad = jnp.concatenate(parts, axis=0).astype(LOW)
    grad_ref[...] = qkv_grad
    sum_ref[...] = jnp.sum(qkv_grad.astype(jnp.float32), axis=1, keepdims=True)
    wq_ref[...] = dot(za_ref[...], qkv_grad, 1, 1).astype(LOW)
    wo_ref[...] = dot(bg_ref[...], att_ref[...], 0, 0).astype(LOW)


def attend_back(branch_all, w_out, qkv, za, attended):
    tokens = za.shape[1]
    width = w_out.shape[1]
    return pl.pallas_call(
        back_kernel,
        in_specs=[VMEM] * 5,
        out_specs=[VMEM] * 4,
        out_shape=(
            jax.ShapeDtypeStruct((3 * width, tokens), LOW),
            jax.ShapeDtypeStruct((3 * width, 1), jnp.float32),
            jax.ShapeDtypeStruct((D, 3 * width), LOW),
            jax.ShapeDtypeStruct((D, width), LOW),
        ),
        compiler_params=BIG,
        name="attend_back",
    )(branch_all, w_out, qkv, za, attended)


def first_kernel(core_ref, w_ref, grad_ref, x_ref, mean_ref, inv_ref, gain_ref, theirs_ref, mine_ref, sum_ref):
    n_row, rows, tokens = theirs_ref.shape
    width = rows - 16
    first = jnp.zeros((1, tokens), jnp.float32)
    second = jnp.zeros((1, tokens), jnp.float32)
    blocks = []
    for slot in range(D // width):
        here = slice(slot * width, (slot + 1) * width)
        part = dot(w_ref[here], grad_ref[...], 1, 0)
        normed = (x_ref[here].astype(jnp.float32) - mean_ref[...]) * inv_ref[...]
        product = part * normed
        sum_ref[here, 0:1] = jnp.sum(product, axis=1, keepdims=True)
        sum_ref[here, 1:2] = jnp.sum(part, axis=1, keepdims=True)
        first += jnp.sum(part * gain_ref[here], axis=0, keepdims=True)
        second += jnp.sum(product * gain_ref[here], axis=0, keepdims=True)
        blocks.append(part.astype(LOW))
    line = lax.broadcasted_iota(jnp.int32, (16, tokens), 0)
    sums = jnp.where(line == 0, first, jnp.where(line == 1, second, 0.0)).astype(LOW)
    for near, ref in ((False, theirs_ref), (True, mine_ref)):
        for core in range(2):

            @pl.when((core_ref[0] == core) == near)
            def _(core=core, ref=ref):
                for row in range(n_row):
                    ref[row, :width] = blocks[core * n_row + row]
                    ref[row, width:] = sums


def first_back(core, w_mixed, qkv_grad, x_all, x_mean, inverse, gain, width, n_row):
    tokens = x_all.shape[1]
    return pl.pallas_call(
        first_kernel,
        in_specs=[SMEM] + [VMEM] * 6,
        out_specs=[VMEM] * 3,
        out_shape=(
            jax.ShapeDtypeStruct((n_row, width + 16, tokens), LOW),
            jax.ShapeDtypeStruct((n_row, width + 16, tokens), LOW),
            jax.ShapeDtypeStruct((D, 2), jnp.float32),
        ),
        compiler_params=BIG,
        name="first_back",
    )(core, w_mixed, qkv_grad, x_all, x_mean, inverse, gain)


def adam_update(weights, moment_one, second, gradient, step_rate, weight_decay):
    moment_one = BETA_ONE * moment_one + (1.0 - BETA_ONE) * gradient
    second = BETA_TWO * second + (1.0 - BETA_TWO) * gradient * gradient
    direction = (
        moment_one / (1.0 - BETA_ONE**STEP) / (jnp.sqrt(second / (1.0 - BETA_TWO**STEP)) + ADAM_EPS)
    )
    return (weights - step_rate * (direction + weight_decay * weights), moment_one, second)


def shards(
    inputs,
    cotangent,
    qkv_master,
    out_master,
    up_master,
    down_master,
    qkv_first,
    out_first,
    up_first,
    down_first,
    qkv_second,
    out_second,
    up_second,
    down_second,
    norm_gains,
    gain_first,
    gain_second,
    biases,
    bias_first,
    bias_second,
):
    tokens, width = inputs.shape
    n_row = lax.axis_size("row")
    n_col = lax.axis_size("col")
    n_dp = lax.axis_size("dp")
    row = lax.axis_index("row")
    core = lax.axis_index("col")
    core_of = core.reshape(1).astype(jnp.int32)
    group = n_row * n_col
    heads = width // HEAD
    hidden_width = FF // group
    own = core * n_row + row
    chunk = -(-tokens // (group * 16)) * 16
    padded = chunk * group
    half = padded // n_col
    shard_rows = qkv_master.shape[0]

    place = jnp.arange(D)
    feature = (
        ((place // width) % n_row) * n_col + place // (width * n_row)
    ) * width + place % width
    place = (feature % n_dp) * (D // n_dp) + feature // n_dp
    order = (lax.broadcasted_iota(jnp.int32, (D, D), 1) == place[:, None]).astype(LOW)
    order = lax.optimization_barrier(order)

    def mixed(vector):
        return vector.reshape(n_row, n_col, width).transpose(1, 0, 2).reshape(D)

    def plain(vector):
        return vector.reshape(n_col, n_row, width).transpose(1, 0, 2).reshape(D)

    def dealt(vector):
        return vector.reshape(D // n_dp, n_dp).T.reshape(D)

    def undealt(vector):
        return vector.reshape(n_dp, D // n_dp).T.reshape(D)

    def to_owner(rows, parts):
        return rows.reshape(shard_rows, parts, -1).transpose(1, 0, 2)

    def scattered(gradient):
        return sum_blocks(gradient.reshape(n_dp, D // n_dp, -1), "dp").astype(LOW)

    def returned(rows):
        blocks = exchange_rows(rows.reshape(n_row, shard_rows, -1))
        return blocks.astype(jnp.float32)

    def widened(blocks):
        return blocks.transpose(1, 0, 2).reshape(shard_rows, -1)

    def long(array):
        return jnp.pad(array, ((0, 0), (0, padded - tokens)))

    first_rows = jnp.concatenate(
        [
            to_owner(qkv_master[:, 0].astype(LOW), n_row),
            to_owner(out_master[:, :, 0].T.astype(LOW), n_row),
        ],
        axis=2,
    )
    first_rows = exchange_rows(first_rows).reshape(D // n_dp, -1)
    x_own = long(inputs.T)
    x_rows = lax.all_gather(x_own, "row", axis=0, tiled=True)
    x_all = both_cores(x_rows)
    w_first = send_copies(first_rows, "dp")
    w_qkv = w_first[:, : 3 * width]
    w_out = w_first[:, 3 * width :]
    rest = jnp.concatenate(
        [
            to_owner(up_master[:, 0].astype(LOW), n_row),
            to_owner(down_master[:, :, 0].T.astype(LOW), n_row),
        ],
        axis=2,
    )
    rest = exchange_rows(rest + zero_of(w_first).astype(LOW)).reshape(D // n_dp, -1)
    w_rest = send_copies(rest, "dp")
    w_up = w_rest[:, :hidden_width]
    w_down = w_rest[:, hidden_width:]
    cot_own = long(cotangent.T) + zero_of(x_rows).astype(LOW)
    cot_all = lax.all_gather(cot_own, ("row", "col"), axis=0, tiled=True)

    gain_one = mixed(norm_gains[0])
    gain_two = dealt(norm_gains[1])
    shift_one = mixed(biases[:D])
    shift_two = dealt(biases[D : 2 * D])
    query_bias = lax.dynamic_slice_in_dim(biases, 2 * D + own * width, width).reshape(heads, HEAD)
    value_bias = lax.dynamic_slice_in_dim(biases, 3 * D + own * width, width).reshape(heads, HEAD)
    out_bias = dealt(biases[4 * D : 5 * D])
    feature_start = (row * n_col + core) * width
    down_bias = lax.dynamic_slice_in_dim(biases, 5 * D + feature_start, width)
    up_bias = lax.dynamic_slice_in_dim(biases, 6 * D + own * hidden_width, hidden_width)
    qkv_bias = jnp.stack([query_bias, jnp.zeros_like(query_bias), value_bias], axis=1).reshape(
        3 * width, 1
    )

    x_full = x_all.astype(jnp.float32)
    x_mean = jnp.sum(x_full, axis=0, keepdims=True) / D
    center = x_full - x_mean
    inverse_one = lax.rsqrt(jnp.sum(center * center, axis=0, keepdims=True) / D + NORM_EPS)
    za = (center * inverse_one * gain_one[:, None] + shift_one[:, None]).astype(LOW)
    za = dot(order, za, 0, 0, LOW)

    qkv, attended, theirs, mine = attend(core_of, w_qkv, za, qkv_bias, w_out)
    branch = sum_over_rows(mine.astype(jnp.float32) + swap_cores(theirs).astype(jnp.float32))

    pick = lax.broadcasted_iota(jnp.int32, (chunk, padded), 0) + own * chunk
    pick = (lax.broadcasted_iota(jnp.int32, (chunk, padded), 1) == pick).astype(LOW)
    x_mine = dot(dot(pick, x_all, 1, 1, LOW), order, 1, 0)
    cot_mixed = cot_all.reshape(n_row, n_col, width, padded).transpose(1, 0, 2, 3)
    cot_tokens = dot(cot_mixed.reshape(D, padded), order, 0, 0, LOW)
    active_grad = dot(cot_tokens, w_down, 1, 0)
    cot_mine = take(cot_tokens, own, chunk).astype(jnp.float32)
    qkv_mixed = dot(order, w_qkv, 1, 0, LOW)
    down_mixed = dot(order, w_down, 1, 0, LOW)

    middle = x_mine + branch + out_bias[None, :]
    center = middle - jnp.sum(middle, axis=1, keepdims=True) / D
    inverse_two = lax.rsqrt(jnp.sum(center * center, axis=1, keepdims=True) / D + NORM_EPS)
    normed_two = center * inverse_two
    zb = (normed_two * gain_two + shift_two).astype(LOW)
    zb = both_cores(lax.all_gather(zb, "row", axis=0, tiled=True))

    active, hidden_grad, two_parts, up_sums = mlp(core_of, zb, w_up, up_bias[None, :], active_grad)
    two_grad = sum_over_rows(
        two_parts[half:].astype(jnp.float32) + swap_cores(two_parts[:half]).astype(jnp.float32)
    )

    middle_mixed = dot(order, middle.astype(LOW), 1, 1, LOW)
    result = dot(down_mixed, active, 1, 1) + dot(middle_mixed, pick, 1, 0)
    result = result.astype(LOW).reshape(n_col, D // n_col, padded)
    theirs = lax.dynamic_index_in_dim(result, 1 - core, 0, keepdims=False)
    mine = lax.dynamic_index_in_dim(result, core, 0, keepdims=False)
    result = mine.astype(jnp.float32) + swap_cores(theirs).astype(jnp.float32)
    rest_grad = jnp.concatenate(
        [dot(zb, hidden_grad, 0, 0, LOW), dot(cot_tokens, active, 0, 0, LOW)], axis=1
    )
    rest_rows = scattered(rest_grad)

    scaled = two_grad * gain_two
    first_sum = jnp.sum(scaled, axis=1, keepdims=True) / D
    second_sum = jnp.sum(scaled * normed_two, axis=1, keepdims=True) / D
    middle_grad = cot_mine + inverse_two * (scaled - first_sum - normed_two * second_sum)
    middle_grad = middle_grad.astype(LOW)
    branch_all = both_cores(lax.all_gather(middle_grad, "row", axis=0, tiled=True))

    result = (result + zero_of(branch_all)).astype(LOW).reshape(n_row, width, padded)
    result = sum_blocks(result, "row") + down_bias[:, None]
    result = result.astype(LOW)[:, :tokens].T

    qkv_grad, bias_sums, qkv_full, out_full = attend_back(branch_all, w_out, qkv, za, attended)
    theirs, mine, one_sums = first_back(
        core_of, qkv_mixed, qkv_grad, x_all, x_mean, inverse_one, gain_one[:, None], width, n_row
    )
    first_rows = scattered(jnp.concatenate([qkv_full, out_full], axis=1))
    pair = mine.astype(jnp.float32) + swap_cores(theirs).astype(jnp.float32)
    one_grad = sum_over_rows(pair.reshape(-1, padded))
    own_gain = lax.dynamic_slice_in_dim(norm_gains[0], feature_start, width)[:, None]
    own_normed = (x_own.astype(jnp.float32) - x_mean) * inverse_one
    own_order = lax.dynamic_slice_in_dim(order, own * width, width, axis=0)
    own_middle = dot(own_order, branch_all, 1, 1)
    input_grad = own_middle + inverse_one * (
        one_grad[:width] * own_gain
        - one_grad[width : width + 1] / D
        - own_normed * (one_grad[width + 1 : width + 2] / D)
    )
    input_grad = input_grad.astype(LOW)[:, :tokens].T

    last = returned(first_rows)
    qkv_blocks = last[:, :, : 3 * width]
    out_blocks = last[:, :, 3 * width :]

    bias_sums = bias_sums.reshape(heads, 3, HEAD)
    shared = jnp.stack(
        [
            jnp.sum(two_grad * normed_two, axis=0),
            jnp.sum(two_grad, axis=0),
            jnp.sum(middle_grad, axis=0, dtype=jnp.float32),
            jnp.sum(cot_mine, axis=0),
        ]
    )
    shared = shared.reshape(4, n_dp, D // n_dp).transpose(0, 2, 1).reshape(4, D)
    bias_grad = jnp.concatenate(
        [
            plain(one_sums[:, 0]),
            shared[0],
            plain(one_sums[:, 1]),
            shared[1],
            jnp.zeros((2 * D,), jnp.float32),
            shared[2],
            shared[3],
            jnp.zeros((FF,), jnp.float32),
        ]
    )
    for piece, offset in (
        (bias_sums[:, 0].reshape(width), 4 * D + own * width),
        (bias_sums[:, 2].reshape(width), 5 * D + own * width),
        (up_sums[0], 8 * D + own * hidden_width),
    ):
        bias_grad = lax.dynamic_update_slice_in_dim(bias_grad, piece, offset, 0)
    total = all_sum(bias_grad)
    gain_total = total[: 2 * D].reshape(2, D)
    bias_total = total[2 * D :]

    later = zero_of(qkv_grad)
    first = returned(rest_rows)
    up_blocks = first[:, :, :hidden_width]
    down_blocks = first[:, :, hidden_width:]
    q_new = adam_update(
        qkv_master, qkv_first, qkv_second, widened(qkv_blocks)[:, None], 0.03, 0.1
    )
    o_new = adam_update(
        out_master, out_first, out_second, widened(out_blocks).T[:, :, None], 0.12, 0.1
    )
    u_new = adam_update(
        up_master, up_first, up_second, widened(up_blocks + later)[:, None], 0.03, 0.1
    )
    d_new = adam_update(
        down_master, down_first, down_second, widened(down_blocks + later).T[:, :, None], 0.02, 0.1
    )
    g_new = adam_update(norm_gains, gain_first, gain_second, gain_total, 0.5, 0.0)
    b_new = adam_update(biases, bias_first, bias_second, bias_total, 0.5, 0.0)
    return (result, input_grad, *q_new, *o_new, *u_new, *d_new, *g_new, *b_new)


def solution(mesh):
    token_spec = P("dp", ("row", "col"))
    wide = P("row", "dp", "col")
    tall = P("col", "row", "dp")
    return jax.shard_map(
        shards,
        mesh=mesh,
        in_specs=(token_spec,) * 2 + (wide, tall, wide, tall) * 3 + (P(),) * 6,
        out_specs=(token_spec,) * 2
        + (wide,) * 3
        + (tall,) * 3
        + (wide,) * 3
        + (tall,) * 3
        + (P(),) * 6,
        check_vma=False,
    )
```

```python
from functools import partial

import jax
import jax.numpy as jnp
from jax import lax
from jax.experimental import pallas as pl
from jax.experimental.pallas import tpu as pltpu
from jax.sharding import PartitionSpec as P

D = 1152
FF = 4304
HEAD = 72
SEQ = 729
STEP = 10

NORM_EPS = 1e-06
ADAM_EPS = 1e-08
BETA_ONE = 0.9
BETA_TWO = 0.999
LOW = jnp.bfloat16


def dot(left, right, left_dim, right_dim, out=jnp.float32, precision=None):
    return lax.dot_general(
        left,
        right,
        (((left_dim,), (right_dim,)), ((), ())),
        precision=precision,
        preferred_element_type=out,
    )


def take(array, index, size):
    return lax.dynamic_slice_in_dim(array, index * size, size, axis=0)


def swap_cores(array):
    n_col = lax.axis_size("col")
    return lax.ppermute(array, "col", [(i, (i + 1) % n_col) for i in range(n_col)])


def both_cores(rows):
    pieces = [
        lax.all_gather(piece, "col", axis=0) for piece in jnp.split(rows, 2, axis=0)
    ]
    return jnp.concatenate(pieces, axis=1).reshape(-1, rows.shape[1])


def gather_parts(block, axis):
    size = lax.axis_size(axis)
    if size > 4:
        copies = jnp.broadcast_to(block, (size,) + block.shape)
        return [lax.all_to_all(copies, axis, 0, 0).reshape(-1, block.shape[1])]
    return [block] + [
        lax.ppermute(block, axis, [(i, i ^ step) for i in range(size)]) for step in range(1, size)
    ]


def zero_of(array):
    first = lax.slice(array, (0,) * array.ndim, (1,) * array.ndim)
    return first.reshape(()).astype(jnp.float32) * 0.0


def exchange_rows(blocks):
    return lax.all_to_all(blocks, "row", 0, 0)


def sum_parts(blocks, axis, later):
    size = lax.axis_size(axis)
    if size > 4:
        blocks = lax.all_to_all(blocks, axis, 0, 0)
        return jnp.sum(blocks.astype(jnp.float32) + later, axis=0).astype(LOW)
    got = [
        lax.ppermute(blocks[step], axis, [(i, i ^ step) for i in range(size)])
        for step in range(1, size)
    ]
    total = blocks[0].astype(jnp.float32) + later
    for block in got:
        total = total + block.astype(jnp.float32)
    return total.astype(LOW)


def sum_over_rows(half):
    summed = lax.psum_scatter(half.astype(LOW), "row", scatter_dimension=0, tiled=True)
    return summed.astype(jnp.float32)


def all_sum(vector):
    for axis in ("col", "row", "dp"):
        size = lax.axis_size(axis)
        if size & (size - 1) or size > 4:
            vector = lax.psum(vector, axis)
            continue
        step = 1
        while step < size:
            vector = vector + lax.ppermute(vector, axis, [(i, i ^ step) for i in range(size)])
            step *= 2
    return vector


VMEM = pl.BlockSpec(memory_space=pltpu.VMEM)
SMEM = pl.BlockSpec(memory_space=pltpu.SMEM)
ANY = pl.BlockSpec(memory_space=pl.ANY)
BIG = pltpu.CompilerParams(vmem_limit_bytes=56 * 1024 * 1024)


def prepare_kernel(parts, after_ref, wide_ref, tall_ref, out_ref):
    del after_ref
    arrays = [ref[:, 0, :].astype(LOW) for ref in (wide_ref, tall_ref)]
    for part in range(parts):
        pieces = []
        for array in arrays:
            size = array.shape[1] // parts
            pieces.append(array[:, part * size : (part + 1) * size])
        out_ref[part] = jnp.concatenate(pieces, axis=1)


def prepare(after, wide, tall, parts):
    rows = wide.shape[0]
    size = (wide.shape[2] + tall.shape[2]) // parts
    return pl.pallas_call(
        partial(prepare_kernel, parts),
        in_specs=[ANY, VMEM, VMEM],
        out_specs=VMEM,
        out_shape=jax.ShapeDtypeStruct((parts, rows, size), LOW),
        compiler_params=BIG,
        name="prepare",
    )(after, wide, tall)


def adam_kernel(rates, after_ref, blocks_ref, *refs):
    del after_ref
    parts = blocks_ref.shape[0]
    start = 0
    for index, rate in enumerate(rates):
        weight, first, second = refs[3 * index : 3 * index + 3]
        size = weight.shape[2] // parts
        gradient = jnp.concatenate(
            [blocks_ref[part, :, start : start + size] for part in range(parts)], axis=1
        ).astype(jnp.float32)
        start += size
        new = adam_update(weight[:, 0, :], first[:, 0, :], second[:, 0, :], gradient, rate, 0.1)
        for array, ref in zip(new, refs[3 * len(rates) + 3 * index :]):
            ref[:, 0, :] = array


def adam(after, blocks, rates, *arrays):
    return pl.pallas_call(
        partial(adam_kernel, rates),
        in_specs=[ANY] + [VMEM] * (1 + len(arrays)),
        out_specs=[VMEM] * len(arrays),
        out_shape=[jax.ShapeDtypeStruct(a.shape, jnp.float32) for a in arrays],
        compiler_params=BIG,
        name="adam",
    )(after, blocks, *arrays)


def assembled(place, parts, scratch):
    if len(parts) == 1:
        return parts[0][...]
    for step, part in enumerate(parts):
        scratch[place ^ step] = part[...]
    return scratch[...].reshape(-1, scratch.shape[2])


def part_scratch(parts):
    return pltpu.VMEM((len(parts),) + parts[0].shape, LOW)


def store_parts(place, array, ref):
    count, rows = ref.shape[:2]
    if count > 4:
        ref[...] = array.reshape(ref.shape)
        return
    for index in range(count):
        ref[place ^ index] = array[index * rows : (index + 1) * rows]


def head_probs(queries, key_rows):
    scores = dot(queries, key_rows, 0, 0) * HEAD ** (-0.5)
    scores = jnp.where(lax.broadcasted_iota(jnp.int32, scores.shape, 1) < SEQ, scores, -1e30)
    exponent = jnp.exp(scores - jnp.max(scores, axis=1, keepdims=True))
    return exponent * (1.0 / jnp.sum(exponent, axis=1, keepdims=True))


def split_cores(core, first, second, theirs_ref, mine_ref):
    @pl.when(core == 0)
    def _():
        mine_ref[...] = first
        theirs_ref[...] = second

    @pl.when(core != 0)
    def _():
        mine_ref[...] = second
        theirs_ref[...] = first


def attend_kernel(place_ref, za_ref, bias_ref, *refs):
    *parts, w_ref, qkv_ref, att_ref, theirs_ref, mine_ref, scratch = refs
    w_ref[...] = assembled(place_ref[1], parts, scratch)
    heads = qkv_ref.shape[0]
    split = heads * 3 * HEAD
    qkv = dot(w_ref[:, :split], za_ref[...], 0, 0) + bias_ref[...]
    outs = []
    for head in range(heads):
        for t in range(3):
            start = (head * 3 + t) * HEAD
            qkv_ref[head, t] = qkv[start : start + HEAD].astype(LOW)
        probs = head_probs(qkv_ref[head, 0], qkv_ref[head, 1]).astype(LOW)
        outs.append(dot(qkv_ref[head, 2], probs, 1, 1))
    attended = jnp.concatenate(outs, axis=0).T.astype(LOW)
    att_ref[...] = attended
    branch = dot(attended, w_ref[:, split:], 1, 1).astype(LOW)
    half = branch.shape[0] // 2
    split_cores(place_ref[0], branch[:half], branch[half:], theirs_ref, mine_ref)


def attend(place, za, qkv_bias, parts, width):
    tokens = za.shape[1]
    return pl.pallas_call(
        attend_kernel,
        in_specs=[SMEM, VMEM, VMEM] + [VMEM] * len(parts),
        out_specs=[VMEM] * 5,
        out_shape=(
            jax.ShapeDtypeStruct((D, 4 * width), LOW),
            jax.ShapeDtypeStruct((width // HEAD, 3, HEAD, tokens), LOW),
            jax.ShapeDtypeStruct((tokens, width), LOW),
            jax.ShapeDtypeStruct((tokens // 2, D), LOW),
            jax.ShapeDtypeStruct((tokens // 2, D), LOW),
        ),
        scratch_shapes=[part_scratch(parts)],
        compiler_params=BIG,
        name="attend",
    )(place, za, qkv_bias, *parts)


def own_tokens(place_ref, chunk, tokens):
    pick = lax.broadcasted_iota(jnp.int32, (chunk, tokens), 0) + place_ref[2] * chunk
    return (lax.broadcasted_iota(jnp.int32, (chunk, tokens), 1) == pick).astype(LOW)


def beside_kernel(n_row, place_ref, after_ref, order_ref, cot_ref, w_ref, x_ref, tokens_ref, mixed_ref, mine_ref):
    del after_ref
    group, width = cot_ref.shape[:2]
    n_col = group // n_row
    order = order_ref[...]
    cot = [cot_ref[row * n_col + core] for core in range(n_col) for row in range(n_row)]
    tokens_ref[...] = dot(jnp.concatenate(cot, axis=0), order, 0, 0).astype(LOW)
    mixed_ref[...] = dot(order, w_ref[:, : 3 * width], 1, 0).astype(LOW)
    pick = own_tokens(place_ref, mine_ref.shape[0], x_ref.shape[1])
    mine_ref[...] = dot(dot(pick, x_ref[...], 1, 1).astype(LOW), order, 1, 0)


def beside(place, after, order, cot_all, w_first, x_all, n_row, chunk):
    group, width, tokens = cot_all.shape
    return pl.pallas_call(
        partial(beside_kernel, n_row),
        in_specs=[SMEM, ANY] + [VMEM] * 4,
        out_specs=[VMEM] * 3,
        out_shape=(
            jax.ShapeDtypeStruct((tokens, D), LOW),
            jax.ShapeDtypeStruct((D, 3 * width), LOW),
            jax.ShapeDtypeStruct((chunk, D), jnp.float32),
        ),
        compiler_params=BIG,
        name="beside",
    )(place, after, order, cot_all, w_first, x_all)


def before_kernel(place_ref, after_ref, order_ref, cot_ref, *refs):
    del after_ref
    *parts, up_ref, grad_ref, mixed_ref, scratch = refs
    w_rest = assembled(place_ref[1], parts, scratch)
    wide = up_ref.shape[1]
    up_ref[...] = w_rest[:, :wide]
    w_down = w_rest[:, wide:]
    grad_ref[...] = dot(cot_ref[...], w_down, 1, 0)
    mixed_ref[...] = dot(order_ref[...], w_down, 1, 0).astype(LOW)


def before(place, after, order, cot_tokens, parts):
    wide = parts[0].shape[1] // 2
    return pl.pallas_call(
        before_kernel,
        in_specs=[SMEM, ANY, VMEM, VMEM] + [VMEM] * len(parts),
        out_specs=[VMEM] * 3,
        out_shape=(
            jax.ShapeDtypeStruct((D, wide), LOW),
            jax.ShapeDtypeStruct((cot_tokens.shape[0], wide), jnp.float32),
            jax.ShapeDtypeStruct((D, wide), LOW),
        ),
        scratch_shapes=[part_scratch(parts)],
        compiler_params=BIG,
        name="before",
    )(place, after, order, cot_tokens, *parts)


def behind_kernel(
    place_ref, after_ref, zb_ref, hid_ref, cot_ref, act_ref, down_ref, mid_ref, grad_ref, theirs_ref, mine_ref
):
    del after_ref
    active = act_ref[...]
    up_grad = dot(zb_ref[...], hid_ref[...], 0, 0).astype(LOW)
    down_grad = dot(cot_ref[...], active, 0, 0).astype(LOW)
    store_parts(place_ref[1], jnp.concatenate([up_grad, down_grad], axis=1), grad_ref)
    pick = own_tokens(place_ref, mid_ref.shape[1], active.shape[0])
    result = dot(down_ref[...], active, 1, 1) + dot(mid_ref[...], pick, 1, 0)
    result = result.astype(LOW)
    half = D // 2
    split_cores(place_ref[0], result[:half], result[half:], theirs_ref, mine_ref)


def behind(place, after, zb, hidden_grad, cot_tokens, active, down_mixed, middle_mixed, n_dp):
    tokens, wide = active.shape
    return pl.pallas_call(
        behind_kernel,
        in_specs=[SMEM, ANY] + [VMEM] * 6,
        out_specs=[VMEM] * 3,
        out_shape=(
            jax.ShapeDtypeStruct((n_dp, D // n_dp, 2 * wide), LOW),
            jax.ShapeDtypeStruct((D // 2, tokens), LOW),
            jax.ShapeDtypeStruct((D // 2, tokens), LOW),
        ),
        compiler_params=BIG,
        name="behind",
    )(place, after, zb, hidden_grad, cot_tokens, active, down_mixed, middle_mixed)


def mlp_kernel(core_ref, zb_ref, up_ref, bias_ref, grad_ref, act_ref, hid_ref, two_ref, sum_ref):
    hidden = dot(zb_ref[...], up_ref[...], 1, 0) + bias_ref[...]
    square = hidden * hidden
    slope = 0.7978845608028654 * (1.0 + 0.044715 * square)
    bent = jnp.tanh(hidden * slope)
    gate = 0.5 * (1.0 + bent)
    act_ref[...] = (hidden * gate).astype(LOW)
    steep = gate + 0.5 * hidden * (1.0 - bent * bent) * (
        0.7978845608028654 * (1.0 + 3 * 0.044715 * square)
    )
    hidden_grad = (grad_ref[...] * steep).astype(LOW)
    hid_ref[...] = hidden_grad
    two_ref[...] = dot(hidden_grad, up_ref[...], 1, 1).astype(LOW)

    @pl.when(pl.program_id(0) == 0)
    def _():
        sum_ref[...] = jnp.zeros(sum_ref.shape, jnp.float32)

    sum_ref[...] += jnp.sum(hidden_grad.astype(jnp.float32), axis=0, keepdims=True)


def mlp(core, zb, w_up, up_bias, active_grad):
    tokens = zb.shape[0]
    wide = w_up.shape[1]
    steps = 6
    block = tokens // steps
    turned = lambda i, c: ((i + (steps // 2) * (1 - c[0])) % steps, 0)
    whole = lambda i, c: (0, 0)
    return pl.pallas_call(
        mlp_kernel,
        grid_spec=pltpu.PrefetchScalarGridSpec(
            num_scalar_prefetch=1,
            grid=(steps,),
            in_specs=[
                pl.BlockSpec((block, D), turned),
                pl.BlockSpec((D, wide), whole),
                pl.BlockSpec((1, wide), whole),
                pl.BlockSpec((block, wide), turned),
            ],
            out_specs=[
                pl.BlockSpec((block, wide), turned),
                pl.BlockSpec((block, wide), turned),
                pl.BlockSpec((block, D), lambda i, c: (i, 0)),
                pl.BlockSpec((1, wide), whole),
            ],
        ),
        out_shape=(
            jax.ShapeDtypeStruct((tokens, wide), LOW),
            jax.ShapeDtypeStruct((tokens, wide), LOW),
            jax.ShapeDtypeStruct((tokens, D), LOW),
            jax.ShapeDtypeStruct((1, wide), jnp.float32),
        ),
        compiler_params=BIG,
        name="mlp",
    )(core, zb, w_up, up_bias, active_grad)


def back_kernel(place_ref, bg_ref, w_ref, qkv_ref, za_ref, att_ref, grad_ref, sum_ref, wg_ref):
    heads = qkv_ref.shape[0]
    attended_grad = dot(bg_ref[...], w_ref[:, heads * 3 * HEAD :], 1, 0).T
    scale = HEAD ** (-0.5)
    parts = []
    for head in range(heads):
        queries, key_rows, values = qkv_ref[head, 0], qkv_ref[head, 1], qkv_ref[head, 2]
        grad = attended_grad[head * HEAD : (head + 1) * HEAD].astype(LOW)
        probs = head_probs(queries, key_rows)
        probs_grad = dot(grad, values, 0, 0)
        inner = jnp.sum(probs * probs_grad, axis=1, keepdims=True)
        scores_grad = (probs * (probs_grad - inner)).astype(LOW)
        parts.append(dot(key_rows, scores_grad, 1, 1) * scale)
        parts.append(dot(queries, scores_grad, 1, 0) * scale)
        parts.append(dot(grad, probs.astype(LOW), 1, 0))
    qkv_grad = jnp.concatenate(parts, axis=0).astype(LOW)
    grad_ref[...] = qkv_grad
    sum_ref[...] = jnp.sum(qkv_grad.astype(jnp.float32), axis=1, keepdims=True)
    qkv_part = dot(za_ref[...], qkv_grad, 1, 1).astype(LOW)
    out_part = dot(bg_ref[...], att_ref[...], 0, 0).astype(LOW)
    store_parts(place_ref[1], jnp.concatenate([qkv_part, out_part], axis=1), wg_ref)


def attend_back(place, branch_all, w_first, qkv, za, attended, n_dp):
    tokens, width = attended.shape
    return pl.pallas_call(
        back_kernel,
        in_specs=[SMEM] + [VMEM] * 5,
        out_specs=[VMEM] * 3,
        out_shape=(
            jax.ShapeDtypeStruct((3 * width, tokens), LOW),
            jax.ShapeDtypeStruct((3 * width, 1), jnp.float32),
            jax.ShapeDtypeStruct((n_dp, D // n_dp, 4 * width), LOW),
        ),
        compiler_params=BIG,
        name="attend_back",
    )(place, branch_all, w_first, qkv, za, attended)


def first_kernel(core_ref, w_ref, grad_ref, x_ref, mean_ref, inv_ref, gain_ref, theirs_ref, mine_ref, sum_ref):
    n_row, rows, tokens = theirs_ref.shape
    width = rows - 16
    first = jnp.zeros((1, tokens), jnp.float32)
    second = jnp.zeros((1, tokens), jnp.float32)
    blocks = []
    for slot in range(D // width):
        here = slice(slot * width, (slot + 1) * width)
        part = dot(w_ref[here], grad_ref[...], 1, 0)
        normed = (x_ref[here].astype(jnp.float32) - mean_ref[...]) * inv_ref[...]
        product = part * normed
        sum_ref[here, 0:1] = jnp.sum(product, axis=1, keepdims=True)
        sum_ref[here, 1:2] = jnp.sum(part, axis=1, keepdims=True)
        first += jnp.sum(part * gain_ref[here], axis=0, keepdims=True)
        second += jnp.sum(product * gain_ref[here], axis=0, keepdims=True)
        blocks.append(part.astype(LOW))
    line = lax.broadcasted_iota(jnp.int32, (16, tokens), 0)
    sums = jnp.where(line == 0, first, jnp.where(line == 1, second, 0.0)).astype(LOW)
    for near, ref in ((False, theirs_ref), (True, mine_ref)):
        for core in range(2):

            @pl.when((core_ref[0] == core) == near)
            def _(core=core, ref=ref):
                for row in range(n_row):
                    ref[row, :width] = blocks[core * n_row + row]
                    ref[row, width:] = sums


def first_back(core, w_mixed, qkv_grad, x_all, x_mean, inverse, gain, width, n_row):
    tokens = x_all.shape[1]
    return pl.pallas_call(
        first_kernel,
        in_specs=[SMEM] + [VMEM] * 6,
        out_specs=[VMEM] * 3,
        out_shape=(
            jax.ShapeDtypeStruct((n_row, width + 16, tokens), LOW),
            jax.ShapeDtypeStruct((n_row, width + 16, tokens), LOW),
            jax.ShapeDtypeStruct((D, 2), jnp.float32),
        ),
        compiler_params=BIG,
        name="first_back",
    )(core, w_mixed, qkv_grad, x_all, x_mean, inverse, gain)


def adam_update(weights, moment_one, second, gradient, step_rate, weight_decay):
    moment_one = BETA_ONE * moment_one + (1.0 - BETA_ONE) * gradient
    second = BETA_TWO * second + (1.0 - BETA_TWO) * gradient * gradient
    direction = (
        moment_one / (1.0 - BETA_ONE**STEP) / (jnp.sqrt(second / (1.0 - BETA_TWO**STEP)) + ADAM_EPS)
    )
    return (weights - step_rate * (direction + weight_decay * weights), moment_one, second)


def shards(
    inputs,
    cotangent,
    qkv_master,
    out_master,
    up_master,
    down_master,
    qkv_first,
    out_first,
    up_first,
    down_first,
    qkv_second,
    out_second,
    up_second,
    down_second,
    norm_gains,
    gain_first,
    gain_second,
    biases,
    bias_first,
    bias_second,
):
    tokens, width = inputs.shape
    n_row = lax.axis_size("row")
    n_col = lax.axis_size("col")
    n_dp = lax.axis_size("dp")
    row = lax.axis_index("row")
    core = lax.axis_index("col")
    group = n_row * n_col
    heads = width // HEAD
    hidden_width = FF // group
    own = core * n_row + row
    place = jnp.stack([core, lax.axis_index("dp"), own]).astype(jnp.int32)
    chunk = -(-tokens // (group * 16)) * 16
    padded = chunk * group
    half = padded // n_col
    shard_rows = qkv_master.shape[0]

    index = jnp.arange(D)
    feature = (
        ((index // width) % n_row) * n_col + index // (width * n_row)
    ) * width + index % width
    index = (feature % n_dp) * (D // n_dp) + feature // n_dp
    order = (lax.broadcasted_iota(jnp.int32, (D, D), 1) == index[:, None]).astype(LOW)
    order = lax.optimization_barrier(order)

    def mixed(vector):
        return vector.reshape(n_row, n_col, width).transpose(1, 0, 2).reshape(D)

    def dealt(vector):
        return vector.reshape(D // n_dp, n_dp).T.reshape(D)

    def returned(rows):
        return exchange_rows(rows.reshape(n_row, shard_rows, -1))

    def long(array):
        return jnp.pad(array, ((0, 0), (0, padded - tokens)))

    flat = lambda array: array.transpose(1, 2, 0)
    tall = lambda array: array.transpose(2, 0, 1)
    first_rows = prepare(place, qkv_master, flat(out_master), n_row)
    first_rows = exchange_rows(first_rows).reshape(D // n_dp, -1)
    x_own = long(inputs.T)
    x_rows = lax.all_gather(x_own, "row", axis=0, tiled=True)
    first_parts = gather_parts(first_rows, "dp")
    rest = prepare(x_rows, up_master, flat(down_master), n_row)
    rest = exchange_rows(rest).reshape(D // n_dp, -1)
    rest_parts = gather_parts(rest, "dp")
    x_all = both_cores(x_rows)
    cot_own = long(cotangent.T) + zero_of(x_rows).astype(LOW)
    cot_all = lax.all_gather(cot_own, ("row", "col"), axis=0)

    gain_one = mixed(norm_gains[0])
    gain_two = dealt(norm_gains[1])
    shift_one = mixed(biases[:D])
    shift_two = dealt(biases[D : 2 * D])
    query_bias = lax.dynamic_slice_in_dim(biases, 2 * D + own * width, width).reshape(heads, HEAD)
    value_bias = lax.dynamic_slice_in_dim(biases, 3 * D + own * width, width).reshape(heads, HEAD)
    out_bias = dealt(biases[4 * D : 5 * D])
    feature_start = (row * n_col + core) * width
    down_bias = lax.dynamic_slice_in_dim(biases, 5 * D + feature_start, width)
    up_bias = lax.dynamic_slice_in_dim(biases, 6 * D + own * hidden_width, hidden_width)
    qkv_bias = jnp.stack([query_bias, jnp.zeros_like(query_bias), value_bias], axis=1).reshape(
        3 * width, 1
    )

    x_full = x_all.astype(jnp.float32)
    x_mean = jnp.sum(x_full, axis=0, keepdims=True) / D
    center = x_full - x_mean
    inverse_one = lax.rsqrt(jnp.sum(center * center, axis=0, keepdims=True) / D + NORM_EPS)
    za = (center * inverse_one * gain_one[:, None] + shift_one[:, None]).astype(LOW)
    za = dot(order, za, 0, 0, LOW)

    w_first, qkv, attended, theirs, mine = attend(place, za, qkv_bias, first_parts, width)
    pair = (mine.astype(jnp.float32) + swap_cores(theirs).astype(jnp.float32)).astype(LOW)
    branch = sum_over_rows(pair)
    cot_tokens, qkv_mixed, x_mine = beside(
        place, pair, order, cot_all, w_first, x_all, n_row, chunk
    )
    cot_mine = take(cot_tokens, own, chunk).astype(jnp.float32)

    middle = x_mine + branch + out_bias[None, :]
    center = middle - jnp.sum(middle, axis=1, keepdims=True) / D
    inverse_two = lax.rsqrt(jnp.sum(center * center, axis=1, keepdims=True) / D + NORM_EPS)
    normed_two = center * inverse_two
    zb = (normed_two * gain_two + shift_two).astype(LOW)
    zb_rows = lax.all_gather(zb, "row", axis=0, tiled=True)
    w_up, active_grad, down_mixed = before(place, zb_rows, order, cot_tokens, rest_parts)
    zb = both_cores(zb_rows)

    core_of = core.reshape(1).astype(jnp.int32)
    active, hidden_grad, two_parts, up_sums = mlp(core_of, zb, w_up, up_bias[None, :], active_grad)
    pair = two_parts[half:].astype(jnp.float32) + swap_cores(two_parts[:half]).astype(jnp.float32)
    pair = pair.astype(LOW)
    two_grad = sum_over_rows(pair)

    middle_mixed = dot(order, middle.astype(LOW), 1, 1, LOW)
    rest_grad, theirs, mine = behind(
        place, pair, zb, hidden_grad, cot_tokens, active, down_mixed, middle_mixed, n_dp
    )
    result = mine.astype(jnp.float32) + swap_cores(theirs).astype(jnp.float32)

    scaled = two_grad * gain_two
    first_sum = jnp.sum(scaled, axis=1, keepdims=True) / D
    second_sum = jnp.sum(scaled * normed_two, axis=1, keepdims=True) / D
    middle_grad = cot_mine + inverse_two * (scaled - first_sum - normed_two * second_sum)
    middle_grad = middle_grad.astype(LOW)
    branch_rows = lax.all_gather(middle_grad, "row", axis=0, tiled=True)
    later = zero_of(branch_rows)
    result = sum_over_rows(result + later) + down_bias[:, None]
    result = result.astype(LOW)[:, :tokens].T
    branch_all = both_cores(branch_rows)

    qkv_grad, bias_sums, first_grad = attend_back(
        place, branch_all, w_first, qkv, za, attended, n_dp
    )
    theirs, mine, one_sums = first_back(
        core_of, qkv_mixed, qkv_grad, x_all, x_mean, inverse_one, gain_one[:, None], width, n_row
    )
    pair = (mine.astype(jnp.float32) + swap_cores(theirs).astype(jnp.float32)).astype(LOW)
    one_grad = sum_over_rows(pair.reshape(-1, padded))
    first_rows = sum_parts(first_grad, "dp", 0.0)
    rest_rows = sum_parts(rest_grad, "dp", later)

    own_gain = lax.dynamic_slice_in_dim(norm_gains[0], feature_start, width)[:, None]
    own_normed = (x_own.astype(jnp.float32) - x_mean) * inverse_one
    own_order = lax.dynamic_slice_in_dim(order, own * width, width, axis=0)
    own_middle = dot(own_order, branch_all, 1, 1)
    input_grad = own_middle + inverse_one * (
        one_grad[:width] * own_gain
        - one_grad[width : width + 1] / D
        - own_normed * (one_grad[width + 1 : width + 2] / D)
    )
    input_grad = input_grad.astype(LOW)[:, :tokens].T

    later = zero_of(pair)
    bias_sums = bias_sums.reshape(heads, 3, HEAD)
    all_rows = jnp.stack(
        [
            one_sums[:, 0],
            one_sums[:, 1],
            jnp.sum(two_grad * normed_two, axis=0),
            jnp.sum(two_grad, axis=0),
            jnp.sum(middle_grad, axis=0, dtype=jnp.float32),
            jnp.sum(cot_mine, axis=0),
        ]
    )
    own_row = jnp.concatenate(
        [bias_sums[:, 0].reshape(width), bias_sums[:, 2].reshape(width), up_sums[0]]
    )
    own_row = jnp.pad(own_row, (0, D - own_row.shape[0]))
    own_rows = jnp.where(jnp.arange(group)[:, None] == own, own_row[None, :], 0.0)
    total = all_sum(jnp.concatenate([jnp.pad(all_rows, ((0, 2), (0, 0))), own_rows]) + later)
    one_rows = total[:2].reshape(2, n_col, n_row, width).transpose(0, 2, 1, 3).reshape(2, D)
    two_rows = total[2:6].reshape(4, n_dp, D // n_dp).transpose(0, 2, 1).reshape(4, D)
    own_rows = total[8:]
    gain_total = jnp.stack([one_rows[0], two_rows[0]])
    bias_total = jnp.concatenate(
        [
            one_rows[1],
            two_rows[1],
            own_rows[:, :width].reshape(D),
            own_rows[:, width : 2 * width].reshape(D),
            two_rows[2],
            two_rows[3],
            own_rows[:, 2 * width : 2 * width + hidden_width].reshape(FF),
        ]
    )

    rest_new = adam(
        pair,
        returned(rest_rows),
        (0.03, 0.02),
        up_master,
        up_first,
        up_second,
        flat(down_master),
        flat(down_first),
        flat(down_second),
    )
    first_new = adam(
        pair,
        returned(first_rows),
        (0.03, 0.12),
        qkv_master,
        qkv_first,
        qkv_second,
        flat(out_master),
        flat(out_first),
        flat(out_second),
    )
    g_new = adam_update(norm_gains, gain_first, gain_second, gain_total, 0.5, 0.0)
    b_new = adam_update(biases, bias_first, bias_second, bias_total, 0.5, 0.0)
    return (
        result,
        input_grad,
        *first_new[:3],
        *(tall(array) for array in first_new[3:]),
        *rest_new[:3],
        *(tall(array) for array in rest_new[3:]),
        *g_new,
        *b_new,
    )


def solution(mesh):
    token_spec = P("dp", ("row", "col"))
    wide = P("row", "dp", "col")
    tall = P("col", "row", "dp")
    return jax.shard_map(
        shards,
        mesh=mesh,
        in_specs=(token_spec,) * 2 + (wide, tall, wide, tall) * 3 + (P(),) * 6,
        out_specs=(token_spec,) * 2
        + (wide,) * 3
        + (tall,) * 3
        + (wide,) * 3
        + (tall,) * 3
        + (P(),) * 6,
        check_vma=False,
    )
```

```python
from functools import partial

import jax
import jax.numpy as jnp
from jax import lax
from jax.experimental import pallas as pl
from jax.experimental.pallas import tpu as pltpu
from jax.sharding import PartitionSpec as P

D = 1152
FF = 4304
HEAD = 72
SEQ = 729
STEP = 10

NORM_EPS = 1e-06
ADAM_EPS = 1e-08
BETA_ONE = 0.9
BETA_TWO = 0.999
LOW = jnp.bfloat16


def dot(left, right, left_dim, right_dim, out=jnp.float32, precision=None):
    return lax.dot_general(
        left,
        right,
        (((left_dim,), (right_dim,)), ((), ())),
        precision=precision,
        preferred_element_type=out,
    )


def take(array, index, size):
    return lax.dynamic_slice_in_dim(array, index * size, size, axis=0)


def swap_cores(array):
    n_col = lax.axis_size("col")
    return lax.ppermute(array, "col", [(i, (i + 1) % n_col) for i in range(n_col)])


def both_cores(rows):
    pieces = [
        lax.all_gather(piece, "col", axis=0) for piece in jnp.split(rows, 2, axis=0)
    ]
    return jnp.concatenate(pieces, axis=1).reshape(-1, rows.shape[1])


def gather_parts(block, axis):
    size = lax.axis_size(axis)
    if size > 4:
        copies = jnp.broadcast_to(block, (size,) + block.shape)
        return [lax.all_to_all(copies, axis, 0, 0).reshape(-1, block.shape[1])]
    return [block] + [
        lax.ppermute(block, axis, [(i, i ^ step) for i in range(size)]) for step in range(1, size)
    ]


def zero_of(array):
    first = lax.slice(array, (0,) * array.ndim, (1,) * array.ndim)
    return first.reshape(()).astype(jnp.float32) * 0.0


def exchange_rows(blocks):
    return lax.all_to_all(blocks, "row", 0, 0)


def sum_blocks(blocks, axis, later):
    blocks = lax.all_to_all(blocks, axis, 0, 0)
    return jnp.sum(blocks.astype(jnp.float32) + later, axis=0).astype(LOW)


def sum_over_rows(half):
    summed = lax.psum_scatter(half.astype(LOW), "row", scatter_dimension=0, tiled=True)
    return summed.astype(jnp.float32)


def all_sum(vector):
    for axis in ("col", "row", "dp"):
        size = lax.axis_size(axis)
        if size & (size - 1) or size > 4:
            vector = lax.psum(vector, axis)
            continue
        step = 1
        while step < size:
            vector = vector + lax.ppermute(vector, axis, [(i, i ^ step) for i in range(size)])
            step *= 2
    return vector


VMEM = pl.BlockSpec(memory_space=pltpu.VMEM)
SMEM = pl.BlockSpec(memory_space=pltpu.SMEM)
ANY = pl.BlockSpec(memory_space=pl.ANY)
BIG = pltpu.CompilerParams(vmem_limit_bytes=56 * 1024 * 1024)


def prepare_kernel(parts, after_ref, wide_ref, tall_ref, out_ref):
    del after_ref
    arrays = [ref[:, 0, :].astype(LOW) for ref in (wide_ref, tall_ref)]
    for part in range(parts):
        pieces = []
        for array in arrays:
            size = array.shape[1] // parts
            pieces.append(array[:, part * size : (part + 1) * size])
        out_ref[part] = jnp.concatenate(pieces, axis=1)


def prepare(after, wide, tall, parts):
    rows = wide.shape[0]
    size = (wide.shape[2] + tall.shape[2]) // parts
    return pl.pallas_call(
        partial(prepare_kernel, parts),
        in_specs=[ANY, VMEM, VMEM],
        out_specs=VMEM,
        out_shape=jax.ShapeDtypeStruct((parts, rows, size), LOW),
        compiler_params=BIG,
        name="prepare",
    )(after, wide, tall)


def adam_kernel(rates, after_ref, blocks_ref, *refs):
    del after_ref
    parts = blocks_ref.shape[0]
    start = 0
    for index, rate in enumerate(rates):
        weight, first, second = refs[3 * index : 3 * index + 3]
        size = weight.shape[2] // parts
        gradient = jnp.concatenate(
            [blocks_ref[part, :, start : start + size] for part in range(parts)], axis=1
        ).astype(jnp.float32)
        start += size
        new = adam_update(weight[:, 0, :], first[:, 0, :], second[:, 0, :], gradient, rate, 0.1)
        for array, ref in zip(new, refs[3 * len(rates) + 3 * index :]):
            ref[:, 0, :] = array


def adam(after, blocks, rates, *arrays):
    return pl.pallas_call(
        partial(adam_kernel, rates),
        in_specs=[ANY] + [VMEM] * (1 + len(arrays)),
        out_specs=[VMEM] * len(arrays),
        out_shape=[jax.ShapeDtypeStruct(a.shape, jnp.float32) for a in arrays],
        compiler_params=BIG,
        name="adam",
    )(after, blocks, *arrays)


def assembled(place, parts, scratch):
    if len(parts) == 1:
        return parts[0][...]
    for step, part in enumerate(parts):
        scratch[place ^ step] = part[...]
    return scratch[...].reshape(-1, scratch.shape[2])


def part_scratch(parts):
    return pltpu.VMEM((len(parts),) + parts[0].shape, LOW)


def head_probs(queries, key_rows):
    scores = dot(queries, key_rows, 0, 0) * HEAD ** (-0.5)
    scores = jnp.where(lax.broadcasted_iota(jnp.int32, scores.shape, 1) < SEQ, scores, -1e30)
    exponent = jnp.exp(scores - jnp.max(scores, axis=1, keepdims=True))
    return exponent * (1.0 / jnp.sum(exponent, axis=1, keepdims=True))


def split_cores(core, first, second, theirs_ref, mine_ref):
    @pl.when(core == 0)
    def _():
        mine_ref[...] = first
        theirs_ref[...] = second

    @pl.when(core != 0)
    def _():
        mine_ref[...] = second
        theirs_ref[...] = first


def attend_kernel(place_ref, after_ref, za_ref, bias_ref, *refs):
    del after_ref
    *parts, w_ref, qkv_ref, att_ref, theirs_ref, mine_ref, scratch = refs
    w_ref[...] = assembled(place_ref[1], parts, scratch)
    heads = qkv_ref.shape[0]
    split = heads * 3 * HEAD
    qkv = dot(w_ref[:, :split], za_ref[...], 0, 0) + bias_ref[...]
    outs = []
    for head in range(heads):
        for t in range(3):
            start = (head * 3 + t) * HEAD
            qkv_ref[head, t] = qkv[start : start + HEAD].astype(LOW)
        probs = head_probs(qkv_ref[head, 0], qkv_ref[head, 1]).astype(LOW)
        outs.append(dot(qkv_ref[head, 2], probs, 1, 1))
    attended = jnp.concatenate(outs, axis=0).T.astype(LOW)
    att_ref[...] = attended
    branch = dot(attended, w_ref[:, split:], 1, 1).astype(LOW)
    half = branch.shape[0] // 2
    split_cores(place_ref[0], branch[:half], branch[half:], theirs_ref, mine_ref)


def attend(place, after, za, qkv_bias, parts, width):
    tokens = za.shape[1]
    return pl.pallas_call(
        attend_kernel,
        in_specs=[SMEM, ANY, VMEM, VMEM] + [VMEM] * len(parts),
        out_specs=[VMEM] * 5,
        out_shape=(
            jax.ShapeDtypeStruct((D, 4 * width), LOW),
            jax.ShapeDtypeStruct((width // HEAD, 3, HEAD, tokens), LOW),
            jax.ShapeDtypeStruct((tokens, width), LOW),
            jax.ShapeDtypeStruct((tokens // 2, D), LOW),
            jax.ShapeDtypeStruct((tokens // 2, D), LOW),
        ),
        scratch_shapes=[part_scratch(parts)],
        compiler_params=BIG,
        name="attend",
    )(place, after, za, qkv_bias, *parts)


def own_tokens(place_ref, chunk, tokens):
    pick = lax.broadcasted_iota(jnp.int32, (chunk, tokens), 0) + place_ref[2] * chunk
    return (lax.broadcasted_iota(jnp.int32, (chunk, tokens), 1) == pick).astype(LOW)


def beside_kernel(n_row, place_ref, after_ref, order_ref, cot_ref, w_ref, x_ref, tokens_ref, mixed_ref, mine_ref):
    del after_ref
    group, width = cot_ref.shape[:2]
    n_col = group // n_row
    order = order_ref[...]
    cot = [cot_ref[row * n_col + core] for core in range(n_col) for row in range(n_row)]
    tokens_ref[...] = dot(jnp.concatenate(cot, axis=0), order, 0, 0).astype(LOW)
    mixed_ref[...] = dot(order, w_ref[:, : 3 * width], 1, 0).astype(LOW)
    pick = own_tokens(place_ref, mine_ref.shape[0], x_ref.shape[1])
    mine_ref[...] = dot(dot(pick, x_ref[...], 1, 1).astype(LOW), order, 1, 0)


def beside(place, after, order, cot_all, w_first, x_all, n_row, chunk):
    group, width, tokens = cot_all.shape
    return pl.pallas_call(
        partial(beside_kernel, n_row),
        in_specs=[SMEM, ANY] + [VMEM] * 4,
        out_specs=[VMEM] * 3,
        out_shape=(
            jax.ShapeDtypeStruct((tokens, D), LOW),
            jax.ShapeDtypeStruct((D, 3 * width), LOW),
            jax.ShapeDtypeStruct((chunk, D), jnp.float32),
        ),
        compiler_params=BIG,
        name="beside",
    )(place, after, order, cot_all, w_first, x_all)


def before_kernel(place_ref, after_ref, order_ref, cot_ref, *refs):
    del after_ref
    *parts, up_ref, grad_ref, mixed_ref, scratch = refs
    w_rest = assembled(place_ref[1], parts, scratch)
    wide = up_ref.shape[1]
    up_ref[...] = w_rest[:, :wide]
    w_down = w_rest[:, wide:]
    grad_ref[...] = dot(cot_ref[...], w_down, 1, 0)
    mixed_ref[...] = dot(order_ref[...], w_down, 1, 0).astype(LOW)


def before(place, after, order, cot_tokens, parts):
    wide = parts[0].shape[1] // 2
    return pl.pallas_call(
        before_kernel,
        in_specs=[SMEM, ANY, VMEM, VMEM] + [VMEM] * len(parts),
        out_specs=[VMEM] * 3,
        out_shape=(
            jax.ShapeDtypeStruct((D, wide), LOW),
            jax.ShapeDtypeStruct((cot_tokens.shape[0], wide), jnp.float32),
            jax.ShapeDtypeStruct((D, wide), LOW),
        ),
        scratch_shapes=[part_scratch(parts)],
        compiler_params=BIG,
        name="before",
    )(place, after, order, cot_tokens, *parts)


def behind_kernel(
    place_ref, after_ref, zb_ref, hid_ref, cot_ref, act_ref, down_ref, mid_ref, grad_ref, theirs_ref, mine_ref
):
    del after_ref
    active = act_ref[...]
    up_grad = dot(zb_ref[...], hid_ref[...], 0, 0).astype(LOW)
    down_grad = dot(cot_ref[...], active, 0, 0).astype(LOW)
    grad_ref[...] = jnp.concatenate([up_grad, down_grad], axis=1).reshape(grad_ref.shape)
    pick = own_tokens(place_ref, mid_ref.shape[1], active.shape[0])
    result = dot(down_ref[...], active, 1, 1) + dot(mid_ref[...], pick, 1, 0)
    result = result.astype(LOW)
    half = D // 2
    split_cores(place_ref[0], result[:half], result[half:], theirs_ref, mine_ref)


def behind(place, after, zb, hidden_grad, cot_tokens, active, down_mixed, middle_mixed, n_dp):
    tokens, wide = active.shape
    return pl.pallas_call(
        behind_kernel,
        in_specs=[SMEM, ANY] + [VMEM] * 6,
        out_specs=[VMEM] * 3,
        out_shape=(
            jax.ShapeDtypeStruct((n_dp, D // n_dp, 2 * wide), LOW),
            jax.ShapeDtypeStruct((D // 2, tokens), LOW),
            jax.ShapeDtypeStruct((D // 2, tokens), LOW),
        ),
        compiler_params=BIG,
        name="behind",
    )(place, after, zb, hidden_grad, cot_tokens, active, down_mixed, middle_mixed)


def mlp_kernel(
    core_ref, zb_ref, up_ref, bias_ref, grad_ref, act_ref, hid_ref, theirs_ref, mine_ref, sum_ref
):
    step = pl.program_id(0)
    near = step >= pl.num_programs(0) // 2
    hidden = dot(zb_ref[...], up_ref[...], 1, 0) + bias_ref[...]
    square = hidden * hidden
    slope = 0.7978845608028654 * (1.0 + 0.044715 * square)
    bent = jnp.tanh(hidden * slope)
    gate = 0.5 * (1.0 + bent)
    act_ref[...] = (hidden * gate).astype(LOW)
    steep = gate + 0.5 * hidden * (1.0 - bent * bent) * (
        0.7978845608028654 * (1.0 + 3 * 0.044715 * square)
    )
    hidden_grad = (grad_ref[...] * steep).astype(LOW)
    hid_ref[...] = hidden_grad
    two_grad = dot(hidden_grad, up_ref[...], 1, 1).astype(LOW)

    @pl.when(near)
    def _():
        mine_ref[...] = two_grad

    @pl.when(jnp.logical_not(near))
    def _():
        theirs_ref[...] = two_grad

    @pl.when(step == 0)
    def _():
        sum_ref[...] = jnp.zeros(sum_ref.shape, jnp.float32)

    sum_ref[...] += jnp.sum(hidden_grad.astype(jnp.float32), axis=0, keepdims=True)


def mlp(core, zb, w_up, up_bias, active_grad):
    tokens = zb.shape[0]
    wide = w_up.shape[1]
    steps = 6
    block = tokens // steps
    turned = lambda i, c: ((i + (steps // 2) * (1 - c[0])) % steps, 0)
    whole = lambda i, c: (0, 0)
    return pl.pallas_call(
        mlp_kernel,
        grid_spec=pltpu.PrefetchScalarGridSpec(
            num_scalar_prefetch=1,
            grid=(steps,),
            in_specs=[
                pl.BlockSpec((block, D), turned),
                pl.BlockSpec((D, wide), whole),
                pl.BlockSpec((1, wide), whole),
                pl.BlockSpec((block, wide), turned),
            ],
            out_specs=[
                pl.BlockSpec((block, wide), turned),
                pl.BlockSpec((block, wide), turned),
                pl.BlockSpec((block, D), lambda i, c: (jnp.minimum(i, steps // 2 - 1), 0)),
                pl.BlockSpec((block, D), lambda i, c: (jnp.maximum(i - steps // 2, 0), 0)),
                pl.BlockSpec((1, wide), whole),
            ],
        ),
        out_shape=(
            jax.ShapeDtypeStruct((tokens, wide), LOW),
            jax.ShapeDtypeStruct((tokens, wide), LOW),
            jax.ShapeDtypeStruct((tokens // 2, D), LOW),
            jax.ShapeDtypeStruct((tokens // 2, D), LOW),
            jax.ShapeDtypeStruct((1, wide), jnp.float32),
        ),
        compiler_params=BIG,
        name="mlp",
    )(core, zb, w_up, up_bias, active_grad)


def back_kernel(bg_ref, w_ref, qkv_ref, za_ref, att_ref, grad_ref, sum_ref, wg_ref):
    heads = qkv_ref.shape[0]
    attended_grad = dot(bg_ref[...], w_ref[:, heads * 3 * HEAD :], 1, 0).T
    scale = HEAD ** (-0.5)
    parts = []
    for head in range(heads):
        queries, key_rows, values = qkv_ref[head, 0], qkv_ref[head, 1], qkv_ref[head, 2]
        grad = attended_grad[head * HEAD : (head + 1) * HEAD].astype(LOW)
        probs = head_probs(queries, key_rows)
        probs_grad = dot(grad, values, 0, 0)
        inner = jnp.sum(probs * probs_grad, axis=1, keepdims=True)
        scores_grad = (probs * (probs_grad - inner)).astype(LOW)
        parts.append(dot(key_rows, scores_grad, 1, 1) * scale)
        parts.append(dot(queries, scores_grad, 1, 0) * scale)
        parts.append(dot(grad, probs.astype(LOW), 1, 0))
    qkv_grad = jnp.concatenate(parts, axis=0).astype(LOW)
    grad_ref[...] = qkv_grad
    sum_ref[...] = jnp.sum(qkv_grad.astype(jnp.float32), axis=1, keepdims=True)
    qkv_part = dot(za_ref[...], qkv_grad, 1, 1).astype(LOW)
    out_part = dot(bg_ref[...], att_ref[...], 0, 0).astype(LOW)
    wg_ref[...] = jnp.concatenate([qkv_part, out_part], axis=1).reshape(wg_ref.shape)


def attend_back(branch_all, w_first, qkv, za, attended, n_dp):
    tokens, width = attended.shape
    return pl.pallas_call(
        back_kernel,
        in_specs=[VMEM] * 5,
        out_specs=[VMEM] * 3,
        out_shape=(
            jax.ShapeDtypeStruct((3 * width, tokens), LOW),
            jax.ShapeDtypeStruct((3 * width, 1), jnp.float32),
            jax.ShapeDtypeStruct((n_dp, D // n_dp, 4 * width), LOW),
        ),
        compiler_params=BIG,
        name="attend_back",
    )(branch_all, w_first, qkv, za, attended)


def first_kernel(core_ref, w_ref, grad_ref, x_ref, mean_ref, inv_ref, gain_ref, theirs_ref, mine_ref, sum_ref):
    n_row, rows, tokens = theirs_ref.shape
    width = rows - 16
    first = jnp.zeros((1, tokens), jnp.float32)
    second = jnp.zeros((1, tokens), jnp.float32)
    blocks = []
    for slot in range(D // width):
        here = slice(slot * width, (slot + 1) * width)
        part = dot(w_ref[here], grad_ref[...], 1, 0)
        normed = (x_ref[here].astype(jnp.float32) - mean_ref[...]) * inv_ref[...]
        product = part * normed
        sum_ref[here, 0:1] = jnp.sum(product, axis=1, keepdims=True)
        sum_ref[here, 1:2] = jnp.sum(part, axis=1, keepdims=True)
        first += jnp.sum(part * gain_ref[here], axis=0, keepdims=True)
        second += jnp.sum(product * gain_ref[here], axis=0, keepdims=True)
        blocks.append(part.astype(LOW))
    line = lax.broadcasted_iota(jnp.int32, (16, tokens), 0)
    sums = jnp.where(line == 0, first, jnp.where(line == 1, second, 0.0)).astype(LOW)
    for near, ref in ((False, theirs_ref), (True, mine_ref)):
        for core in range(2):

            @pl.when((core_ref[0] == core) == near)
            def _(core=core, ref=ref):
                for row in range(n_row):
                    ref[row, :width] = blocks[core * n_row + row]
                    ref[row, width:] = sums


def first_back(core, w_mixed, qkv_grad, x_all, x_mean, inverse, gain, width, n_row):
    tokens = x_all.shape[1]
    return pl.pallas_call(
        first_kernel,
        in_specs=[SMEM] + [VMEM] * 6,
        out_specs=[VMEM] * 3,
        out_shape=(
            jax.ShapeDtypeStruct((n_row, width + 16, tokens), LOW),
            jax.ShapeDtypeStruct((n_row, width + 16, tokens), LOW),
            jax.ShapeDtypeStruct((D, 2), jnp.float32),
        ),
        compiler_params=BIG,
        name="first_back",
    )(core, w_mixed, qkv_grad, x_all, x_mean, inverse, gain)


def adam_update(weights, moment_one, second, gradient, step_rate, weight_decay):
    moment_one = BETA_ONE * moment_one + (1.0 - BETA_ONE) * gradient
    second = BETA_TWO * second + (1.0 - BETA_TWO) * gradient * gradient
    direction = (
        moment_one / (1.0 - BETA_ONE**STEP) / (jnp.sqrt(second / (1.0 - BETA_TWO**STEP)) + ADAM_EPS)
    )
    return (weights - step_rate * (direction + weight_decay * weights), moment_one, second)


def shards(
    inputs,
    cotangent,
    qkv_master,
    out_master,
    up_master,
    down_master,
    qkv_first,
    out_first,
    up_first,
    down_first,
    qkv_second,
    out_second,
    up_second,
    down_second,
    norm_gains,
    gain_first,
    gain_second,
    biases,
    bias_first,
    bias_second,
):
    tokens, width = inputs.shape
    n_row = lax.axis_size("row")
    n_col = lax.axis_size("col")
    n_dp = lax.axis_size("dp")
    row = lax.axis_index("row")
    core = lax.axis_index("col")
    group = n_row * n_col
    heads = width // HEAD
    hidden_width = FF // group
    own = core * n_row + row
    place = jnp.stack([core, lax.axis_index("dp"), own]).astype(jnp.int32)
    chunk = -(-tokens // (group * 16)) * 16
    padded = chunk * group
    shard_rows = qkv_master.shape[0]

    index = jnp.arange(D)
    feature = (
        ((index // width) % n_row) * n_col + index // (width * n_row)
    ) * width + index % width
    index = (feature % n_dp) * (D // n_dp) + feature // n_dp
    order = (lax.broadcasted_iota(jnp.int32, (D, D), 1) == index[:, None]).astype(LOW)
    order = lax.optimization_barrier(order)

    def mixed(vector):
        return vector.reshape(n_row, n_col, width).transpose(1, 0, 2).reshape(D)

    def dealt(vector):
        return vector.reshape(D // n_dp, n_dp).T.reshape(D)

    def returned(rows):
        return exchange_rows(rows.reshape(n_row, shard_rows, -1))

    def long(array):
        return jnp.pad(array, ((0, 0), (0, padded - tokens)))

    flat = lambda array: array.transpose(1, 2, 0)
    tall = lambda array: array.transpose(2, 0, 1)
    first_rows = prepare(place, qkv_master, flat(out_master), n_row)
    first_rows = exchange_rows(first_rows).reshape(D // n_dp, -1)
    x_own = long(inputs.T)
    x_after = x_own + zero_of(first_rows).astype(LOW)
    x_rows = lax.all_gather(x_after, "row", axis=0, tiled=True)
    first_parts = gather_parts(first_rows, "dp")
    rest = prepare(x_rows, up_master, flat(down_master), n_row)
    rest = exchange_rows(rest).reshape(D // n_dp, -1)
    rest_parts = gather_parts(rest, "dp")
    x_all = both_cores(x_rows)
    cot_own = long(cotangent.T) + zero_of(rest).astype(LOW)
    cot_all = lax.all_gather(cot_own, ("row", "col"), axis=0)

    gain_one = mixed(norm_gains[0])
    gain_two = dealt(norm_gains[1])
    shift_one = mixed(biases[:D])
    shift_two = dealt(biases[D : 2 * D])
    query_bias = lax.dynamic_slice_in_dim(biases, 2 * D + own * width, width).reshape(heads, HEAD)
    value_bias = lax.dynamic_slice_in_dim(biases, 3 * D + own * width, width).reshape(heads, HEAD)
    out_bias = dealt(biases[4 * D : 5 * D])
    feature_start = (row * n_col + core) * width
    down_bias = lax.dynamic_slice_in_dim(biases, 5 * D + feature_start, width)
    up_bias = lax.dynamic_slice_in_dim(biases, 6 * D + own * hidden_width, hidden_width)
    qkv_bias = jnp.stack([query_bias, jnp.zeros_like(query_bias), value_bias], axis=1).reshape(
        3 * width, 1
    )

    x_full = x_all.astype(jnp.float32)
    x_mean = jnp.sum(x_full, axis=0, keepdims=True) / D
    center = x_full - x_mean
    inverse_one = lax.rsqrt(jnp.sum(center * center, axis=0, keepdims=True) / D + NORM_EPS)
    za = (center * inverse_one * gain_one[:, None] + shift_one[:, None]).astype(LOW)
    za = dot(order, za, 0, 0, LOW)

    w_first, qkv, attended, theirs, mine = attend(place, rest, za, qkv_bias, first_parts, width)
    pair = (mine.astype(jnp.float32) + swap_cores(theirs).astype(jnp.float32)).astype(LOW)
    branch = sum_over_rows(pair)
    cot_tokens, qkv_mixed, x_mine = beside(
        place, pair, order, cot_all, w_first, x_all, n_row, chunk
    )
    cot_mine = take(cot_tokens, own, chunk).astype(jnp.float32)

    middle = x_mine + branch + out_bias[None, :]
    center = middle - jnp.sum(middle, axis=1, keepdims=True) / D
    inverse_two = lax.rsqrt(jnp.sum(center * center, axis=1, keepdims=True) / D + NORM_EPS)
    normed_two = center * inverse_two
    zb = (normed_two * gain_two + shift_two).astype(LOW)
    zb_rows = lax.all_gather(zb, "row", axis=0, tiled=True)
    w_up, active_grad, down_mixed = before(place, zb_rows, order, cot_tokens, rest_parts)
    zb = both_cores(zb_rows)

    core_of = core.reshape(1).astype(jnp.int32)
    active, hidden_grad, theirs, mine, up_sums = mlp(
        core_of, zb, w_up, up_bias[None, :], active_grad
    )
    pair = (mine.astype(jnp.float32) + swap_cores(theirs).astype(jnp.float32)).astype(LOW)
    two_grad = sum_over_rows(pair)

    middle_mixed = dot(order, middle.astype(LOW), 1, 1, LOW)
    rest_grad, theirs, mine = behind(
        place, pair, zb, hidden_grad, cot_tokens, active, down_mixed, middle_mixed, n_dp
    )
    result = mine.astype(jnp.float32) + swap_cores(theirs).astype(jnp.float32)

    scaled = two_grad * gain_two
    first_sum = jnp.sum(scaled, axis=1, keepdims=True) / D
    second_sum = jnp.sum(scaled * normed_two, axis=1, keepdims=True) / D
    middle_grad = cot_mine + inverse_two * (scaled - first_sum - normed_two * second_sum)
    middle_grad = middle_grad.astype(LOW)
    branch_rows = lax.all_gather(middle_grad, "row", axis=0, tiled=True)
    later = zero_of(branch_rows)
    result = sum_over_rows(result + later) + down_bias[:, None]
    result = result.astype(LOW)[:, :tokens].T
    branch_all = both_cores(branch_rows)

    qkv_grad, bias_sums, first_grad = attend_back(
        branch_all, w_first, qkv, za, attended, n_dp
    )
    theirs, mine, one_sums = first_back(
        core_of, qkv_mixed, qkv_grad, x_all, x_mean, inverse_one, gain_one[:, None], width, n_row
    )
    pair = (mine.astype(jnp.float32) + swap_cores(theirs).astype(jnp.float32)).astype(LOW)
    one_grad = sum_over_rows(pair.reshape(-1, padded))
    first_rows = sum_blocks(first_grad, "dp", 0.0)
    rest_rows = sum_blocks(rest_grad, "dp", later)

    own_gain = lax.dynamic_slice_in_dim(norm_gains[0], feature_start, width)[:, None]
    own_normed = (x_own.astype(jnp.float32) - x_mean) * inverse_one
    own_order = lax.dynamic_slice_in_dim(order, own * width, width, axis=0)
    own_middle = dot(own_order, branch_all, 1, 1)
    input_grad = own_middle + inverse_one * (
        one_grad[:width] * own_gain
        - one_grad[width : width + 1] / D
        - own_normed * (one_grad[width + 1 : width + 2] / D)
    )
    input_grad = input_grad.astype(LOW)[:, :tokens].T

    later = zero_of(pair)
    bias_sums = bias_sums.reshape(heads, 3, HEAD)
    all_rows = jnp.stack(
        [
            one_sums[:, 0],
            one_sums[:, 1],
            jnp.sum(two_grad * normed_two, axis=0),
            jnp.sum(two_grad, axis=0),
            jnp.sum(middle_grad, axis=0, dtype=jnp.float32),
            jnp.sum(cot_mine, axis=0),
        ]
    )
    own_row = jnp.concatenate(
        [bias_sums[:, 0].reshape(width), bias_sums[:, 2].reshape(width), up_sums[0]]
    )
    own_row = jnp.pad(own_row, (0, D - own_row.shape[0]))
    own_rows = jnp.where(jnp.arange(group)[:, None] == own, own_row[None, :], 0.0)
    total = all_sum(jnp.concatenate([jnp.pad(all_rows, ((0, 2), (0, 0))), own_rows]) + later)
    one_rows = total[:2].reshape(2, n_col, n_row, width).transpose(0, 2, 1, 3).reshape(2, D)
    two_rows = total[2:6].reshape(4, n_dp, D // n_dp).transpose(0, 2, 1).reshape(4, D)
    own_rows = total[8:]
    gain_total = jnp.stack([one_rows[0], two_rows[0]])
    bias_total = jnp.concatenate(
        [
            one_rows[1],
            two_rows[1],
            own_rows[:, :width].reshape(D),
            own_rows[:, width : 2 * width].reshape(D),
            two_rows[2],
            two_rows[3],
            own_rows[:, 2 * width : 2 * width + hidden_width].reshape(FF),
        ]
    )

    rest_new = adam(
        pair,
        returned(rest_rows),
        (0.03, 0.02),
        up_master,
        up_first,
        up_second,
        flat(down_master),
        flat(down_first),
        flat(down_second),
    )
    first_new = adam(
        pair,
        returned(first_rows),
        (0.03, 0.12),
        qkv_master,
        qkv_first,
        qkv_second,
        flat(out_master),
        flat(out_first),
        flat(out_second),
    )
    g_new = adam_update(norm_gains, gain_first, gain_second, gain_total, 0.5, 0.0)
    b_new = adam_update(biases, bias_first, bias_second, bias_total, 0.5, 0.0)
    return (
        result,
        input_grad,
        *first_new[:3],
        *(tall(array) for array in first_new[3:]),
        *rest_new[:3],
        *(tall(array) for array in rest_new[3:]),
        *g_new,
        *b_new,
    )


def solution(mesh):
    token_spec = P("dp", ("row", "col"))
    wide = P("row", "dp", "col")
    tall = P("col", "row", "dp")
    return jax.shard_map(
        shards,
        mesh=mesh,
        in_specs=(token_spec,) * 2 + (wide, tall, wide, tall) * 3 + (P(),) * 6,
        out_specs=(token_spec,) * 2
        + (wide,) * 3
        + (tall,) * 3
        + (wide,) * 3
        + (tall,) * 3
        + (P(),) * 6,
        check_vma=False,
    )
```

```python
from functools import partial

import jax
import jax.numpy as jnp
from jax import lax
from jax.experimental import pallas as pl
from jax.experimental.pallas import tpu as pltpu
from jax.sharding import PartitionSpec as P

D = 1152
FF = 4304
HEAD = 72
SEQ = 729
STEP = 10

NORM_EPS = 1e-06
ADAM_EPS = 1e-08
BETA_ONE = 0.9
BETA_TWO = 0.999
LOW = jnp.bfloat16


def dot(left, right, left_dim, right_dim, out=jnp.float32, precision=None):
    return lax.dot_general(
        left,
        right,
        (((left_dim,), (right_dim,)), ((), ())),
        precision=precision,
        preferred_element_type=out,
    )


def take(array, index, size):
    return lax.dynamic_slice_in_dim(array, index * size, size, axis=0)


def swap_cores(array):
    n_col = lax.axis_size("col")
    return lax.ppermute(array, "col", [(i, (i + 1) % n_col) for i in range(n_col)])


def gather_parts(block, axis):
    size = lax.axis_size(axis)
    if size > 4:
        copies = jnp.broadcast_to(block, (size,) + block.shape)
        return [lax.all_to_all(copies, axis, 0, 0).reshape(-1, block.shape[1])]
    return [block] + [
        lax.ppermute(block, axis, [(i, i ^ step) for i in range(size)]) for step in range(1, size)
    ]


def zero_of(array):
    first = lax.slice(array, (0,) * array.ndim, (1,) * array.ndim)
    return first.reshape(()).astype(jnp.float32) * 0.0


def exchange_rows(blocks):
    return lax.all_to_all(blocks, "row", 0, 0)


def sum_blocks(blocks, axis, later):
    blocks = lax.all_to_all(blocks, axis, 0, 0)
    return jnp.sum(blocks.astype(jnp.float32) + later, axis=0).astype(LOW)


def sum_over_rows(half):
    summed = lax.psum_scatter(half.astype(LOW), "row", scatter_dimension=0, tiled=True)
    return summed.astype(jnp.float32)


def all_sum(vector):
    for axis in ("col", "row", "dp"):
        size = lax.axis_size(axis)
        if size & (size - 1) or size > 4:
            vector = lax.psum(vector, axis)
            continue
        step = 1
        while step < size:
            vector = vector + lax.ppermute(vector, axis, [(i, i ^ step) for i in range(size)])
            step *= 2
    return vector


VMEM = pl.BlockSpec(memory_space=pltpu.VMEM)
SMEM = pl.BlockSpec(memory_space=pltpu.SMEM)
ANY = pl.BlockSpec(memory_space=pl.ANY)
BIG = pltpu.CompilerParams(vmem_limit_bytes=56 * 1024 * 1024)


def prepare_kernel(parts, after_ref, wide_ref, tall_ref, rows_ref, out_ref, long_ref):
    del after_ref
    long_ref[...] = jnp.zeros(long_ref.shape, long_ref.dtype)
    long_ref[:, : rows_ref.shape[1]] = rows_ref[...]
    arrays = [ref[:, 0, :].astype(LOW) for ref in (wide_ref, tall_ref)]
    for part in range(parts):
        pieces = []
        for array in arrays:
            size = array.shape[1] // parts
            pieces.append(array[:, part * size : (part + 1) * size])
        out_ref[part] = jnp.concatenate(pieces, axis=1)


def prepare(after, wide, tall, parts, rows, padded):
    size = (wide.shape[2] + tall.shape[2]) // parts
    return pl.pallas_call(
        partial(prepare_kernel, parts),
        in_specs=[ANY, VMEM, VMEM, VMEM],
        out_specs=[VMEM] * 2,
        out_shape=(
            jax.ShapeDtypeStruct((parts, wide.shape[0], size), LOW),
            jax.ShapeDtypeStruct((rows.shape[0], padded), LOW),
        ),
        compiler_params=BIG,
        name="prepare",
    )(after, wide, tall, rows)


def norm_kernel(place_ref, mine_ref, theirs_ref, gain_ref, shift_ref, turn_ref, x_ref, za_ref, mean_ref, inv_ref):
    core = place_ref[0]
    x_ref[core] = mine_ref[...]
    x_ref[1 - core] = theirs_ref[...]
    x_full = x_ref[...].reshape(za_ref.shape).astype(jnp.float32)
    mean = jnp.sum(x_full, axis=0, keepdims=True) / D
    center = x_full - mean
    inverse = lax.rsqrt(jnp.sum(center * center, axis=0, keepdims=True) / D + NORM_EPS)
    mean_ref[...] = mean
    inv_ref[...] = inverse
    z_one = (center * inverse * gain_ref[...] + shift_ref[...]).astype(LOW)
    za_ref[...] = dot(turn_ref[...], z_one, 1, 0).astype(LOW)


def norm_first(place, mine, theirs, gain, shift, turn):
    rows, tokens = mine.shape
    return pl.pallas_call(
        norm_kernel,
        in_specs=[SMEM] + [VMEM] * 5,
        out_specs=[VMEM] * 4,
        out_shape=(
            jax.ShapeDtypeStruct((2, rows, tokens), LOW),
            jax.ShapeDtypeStruct((2 * rows, tokens), LOW),
            jax.ShapeDtypeStruct((1, tokens), jnp.float32),
            jax.ShapeDtypeStruct((1, tokens), jnp.float32),
        ),
        compiler_params=BIG,
        name="norm_first",
    )(place, mine, theirs, gain, shift, turn)


def adam_kernel(rates, after_ref, blocks_ref, *refs):
    del after_ref
    parts = blocks_ref.shape[0]
    start = 0
    for index, rate in enumerate(rates):
        weight, first, second = refs[3 * index : 3 * index + 3]
        size = weight.shape[2] // parts
        gradient = jnp.concatenate(
            [blocks_ref[part, :, start : start + size] for part in range(parts)], axis=1
        ).astype(jnp.float32)
        start += size
        new = adam_update(weight[:, 0, :], first[:, 0, :], second[:, 0, :], gradient, rate, 0.1)
        for array, ref in zip(new, refs[3 * len(rates) + 3 * index :]):
            ref[:, 0, :] = array


def adam(after, blocks, rates, *arrays):
    return pl.pallas_call(
        partial(adam_kernel, rates),
        in_specs=[ANY] + [VMEM] * (1 + len(arrays)),
        out_specs=[VMEM] * len(arrays),
        out_shape=[jax.ShapeDtypeStruct(a.shape, jnp.float32) for a in arrays],
        compiler_params=BIG,
        name="adam",
    )(after, blocks, *arrays)


def assembled(place, parts, scratch):
    if len(parts) == 1:
        return parts[0][...]
    for step, part in enumerate(parts):
        scratch[place ^ step] = part[...]
    return scratch[...].reshape(-1, scratch.shape[2])


def part_scratch(parts):
    return pltpu.VMEM((len(parts),) + parts[0].shape, LOW)


def head_probs(queries, key_rows):
    scores = dot(queries, key_rows, 0, 0) * HEAD ** (-0.5)
    scores = jnp.where(lax.broadcasted_iota(jnp.int32, scores.shape, 1) < SEQ, scores, -1e30)
    exponent = jnp.exp(scores - jnp.max(scores, axis=1, keepdims=True))
    return exponent * (1.0 / jnp.sum(exponent, axis=1, keepdims=True))


def split_cores(core, first, second, theirs_ref, mine_ref):
    @pl.when(core == 0)
    def _():
        mine_ref[...] = first
        theirs_ref[...] = second

    @pl.when(core != 0)
    def _():
        mine_ref[...] = second
        theirs_ref[...] = first


def attend_kernel(place_ref, after_ref, za_ref, bias_ref, *refs):
    del after_ref
    *parts, w_ref, qkv_ref, att_ref, theirs_ref, mine_ref, scratch = refs
    w_ref[...] = assembled(place_ref[1], parts, scratch)
    heads = qkv_ref.shape[0]
    split = heads * 3 * HEAD
    qkv = dot(w_ref[:, :split], za_ref[...], 0, 0) + bias_ref[...]
    outs = []
    for head in range(heads):
        for t in range(3):
            start = (head * 3 + t) * HEAD
            qkv_ref[head, t] = qkv[start : start + HEAD].astype(LOW)
        probs = head_probs(qkv_ref[head, 0], qkv_ref[head, 1]).astype(LOW)
        outs.append(dot(qkv_ref[head, 2], probs, 1, 1))
    attended = jnp.concatenate(outs, axis=0).T.astype(LOW)
    att_ref[...] = attended
    branch = dot(attended, w_ref[:, split:], 1, 1).astype(LOW)
    half = branch.shape[0] // 2
    split_cores(place_ref[0], branch[:half], branch[half:], theirs_ref, mine_ref)


def attend(place, after, za, qkv_bias, parts, width):
    tokens = za.shape[1]
    return pl.pallas_call(
        attend_kernel,
        in_specs=[SMEM, ANY, VMEM, VMEM] + [VMEM] * len(parts),
        out_specs=[VMEM] * 5,
        out_shape=(
            jax.ShapeDtypeStruct((D, 4 * width), LOW),
            jax.ShapeDtypeStruct((width // HEAD, 3, HEAD, tokens), LOW),
            jax.ShapeDtypeStruct((tokens, width), LOW),
            jax.ShapeDtypeStruct((tokens // 2, D), LOW),
            jax.ShapeDtypeStruct((tokens // 2, D), LOW),
        ),
        scratch_shapes=[part_scratch(parts)],
        compiler_params=BIG,
        name="attend",
    )(place, after, za, qkv_bias, *parts)


def own_tokens(place_ref, chunk, tokens):
    pick = lax.broadcasted_iota(jnp.int32, (chunk, tokens), 0) + place_ref[2] * chunk
    return (lax.broadcasted_iota(jnp.int32, (chunk, tokens), 1) == pick).astype(LOW)


def beside_kernel(n_row, place_ref, after_ref, order_ref, cot_ref, w_ref, x_ref, tokens_ref, mixed_ref, mine_ref):
    del after_ref
    group, width = cot_ref.shape[:2]
    n_col = group // n_row
    order = order_ref[...]
    cot = [cot_ref[row * n_col + core] for core in range(n_col) for row in range(n_row)]
    tokens_ref[...] = dot(jnp.concatenate(cot, axis=0), order, 0, 0).astype(LOW)
    mixed_ref[...] = dot(order, w_ref[:, : 3 * width], 1, 0).astype(LOW)
    pick = own_tokens(place_ref, mine_ref.shape[0], x_ref.shape[1])
    mine_ref[...] = dot(dot(pick, x_ref[...], 1, 1).astype(LOW), order, 1, 0)


def beside(place, after, order, cot_all, w_first, x_all, n_row, chunk):
    group, width, tokens = cot_all.shape
    return pl.pallas_call(
        partial(beside_kernel, n_row),
        in_specs=[SMEM, ANY] + [VMEM] * 4,
        out_specs=[VMEM] * 3,
        out_shape=(
            jax.ShapeDtypeStruct((tokens, D), LOW),
            jax.ShapeDtypeStruct((D, 3 * width), LOW),
            jax.ShapeDtypeStruct((chunk, D), jnp.float32),
        ),
        compiler_params=BIG,
        name="beside",
    )(place, after, order, cot_all, w_first, x_all)


def before_kernel(place_ref, after_ref, order_ref, cot_ref, *refs):
    del after_ref
    *parts, up_ref, grad_ref, mixed_ref, scratch = refs
    w_rest = assembled(place_ref[1], parts, scratch)
    wide = up_ref.shape[1]
    up_ref[...] = w_rest[:, :wide]
    w_down = w_rest[:, wide:]
    grad_ref[...] = dot(cot_ref[...], w_down, 1, 0)
    mixed_ref[...] = dot(order_ref[...], w_down, 1, 0).astype(LOW)


def before(place, after, order, cot_tokens, parts):
    wide = parts[0].shape[1] // 2
    return pl.pallas_call(
        before_kernel,
        in_specs=[SMEM, ANY, VMEM, VMEM] + [VMEM] * len(parts),
        out_specs=[VMEM] * 3,
        out_shape=(
            jax.ShapeDtypeStruct((D, wide), LOW),
            jax.ShapeDtypeStruct((cot_tokens.shape[0], wide), jnp.float32),
            jax.ShapeDtypeStruct((D, wide), LOW),
        ),
        scratch_shapes=[part_scratch(parts)],
        compiler_params=BIG,
        name="before",
    )(place, after, order, cot_tokens, *parts)


def behind_kernel(
    place_ref, after_ref, zb_ref, hid_ref, cot_ref, act_ref, down_ref, mid_ref, grad_ref, theirs_ref, mine_ref
):
    del after_ref
    active = act_ref[...]
    up_grad = dot(zb_ref[...], hid_ref[...], 0, 0).astype(LOW)
    down_grad = dot(cot_ref[...], active, 0, 0).astype(LOW)
    grad_ref[...] = jnp.concatenate([up_grad, down_grad], axis=1).reshape(grad_ref.shape)
    pick = own_tokens(place_ref, mid_ref.shape[1], active.shape[0])
    result = dot(down_ref[...], active, 1, 1) + dot(mid_ref[...], pick, 1, 0)
    result = result.astype(LOW)
    half = D // 2
    split_cores(place_ref[0], result[:half], result[half:], theirs_ref, mine_ref)


def behind(place, after, zb, hidden_grad, cot_tokens, active, down_mixed, middle_mixed, n_dp):
    tokens, wide = active.shape
    return pl.pallas_call(
        behind_kernel,
        in_specs=[SMEM, ANY] + [VMEM] * 6,
        out_specs=[VMEM] * 3,
        out_shape=(
            jax.ShapeDtypeStruct((n_dp, D // n_dp, 2 * wide), LOW),
            jax.ShapeDtypeStruct((D // 2, tokens), LOW),
            jax.ShapeDtypeStruct((D // 2, tokens), LOW),
        ),
        compiler_params=BIG,
        name="behind",
    )(place, after, zb, hidden_grad, cot_tokens, active, down_mixed, middle_mixed)


def mlp_kernel(
    core_ref, zb_ref, up_ref, bias_ref, grad_ref, act_ref, hid_ref, theirs_ref, mine_ref, sum_ref
):
    step = pl.program_id(0)
    near = step >= pl.num_programs(0) // 2
    hidden = dot(zb_ref[...], up_ref[...], 1, 0) + bias_ref[...]
    square = hidden * hidden
    slope = 0.7978845608028654 * (1.0 + 0.044715 * square)
    bent = jnp.tanh(hidden * slope)
    gate = 0.5 * (1.0 + bent)
    act_ref[...] = (hidden * gate).astype(LOW)
    steep = gate + 0.5 * hidden * (1.0 - bent * bent) * (
        0.7978845608028654 * (1.0 + 3 * 0.044715 * square)
    )
    hidden_grad = (grad_ref[...] * steep).astype(LOW)
    hid_ref[...] = hidden_grad
    two_grad = dot(hidden_grad, up_ref[...], 1, 1).astype(LOW)

    @pl.when(near)
    def _():
        mine_ref[...] = two_grad

    @pl.when(jnp.logical_not(near))
    def _():
        theirs_ref[...] = two_grad

    @pl.when(step == 0)
    def _():
        sum_ref[...] = jnp.zeros(sum_ref.shape, jnp.float32)

    sum_ref[...] += jnp.sum(hidden_grad.astype(jnp.float32), axis=0, keepdims=True)


def mlp(core, zb, w_up, up_bias, active_grad):
    tokens = zb.shape[0]
    wide = w_up.shape[1]
    steps = 6
    block = tokens // steps
    turned = lambda i, c: ((i + (steps // 2) * (1 - c[0])) % steps, 0)
    whole = lambda i, c: (0, 0)
    return pl.pallas_call(
        mlp_kernel,
        grid_spec=pltpu.PrefetchScalarGridSpec(
            num_scalar_prefetch=1,
            grid=(steps,),
            in_specs=[
                pl.BlockSpec((block, D), turned),
                pl.BlockSpec((D, wide), whole),
                pl.BlockSpec((1, wide), whole),
                pl.BlockSpec((block, wide), turned),
            ],
            out_specs=[
                pl.BlockSpec((block, wide), turned),
                pl.BlockSpec((block, wide), turned),
                pl.BlockSpec((block, D), lambda i, c: (jnp.minimum(i, steps // 2 - 1), 0)),
                pl.BlockSpec((block, D), lambda i, c: (jnp.maximum(i - steps // 2, 0), 0)),
                pl.BlockSpec((1, wide), whole),
            ],
        ),
        out_shape=(
            jax.ShapeDtypeStruct((tokens, wide), LOW),
            jax.ShapeDtypeStruct((tokens, wide), LOW),
            jax.ShapeDtypeStruct((tokens // 2, D), LOW),
            jax.ShapeDtypeStruct((tokens // 2, D), LOW),
            jax.ShapeDtypeStruct((1, wide), jnp.float32),
        ),
        compiler_params=BIG,
        name="mlp",
    )(core, zb, w_up, up_bias, active_grad)


def back_kernel(after_ref, bg_ref, w_ref, qkv_ref, za_ref, att_ref, grad_ref, sum_ref, wg_ref):
    del after_ref
    heads = qkv_ref.shape[0]
    attended_grad = dot(bg_ref[...], w_ref[:, heads * 3 * HEAD :], 1, 0).T
    scale = HEAD ** (-0.5)
    parts = []
    for head in range(heads):
        queries, key_rows, values = qkv_ref[head, 0], qkv_ref[head, 1], qkv_ref[head, 2]
        grad = attended_grad[head * HEAD : (head + 1) * HEAD].astype(LOW)
        probs = head_probs(queries, key_rows)
        probs_grad = dot(grad, values, 0, 0)
        inner = jnp.sum(probs * probs_grad, axis=1, keepdims=True)
        scores_grad = (probs * (probs_grad - inner)).astype(LOW)
        parts.append(dot(key_rows, scores_grad, 1, 1) * scale)
        parts.append(dot(queries, scores_grad, 1, 0) * scale)
        parts.append(dot(grad, probs.astype(LOW), 1, 0))
    qkv_grad = jnp.concatenate(parts, axis=0).astype(LOW)
    grad_ref[...] = qkv_grad
    sum_ref[...] = jnp.sum(qkv_grad.astype(jnp.float32), axis=1, keepdims=True)
    qkv_part = dot(za_ref[...], qkv_grad, 1, 1).astype(LOW)
    out_part = dot(bg_ref[...], att_ref[...], 0, 0).astype(LOW)
    wg_ref[...] = jnp.concatenate([qkv_part, out_part], axis=1).reshape(wg_ref.shape)


def attend_back(after, branch_all, w_first, qkv, za, attended, n_dp):
    tokens, width = attended.shape
    return pl.pallas_call(
        back_kernel,
        in_specs=[ANY] + [VMEM] * 5,
        out_specs=[VMEM] * 3,
        out_shape=(
            jax.ShapeDtypeStruct((3 * width, tokens), LOW),
            jax.ShapeDtypeStruct((3 * width, 1), jnp.float32),
            jax.ShapeDtypeStruct((n_dp, D // n_dp, 4 * width), LOW),
        ),
        compiler_params=BIG,
        name="attend_back",
    )(after, branch_all, w_first, qkv, za, attended)


def first_kernel(core_ref, w_ref, grad_ref, x_ref, mean_ref, inv_ref, gain_ref, theirs_ref, mine_ref, sum_ref):
    n_row, rows, tokens = theirs_ref.shape
    width = rows - 16
    first = jnp.zeros((1, tokens), jnp.float32)
    second = jnp.zeros((1, tokens), jnp.float32)
    blocks = []
    for slot in range(D // width):
        here = slice(slot * width, (slot + 1) * width)
        part = dot(w_ref[here], grad_ref[...], 1, 0)
        normed = (x_ref[here].astype(jnp.float32) - mean_ref[...]) * inv_ref[...]
        product = part * normed
        sum_ref[here, 0:1] = jnp.sum(product, axis=1, keepdims=True)
        sum_ref[here, 1:2] = jnp.sum(part, axis=1, keepdims=True)
        first += jnp.sum(part * gain_ref[here], axis=0, keepdims=True)
        second += jnp.sum(product * gain_ref[here], axis=0, keepdims=True)
        blocks.append(part.astype(LOW))
    line = lax.broadcasted_iota(jnp.int32, (16, tokens), 0)
    sums = jnp.where(line == 0, first, jnp.where(line == 1, second, 0.0)).astype(LOW)
    for near, ref in ((False, theirs_ref), (True, mine_ref)):
        for core in range(2):

            @pl.when((core_ref[0] == core) == near)
            def _(core=core, ref=ref):
                for row in range(n_row):
                    ref[row, :width] = blocks[core * n_row + row]
                    ref[row, width:] = sums


def first_back(core, w_mixed, qkv_grad, x_all, x_mean, inverse, gain, width, n_row):
    tokens = x_all.shape[1]
    return pl.pallas_call(
        first_kernel,
        in_specs=[SMEM] + [VMEM] * 6,
        out_specs=[VMEM] * 3,
        out_shape=(
            jax.ShapeDtypeStruct((n_row, width + 16, tokens), LOW),
            jax.ShapeDtypeStruct((n_row, width + 16, tokens), LOW),
            jax.ShapeDtypeStruct((D, 2), jnp.float32),
        ),
        compiler_params=BIG,
        name="first_back",
    )(core, w_mixed, qkv_grad, x_all, x_mean, inverse, gain)


def adam_update(weights, moment_one, second, gradient, step_rate, weight_decay):
    moment_one = BETA_ONE * moment_one + (1.0 - BETA_ONE) * gradient
    second = BETA_TWO * second + (1.0 - BETA_TWO) * gradient * gradient
    direction = (
        moment_one / (1.0 - BETA_ONE**STEP) / (jnp.sqrt(second / (1.0 - BETA_TWO**STEP)) + ADAM_EPS)
    )
    return (weights - step_rate * (direction + weight_decay * weights), moment_one, second)


def shards(
    inputs,
    cotangent,
    qkv_master,
    out_master,
    up_master,
    down_master,
    qkv_first,
    out_first,
    up_first,
    down_first,
    qkv_second,
    out_second,
    up_second,
    down_second,
    norm_gains,
    gain_first,
    gain_second,
    biases,
    bias_first,
    bias_second,
):
    tokens, width = inputs.shape
    n_row = lax.axis_size("row")
    n_col = lax.axis_size("col")
    n_dp = lax.axis_size("dp")
    row = lax.axis_index("row")
    core = lax.axis_index("col")
    group = n_row * n_col
    heads = width // HEAD
    hidden_width = FF // group
    own = core * n_row + row
    place = jnp.stack([core, lax.axis_index("dp"), own]).astype(jnp.int32)
    chunk = -(-tokens // (group * 16)) * 16
    padded = chunk * group
    shard_rows = qkv_master.shape[0]

    index = jnp.arange(D)
    feature = (
        ((index // width) % n_row) * n_col + index // (width * n_row)
    ) * width + index % width
    index = (feature % n_dp) * (D // n_dp) + feature // n_dp
    order = (lax.broadcasted_iota(jnp.int32, (D, D), 1) == index[:, None]).astype(LOW)
    turn = (lax.broadcasted_iota(jnp.int32, (D, D), 0) == index[None, :]).astype(LOW)
    order, turn = lax.optimization_barrier((order, turn))

    def mixed(vector):
        return vector.reshape(n_row, n_col, width).transpose(1, 0, 2).reshape(D)

    def dealt(vector):
        return vector.reshape(D // n_dp, n_dp).T.reshape(D)

    def returned(rows):
        return exchange_rows(rows.reshape(n_row, shard_rows, -1))

    flat = lambda array: array.transpose(1, 2, 0)
    tall = lambda array: array.transpose(2, 0, 1)
    first_rows, x_own = prepare(place, qkv_master, flat(out_master), n_row, inputs.T, padded)
    first_rows = exchange_rows(first_rows).reshape(D // n_dp, -1)
    x_rows = lax.all_gather(x_own, "row", axis=0, tiled=True)
    first_parts = gather_parts(first_rows, "dp")
    rest, cot_own = prepare(
        x_rows, up_master, flat(down_master), n_row, cotangent.T, padded
    )
    rest = exchange_rows(rest).reshape(D // n_dp, -1)
    rest_parts = gather_parts(rest, "dp")
    cot_all = lax.all_gather(cot_own, ("row", "col"), axis=0)

    gain_one = mixed(norm_gains[0])
    gain_two = dealt(norm_gains[1])
    shift_one = mixed(biases[:D])
    shift_two = dealt(biases[D : 2 * D])
    query_bias = lax.dynamic_slice_in_dim(biases, 2 * D + own * width, width).reshape(heads, HEAD)
    value_bias = lax.dynamic_slice_in_dim(biases, 3 * D + own * width, width).reshape(heads, HEAD)
    out_bias = dealt(biases[4 * D : 5 * D])
    feature_start = (row * n_col + core) * width
    down_bias = lax.dynamic_slice_in_dim(biases, 5 * D + feature_start, width)
    up_bias = lax.dynamic_slice_in_dim(biases, 6 * D + own * hidden_width, hidden_width)
    qkv_bias = jnp.stack([query_bias, jnp.zeros_like(query_bias), value_bias], axis=1).reshape(
        3 * width, 1
    )

    x_all, za, x_mean, inverse_one = norm_first(
        place, x_rows, swap_cores(x_rows), gain_one[:, None], shift_one[:, None], turn
    )
    x_all = x_all.reshape(D, padded)

    w_first, qkv, attended, theirs, mine = attend(place, rest, za, qkv_bias, first_parts, width)
    pair = (mine.astype(jnp.float32) + swap_cores(theirs).astype(jnp.float32)).astype(LOW)
    branch = sum_over_rows(pair)
    cot_tokens, qkv_mixed, x_mine = beside(
        place, pair, order, cot_all, w_first, x_all, n_row, chunk
    )
    cot_mine = take(cot_tokens, own, chunk).astype(jnp.float32)

    middle = x_mine + branch + out_bias[None, :]
    center = middle - jnp.sum(middle, axis=1, keepdims=True) / D
    inverse_two = lax.rsqrt(jnp.sum(center * center, axis=1, keepdims=True) / D + NORM_EPS)
    normed_two = center * inverse_two
    zb = (normed_two * gain_two + shift_two).astype(LOW)
    w_up, active_grad, down_mixed = before(place, zb, order, cot_tokens, rest_parts)
    zb = lax.all_gather(zb, ("col", "row"), axis=0, tiled=True)

    core_of = core.reshape(1).astype(jnp.int32)
    active, hidden_grad, theirs, mine, up_sums = mlp(
        core_of, zb, w_up, up_bias[None, :], active_grad
    )
    pair = (mine.astype(jnp.float32) + swap_cores(theirs).astype(jnp.float32)).astype(LOW)
    two_grad = sum_over_rows(pair)

    middle_mixed = dot(order, middle.astype(LOW), 1, 1, LOW)
    rest_grad, theirs, mine = behind(
        place, pair, zb, hidden_grad, cot_tokens, active, down_mixed, middle_mixed, n_dp
    )
    result = mine.astype(jnp.float32) + swap_cores(theirs).astype(jnp.float32)

    scaled = two_grad * gain_two
    first_sum = jnp.sum(scaled, axis=1, keepdims=True) / D
    second_sum = jnp.sum(scaled * normed_two, axis=1, keepdims=True) / D
    middle_grad = cot_mine + inverse_two * (scaled - first_sum - normed_two * second_sum)
    middle_grad = middle_grad.astype(LOW)
    branch_all = lax.all_gather(middle_grad, ("col", "row"), axis=0, tiled=True)
    later = zero_of(middle_grad)
    result = sum_over_rows(result + later) + down_bias[:, None]
    result = result.astype(LOW)[:, :tokens].T
    rest_rows = sum_blocks(rest_grad, "dp", later)
    rest_rows = rest_rows + zero_of(branch_all).astype(LOW)

    qkv_grad, bias_sums, first_grad = attend_back(
        rest_rows, branch_all, w_first, qkv, za, attended, n_dp
    )
    theirs, mine, one_sums = first_back(
        core_of, qkv_mixed, qkv_grad, x_all, x_mean, inverse_one, gain_one[:, None], width, n_row
    )
    pair = (mine.astype(jnp.float32) + swap_cores(theirs).astype(jnp.float32)).astype(LOW)
    one_grad = sum_over_rows(pair.reshape(-1, padded))
    first_rows = sum_blocks(first_grad, "dp", 0.0)

    own_gain = lax.dynamic_slice_in_dim(norm_gains[0], feature_start, width)[:, None]
    own_normed = (x_own.astype(jnp.float32) - x_mean) * inverse_one
    own_order = lax.dynamic_slice_in_dim(order, own * width, width, axis=0)
    own_middle = dot(own_order, branch_all, 1, 1)
    input_grad = own_middle + inverse_one * (
        one_grad[:width] * own_gain
        - one_grad[width : width + 1] / D
        - own_normed * (one_grad[width + 1 : width + 2] / D)
    )
    input_grad = input_grad.astype(LOW)[:, :tokens].T

    later = zero_of(pair)
    bias_sums = bias_sums.reshape(heads, 3, HEAD)
    all_rows = jnp.stack(
        [
            one_sums[:, 0],
            one_sums[:, 1],
            jnp.sum(two_grad * normed_two, axis=0),
            jnp.sum(two_grad, axis=0),
            jnp.sum(middle_grad, axis=0, dtype=jnp.float32),
            jnp.sum(cot_mine, axis=0),
        ]
    )
    own_row = jnp.concatenate(
        [bias_sums[:, 0].reshape(width), bias_sums[:, 2].reshape(width), up_sums[0]]
    )
    own_row = jnp.pad(own_row, (0, D - own_row.shape[0]))
    own_rows = jnp.where(jnp.arange(group)[:, None] == own, own_row[None, :], 0.0)
    total = all_sum(jnp.concatenate([jnp.pad(all_rows, ((0, 2), (0, 0))), own_rows]) + later)
    one_rows = total[:2].reshape(2, n_col, n_row, width).transpose(0, 2, 1, 3).reshape(2, D)
    two_rows = total[2:6].reshape(4, n_dp, D // n_dp).transpose(0, 2, 1).reshape(4, D)
    own_rows = total[8:]
    gain_total = jnp.stack([one_rows[0], two_rows[0]])
    bias_total = jnp.concatenate(
        [
            one_rows[1],
            two_rows[1],
            own_rows[:, :width].reshape(D),
            own_rows[:, width : 2 * width].reshape(D),
            two_rows[2],
            two_rows[3],
            own_rows[:, 2 * width : 2 * width + hidden_width].reshape(FF),
        ]
    )

    rest_new = adam(
        pair,
        returned(rest_rows),
        (0.03, 0.02),
        up_master,
        up_first,
        up_second,
        flat(down_master),
        flat(down_first),
        flat(down_second),
    )
    first_new = adam(
        pair,
        returned(first_rows),
        (0.03, 0.12),
        qkv_master,
        qkv_first,
        qkv_second,
        flat(out_master),
        flat(out_first),
        flat(out_second),
    )
    g_new = adam_update(norm_gains, gain_first, gain_second, gain_total, 0.5, 0.0)
    b_new = adam_update(biases, bias_first, bias_second, bias_total, 0.5, 0.0)
    return (
        result,
        input_grad,
        *first_new[:3],
        *(tall(array) for array in first_new[3:]),
        *rest_new[:3],
        *(tall(array) for array in rest_new[3:]),
        *g_new,
        *b_new,
    )


def solution(mesh):
    token_spec = P("dp", ("row", "col"))
    wide = P("row", "dp", "col")
    tall = P("col", "row", "dp")
    return jax.shard_map(
        shards,
        mesh=mesh,
        in_specs=(token_spec,) * 2 + (wide, tall, wide, tall) * 3 + (P(),) * 6,
        out_specs=(token_spec,) * 2
        + (wide,) * 3
        + (tall,) * 3
        + (wide,) * 3
        + (tall,) * 3
        + (P(),) * 6,
        check_vma=False,
    )
```

```python
from functools import partial

import jax
import jax.numpy as jnp
from jax import lax
from jax.experimental import pallas as pl
from jax.experimental.pallas import tpu as pltpu
from jax.sharding import PartitionSpec as P

D = 1152
FF = 4304
HEAD = 72
SEQ = 729
STEP = 10

NORM_EPS = 1e-06
ADAM_EPS = 1e-08
BETA_ONE = 0.9
BETA_TWO = 0.999
LOW = jnp.bfloat16


def dot(left, right, left_dim, right_dim, out=jnp.float32, precision=None):
    return lax.dot_general(
        left,
        right,
        (((left_dim,), (right_dim,)), ((), ())),
        precision=precision,
        preferred_element_type=out,
    )


def take(array, index, size):
    return lax.dynamic_slice_in_dim(array, index * size, size, axis=0)


def swap_cores(array):
    n_col = lax.axis_size("col")
    return lax.ppermute(array, "col", [(i, (i + 1) % n_col) for i in range(n_col)])


def gather_parts(block, axis):
    size = lax.axis_size(axis)
    if size > 4:
        copies = jnp.broadcast_to(block, (size,) + block.shape)
        return [lax.all_to_all(copies, axis, 0, 0).reshape(-1, block.shape[1])]
    return [block] + [
        lax.ppermute(block, axis, [(i, i ^ step) for i in range(size)]) for step in range(1, size)
    ]


def zero_of(array):
    first = lax.slice(array, (0,) * array.ndim, (1,) * array.ndim)
    return first.reshape(()).astype(jnp.float32) * 0.0


def exchange_rows(blocks):
    return lax.all_to_all(blocks, "row", 0, 0)


def sum_blocks(blocks, axis, later):
    blocks = lax.all_to_all(blocks, axis, 0, 0)
    return jnp.sum(blocks.astype(jnp.float32) + later, axis=0).astype(LOW)


def sum_over_rows(half):
    summed = lax.psum_scatter(half.astype(LOW), "row", scatter_dimension=0, tiled=True)
    return summed.astype(jnp.float32)


def all_sum(vector):
    for axis in ("col", "row", "dp"):
        size = lax.axis_size(axis)
        if size & (size - 1) or size > 4:
            vector = lax.psum(vector, axis)
            continue
        step = 1
        while step < size:
            vector = vector + lax.ppermute(vector, axis, [(i, i ^ step) for i in range(size)])
            step *= 2
    return vector


VMEM = pl.BlockSpec(memory_space=pltpu.VMEM)
SMEM = pl.BlockSpec(memory_space=pltpu.SMEM)
ANY = pl.BlockSpec(memory_space=pl.ANY)
BIG = pltpu.CompilerParams(vmem_limit_bytes=56 * 1024 * 1024)


def prepare_kernel(parts, after_ref, wide_ref, tall_ref, rows_ref, out_ref, long_ref):
    del after_ref
    long_ref[...] = jnp.zeros(long_ref.shape, long_ref.dtype)
    long_ref[:, : rows_ref.shape[1]] = rows_ref[...]
    arrays = [ref[:, 0, :].astype(LOW) for ref in (wide_ref, tall_ref)]
    for part in range(parts):
        pieces = []
        for array in arrays:
            size = array.shape[1] // parts
            pieces.append(array[:, part * size : (part + 1) * size])
        out_ref[part] = jnp.concatenate(pieces, axis=1)


def prepare(after, wide, tall, parts, rows, padded):
    size = (wide.shape[2] + tall.shape[2]) // parts
    return pl.pallas_call(
        partial(prepare_kernel, parts),
        in_specs=[ANY, VMEM, VMEM, VMEM],
        out_specs=[VMEM] * 2,
        out_shape=(
            jax.ShapeDtypeStruct((parts, wide.shape[0], size), LOW),
            jax.ShapeDtypeStruct((rows.shape[0], padded), LOW),
        ),
        compiler_params=BIG,
        name="prepare",
    )(after, wide, tall, rows)


def norm_kernel(n_row, vectors_ref, x_ref, turn_ref, za_ref, mean_ref, inv_ref, gain_ref):
    columns = vectors_ref[...].T
    gain = mixed_rows(columns[:, 0:1], n_row)
    gain_ref[...] = gain
    x_full = x_ref[...].astype(jnp.float32)
    mean = jnp.sum(x_full, axis=0, keepdims=True) / D
    center = x_full - mean
    inverse = lax.rsqrt(jnp.sum(center * center, axis=0, keepdims=True) / D + NORM_EPS)
    mean_ref[...] = mean
    inv_ref[...] = inverse
    z_one = (center * inverse * gain + mixed_rows(columns[:, 2:3], n_row)).astype(LOW)
    za_ref[...] = dot(turn_ref[...], z_one, 1, 0).astype(LOW)


def mixed_rows(column, n_row):
    n_col = 2
    width = D // (n_row * n_col)
    blocks = [
        column[(row * n_col + core) * width : (row * n_col + core + 1) * width]
        for core in range(n_col)
        for row in range(n_row)
    ]
    return jnp.concatenate(blocks, axis=0)


def norm_first(vectors, x_all, turn, n_row):
    tokens = x_all.shape[1]
    return pl.pallas_call(
        partial(norm_kernel, n_row),
        in_specs=[VMEM] * 3,
        out_specs=[VMEM] * 4,
        out_shape=(
            jax.ShapeDtypeStruct((D, tokens), LOW),
            jax.ShapeDtypeStruct((1, tokens), jnp.float32),
            jax.ShapeDtypeStruct((1, tokens), jnp.float32),
            jax.ShapeDtypeStruct((D, 1), jnp.float32),
        ),
        compiler_params=BIG,
        name="norm_first",
    )(vectors, x_all, turn)


def own_kernel(n_row, place_ref, after_ref, vectors_ref, x_ref, turn_ref, mine_ref, dealt_ref):
    del after_ref
    pick = own_tokens(place_ref, mine_ref.shape[0], x_ref.shape[1])
    mine_ref[...] = dot(dot(pick, x_ref[...], 1, 1).astype(LOW), turn_ref[...], 1, 1)
    rest = mixed_rows(vectors_ref[...].T, n_row).T
    pieces = []
    for _ in range(3):
        piece = rest.astype(LOW)
        rest = rest - piece.astype(jnp.float32)
        pieces.append(piece)
    total = dot(pieces[0], turn_ref[...], 1, 1)
    for piece in pieces[1:]:
        total = total + dot(piece, turn_ref[...], 1, 1)
    dealt_ref[...] = total


def own_rows_of(place, after, vectors, x_all, turn, n_row, chunk):
    return pl.pallas_call(
        partial(own_kernel, n_row),
        in_specs=[SMEM, ANY] + [VMEM] * 3,
        out_specs=[VMEM] * 2,
        out_shape=(
            jax.ShapeDtypeStruct((chunk, D), jnp.float32),
            jax.ShapeDtypeStruct((8, D), jnp.float32),
        ),
        compiler_params=BIG,
        name="own_rows",
    )(place, after, vectors, x_all, turn)


def adam_kernel(rates, after_ref, blocks_ref, *refs):
    del after_ref
    parts = blocks_ref.shape[0]
    start = 0
    for index, rate in enumerate(rates):
        weight, first, second = refs[3 * index : 3 * index + 3]
        size = weight.shape[2] // parts
        gradient = jnp.concatenate(
            [blocks_ref[part, :, start : start + size] for part in range(parts)], axis=1
        ).astype(jnp.float32)
        start += size
        new = adam_update(weight[:, 0, :], first[:, 0, :], second[:, 0, :], gradient, rate, 0.1)
        for array, ref in zip(new, refs[3 * len(rates) + 3 * index :]):
            ref[:, 0, :] = array


def adam(after, blocks, rates, *arrays):
    return pl.pallas_call(
        partial(adam_kernel, rates),
        in_specs=[ANY] + [VMEM] * (1 + len(arrays)),
        out_specs=[VMEM] * len(arrays),
        out_shape=[jax.ShapeDtypeStruct(a.shape, jnp.float32) for a in arrays],
        compiler_params=BIG,
        name="adam",
    )(after, blocks, *arrays)


def assembled(place, parts, scratch):
    if len(parts) == 1:
        return parts[0][...]
    for step, part in enumerate(parts):
        scratch[place ^ step] = part[...]
    return scratch[...].reshape(-1, scratch.shape[2])


def part_scratch(parts):
    return pltpu.VMEM((len(parts),) + parts[0].shape, LOW)


def head_probs(queries, key_rows):
    scores = dot(queries, key_rows, 0, 0) * HEAD ** (-0.5)
    scores = jnp.where(lax.broadcasted_iota(jnp.int32, scores.shape, 1) < SEQ, scores, -1e30)
    exponent = jnp.exp(scores - jnp.max(scores, axis=1, keepdims=True))
    return exponent * (1.0 / jnp.sum(exponent, axis=1, keepdims=True))


def split_cores(core, first, second, theirs_ref, mine_ref):
    @pl.when(core == 0)
    def _():
        mine_ref[...] = first
        theirs_ref[...] = second

    @pl.when(core != 0)
    def _():
        mine_ref[...] = second
        theirs_ref[...] = first


def attend_kernel(place_ref, after_ref, za_ref, bias_ref, *refs):
    del after_ref
    *parts, w_ref, qkv_ref, att_ref, theirs_ref, mine_ref, scratch = refs
    w_ref[...] = assembled(place_ref[1], parts, scratch)
    heads = qkv_ref.shape[0]
    split = heads * 3 * HEAD
    qkv = dot(w_ref[:, :split], za_ref[...], 0, 0) + bias_ref[...]
    outs = []
    for head in range(heads):
        for t in range(3):
            start = (head * 3 + t) * HEAD
            qkv_ref[head, t] = qkv[start : start + HEAD].astype(LOW)
        probs = head_probs(qkv_ref[head, 0], qkv_ref[head, 1]).astype(LOW)
        outs.append(dot(qkv_ref[head, 2], probs, 1, 1))
    attended = jnp.concatenate(outs, axis=0).T.astype(LOW)
    att_ref[...] = attended
    branch = dot(attended, w_ref[:, split:], 1, 1).astype(LOW)
    half = branch.shape[0] // 2
    split_cores(place_ref[0], branch[:half], branch[half:], theirs_ref, mine_ref)


def attend(place, after, za, qkv_bias, parts, width):
    tokens = za.shape[1]
    return pl.pallas_call(
        attend_kernel,
        in_specs=[SMEM, ANY, VMEM, VMEM] + [VMEM] * len(parts),
        out_specs=[VMEM] * 5,
        out_shape=(
            jax.ShapeDtypeStruct((D, 4 * width), LOW),
            jax.ShapeDtypeStruct((width // HEAD, 3, HEAD, tokens), LOW),
            jax.ShapeDtypeStruct((tokens, width), LOW),
            jax.ShapeDtypeStruct((tokens // 2, D), LOW),
            jax.ShapeDtypeStruct((tokens // 2, D), LOW),
        ),
        scratch_shapes=[part_scratch(parts)],
        compiler_params=BIG,
        name="attend",
    )(place, after, za, qkv_bias, *parts)


def own_tokens(place_ref, chunk, tokens):
    pick = lax.broadcasted_iota(jnp.int32, (chunk, tokens), 0) + place_ref[2] * chunk
    return (lax.broadcasted_iota(jnp.int32, (chunk, tokens), 1) == pick).astype(LOW)


def beside_kernel(n_row, after_ref, order_ref, cot_ref, w_ref, tokens_ref, mixed_ref):
    del after_ref
    group, width = cot_ref.shape[:2]
    n_col = group // n_row
    order = order_ref[...]
    cot = [cot_ref[row * n_col + core] for core in range(n_col) for row in range(n_row)]
    tokens_ref[...] = dot(jnp.concatenate(cot, axis=0), order, 0, 0).astype(LOW)
    mixed_ref[...] = dot(order, w_ref[:, : 3 * width], 1, 0).astype(LOW)


def beside(after, order, cot_all, w_first, n_row):
    group, width, tokens = cot_all.shape
    return pl.pallas_call(
        partial(beside_kernel, n_row),
        in_specs=[ANY] + [VMEM] * 3,
        out_specs=[VMEM] * 2,
        out_shape=(
            jax.ShapeDtypeStruct((tokens, D), LOW),
            jax.ShapeDtypeStruct((D, 3 * width), LOW),
        ),
        compiler_params=BIG,
        name="beside",
    )(after, order, cot_all, w_first)


def before_kernel(place_ref, after_ref, order_ref, cot_ref, *refs):
    del after_ref
    *parts, up_ref, grad_ref, mixed_ref, scratch = refs
    w_rest = assembled(place_ref[1], parts, scratch)
    wide = up_ref.shape[1]
    up_ref[...] = w_rest[:, :wide]
    w_down = w_rest[:, wide:]
    grad_ref[...] = dot(cot_ref[...], w_down, 1, 0)
    mixed_ref[...] = dot(order_ref[...], w_down, 1, 0).astype(LOW)


def before(place, after, order, cot_tokens, parts):
    wide = parts[0].shape[1] // 2
    return pl.pallas_call(
        before_kernel,
        in_specs=[SMEM, ANY, VMEM, VMEM] + [VMEM] * len(parts),
        out_specs=[VMEM] * 3,
        out_shape=(
            jax.ShapeDtypeStruct((D, wide), LOW),
            jax.ShapeDtypeStruct((cot_tokens.shape[0], wide), jnp.float32),
            jax.ShapeDtypeStruct((D, wide), LOW),
        ),
        scratch_shapes=[part_scratch(parts)],
        compiler_params=BIG,
        name="before",
    )(place, after, order, cot_tokens, *parts)


def behind_kernel(
    place_ref, after_ref, zb_ref, hid_ref, cot_ref, act_ref, down_ref, mid_ref, grad_ref, theirs_ref, mine_ref
):
    del after_ref
    active = act_ref[...]
    up_grad = dot(zb_ref[...], hid_ref[...], 0, 0).astype(LOW)
    down_grad = dot(cot_ref[...], active, 0, 0).astype(LOW)
    grad_ref[...] = jnp.concatenate([up_grad, down_grad], axis=1).reshape(grad_ref.shape)
    pick = own_tokens(place_ref, mid_ref.shape[1], active.shape[0])
    result = dot(down_ref[...], active, 1, 1) + dot(mid_ref[...], pick, 1, 0)
    result = result.astype(LOW)
    half = D // 2
    split_cores(place_ref[0], result[:half], result[half:], theirs_ref, mine_ref)


def behind(place, after, zb, hidden_grad, cot_tokens, active, down_mixed, middle_mixed, n_dp):
    tokens, wide = active.shape
    return pl.pallas_call(
        behind_kernel,
        in_specs=[SMEM, ANY] + [VMEM] * 6,
        out_specs=[VMEM] * 3,
        out_shape=(
            jax.ShapeDtypeStruct((n_dp, D // n_dp, 2 * wide), LOW),
            jax.ShapeDtypeStruct((D // 2, tokens), LOW),
            jax.ShapeDtypeStruct((D // 2, tokens), LOW),
        ),
        compiler_params=BIG,
        name="behind",
    )(place, after, zb, hidden_grad, cot_tokens, active, down_mixed, middle_mixed)


def mlp_kernel(
    core_ref, zb_ref, up_ref, bias_ref, grad_ref, act_ref, hid_ref, theirs_ref, mine_ref, sum_ref
):
    step = pl.program_id(0)
    near = step >= pl.num_programs(0) // 2
    hidden = dot(zb_ref[...], up_ref[...], 1, 0) + bias_ref[...]
    square = hidden * hidden
    slope = 0.7978845608028654 * (1.0 + 0.044715 * square)
    bent = jnp.tanh(hidden * slope)
    gate = 0.5 * (1.0 + bent)
    act_ref[...] = (hidden * gate).astype(LOW)
    steep = gate + 0.5 * hidden * (1.0 - bent * bent) * (
        0.7978845608028654 * (1.0 + 3 * 0.044715 * square)
    )
    hidden_grad = (grad_ref[...] * steep).astype(LOW)
    hid_ref[...] = hidden_grad
    two_grad = dot(hidden_grad, up_ref[...], 1, 1).astype(LOW)

    @pl.when(near)
    def _():
        mine_ref[...] = two_grad

    @pl.when(jnp.logical_not(near))
    def _():
        theirs_ref[...] = two_grad

    @pl.when(step == 0)
    def _():
        sum_ref[...] = jnp.zeros(sum_ref.shape, jnp.float32)

    sum_ref[...] += jnp.sum(hidden_grad.astype(jnp.float32), axis=0, keepdims=True)


def mlp(core, zb, w_up, up_bias, active_grad):
    tokens = zb.shape[0]
    wide = w_up.shape[1]
    steps = 6
    block = tokens // steps
    turned = lambda i, c: ((i + (steps // 2) * (1 - c[0])) % steps, 0)
    whole = lambda i, c: (0, 0)
    return pl.pallas_call(
        mlp_kernel,
        grid_spec=pltpu.PrefetchScalarGridSpec(
            num_scalar_prefetch=1,
            grid=(steps,),
            in_specs=[
                pl.BlockSpec((block, D), turned),
                pl.BlockSpec((D, wide), whole),
                pl.BlockSpec((1, wide), whole),
                pl.BlockSpec((block, wide), turned),
            ],
            out_specs=[
                pl.BlockSpec((block, wide), turned),
                pl.BlockSpec((block, wide), turned),
                pl.BlockSpec((block, D), lambda i, c: (jnp.minimum(i, steps // 2 - 1), 0)),
                pl.BlockSpec((block, D), lambda i, c: (jnp.maximum(i - steps // 2, 0), 0)),
                pl.BlockSpec((1, wide), whole),
            ],
        ),
        out_shape=(
            jax.ShapeDtypeStruct((tokens, wide), LOW),
            jax.ShapeDtypeStruct((tokens, wide), LOW),
            jax.ShapeDtypeStruct((tokens // 2, D), LOW),
            jax.ShapeDtypeStruct((tokens // 2, D), LOW),
            jax.ShapeDtypeStruct((1, wide), jnp.float32),
        ),
        compiler_params=BIG,
        name="mlp",
    )(core, zb, w_up, up_bias, active_grad)


def back_kernel(after_ref, bg_ref, w_ref, qkv_ref, za_ref, att_ref, grad_ref, sum_ref, wg_ref):
    del after_ref
    heads = qkv_ref.shape[0]
    attended_grad = dot(bg_ref[...], w_ref[:, heads * 3 * HEAD :], 1, 0).T
    scale = HEAD ** (-0.5)
    parts = []
    for head in range(heads):
        queries, key_rows, values = qkv_ref[head, 0], qkv_ref[head, 1], qkv_ref[head, 2]
        grad = attended_grad[head * HEAD : (head + 1) * HEAD].astype(LOW)
        probs = head_probs(queries, key_rows)
        probs_grad = dot(grad, values, 0, 0)
        inner = jnp.sum(probs * probs_grad, axis=1, keepdims=True)
        scores_grad = (probs * (probs_grad - inner)).astype(LOW)
        parts.append(dot(key_rows, scores_grad, 1, 1) * scale)
        parts.append(dot(queries, scores_grad, 1, 0) * scale)
        parts.append(dot(grad, probs.astype(LOW), 1, 0))
    qkv_grad = jnp.concatenate(parts, axis=0).astype(LOW)
    grad_ref[...] = qkv_grad
    sum_ref[...] = jnp.sum(qkv_grad.astype(jnp.float32), axis=1, keepdims=True)
    qkv_part = dot(za_ref[...], qkv_grad, 1, 1).astype(LOW)
    out_part = dot(bg_ref[...], att_ref[...], 0, 0).astype(LOW)
    wg_ref[...] = jnp.concatenate([qkv_part, out_part], axis=1).reshape(wg_ref.shape)


def attend_back(after, branch_all, w_first, qkv, za, attended, n_dp):
    tokens, width = attended.shape
    return pl.pallas_call(
        back_kernel,
        in_specs=[ANY] + [VMEM] * 5,
        out_specs=[VMEM] * 3,
        out_shape=(
            jax.ShapeDtypeStruct((3 * width, tokens), LOW),
            jax.ShapeDtypeStruct((3 * width, 1), jnp.float32),
            jax.ShapeDtypeStruct((n_dp, D // n_dp, 4 * width), LOW),
        ),
        compiler_params=BIG,
        name="attend_back",
    )(after, branch_all, w_first, qkv, za, attended)


def first_kernel(core_ref, w_ref, grad_ref, x_ref, mean_ref, inv_ref, gain_ref, theirs_ref, mine_ref, sum_ref):
    n_row, rows, tokens = theirs_ref.shape
    width = rows - 16
    first = jnp.zeros((1, tokens), jnp.float32)
    second = jnp.zeros((1, tokens), jnp.float32)
    blocks = []
    for slot in range(D // width):
        here = slice(slot * width, (slot + 1) * width)
        part = dot(w_ref[here], grad_ref[...], 1, 0)
        normed = (x_ref[here].astype(jnp.float32) - mean_ref[...]) * inv_ref[...]
        product = part * normed
        sum_ref[here, 0:1] = jnp.sum(product, axis=1, keepdims=True)
        sum_ref[here, 1:2] = jnp.sum(part, axis=1, keepdims=True)
        first += jnp.sum(part * gain_ref[here], axis=0, keepdims=True)
        second += jnp.sum(product * gain_ref[here], axis=0, keepdims=True)
        blocks.append(part.astype(LOW))
    line = lax.broadcasted_iota(jnp.int32, (16, tokens), 0)
    sums = jnp.where(line == 0, first, jnp.where(line == 1, second, 0.0)).astype(LOW)
    for near, ref in ((False, theirs_ref), (True, mine_ref)):
        for core in range(2):

            @pl.when((core_ref[0] == core) == near)
            def _(core=core, ref=ref):
                for row in range(n_row):
                    ref[row, :width] = blocks[core * n_row + row]
                    ref[row, width:] = sums


def first_back(core, w_mixed, qkv_grad, x_all, x_mean, inverse, gain, width, n_row):
    tokens = x_all.shape[1]
    return pl.pallas_call(
        first_kernel,
        in_specs=[SMEM] + [VMEM] * 6,
        out_specs=[VMEM] * 3,
        out_shape=(
            jax.ShapeDtypeStruct((n_row, width + 16, tokens), LOW),
            jax.ShapeDtypeStruct((n_row, width + 16, tokens), LOW),
            jax.ShapeDtypeStruct((D, 2), jnp.float32),
        ),
        compiler_params=BIG,
        name="first_back",
    )(core, w_mixed, qkv_grad, x_all, x_mean, inverse, gain)


def adam_update(weights, moment_one, second, gradient, step_rate, weight_decay):
    moment_one = BETA_ONE * moment_one + (1.0 - BETA_ONE) * gradient
    second = BETA_TWO * second + (1.0 - BETA_TWO) * gradient * gradient
    direction = (
        moment_one / (1.0 - BETA_ONE**STEP) / (jnp.sqrt(second / (1.0 - BETA_TWO**STEP)) + ADAM_EPS)
    )
    return (weights - step_rate * (direction + weight_decay * weights), moment_one, second)


def shards(
    inputs,
    cotangent,
    qkv_master,
    out_master,
    up_master,
    down_master,
    qkv_first,
    out_first,
    up_first,
    down_first,
    qkv_second,
    out_second,
    up_second,
    down_second,
    norm_gains,
    gain_first,
    gain_second,
    biases,
    bias_first,
    bias_second,
):
    tokens, width = inputs.shape
    n_row = lax.axis_size("row")
    n_col = lax.axis_size("col")
    n_dp = lax.axis_size("dp")
    row = lax.axis_index("row")
    core = lax.axis_index("col")
    group = n_row * n_col
    heads = width // HEAD
    hidden_width = FF // group
    own = core * n_row + row
    place = jnp.stack([core, lax.axis_index("dp"), own]).astype(jnp.int32)
    chunk = -(-tokens // (group * 16)) * 16
    padded = chunk * group
    shard_rows = qkv_master.shape[0]

    index = jnp.arange(D)
    feature = (
        ((index // width) % n_row) * n_col + index // (width * n_row)
    ) * width + index % width
    index = (feature % n_dp) * (D // n_dp) + feature // n_dp
    order = (lax.broadcasted_iota(jnp.int32, (D, D), 1) == index[:, None]).astype(LOW)
    turn = (lax.broadcasted_iota(jnp.int32, (D, D), 0) == index[None, :]).astype(LOW)
    order, turn = lax.optimization_barrier((order, turn))

    def returned(rows):
        return exchange_rows(rows.reshape(n_row, shard_rows, -1))

    flat = lambda array: array.transpose(1, 2, 0)
    tall = lambda array: array.transpose(2, 0, 1)
    first_rows, x_own = prepare(place, qkv_master, flat(out_master), n_row, inputs.T, padded)
    first_rows = exchange_rows(first_rows).reshape(D // n_dp, -1)
    x_all = lax.all_gather(x_own, ("col", "row"), axis=0, tiled=True)
    first_parts = gather_parts(first_rows, "dp")
    rest, cot_own = prepare(
        x_all, up_master, flat(down_master), n_row, cotangent.T, padded
    )
    rest = exchange_rows(rest).reshape(D // n_dp, -1)
    rest_parts = gather_parts(rest, "dp")
    cot_all = lax.all_gather(cot_own, ("row", "col"), axis=0)

    vectors = jnp.concatenate([norm_gains, biases[: 6 * D].reshape(6, D)])
    query_bias = lax.dynamic_slice_in_dim(biases, 2 * D + own * width, width).reshape(heads, HEAD)
    value_bias = lax.dynamic_slice_in_dim(biases, 3 * D + own * width, width).reshape(heads, HEAD)
    feature_start = (row * n_col + core) * width
    down_bias = lax.dynamic_slice_in_dim(biases, 5 * D + feature_start, width)
    up_bias = lax.dynamic_slice_in_dim(biases, 6 * D + own * hidden_width, hidden_width)
    qkv_bias = jnp.stack([query_bias, jnp.zeros_like(query_bias), value_bias], axis=1).reshape(
        3 * width, 1
    )

    za, x_mean, inverse_one, gain_one = norm_first(vectors, x_all, turn, n_row)

    w_first, qkv, attended, theirs, mine = attend(place, rest, za, qkv_bias, first_parts, width)
    pair = (mine.astype(jnp.float32) + swap_cores(theirs).astype(jnp.float32)).astype(LOW)
    branch = sum_over_rows(pair)
    x_mine, dealt = own_rows_of(place, pair, vectors, x_all, turn, n_row, chunk)
    gain_two, shift_two, out_bias = dealt[1], dealt[3], dealt[6]

    middle = x_mine + branch + (out_bias + zero_of(rest_parts[-1]))[None, :]
    center = middle - jnp.sum(middle, axis=1, keepdims=True) / D
    inverse_two = lax.rsqrt(jnp.sum(center * center, axis=1, keepdims=True) / D + NORM_EPS)
    normed_two = center * inverse_two
    zb = (normed_two * gain_two + shift_two).astype(LOW)
    cot_tokens, qkv_mixed = beside(zb, order, cot_all, w_first, n_row)
    cot_mine = take(cot_tokens, own, chunk).astype(jnp.float32)
    w_up, active_grad, down_mixed = before(place, zb, order, cot_tokens, rest_parts)
    zb = lax.all_gather(zb, ("col", "row"), axis=0, tiled=True)

    core_of = core.reshape(1).astype(jnp.int32)
    active, hidden_grad, theirs, mine, up_sums = mlp(
        core_of, zb, w_up, up_bias[None, :], active_grad
    )
    pair = (mine.astype(jnp.float32) + swap_cores(theirs).astype(jnp.float32)).astype(LOW)
    two_grad = sum_over_rows(pair)

    middle_mixed = dot(order, middle.astype(LOW), 1, 1, LOW)
    rest_grad, theirs, mine = behind(
        place, pair, zb, hidden_grad, cot_tokens, active, down_mixed, middle_mixed, n_dp
    )
    result = (mine.astype(jnp.float32) + swap_cores(theirs).astype(jnp.float32)).astype(LOW)

    scaled = two_grad * gain_two
    first_sum = jnp.sum(scaled, axis=1, keepdims=True) / D
    second_sum = jnp.sum(scaled * normed_two, axis=1, keepdims=True) / D
    middle_grad = cot_mine + zero_of(result) + inverse_two * (scaled - first_sum - normed_two * second_sum)
    middle_grad = middle_grad.astype(LOW)
    branch_all = lax.all_gather(middle_grad, ("col", "row"), axis=0, tiled=True)
    later = zero_of(middle_grad)
    result = sum_over_rows(result) + down_bias[:, None]
    result = result.astype(LOW)[:, :tokens].T
    rest_rows = sum_blocks(rest_grad, "dp", later)
    rest_rows = rest_rows + zero_of(branch_all).astype(LOW)

    qkv_grad, bias_sums, first_grad = attend_back(
        rest_rows, branch_all, w_first, qkv, za, attended, n_dp
    )
    theirs, mine, one_sums = first_back(
        core_of, qkv_mixed, qkv_grad, x_all, x_mean, inverse_one, gain_one, width, n_row
    )
    rest_blocks = returned(rest_rows)
    pair = mine.astype(jnp.float32) + zero_of(rest_blocks)
    pair = (pair + swap_cores(theirs).astype(jnp.float32)).astype(LOW)
    one_grad = sum_over_rows(pair.reshape(-1, padded))
    first_rows = sum_blocks(first_grad, "dp", 0.0)

    own_gain = lax.dynamic_slice_in_dim(norm_gains[0], feature_start, width)[:, None]
    own_normed = (x_own.astype(jnp.float32) - x_mean) * inverse_one
    own_order = lax.dynamic_slice_in_dim(order, own * width, width, axis=0)
    own_middle = dot(own_order, branch_all, 1, 1)
    input_grad = own_middle + inverse_one * (
        one_grad[:width] * own_gain
        - one_grad[width : width + 1] / D
        - own_normed * (one_grad[width + 1 : width + 2] / D)
    )
    input_grad = input_grad.astype(LOW)[:, :tokens].T

    later = zero_of(pair)
    bias_sums = bias_sums.reshape(heads, 3, HEAD)
    all_rows = jnp.stack(
        [
            one_sums[:, 0],
            one_sums[:, 1],
            jnp.sum(two_grad * normed_two, axis=0),
            jnp.sum(two_grad, axis=0),
            jnp.sum(middle_grad, axis=0, dtype=jnp.float32),
            jnp.sum(cot_mine, axis=0),
        ]
    )
    own_row = jnp.concatenate(
        [bias_sums[:, 0].reshape(width), bias_sums[:, 2].reshape(width), up_sums[0]]
    )
    own_row = jnp.pad(own_row, (0, D - own_row.shape[0]))
    own_rows = jnp.where(jnp.arange(group)[:, None] == own, own_row[None, :], 0.0)
    total = all_sum(jnp.concatenate([jnp.pad(all_rows, ((0, 2), (0, 0))), own_rows]) + later)
    one_rows = total[:2].reshape(2, n_col, n_row, width).transpose(0, 2, 1, 3).reshape(2, D)
    two_rows = total[2:6].reshape(4, n_dp, D // n_dp).transpose(0, 2, 1).reshape(4, D)
    own_rows = total[8:]
    gain_total = jnp.stack([one_rows[0], two_rows[0]])
    bias_total = jnp.concatenate(
        [
            one_rows[1],
            two_rows[1],
            own_rows[:, :width].reshape(D),
            own_rows[:, width : 2 * width].reshape(D),
            two_rows[2],
            two_rows[3],
            own_rows[:, 2 * width : 2 * width + hidden_width].reshape(FF),
        ]
    )

    rest_new = adam(
        pair,
        rest_blocks,
        (0.03, 0.02),
        up_master,
        up_first,
        up_second,
        flat(down_master),
        flat(down_first),
        flat(down_second),
    )
    first_new = adam(
        pair,
        returned(first_rows),
        (0.03, 0.12),
        qkv_master,
        qkv_first,
        qkv_second,
        flat(out_master),
        flat(out_first),
        flat(out_second),
    )
    g_new = adam_update(norm_gains, gain_first, gain_second, gain_total, 0.5, 0.0)
    b_new = adam_update(biases, bias_first, bias_second, bias_total, 0.5, 0.0)
    return (
        result,
        input_grad,
        *first_new[:3],
        *(tall(array) for array in first_new[3:]),
        *rest_new[:3],
        *(tall(array) for array in rest_new[3:]),
        *g_new,
        *b_new,
    )


def solution(mesh):
    token_spec = P("dp", ("row", "col"))
    wide = P("row", "dp", "col")
    tall = P("col", "row", "dp")
    return jax.shard_map(
        shards,
        mesh=mesh,
        in_specs=(token_spec,) * 2 + (wide, tall, wide, tall) * 3 + (P(),) * 6,
        out_specs=(token_spec,) * 2
        + (wide,) * 3
        + (tall,) * 3
        + (wide,) * 3
        + (tall,) * 3
        + (P(),) * 6,
        check_vma=False,
    )
```

```python
from functools import partial

import jax
import jax.numpy as jnp
from jax import lax
from jax.experimental import pallas as pl
from jax.experimental.pallas import tpu as pltpu
from jax.sharding import PartitionSpec as P

D = 1152
FF = 4304
HEAD = 72
SEQ = 729
STEP = 10

NORM_EPS = 1e-06
ADAM_EPS = 1e-08
BETA_ONE = 0.9
BETA_TWO = 0.999
LOW = jnp.bfloat16


def dot(left, right, left_dim, right_dim, out=jnp.float32, precision=None):
    return lax.dot_general(
        left,
        right,
        (((left_dim,), (right_dim,)), ((), ())),
        precision=precision,
        preferred_element_type=out,
    )


def take(array, index, size):
    return lax.dynamic_slice_in_dim(array, index * size, size, axis=0)


def swap_cores(array):
    n_col = lax.axis_size("col")
    return lax.ppermute(array, "col", [(i, (i + 1) % n_col) for i in range(n_col)])


def gather_parts(block, axis):
    size = lax.axis_size(axis)
    if size > 4:
        copies = jnp.broadcast_to(block, (size,) + block.shape)
        return [lax.all_to_all(copies, axis, 0, 0).reshape(-1, block.shape[1])]
    return [block] + [
        lax.ppermute(block, axis, [(i, i ^ step) for i in range(size)]) for step in range(1, size)
    ]


def zero_of(array):
    first = lax.slice(array, (0,) * array.ndim, (1,) * array.ndim)
    return first.reshape(()).astype(jnp.float32) * 0.0


def exchange_rows(blocks):
    return lax.all_to_all(blocks, "row", 0, 0)


def sum_blocks(blocks, axis, later):
    blocks = lax.all_to_all(blocks, axis, 0, 0)
    return jnp.sum(blocks.astype(jnp.float32) + later, axis=0).astype(LOW)


def sum_parts(blocks, axis):
    size = lax.axis_size(axis)
    if size > 4:
        return sum_blocks(blocks, axis, 0.0)
    total = blocks[0].astype(jnp.float32)
    for step in range(1, size):
        got = lax.ppermute(blocks[step], axis, [(i, i ^ step) for i in range(size)])
        total = total + got.astype(jnp.float32)
    return total.astype(LOW)


def sum_over_rows(half):
    summed = lax.psum_scatter(half.astype(LOW), "row", scatter_dimension=0, tiled=True)
    return summed.astype(jnp.float32)


def all_sum(vector):
    for axis in ("col", "row", "dp"):
        size = lax.axis_size(axis)
        if size & (size - 1) or size > 4:
            vector = lax.psum(vector, axis)
            continue
        step = 1
        while step < size:
            vector = vector + lax.ppermute(vector, axis, [(i, i ^ step) for i in range(size)])
            step *= 2
    return vector


VMEM = pl.BlockSpec(memory_space=pltpu.VMEM)
SMEM = pl.BlockSpec(memory_space=pltpu.SMEM)
ANY = pl.BlockSpec(memory_space=pl.ANY)
BIG = pltpu.CompilerParams(vmem_limit_bytes=56 * 1024 * 1024)


def prepare_kernel(parts, after_ref, wide_ref, tall_ref, rows_ref, out_ref, long_ref):
    del after_ref
    long_ref[...] = jnp.zeros(long_ref.shape, long_ref.dtype)
    long_ref[:, : rows_ref.shape[1]] = rows_ref[...]
    arrays = [ref[:, 0, :].astype(LOW) for ref in (wide_ref, tall_ref)]
    for part in range(parts):
        pieces = []
        for array in arrays:
            size = array.shape[1] // parts
            pieces.append(array[:, part * size : (part + 1) * size])
        out_ref[part] = jnp.concatenate(pieces, axis=1)


def prepare(after, wide, tall, parts, rows, padded):
    size = (wide.shape[2] + tall.shape[2]) // parts
    return pl.pallas_call(
        partial(prepare_kernel, parts),
        in_specs=[ANY, VMEM, VMEM, VMEM],
        out_specs=[VMEM] * 2,
        out_shape=(
            jax.ShapeDtypeStruct((parts, wide.shape[0], size), LOW),
            jax.ShapeDtypeStruct((rows.shape[0], padded), LOW),
        ),
        compiler_params=BIG,
        name="prepare",
    )(after, wide, tall, rows)


def norm_kernel(n_row, vectors_ref, x_ref, index_ref, *refs):
    za_ref, mean_ref, inv_ref, gain_ref = refs[-4:]
    columns = vectors_ref[...].T
    gain = mixed_rows(columns[:, 0:1], n_row)
    gain_ref[...] = gain
    x_full = x_ref[...].astype(jnp.float32)
    mean = jnp.sum(x_full, axis=0, keepdims=True) / D
    center = x_full - mean
    inverse = lax.rsqrt(jnp.sum(center * center, axis=0, keepdims=True) / D + NORM_EPS)
    mean_ref[...] = mean
    inv_ref[...] = inverse
    z_one = (center * inverse * gain + mixed_rows(columns[:, 2:3], n_row)).astype(LOW)
    turn = (lax.broadcasted_iota(jnp.int32, (D, D), 0) == index_ref[...]).astype(LOW)
    za_ref[...] = dot(turn, z_one, 1, 0).astype(LOW)


def mixed_rows(column, n_row):
    n_col = 2
    width = D // (n_row * n_col)
    blocks = [
        column[(row * n_col + core) * width : (row * n_col + core + 1) * width]
        for core in range(n_col)
        for row in range(n_row)
    ]
    return jnp.concatenate(blocks, axis=0)


def norm_first(after, vectors, x_all, index, n_row):
    tokens = x_all.shape[1]
    return pl.pallas_call(
        partial(norm_kernel, n_row),
        in_specs=[VMEM] * 3 + [ANY] * len(after),
        out_specs=[VMEM] * 4,
        out_shape=(
            jax.ShapeDtypeStruct((D, tokens), LOW),
            jax.ShapeDtypeStruct((1, tokens), jnp.float32),
            jax.ShapeDtypeStruct((1, tokens), jnp.float32),
            jax.ShapeDtypeStruct((D, 1), jnp.float32),
        ),
        compiler_params=BIG,
        name="norm_first",
    )(vectors, x_all, index, *after)


def own_kernel(n_row, place_ref, after_ref, later_ref, vectors_ref, x_ref, order_ref, mine_ref, dealt_ref):
    del after_ref, later_ref
    pick = own_tokens(place_ref, mine_ref.shape[0], x_ref.shape[1])
    mine_ref[...] = dot(dot(pick, x_ref[...], 1, 1).astype(LOW), order_ref[...], 1, 0)
    rest = mixed_rows(vectors_ref[...].T, n_row).T
    pieces = []
    for _ in range(3):
        piece = rest.astype(LOW)
        rest = rest - piece.astype(jnp.float32)
        pieces.append(piece)
    total = dot(pieces[0], order_ref[...], 1, 0)
    for piece in pieces[1:]:
        total = total + dot(piece, order_ref[...], 1, 0)
    dealt_ref[...] = total


def own_rows_of(place, after, later, vectors, x_all, order, n_row, chunk):
    return pl.pallas_call(
        partial(own_kernel, n_row),
        in_specs=[SMEM, ANY, ANY] + [VMEM] * 3,
        out_specs=[VMEM] * 2,
        out_shape=(
            jax.ShapeDtypeStruct((chunk, D), jnp.float32),
            jax.ShapeDtypeStruct((8, D), jnp.float32),
        ),
        compiler_params=BIG,
        name="own_rows",
    )(place, after, later, vectors, x_all, order)


def adam_kernel(rates, after_ref, blocks_ref, *refs):
    del after_ref
    parts = blocks_ref.shape[0]
    start = 0
    for index, rate in enumerate(rates):
        weight, first, second = refs[3 * index : 3 * index + 3]
        size = weight.shape[2] // parts
        gradient = jnp.concatenate(
            [blocks_ref[part, :, start : start + size] for part in range(parts)], axis=1
        ).astype(jnp.float32)
        start += size
        new = adam_update(weight[:, 0, :], first[:, 0, :], second[:, 0, :], gradient, rate, 0.1)
        for array, ref in zip(new, refs[3 * len(rates) + 3 * index :]):
            ref[:, 0, :] = array


def adam(after, blocks, rates, *arrays):
    return pl.pallas_call(
        partial(adam_kernel, rates),
        in_specs=[ANY] + [VMEM] * (1 + len(arrays)),
        out_specs=[VMEM] * len(arrays),
        out_shape=[jax.ShapeDtypeStruct(a.shape, jnp.float32) for a in arrays],
        compiler_params=BIG,
        name="adam",
    )(after, blocks, *arrays)


def assembled(place, parts, scratch):
    if len(parts) == 1:
        return parts[0][...]
    for step, part in enumerate(parts):
        scratch[place ^ step] = part[...]
    return scratch[...].reshape(-1, scratch.shape[2])


def part_scratch(parts):
    return pltpu.VMEM((len(parts),) + parts[0].shape, LOW)


def store_parts(place, array, ref):
    count, rows = ref.shape[:2]
    if count > 4:
        ref[...] = array.reshape(ref.shape)
        return
    for index in range(count):
        ref[place ^ index] = array[index * rows : (index + 1) * rows]


def head_probs(queries, key_rows):
    scores = dot(queries, key_rows, 0, 0) * HEAD ** (-0.5)
    scores = jnp.where(lax.broadcasted_iota(jnp.int32, scores.shape, 1) < SEQ, scores, -1e30)
    exponent = jnp.exp(scores - jnp.max(scores, axis=1, keepdims=True))
    return exponent * (1.0 / jnp.sum(exponent, axis=1, keepdims=True))


def split_cores(core, first, second, theirs_ref, mine_ref):
    @pl.when(core == 0)
    def _():
        mine_ref[...] = first
        theirs_ref[...] = second

    @pl.when(core != 0)
    def _():
        mine_ref[...] = second
        theirs_ref[...] = first


def attend_kernel(place_ref, after_ref, za_ref, bias_ref, *refs):
    del after_ref
    *parts, w_ref, qkv_ref, att_ref, theirs_ref, mine_ref, scratch = refs
    w_ref[...] = assembled(place_ref[1], parts, scratch)
    heads = qkv_ref.shape[0]
    split = heads * 3 * HEAD
    qkv = dot(w_ref[:, :split], za_ref[...], 0, 0) + bias_ref[...]
    outs = []
    for head in range(heads):
        for t in range(3):
            start = (head * 3 + t) * HEAD
            qkv_ref[head, t] = qkv[start : start + HEAD].astype(LOW)
        probs = head_probs(qkv_ref[head, 0], qkv_ref[head, 1]).astype(LOW)
        outs.append(dot(qkv_ref[head, 2], probs, 1, 1))
    attended = jnp.concatenate(outs, axis=0).T.astype(LOW)
    att_ref[...] = attended
    branch = dot(attended, w_ref[:, split:], 1, 1).astype(LOW)
    half = branch.shape[0] // 2
    split_cores(place_ref[0], branch[:half], branch[half:], theirs_ref, mine_ref)


def attend(place, after, za, qkv_bias, parts, width):
    tokens = za.shape[1]
    return pl.pallas_call(
        attend_kernel,
        in_specs=[SMEM, ANY, VMEM, VMEM] + [VMEM] * len(parts),
        out_specs=[VMEM] * 5,
        out_shape=(
            jax.ShapeDtypeStruct((D, 4 * width), LOW),
            jax.ShapeDtypeStruct((width // HEAD, 3, HEAD, tokens), LOW),
            jax.ShapeDtypeStruct((tokens, width), LOW),
            jax.ShapeDtypeStruct((tokens // 2, D), LOW),
            jax.ShapeDtypeStruct((tokens // 2, D), LOW),
        ),
        scratch_shapes=[part_scratch(parts)],
        compiler_params=BIG,
        name="attend",
    )(place, after, za, qkv_bias, *parts)


def own_tokens(place_ref, chunk, tokens):
    pick = lax.broadcasted_iota(jnp.int32, (chunk, tokens), 0) + place_ref[2] * chunk
    return (lax.broadcasted_iota(jnp.int32, (chunk, tokens), 1) == pick).astype(LOW)


def beside_kernel(n_row, after_ref, order_ref, cot_ref, w_ref, tokens_ref, mixed_ref):
    del after_ref
    group, width = cot_ref.shape[:2]
    n_col = group // n_row
    order = order_ref[...]
    cot = [cot_ref[row * n_col + core] for core in range(n_col) for row in range(n_row)]
    tokens_ref[...] = dot(jnp.concatenate(cot, axis=0), order, 0, 0).astype(LOW)
    mixed_ref[...] = dot(order, w_ref[:, : 3 * width], 1, 0).astype(LOW)


def beside(after, order, cot_all, w_first, n_row):
    group, width, tokens = cot_all.shape
    return pl.pallas_call(
        partial(beside_kernel, n_row),
        in_specs=[ANY] + [VMEM] * 3,
        out_specs=[VMEM] * 2,
        out_shape=(
            jax.ShapeDtypeStruct((tokens, D), LOW),
            jax.ShapeDtypeStruct((D, 3 * width), LOW),
        ),
        compiler_params=BIG,
        name="beside",
    )(after, order, cot_all, w_first)


def before_kernel(place_ref, after_ref, order_ref, cot_ref, *refs):
    del after_ref
    *parts, up_ref, grad_ref, mixed_ref, scratch = refs
    w_rest = assembled(place_ref[1], parts, scratch)
    wide = up_ref.shape[1]
    up_ref[...] = w_rest[:, :wide]
    w_down = w_rest[:, wide:]
    grad_ref[...] = dot(cot_ref[...], w_down, 1, 0)
    mixed_ref[...] = dot(order_ref[...], w_down, 1, 0).astype(LOW)


def before(place, after, order, cot_tokens, parts):
    wide = parts[0].shape[1] // 2
    return pl.pallas_call(
        before_kernel,
        in_specs=[SMEM, ANY, VMEM, VMEM] + [VMEM] * len(parts),
        out_specs=[VMEM] * 3,
        out_shape=(
            jax.ShapeDtypeStruct((D, wide), LOW),
            jax.ShapeDtypeStruct((cot_tokens.shape[0], wide), jnp.float32),
            jax.ShapeDtypeStruct((D, wide), LOW),
        ),
        scratch_shapes=[part_scratch(parts)],
        compiler_params=BIG,
        name="before",
    )(place, after, order, cot_tokens, *parts)


def behind_kernel(
    place_ref, after_ref, zb_ref, hid_ref, cot_ref, act_ref, down_ref, mid_ref, grad_ref, theirs_ref, mine_ref
):
    del after_ref
    active = act_ref[...]
    up_grad = dot(zb_ref[...], hid_ref[...], 0, 0).astype(LOW)
    down_grad = dot(cot_ref[...], active, 0, 0).astype(LOW)
    grad_ref[...] = jnp.concatenate([up_grad, down_grad], axis=1).reshape(grad_ref.shape)
    pick = own_tokens(place_ref, mid_ref.shape[1], active.shape[0])
    result = dot(down_ref[...], active, 1, 1) + dot(mid_ref[...], pick, 1, 0)
    result = result.astype(LOW)
    half = D // 2
    split_cores(place_ref[0], result[:half], result[half:], theirs_ref, mine_ref)


def behind(place, after, zb, hidden_grad, cot_tokens, active, down_mixed, middle_mixed, n_dp):
    tokens, wide = active.shape
    return pl.pallas_call(
        behind_kernel,
        in_specs=[SMEM, ANY] + [VMEM] * 6,
        out_specs=[VMEM] * 3,
        out_shape=(
            jax.ShapeDtypeStruct((n_dp, D // n_dp, 2 * wide), LOW),
            jax.ShapeDtypeStruct((D // 2, tokens), LOW),
            jax.ShapeDtypeStruct((D // 2, tokens), LOW),
        ),
        compiler_params=BIG,
        name="behind",
    )(place, after, zb, hidden_grad, cot_tokens, active, down_mixed, middle_mixed)


def mlp_kernel(
    core_ref, zb_ref, up_ref, bias_ref, grad_ref, act_ref, hid_ref, theirs_ref, mine_ref, sum_ref
):
    step = pl.program_id(0)
    near = step >= pl.num_programs(0) // 2
    hidden = dot(zb_ref[...], up_ref[...], 1, 0) + bias_ref[...]
    square = hidden * hidden
    slope = 0.7978845608028654 * (1.0 + 0.044715 * square)
    bent = jnp.tanh(hidden * slope)
    gate = 0.5 * (1.0 + bent)
    act_ref[...] = (hidden * gate).astype(LOW)
    steep = gate + 0.5 * hidden * (1.0 - bent * bent) * (
        0.7978845608028654 * (1.0 + 3 * 0.044715 * square)
    )
    hidden_grad = (grad_ref[...] * steep).astype(LOW)
    hid_ref[...] = hidden_grad
    two_grad = dot(hidden_grad, up_ref[...], 1, 1).astype(LOW)

    @pl.when(near)
    def _():
        mine_ref[...] = two_grad

    @pl.when(jnp.logical_not(near))
    def _():
        theirs_ref[...] = two_grad

    @pl.when(step == 0)
    def _():
        sum_ref[...] = jnp.zeros(sum_ref.shape, jnp.float32)

    sum_ref[...] += jnp.sum(hidden_grad.astype(jnp.float32), axis=0, keepdims=True)


def mlp(core, zb, w_up, up_bias, active_grad):
    tokens = zb.shape[0]
    wide = w_up.shape[1]
    steps = 6
    block = tokens // steps
    turned = lambda i, c: ((i + (steps // 2) * (1 - c[0])) % steps, 0)
    whole = lambda i, c: (0, 0)
    return pl.pallas_call(
        mlp_kernel,
        grid_spec=pltpu.PrefetchScalarGridSpec(
            num_scalar_prefetch=1,
            grid=(steps,),
            in_specs=[
                pl.BlockSpec((block, D), turned),
                pl.BlockSpec((D, wide), whole),
                pl.BlockSpec((1, wide), whole),
                pl.BlockSpec((block, wide), turned),
            ],
            out_specs=[
                pl.BlockSpec((block, wide), turned),
                pl.BlockSpec((block, wide), turned),
                pl.BlockSpec((block, D), lambda i, c: (jnp.minimum(i, steps // 2 - 1), 0)),
                pl.BlockSpec((block, D), lambda i, c: (jnp.maximum(i - steps // 2, 0), 0)),
                pl.BlockSpec((1, wide), whole),
            ],
        ),
        out_shape=(
            jax.ShapeDtypeStruct((tokens, wide), LOW),
            jax.ShapeDtypeStruct((tokens, wide), LOW),
            jax.ShapeDtypeStruct((tokens // 2, D), LOW),
            jax.ShapeDtypeStruct((tokens // 2, D), LOW),
            jax.ShapeDtypeStruct((1, wide), jnp.float32),
        ),
        compiler_params=BIG,
        name="mlp",
    )(core, zb, w_up, up_bias, active_grad)


def back_kernel(place_ref, after_ref, bg_ref, w_ref, qkv_ref, za_ref, att_ref, grad_ref, sum_ref, wg_ref):
    del after_ref
    heads = qkv_ref.shape[0]
    attended_grad = dot(bg_ref[...], w_ref[:, heads * 3 * HEAD :], 1, 0).T
    scale = HEAD ** (-0.5)
    parts = []
    for head in range(heads):
        queries, key_rows, values = qkv_ref[head, 0], qkv_ref[head, 1], qkv_ref[head, 2]
        grad = attended_grad[head * HEAD : (head + 1) * HEAD].astype(LOW)
        probs = head_probs(queries, key_rows)
        probs_grad = dot(grad, values, 0, 0)
        inner = jnp.sum(probs * probs_grad, axis=1, keepdims=True)
        scores_grad = (probs * (probs_grad - inner)).astype(LOW)
        parts.append(dot(key_rows, scores_grad, 1, 1) * scale)
        parts.append(dot(queries, scores_grad, 1, 0) * scale)
        parts.append(dot(grad, probs.astype(LOW), 1, 0))
    qkv_grad = jnp.concatenate(parts, axis=0).astype(LOW)
    grad_ref[...] = qkv_grad
    sum_ref[...] = jnp.sum(qkv_grad.astype(jnp.float32), axis=1, keepdims=True)
    qkv_part = dot(za_ref[...], qkv_grad, 1, 1).astype(LOW)
    out_part = dot(bg_ref[...], att_ref[...], 0, 0).astype(LOW)
    store_parts(place_ref[1], jnp.concatenate([qkv_part, out_part], axis=1), wg_ref)


def attend_back(place, after, branch_all, w_first, qkv, za, attended, n_dp):
    tokens, width = attended.shape
    return pl.pallas_call(
        back_kernel,
        in_specs=[SMEM, ANY] + [VMEM] * 5,
        out_specs=[VMEM] * 3,
        out_shape=(
            jax.ShapeDtypeStruct((3 * width, tokens), LOW),
            jax.ShapeDtypeStruct((3 * width, 1), jnp.float32),
            jax.ShapeDtypeStruct((n_dp, D // n_dp, 4 * width), LOW),
        ),
        compiler_params=BIG,
        name="attend_back",
    )(place, after, branch_all, w_first, qkv, za, attended)


def first_kernel(core_ref, w_ref, grad_ref, x_ref, mean_ref, inv_ref, gain_ref, theirs_ref, mine_ref, sum_ref):
    n_row, rows, tokens = theirs_ref.shape
    width = rows - 16
    first = jnp.zeros((1, tokens), jnp.float32)
    second = jnp.zeros((1, tokens), jnp.float32)
    blocks = []
    for slot in range(D // width):
        here = slice(slot * width, (slot + 1) * width)
        part = dot(w_ref[here], grad_ref[...], 1, 0)
        normed = (x_ref[here].astype(jnp.float32) - mean_ref[...]) * inv_ref[...]
        product = part * normed
        sum_ref[here, 0:1] = jnp.sum(product, axis=1, keepdims=True)
        sum_ref[here, 1:2] = jnp.sum(part, axis=1, keepdims=True)
        first += jnp.sum(part * gain_ref[here], axis=0, keepdims=True)
        second += jnp.sum(product * gain_ref[here], axis=0, keepdims=True)
        blocks.append(part.astype(LOW))
    line = lax.broadcasted_iota(jnp.int32, (16, tokens), 0)
    sums = jnp.where(line == 0, first, jnp.where(line == 1, second, 0.0)).astype(LOW)
    for near, ref in ((False, theirs_ref), (True, mine_ref)):
        for core in range(2):

            @pl.when((core_ref[0] == core) == near)
            def _(core=core, ref=ref):
                for row in range(n_row):
                    ref[row, :width] = blocks[core * n_row + row]
                    ref[row, width:] = sums


def first_back(core, w_mixed, qkv_grad, x_all, x_mean, inverse, gain, width, n_row):
    tokens = x_all.shape[1]
    return pl.pallas_call(
        first_kernel,
        in_specs=[SMEM] + [VMEM] * 6,
        out_specs=[VMEM] * 3,
        out_shape=(
            jax.ShapeDtypeStruct((n_row, width + 16, tokens), LOW),
            jax.ShapeDtypeStruct((n_row, width + 16, tokens), LOW),
            jax.ShapeDtypeStruct((D, 2), jnp.float32),
        ),
        compiler_params=BIG,
        name="first_back",
    )(core, w_mixed, qkv_grad, x_all, x_mean, inverse, gain)


def adam_update(weights, moment_one, second, gradient, step_rate, weight_decay):
    moment_one = BETA_ONE * moment_one + (1.0 - BETA_ONE) * gradient
    second = BETA_TWO * second + (1.0 - BETA_TWO) * gradient * gradient
    direction = (
        moment_one / (1.0 - BETA_ONE**STEP) / (jnp.sqrt(second / (1.0 - BETA_TWO**STEP)) + ADAM_EPS)
    )
    return (weights - step_rate * (direction + weight_decay * weights), moment_one, second)


def shards(
    inputs,
    cotangent,
    qkv_master,
    out_master,
    up_master,
    down_master,
    qkv_first,
    out_first,
    up_first,
    down_first,
    qkv_second,
    out_second,
    up_second,
    down_second,
    norm_gains,
    gain_first,
    gain_second,
    biases,
    bias_first,
    bias_second,
):
    tokens, width = inputs.shape
    n_row = lax.axis_size("row")
    n_col = lax.axis_size("col")
    n_dp = lax.axis_size("dp")
    row = lax.axis_index("row")
    core = lax.axis_index("col")
    group = n_row * n_col
    heads = width // HEAD
    hidden_width = FF // group
    own = core * n_row + row
    place = jnp.stack([core, lax.axis_index("dp"), own]).astype(jnp.int32)
    chunk = -(-tokens // (group * 16)) * 16
    padded = chunk * group
    shard_rows = qkv_master.shape[0]

    index = jnp.arange(D)
    feature = (
        ((index // width) % n_row) * n_col + index // (width * n_row)
    ) * width + index % width
    index = (feature % n_dp) * (D // n_dp) + feature // n_dp
    order = (lax.broadcasted_iota(jnp.int32, (D, D), 1) == index[:, None]).astype(LOW)
    order = lax.optimization_barrier(order)

    def returned(rows):
        return exchange_rows(rows.reshape(n_row, shard_rows, -1))

    flat = lambda array: array.transpose(1, 2, 0)
    tall = lambda array: array.transpose(2, 0, 1)
    first_rows, x_own = prepare(place, qkv_master, flat(out_master), n_row, inputs.T, padded)
    first_rows = exchange_rows(first_rows).reshape(D // n_dp, -1)
    x_all = lax.all_gather(x_own, ("col", "row"), axis=0, tiled=True)
    first_parts = gather_parts(first_rows, "dp")
    rest, cot_own = prepare(place, up_master, flat(down_master), n_row, cotangent.T, padded)
    once = zero_of(x_all).astype(LOW)
    sent = exchange_rows(rest + once).reshape(D // n_dp, -1)
    rest_parts = gather_parts(sent, "dp")
    cot_all = lax.all_gather(cot_own + once, ("row", "col"), axis=0)

    vectors = jnp.concatenate([norm_gains, biases[: 6 * D].reshape(6, D)])
    query_bias = lax.dynamic_slice_in_dim(biases, 2 * D + own * width, width).reshape(heads, HEAD)
    value_bias = lax.dynamic_slice_in_dim(biases, 3 * D + own * width, width).reshape(heads, HEAD)
    feature_start = (row * n_col + core) * width
    down_bias = lax.dynamic_slice_in_dim(biases, 5 * D + feature_start, width)
    up_bias = lax.dynamic_slice_in_dim(biases, 6 * D + own * hidden_width, hidden_width)
    qkv_bias = jnp.stack([query_bias, jnp.zeros_like(query_bias), value_bias], axis=1).reshape(
        3 * width, 1
    )

    za, x_mean, inverse_one, gain_one = norm_first(
        (*first_parts[1:], rest), vectors, x_all, index[None, :], n_row
    )

    w_first, qkv, attended, theirs, mine = attend(place, sent, za, qkv_bias, first_parts, width)
    pair = (mine.astype(jnp.float32) + swap_cores(theirs).astype(jnp.float32)).astype(LOW)
    branch = sum_over_rows(pair)
    x_mine, dealt = own_rows_of(
        place, pair, cot_all, vectors, x_all, order, n_row, chunk
    )
    gain_two, shift_two, out_bias = dealt[1], dealt[3], dealt[6]

    middle = x_mine + branch + (out_bias + zero_of(rest_parts[-1]))[None, :]
    center = middle - jnp.sum(middle, axis=1, keepdims=True) / D
    inverse_two = lax.rsqrt(jnp.sum(center * center, axis=1, keepdims=True) / D + NORM_EPS)
    normed_two = center * inverse_two
    zb = (normed_two * gain_two + shift_two).astype(LOW)
    cot_tokens, qkv_mixed = beside(zb, order, cot_all, w_first, n_row)
    cot_mine = take(cot_tokens, own, chunk).astype(jnp.float32)
    w_up, active_grad, down_mixed = before(place, zb, order, cot_tokens, rest_parts)
    zb = lax.all_gather(zb, ("col", "row"), axis=0, tiled=True)

    core_of = core.reshape(1).astype(jnp.int32)
    active, hidden_grad, theirs, mine, up_sums = mlp(
        core_of, zb, w_up, up_bias[None, :], active_grad
    )
    pair = (mine.astype(jnp.float32) + swap_cores(theirs).astype(jnp.float32)).astype(LOW)
    two_grad = sum_over_rows(pair)

    middle_mixed = dot(order, middle.astype(LOW), 1, 1, LOW)
    rest_grad, theirs, mine = behind(
        place, pair, zb, hidden_grad, cot_tokens, active, down_mixed, middle_mixed, n_dp
    )
    result = (mine.astype(jnp.float32) + swap_cores(theirs).astype(jnp.float32)).astype(LOW)

    scaled = two_grad * gain_two
    first_sum = jnp.sum(scaled, axis=1, keepdims=True) / D
    second_sum = jnp.sum(scaled * normed_two, axis=1, keepdims=True) / D
    middle_grad = cot_mine + zero_of(result) + inverse_two * (scaled - first_sum - normed_two * second_sum)
    middle_grad = middle_grad.astype(LOW)
    branch_all = lax.all_gather(middle_grad, ("col", "row"), axis=0, tiled=True)
    later = zero_of(middle_grad)
    summed = lax.psum_scatter(result, "row", scatter_dimension=0, tiled=True)
    result = summed.astype(jnp.float32) + down_bias[:, None]
    result = result.astype(LOW)[:, :tokens].T
    rest_rows = sum_blocks(rest_grad, "dp", later)
    rest_rows = rest_rows + zero_of(branch_all).astype(LOW)

    qkv_grad, bias_sums, first_grad = attend_back(
        place, summed, branch_all, w_first, qkv, za, attended, n_dp
    )
    theirs, mine, one_sums = first_back(
        core_of, qkv_mixed, qkv_grad, x_all, x_mean, inverse_one, gain_one, width, n_row
    )
    rest_blocks = returned(rest_rows)
    pair = mine.astype(jnp.float32) + zero_of(rest_blocks)
    pair = (pair + swap_cores(theirs).astype(jnp.float32)).astype(LOW)
    one_grad = sum_over_rows(pair.reshape(-1, padded))
    first_rows = sum_parts(first_grad, "dp")

    own_gain = lax.dynamic_slice_in_dim(norm_gains[0], feature_start, width)[:, None]
    own_normed = (x_own.astype(jnp.float32) - x_mean) * inverse_one
    own_order = lax.dynamic_slice_in_dim(order, own * width, width, axis=0)
    own_middle = dot(own_order, branch_all, 1, 1)
    input_grad = own_middle + inverse_one * (
        one_grad[:width] * own_gain
        - one_grad[width : width + 1] / D
        - own_normed * (one_grad[width + 1 : width + 2] / D)
    )
    input_grad = input_grad.astype(LOW)[:, :tokens].T

    later = zero_of(pair)
    bias_sums = bias_sums.reshape(heads, 3, HEAD)
    all_rows = jnp.stack(
        [
            one_sums[:, 0],
            one_sums[:, 1],
            jnp.sum(two_grad * normed_two, axis=0),
            jnp.sum(two_grad, axis=0),
            jnp.sum(middle_grad, axis=0, dtype=jnp.float32),
            jnp.sum(cot_mine, axis=0),
        ]
    )
    own_row = jnp.concatenate(
        [bias_sums[:, 0].reshape(width), bias_sums[:, 2].reshape(width), up_sums[0]]
    )
    own_row = jnp.pad(own_row, (0, D - own_row.shape[0]))
    own_rows = jnp.where(jnp.arange(group)[:, None] == own, own_row[None, :], 0.0)
    total = all_sum(jnp.concatenate([jnp.pad(all_rows, ((0, 2), (0, 0))), own_rows]) + later)
    one_rows = total[:2].reshape(2, n_col, n_row, width).transpose(0, 2, 1, 3).reshape(2, D)
    two_rows = total[2:6].reshape(4, n_dp, D // n_dp).transpose(0, 2, 1).reshape(4, D)
    own_rows = total[8:]
    gain_total = jnp.stack([one_rows[0], two_rows[0]])
    bias_total = jnp.concatenate(
        [
            one_rows[1],
            two_rows[1],
            own_rows[:, :width].reshape(D),
            own_rows[:, width : 2 * width].reshape(D),
            two_rows[2],
            two_rows[3],
            own_rows[:, 2 * width : 2 * width + hidden_width].reshape(FF),
        ]
    )

    rest_new = adam(
        pair,
        rest_blocks,
        (0.03, 0.02),
        up_master,
        up_first,
        up_second,
        flat(down_master),
        flat(down_first),
        flat(down_second),
    )
    first_new = adam(
        pair,
        returned(first_rows),
        (0.03, 0.12),
        qkv_master,
        qkv_first,
        qkv_second,
        flat(out_master),
        flat(out_first),
        flat(out_second),
    )
    g_new = adam_update(norm_gains, gain_first, gain_second, gain_total, 0.5, 0.0)
    b_new = adam_update(biases, bias_first, bias_second, bias_total, 0.5, 0.0)
    return (
        result,
        input_grad,
        *first_new[:3],
        *(tall(array) for array in first_new[3:]),
        *rest_new[:3],
        *(tall(array) for array in rest_new[3:]),
        *g_new,
        *b_new,
    )


def solution(mesh):
    token_spec = P("dp", ("row", "col"))
    wide = P("row", "dp", "col")
    tall = P("col", "row", "dp")
    return jax.shard_map(
        shards,
        mesh=mesh,
        in_specs=(token_spec,) * 2 + (wide, tall, wide, tall) * 3 + (P(),) * 6,
        out_specs=(token_spec,) * 2
        + (wide,) * 3
        + (tall,) * 3
        + (wide,) * 3
        + (tall,) * 3
        + (P(),) * 6,
        check_vma=False,
    )
```

```python
from functools import partial

import jax
import jax.numpy as jnp
from jax import lax
from jax.experimental import pallas as pl
from jax.experimental.pallas import tpu as pltpu
from jax.sharding import PartitionSpec as P

D = 1152
FF = 4304
HEAD = 72
SEQ = 729
STEP = 10

NORM_EPS = 1e-06
ADAM_EPS = 1e-08
BETA_ONE = 0.9
BETA_TWO = 0.999
LOW = jnp.bfloat16


def dot(left, right, left_dim, right_dim, out=jnp.float32, precision=None):
    return lax.dot_general(
        left,
        right,
        (((left_dim,), (right_dim,)), ((), ())),
        precision=precision,
        preferred_element_type=out,
    )


def take(array, index, size):
    return lax.dynamic_slice_in_dim(array, index * size, size, axis=0)


def swap_cores(array):
    n_col = lax.axis_size("col")
    return lax.ppermute(array, "col", [(i, (i + 1) % n_col) for i in range(n_col)])


def gather_parts(block, axis):
    size = lax.axis_size(axis)
    if size > 4:
        copies = jnp.broadcast_to(block, (size,) + block.shape)
        return [lax.all_to_all(copies, axis, 0, 0).reshape(-1, block.shape[1])]
    return [block] + [
        lax.ppermute(block, axis, [(i, i ^ step) for i in range(size)]) for step in range(1, size)
    ]


def zero_of(array):
    first = lax.slice(array, (0,) * array.ndim, (1,) * array.ndim)
    return first.reshape(()).astype(jnp.float32) * 0.0


def exchange_rows(blocks):
    return lax.all_to_all(blocks, "row", 0, 0)


def sum_blocks(blocks, axis, later):
    blocks = lax.all_to_all(blocks, axis, 0, 0)
    return jnp.sum(blocks.astype(jnp.float32) + later, axis=0).astype(LOW)


def sum_parts(blocks, axis):
    size = lax.axis_size(axis)
    if size > 4:
        return sum_blocks(blocks, axis, 0.0)
    total = blocks[0].astype(jnp.float32)
    for step in range(1, size):
        got = lax.ppermute(blocks[step], axis, [(i, i ^ step) for i in range(size)])
        total = total + got.astype(jnp.float32)
    return total.astype(LOW)


def sum_over_rows(half):
    summed = lax.psum_scatter(half.astype(LOW), "row", scatter_dimension=0, tiled=True)
    return summed.astype(jnp.float32)


def all_sum(vector):
    for axis in ("col", "row", "dp"):
        size = lax.axis_size(axis)
        if size & (size - 1) or size > 4:
            vector = lax.psum(vector, axis)
            continue
        step = 1
        while step < size:
            vector = vector + lax.ppermute(vector, axis, [(i, i ^ step) for i in range(size)])
            step *= 2
    return vector


VMEM = pl.BlockSpec(memory_space=pltpu.VMEM)
SMEM = pl.BlockSpec(memory_space=pltpu.SMEM)
ANY = pl.BlockSpec(memory_space=pl.ANY)
BIG = pltpu.CompilerParams(vmem_limit_bytes=56 * 1024 * 1024)


def prepare_kernel(parts, after_ref, wide_ref, tall_ref, rows_ref, out_ref, long_ref):
    del after_ref
    long_ref[...] = jnp.zeros(long_ref.shape, long_ref.dtype)
    long_ref[:, : rows_ref.shape[1]] = rows_ref[...]
    arrays = [ref[:, 0, :].astype(LOW) for ref in (wide_ref, tall_ref)]
    for part in range(parts):
        pieces = []
        for array in arrays:
            size = array.shape[1] // parts
            pieces.append(array[:, part * size : (part + 1) * size])
        out_ref[part] = jnp.concatenate(pieces, axis=1)


def prepare(after, wide, tall, parts, rows, padded):
    size = (wide.shape[2] + tall.shape[2]) // parts
    return pl.pallas_call(
        partial(prepare_kernel, parts),
        in_specs=[ANY, VMEM, VMEM, VMEM],
        out_specs=[VMEM] * 2,
        out_shape=(
            jax.ShapeDtypeStruct((parts, wide.shape[0], size), LOW),
            jax.ShapeDtypeStruct((rows.shape[0], padded), LOW),
        ),
        compiler_params=BIG,
        name="prepare",
    )(after, wide, tall, rows)


def norm_kernel(n_row, place_ref, vectors_ref, near_ref, far_ref, index_ref, *refs):
    x_ref, za_ref, mean_ref, inv_ref, gain_ref = refs
    join_cores(place_ref[0], near_ref, far_ref, x_ref)
    columns = vectors_ref[...].T
    gain = mixed_rows(columns[:, 0:1], n_row)
    gain_ref[...] = gain
    x_full = x_ref[...].reshape(za_ref.shape).astype(jnp.float32)
    mean = jnp.sum(x_full, axis=0, keepdims=True) / D
    center = x_full - mean
    inverse = lax.rsqrt(jnp.sum(center * center, axis=0, keepdims=True) / D + NORM_EPS)
    mean_ref[...] = mean
    inv_ref[...] = inverse
    z_one = (center * inverse * gain + mixed_rows(columns[:, 2:3], n_row)).astype(LOW)
    turn = (lax.broadcasted_iota(jnp.int32, (D, D), 0) == index_ref[...]).astype(LOW)
    za_ref[...] = dot(turn, z_one, 1, 0).astype(LOW)


def mixed_rows(column, n_row):
    n_col = 2
    width = D // (n_row * n_col)
    blocks = [
        column[(row * n_col + core) * width : (row * n_col + core + 1) * width]
        for core in range(n_col)
        for row in range(n_row)
    ]
    return jnp.concatenate(blocks, axis=0)


def join_cores(core, near_ref, far_ref, ref):
    ref[core] = near_ref[...]
    ref[1 - core] = far_ref[...]


def norm_first(place, vectors, near, far, index, n_row):
    rows, tokens = near.shape
    return pl.pallas_call(
        partial(norm_kernel, n_row),
        in_specs=[SMEM] + [VMEM] * 4,
        out_specs=[VMEM] * 5,
        out_shape=(
            jax.ShapeDtypeStruct((2, rows, tokens), LOW),
            jax.ShapeDtypeStruct((D, tokens), LOW),
            jax.ShapeDtypeStruct((1, tokens), jnp.float32),
            jax.ShapeDtypeStruct((1, tokens), jnp.float32),
            jax.ShapeDtypeStruct((D, 1), jnp.float32),
        ),
        compiler_params=BIG,
        name="norm_first",
    )(place, vectors, near, far, index)


def own_kernel(n_row, place_ref, after_ref, later_ref, vectors_ref, x_ref, order_ref, mine_ref, dealt_ref):
    del after_ref, later_ref
    pick = own_tokens(place_ref, mine_ref.shape[0], x_ref.shape[1])
    mine_ref[...] = dot(dot(pick, x_ref[...], 1, 1).astype(LOW), order_ref[...], 1, 0)
    rest = mixed_rows(vectors_ref[...].T, n_row).T
    pieces = []
    for _ in range(3):
        piece = rest.astype(LOW)
        rest = rest - piece.astype(jnp.float32)
        pieces.append(piece)
    total = dot(pieces[0], order_ref[...], 1, 0)
    for piece in pieces[1:]:
        total = total + dot(piece, order_ref[...], 1, 0)
    dealt_ref[...] = total


def own_rows_of(place, after, later, vectors, x_all, order, n_row, chunk):
    return pl.pallas_call(
        partial(own_kernel, n_row),
        in_specs=[SMEM, ANY, ANY] + [VMEM] * 3,
        out_specs=[VMEM] * 2,
        out_shape=(
            jax.ShapeDtypeStruct((chunk, D), jnp.float32),
            jax.ShapeDtypeStruct((8, D), jnp.float32),
        ),
        compiler_params=BIG,
        name="own_rows",
    )(place, after, later, vectors, x_all, order)


def adam_kernel(rates, after_ref, blocks_ref, *refs):
    del after_ref
    parts = blocks_ref.shape[0]
    start = 0
    for index, rate in enumerate(rates):
        weight, first, second = refs[3 * index : 3 * index + 3]
        size = weight.shape[2] // parts
        gradient = jnp.concatenate(
            [blocks_ref[part, :, start : start + size] for part in range(parts)], axis=1
        ).astype(jnp.float32)
        start += size
        new = adam_update(weight[:, 0, :], first[:, 0, :], second[:, 0, :], gradient, rate, 0.1)
        for array, ref in zip(new, refs[3 * len(rates) + 3 * index :]):
            ref[:, 0, :] = array


def adam(after, blocks, rates, *arrays):
    return pl.pallas_call(
        partial(adam_kernel, rates),
        in_specs=[ANY] + [VMEM] * (1 + len(arrays)),
        out_specs=[VMEM] * len(arrays),
        out_shape=[jax.ShapeDtypeStruct(a.shape, jnp.float32) for a in arrays],
        compiler_params=BIG,
        name="adam",
    )(after, blocks, *arrays)


def assembled(place, parts, scratch):
    if len(parts) == 1:
        return parts[0][...]
    for step, part in enumerate(parts):
        scratch[place ^ step] = part[...]
    return scratch[...].reshape(-1, scratch.shape[2])


def part_scratch(parts):
    return pltpu.VMEM((len(parts),) + parts[0].shape, LOW)


def store_parts(place, array, ref):
    count, rows = ref.shape[:2]
    if count > 4:
        ref[...] = array.reshape(ref.shape)
        return
    for index in range(count):
        ref[place ^ index] = array[index * rows : (index + 1) * rows]


def head_probs(queries, key_rows):
    scores = dot(queries, key_rows, 0, 0) * HEAD ** (-0.5)
    scores = jnp.where(lax.broadcasted_iota(jnp.int32, scores.shape, 1) < SEQ, scores, -1e30)
    exponent = jnp.exp(scores - jnp.max(scores, axis=1, keepdims=True))
    return exponent * (1.0 / jnp.sum(exponent, axis=1, keepdims=True))


def split_cores(core, first, second, theirs_ref, mine_ref):
    @pl.when(core == 0)
    def _():
        mine_ref[...] = first
        theirs_ref[...] = second

    @pl.when(core != 0)
    def _():
        mine_ref[...] = second
        theirs_ref[...] = first


def attend_kernel(place_ref, after_ref, za_ref, bias_ref, *refs):
    del after_ref
    *parts, w_ref, qkv_ref, att_ref, theirs_ref, mine_ref, scratch = refs
    w_ref[...] = assembled(place_ref[1], parts, scratch)
    heads = qkv_ref.shape[0]
    split = heads * 3 * HEAD
    qkv = dot(w_ref[:, :split], za_ref[...], 0, 0) + bias_ref[...]
    outs = []
    for head in range(heads):
        for t in range(3):
            start = (head * 3 + t) * HEAD
            qkv_ref[head, t] = qkv[start : start + HEAD].astype(LOW)
        probs = head_probs(qkv_ref[head, 0], qkv_ref[head, 1]).astype(LOW)
        outs.append(dot(qkv_ref[head, 2], probs, 1, 1))
    attended = jnp.concatenate(outs, axis=0).T.astype(LOW)
    att_ref[...] = attended
    branch = dot(attended, w_ref[:, split:], 1, 1).astype(LOW)
    half = branch.shape[0] // 2
    split_cores(place_ref[0], branch[:half], branch[half:], theirs_ref, mine_ref)


def attend(place, after, za, qkv_bias, parts, width):
    tokens = za.shape[1]
    return pl.pallas_call(
        attend_kernel,
        in_specs=[SMEM, ANY, VMEM, VMEM] + [VMEM] * len(parts),
        out_specs=[VMEM] * 5,
        out_shape=(
            jax.ShapeDtypeStruct((D, 4 * width), LOW),
            jax.ShapeDtypeStruct((width // HEAD, 3, HEAD, tokens), LOW),
            jax.ShapeDtypeStruct((tokens, width), LOW),
            jax.ShapeDtypeStruct((tokens // 2, D), LOW),
            jax.ShapeDtypeStruct((tokens // 2, D), LOW),
        ),
        scratch_shapes=[part_scratch(parts)],
        compiler_params=BIG,
        name="attend",
    )(place, after, za, qkv_bias, *parts)


def own_tokens(place_ref, chunk, tokens):
    pick = lax.broadcasted_iota(jnp.int32, (chunk, tokens), 0) + place_ref[2] * chunk
    return (lax.broadcasted_iota(jnp.int32, (chunk, tokens), 1) == pick).astype(LOW)


def beside_kernel(n_row, after_ref, order_ref, cot_ref, w_ref, tokens_ref, mixed_ref):
    del after_ref
    group, width = cot_ref.shape[:2]
    n_col = group // n_row
    order = order_ref[...]
    cot = [cot_ref[row * n_col + core] for core in range(n_col) for row in range(n_row)]
    tokens_ref[...] = dot(jnp.concatenate(cot, axis=0), order, 0, 0).astype(LOW)
    mixed_ref[...] = dot(order, w_ref[:, : 3 * width], 1, 0).astype(LOW)


def beside(after, order, cot_all, w_first, n_row):
    group, width, tokens = cot_all.shape
    return pl.pallas_call(
        partial(beside_kernel, n_row),
        in_specs=[ANY] + [VMEM] * 3,
        out_specs=[VMEM] * 2,
        out_shape=(
            jax.ShapeDtypeStruct((tokens, D), LOW),
            jax.ShapeDtypeStruct((D, 3 * width), LOW),
        ),
        compiler_params=BIG,
        name="beside",
    )(after, order, cot_all, w_first)


def before_kernel(place_ref, near_ref, far_ref, order_ref, cot_ref, *refs):
    *parts, zb_ref, up_ref, grad_ref, mixed_ref, scratch = refs
    join_cores(place_ref[0], near_ref, far_ref, zb_ref)
    w_rest = assembled(place_ref[1], parts, scratch)
    wide = up_ref.shape[1]
    up_ref[...] = w_rest[:, :wide]
    w_down = w_rest[:, wide:]
    grad_ref[...] = dot(cot_ref[...], w_down, 1, 0)
    mixed_ref[...] = dot(order_ref[...], w_down, 1, 0).astype(LOW)


def before(place, near, far, order, cot_tokens, parts):
    wide = parts[0].shape[1] // 2
    return pl.pallas_call(
        before_kernel,
        in_specs=[SMEM] + [VMEM] * (4 + len(parts)),
        out_specs=[VMEM] * 4,
        out_shape=(
            jax.ShapeDtypeStruct((2,) + near.shape, LOW),
            jax.ShapeDtypeStruct((D, wide), LOW),
            jax.ShapeDtypeStruct((cot_tokens.shape[0], wide), jnp.float32),
            jax.ShapeDtypeStruct((D, wide), LOW),
        ),
        scratch_shapes=[part_scratch(parts)],
        compiler_params=BIG,
        name="before",
    )(place, near, far, order, cot_tokens, *parts)


def behind_kernel(
    place_ref, after_ref, zb_ref, hid_ref, cot_ref, act_ref, down_ref, mid_ref, grad_ref, theirs_ref, mine_ref
):
    del after_ref
    active = act_ref[...]
    up_grad = dot(zb_ref[...], hid_ref[...], 0, 0).astype(LOW)
    down_grad = dot(cot_ref[...], active, 0, 0).astype(LOW)
    grad_ref[...] = jnp.concatenate([up_grad, down_grad], axis=1).reshape(grad_ref.shape)
    pick = own_tokens(place_ref, mid_ref.shape[1], active.shape[0])
    result = dot(down_ref[...], active, 1, 1) + dot(mid_ref[...], pick, 1, 0)
    result = result.astype(LOW)
    half = D // 2
    split_cores(place_ref[0], result[:half], result[half:], theirs_ref, mine_ref)


def behind(place, after, zb, hidden_grad, cot_tokens, active, down_mixed, middle_mixed, n_dp):
    tokens, wide = active.shape
    return pl.pallas_call(
        behind_kernel,
        in_specs=[SMEM, ANY] + [VMEM] * 6,
        out_specs=[VMEM] * 3,
        out_shape=(
            jax.ShapeDtypeStruct((n_dp, D // n_dp, 2 * wide), LOW),
            jax.ShapeDtypeStruct((D // 2, tokens), LOW),
            jax.ShapeDtypeStruct((D // 2, tokens), LOW),
        ),
        compiler_params=BIG,
        name="behind",
    )(place, after, zb, hidden_grad, cot_tokens, active, down_mixed, middle_mixed)


def mlp_kernel(
    core_ref, zb_ref, up_ref, bias_ref, grad_ref, act_ref, hid_ref, theirs_ref, mine_ref, sum_ref
):
    step = pl.program_id(0)
    near = step >= pl.num_programs(0) // 2
    hidden = dot(zb_ref[...], up_ref[...], 1, 0) + bias_ref[...]
    square = hidden * hidden
    slope = 0.7978845608028654 * (1.0 + 0.044715 * square)
    bent = jnp.tanh(hidden * slope)
    gate = 0.5 * (1.0 + bent)
    act_ref[...] = (hidden * gate).astype(LOW)
    steep = gate + 0.5 * hidden * (1.0 - bent * bent) * (
        0.7978845608028654 * (1.0 + 3 * 0.044715 * square)
    )
    hidden_grad = (grad_ref[...] * steep).astype(LOW)
    hid_ref[...] = hidden_grad
    two_grad = dot(hidden_grad, up_ref[...], 1, 1).astype(LOW)

    @pl.when(near)
    def _():
        mine_ref[...] = two_grad

    @pl.when(jnp.logical_not(near))
    def _():
        theirs_ref[...] = two_grad

    @pl.when(step == 0)
    def _():
        sum_ref[...] = jnp.zeros(sum_ref.shape, jnp.float32)

    sum_ref[...] += jnp.sum(hidden_grad.astype(jnp.float32), axis=0, keepdims=True)


def mlp(core, zb, w_up, up_bias, active_grad):
    tokens = zb.shape[0]
    wide = w_up.shape[1]
    steps = 6
    block = tokens // steps
    turned = lambda i, c: ((i + (steps // 2) * (1 - c[0])) % steps, 0)
    whole = lambda i, c: (0, 0)
    return pl.pallas_call(
        mlp_kernel,
        grid_spec=pltpu.PrefetchScalarGridSpec(
            num_scalar_prefetch=1,
            grid=(steps,),
            in_specs=[
                pl.BlockSpec((block, D), turned),
                pl.BlockSpec((D, wide), whole),
                pl.BlockSpec((1, wide), whole),
                pl.BlockSpec((block, wide), turned),
            ],
            out_specs=[
                pl.BlockSpec((block, wide), turned),
                pl.BlockSpec((block, wide), turned),
                pl.BlockSpec((block, D), lambda i, c: (jnp.minimum(i, steps // 2 - 1), 0)),
                pl.BlockSpec((block, D), lambda i, c: (jnp.maximum(i - steps // 2, 0), 0)),
                pl.BlockSpec((1, wide), whole),
            ],
        ),
        out_shape=(
            jax.ShapeDtypeStruct((tokens, wide), LOW),
            jax.ShapeDtypeStruct((tokens, wide), LOW),
            jax.ShapeDtypeStruct((tokens // 2, D), LOW),
            jax.ShapeDtypeStruct((tokens // 2, D), LOW),
            jax.ShapeDtypeStruct((1, wide), jnp.float32),
        ),
        compiler_params=BIG,
        name="mlp",
    )(core, zb, w_up, up_bias, active_grad)


def back_kernel(
    place_ref, after_ref, near_ref, far_ref, w_ref, qkv_ref, za_ref, att_ref, all_ref, grad_ref, sum_ref, wg_ref
):
    del after_ref
    join_cores(place_ref[0], near_ref, far_ref, all_ref)
    branch_all = all_ref[...].reshape(att_ref.shape[0], D)
    heads = qkv_ref.shape[0]
    attended_grad = dot(branch_all, w_ref[:, heads * 3 * HEAD :], 1, 0).T
    scale = HEAD ** (-0.5)
    parts = []
    for head in range(heads):
        queries, key_rows, values = qkv_ref[head, 0], qkv_ref[head, 1], qkv_ref[head, 2]
        grad = attended_grad[head * HEAD : (head + 1) * HEAD].astype(LOW)
        probs = head_probs(queries, key_rows)
        probs_grad = dot(grad, values, 0, 0)
        inner = jnp.sum(probs * probs_grad, axis=1, keepdims=True)
        scores_grad = (probs * (probs_grad - inner)).astype(LOW)
        parts.append(dot(key_rows, scores_grad, 1, 1) * scale)
        parts.append(dot(queries, scores_grad, 1, 0) * scale)
        parts.append(dot(grad, probs.astype(LOW), 1, 0))
    qkv_grad = jnp.concatenate(parts, axis=0).astype(LOW)
    grad_ref[...] = qkv_grad
    sum_ref[...] = jnp.sum(qkv_grad.astype(jnp.float32), axis=1, keepdims=True)
    qkv_part = dot(za_ref[...], qkv_grad, 1, 1).astype(LOW)
    out_part = dot(branch_all, att_ref[...], 0, 0).astype(LOW)
    store_parts(place_ref[1], jnp.concatenate([qkv_part, out_part], axis=1), wg_ref)


def attend_back(place, after, near, far, w_first, qkv, za, attended, n_dp):
    tokens, width = attended.shape
    return pl.pallas_call(
        back_kernel,
        in_specs=[SMEM, ANY] + [VMEM] * 6,
        out_specs=[VMEM] * 4,
        out_shape=(
            jax.ShapeDtypeStruct((2,) + near.shape, LOW),
            jax.ShapeDtypeStruct((3 * width, tokens), LOW),
            jax.ShapeDtypeStruct((3 * width, 1), jnp.float32),
            jax.ShapeDtypeStruct((n_dp, D // n_dp, 4 * width), LOW),
        ),
        compiler_params=BIG,
        name="attend_back",
    )(place, after, near, far, w_first, qkv, za, attended)


def first_kernel(core_ref, w_ref, grad_ref, x_ref, mean_ref, inv_ref, gain_ref, theirs_ref, mine_ref, sum_ref):
    n_row, rows, tokens = theirs_ref.shape
    width = rows - 16
    first = jnp.zeros((1, tokens), jnp.float32)
    second = jnp.zeros((1, tokens), jnp.float32)
    blocks = []
    for slot in range(D // width):
        here = slice(slot * width, (slot + 1) * width)
        part = dot(w_ref[here], grad_ref[...], 1, 0)
        normed = (x_ref[here].astype(jnp.float32) - mean_ref[...]) * inv_ref[...]
        product = part * normed
        sum_ref[here, 0:1] = jnp.sum(product, axis=1, keepdims=True)
        sum_ref[here, 1:2] = jnp.sum(part, axis=1, keepdims=True)
        first += jnp.sum(part * gain_ref[here], axis=0, keepdims=True)
        second += jnp.sum(product * gain_ref[here], axis=0, keepdims=True)
        blocks.append(part.astype(LOW))
    line = lax.broadcasted_iota(jnp.int32, (16, tokens), 0)
    sums = jnp.where(line == 0, first, jnp.where(line == 1, second, 0.0)).astype(LOW)
    for near, ref in ((False, theirs_ref), (True, mine_ref)):
        for core in range(2):

            @pl.when((core_ref[0] == core) == near)
            def _(core=core, ref=ref):
                for row in range(n_row):
                    ref[row, :width] = blocks[core * n_row + row]
                    ref[row, width:] = sums


def first_back(core, w_mixed, qkv_grad, x_all, x_mean, inverse, gain, width, n_row):
    tokens = x_all.shape[1]
    return pl.pallas_call(
        first_kernel,
        in_specs=[SMEM] + [VMEM] * 6,
        out_specs=[VMEM] * 3,
        out_shape=(
            jax.ShapeDtypeStruct((n_row, width + 16, tokens), LOW),
            jax.ShapeDtypeStruct((n_row, width + 16, tokens), LOW),
            jax.ShapeDtypeStruct((D, 2), jnp.float32),
        ),
        compiler_params=BIG,
        name="first_back",
    )(core, w_mixed, qkv_grad, x_all, x_mean, inverse, gain)


def adam_update(weights, moment_one, second, gradient, step_rate, weight_decay):
    moment_one = BETA_ONE * moment_one + (1.0 - BETA_ONE) * gradient
    second = BETA_TWO * second + (1.0 - BETA_TWO) * gradient * gradient
    direction = (
        moment_one / (1.0 - BETA_ONE**STEP) / (jnp.sqrt(second / (1.0 - BETA_TWO**STEP)) + ADAM_EPS)
    )
    return (weights - step_rate * (direction + weight_decay * weights), moment_one, second)


def shards(
    inputs,
    cotangent,
    qkv_master,
    out_master,
    up_master,
    down_master,
    qkv_first,
    out_first,
    up_first,
    down_first,
    qkv_second,
    out_second,
    up_second,
    down_second,
    norm_gains,
    gain_first,
    gain_second,
    biases,
    bias_first,
    bias_second,
):
    tokens, width = inputs.shape
    n_row = lax.axis_size("row")
    n_col = lax.axis_size("col")
    n_dp = lax.axis_size("dp")
    row = lax.axis_index("row")
    core = lax.axis_index("col")
    group = n_row * n_col
    heads = width // HEAD
    hidden_width = FF // group
    own = core * n_row + row
    place = jnp.stack([core, lax.axis_index("dp"), own]).astype(jnp.int32)
    chunk = -(-tokens // (group * 16)) * 16
    padded = chunk * group
    shard_rows = qkv_master.shape[0]

    index = jnp.arange(D)
    feature = (
        ((index // width) % n_row) * n_col + index // (width * n_row)
    ) * width + index % width
    index = (feature % n_dp) * (D // n_dp) + feature // n_dp
    order = (lax.broadcasted_iota(jnp.int32, (D, D), 1) == index[:, None]).astype(LOW)
    order = lax.optimization_barrier(order)

    def returned(rows):
        return exchange_rows(rows.reshape(n_row, shard_rows, -1))

    flat = lambda array: array.transpose(1, 2, 0)
    tall = lambda array: array.transpose(2, 0, 1)
    first_rows, x_own = prepare(place, qkv_master, flat(out_master), n_row, inputs.T, padded)
    first_rows = exchange_rows(first_rows).reshape(D // n_dp, -1)
    x_after = x_own + zero_of(first_rows).astype(LOW)
    x_rows = lax.all_gather(x_after, "row", axis=0, tiled=True)
    first_parts = gather_parts(first_rows, "dp")
    rest, cot_own = prepare(x_rows, up_master, flat(down_master), n_row, cotangent.T, padded)
    rest = exchange_rows(rest).reshape(D // n_dp, -1)
    rest_parts = gather_parts(rest, "dp")
    cot_all = lax.all_gather(cot_own, ("row", "col"), axis=0)

    vectors = jnp.concatenate([norm_gains, biases[: 6 * D].reshape(6, D)])
    query_bias = lax.dynamic_slice_in_dim(biases, 2 * D + own * width, width).reshape(heads, HEAD)
    value_bias = lax.dynamic_slice_in_dim(biases, 3 * D + own * width, width).reshape(heads, HEAD)
    feature_start = (row * n_col + core) * width
    down_bias = lax.dynamic_slice_in_dim(biases, 5 * D + feature_start, width)
    up_bias = lax.dynamic_slice_in_dim(biases, 6 * D + own * hidden_width, hidden_width)
    qkv_bias = jnp.stack([query_bias, jnp.zeros_like(query_bias), value_bias], axis=1).reshape(
        3 * width, 1
    )

    x_all, za, x_mean, inverse_one, gain_one = norm_first(
        place, vectors, x_rows, swap_cores(x_rows), index[None, :], n_row
    )
    x_all = x_all.reshape(D, padded)

    w_first, qkv, attended, theirs, mine = attend(place, rest, za, qkv_bias, first_parts, width)
    pair = (mine.astype(jnp.float32) + swap_cores(theirs).astype(jnp.float32)).astype(LOW)
    branch = sum_over_rows(pair)
    x_mine, dealt = own_rows_of(
        place, pair, cot_all, vectors, x_all, order, n_row, chunk
    )
    gain_two, shift_two, out_bias = dealt[1], dealt[3], dealt[6]
    cot_tokens, qkv_mixed = beside(pair, order, cot_all, w_first, n_row)
    cot_mine = take(cot_tokens, own, chunk).astype(jnp.float32)

    middle = x_mine + branch + out_bias[None, :]
    center = middle - jnp.sum(middle, axis=1, keepdims=True) / D
    inverse_two = lax.rsqrt(jnp.sum(center * center, axis=1, keepdims=True) / D + NORM_EPS)
    normed_two = center * inverse_two
    zb = (normed_two * gain_two + shift_two).astype(LOW)
    zb_rows = lax.all_gather(zb, "row", axis=0, tiled=True)
    zb, w_up, active_grad, down_mixed = before(
        place, zb_rows, swap_cores(zb_rows), order, cot_tokens, rest_parts
    )
    zb = zb.reshape(padded, D)

    core_of = core.reshape(1).astype(jnp.int32)
    active, hidden_grad, theirs, mine, up_sums = mlp(
        core_of, zb, w_up, up_bias[None, :], active_grad
    )
    pair = (mine.astype(jnp.float32) + swap_cores(theirs).astype(jnp.float32)).astype(LOW)
    two_grad = sum_over_rows(pair)

    middle_mixed = dot(order, middle.astype(LOW), 1, 1, LOW)
    rest_grad, theirs, mine = behind(
        place, pair, zb, hidden_grad, cot_tokens, active, down_mixed, middle_mixed, n_dp
    )
    result = (mine.astype(jnp.float32) + swap_cores(theirs).astype(jnp.float32)).astype(LOW)

    scaled = two_grad * gain_two
    first_sum = jnp.sum(scaled, axis=1, keepdims=True) / D
    second_sum = jnp.sum(scaled * normed_two, axis=1, keepdims=True) / D
    middle_grad = cot_mine + zero_of(result) + inverse_two * (scaled - first_sum - normed_two * second_sum)
    middle_grad = middle_grad.astype(LOW)
    branch_rows = lax.all_gather(middle_grad, "row", axis=0, tiled=True)
    later = zero_of(branch_rows)
    summed = lax.psum_scatter(result, "row", scatter_dimension=0, tiled=True)
    result = summed.astype(jnp.float32) + down_bias[:, None]
    result = result.astype(LOW)[:, :tokens].T
    rest_rows = sum_blocks(rest_grad, "dp", later)

    branch_all, qkv_grad, bias_sums, first_grad = attend_back(
        place, rest_rows, branch_rows, swap_cores(branch_rows), w_first, qkv, za, attended, n_dp
    )
    branch_all = branch_all.reshape(padded, D)
    theirs, mine, one_sums = first_back(
        core_of, qkv_mixed, qkv_grad, x_all, x_mean, inverse_one, gain_one, width, n_row
    )
    rest_blocks = returned(rest_rows)
    first_rows = sum_parts(first_grad, "dp")
    pair = mine.astype(jnp.float32) + (
        zero_of(rest_blocks) + zero_of(summed) + zero_of(first_rows)
    )
    pair = (pair + swap_cores(theirs).astype(jnp.float32)).astype(LOW)
    one_grad = sum_over_rows(pair.reshape(-1, padded))

    own_gain = lax.dynamic_slice_in_dim(norm_gains[0], feature_start, width)[:, None]
    own_normed = (x_own.astype(jnp.float32) - x_mean) * inverse_one
    own_order = lax.dynamic_slice_in_dim(order, own * width, width, axis=0)
    own_middle = dot(own_order, branch_all, 1, 1)
    input_grad = own_middle + inverse_one * (
        one_grad[:width] * own_gain
        - one_grad[width : width + 1] / D
        - own_normed * (one_grad[width + 1 : width + 2] / D)
    )
    input_grad = input_grad.astype(LOW)[:, :tokens].T

    later = zero_of(pair)
    bias_sums = bias_sums.reshape(heads, 3, HEAD)
    all_rows = jnp.stack(
        [
            one_sums[:, 0],
            one_sums[:, 1],
            jnp.sum(two_grad * normed_two, axis=0),
            jnp.sum(two_grad, axis=0),
            jnp.sum(middle_grad, axis=0, dtype=jnp.float32),
            jnp.sum(cot_mine, axis=0),
        ]
    )
    own_row = jnp.concatenate(
        [bias_sums[:, 0].reshape(width), bias_sums[:, 2].reshape(width), up_sums[0]]
    )
    own_row = jnp.pad(own_row, (0, D - own_row.shape[0]))
    own_rows = jnp.where(jnp.arange(group)[:, None] == own, own_row[None, :], 0.0)
    total = all_sum(jnp.concatenate([jnp.pad(all_rows, ((0, 2), (0, 0))), own_rows]) + later)
    one_rows = total[:2].reshape(2, n_col, n_row, width).transpose(0, 2, 1, 3).reshape(2, D)
    two_rows = total[2:6].reshape(4, n_dp, D // n_dp).transpose(0, 2, 1).reshape(4, D)
    own_rows = total[8:]
    gain_total = jnp.stack([one_rows[0], two_rows[0]])
    bias_total = jnp.concatenate(
        [
            one_rows[1],
            two_rows[1],
            own_rows[:, :width].reshape(D),
            own_rows[:, width : 2 * width].reshape(D),
            two_rows[2],
            two_rows[3],
            own_rows[:, 2 * width : 2 * width + hidden_width].reshape(FF),
        ]
    )

    rest_new = adam(
        pair,
        rest_blocks,
        (0.03, 0.02),
        up_master,
        up_first,
        up_second,
        flat(down_master),
        flat(down_first),
        flat(down_second),
    )
    first_new = adam(
        pair,
        returned(first_rows),
        (0.03, 0.12),
        qkv_master,
        qkv_first,
        qkv_second,
        flat(out_master),
        flat(out_first),
        flat(out_second),
    )
    g_new = adam_update(norm_gains, gain_first, gain_second, gain_total, 0.5, 0.0)
    b_new = adam_update(biases, bias_first, bias_second, bias_total, 0.5, 0.0)
    return (
        result,
        input_grad,
        *first_new[:3],
        *(tall(array) for array in first_new[3:]),
        *rest_new[:3],
        *(tall(array) for array in rest_new[3:]),
        *g_new,
        *b_new,
    )


def solution(mesh):
    token_spec = P("dp", ("row", "col"))
    wide = P("row", "dp", "col")
    tall = P("col", "row", "dp")
    return jax.shard_map(
        shards,
        mesh=mesh,
        in_specs=(token_spec,) * 2 + (wide, tall, wide, tall) * 3 + (P(),) * 6,
        out_specs=(token_spec,) * 2
        + (wide,) * 3
        + (tall,) * 3
        + (wide,) * 3
        + (tall,) * 3
        + (P(),) * 6,
        check_vma=False,
    )
```

```python
from functools import partial

import jax
import jax.numpy as jnp
from jax import lax
from jax.experimental import pallas as pl
from jax.experimental.pallas import tpu as pltpu
from jax.sharding import PartitionSpec as P

D = 1152
FF = 4304
HEAD = 72
SEQ = 729
STEP = 10

NORM_EPS = 1e-06
ADAM_EPS = 1e-08
BETA_ONE = 0.9
BETA_TWO = 0.999
LOW = jnp.bfloat16


def dot(left, right, left_dim, right_dim, out=jnp.float32, precision=None):
    return lax.dot_general(
        left,
        right,
        (((left_dim,), (right_dim,)), ((), ())),
        precision=precision,
        preferred_element_type=out,
    )


def take(array, index, size):
    return lax.dynamic_slice_in_dim(array, index * size, size, axis=0)


def swap_cores(array):
    n_col = lax.axis_size("col")
    return lax.ppermute(array, "col", [(i, (i + 1) % n_col) for i in range(n_col)])


def both_cores(rows):
    pieces = [
        lax.all_gather(piece, "col", axis=0) for piece in jnp.split(rows, 2, axis=0)
    ]
    return jnp.concatenate(pieces, axis=1).reshape(-1, rows.shape[1])


def gather_parts(block, axis):
    size = lax.axis_size(axis)
    if size > 4:
        copies = jnp.broadcast_to(block, (size,) + block.shape)
        return [lax.all_to_all(copies, axis, 0, 0).reshape(-1, block.shape[1])]
    return [block] + [
        lax.ppermute(block, axis, [(i, i ^ step) for i in range(size)]) for step in range(1, size)
    ]


def zero_of(array):
    first = lax.slice(array, (0,) * array.ndim, (1,) * array.ndim)
    return first.reshape(()).astype(jnp.float32) * 0.0


def exchange_rows(blocks):
    return lax.all_to_all(blocks, "row", 0, 0)


def sum_blocks(blocks, axis, later):
    blocks = lax.all_to_all(blocks, axis, 0, 0)
    return jnp.sum(blocks.astype(jnp.float32) + later, axis=0).astype(LOW)


def sum_over_rows(half):
    summed = lax.psum_scatter(half.astype(LOW), "row", scatter_dimension=0, tiled=True)
    return summed.astype(jnp.float32)


def all_sum(vector):
    for axis in ("col", "row", "dp"):
        size = lax.axis_size(axis)
        if size & (size - 1) or size > 4:
            vector = lax.psum(vector, axis)
            continue
        step = 1
        while step < size:
            vector = vector + lax.ppermute(vector, axis, [(i, i ^ step) for i in range(size)])
            step *= 2
    return vector


VMEM = pl.BlockSpec(memory_space=pltpu.VMEM)
SMEM = pl.BlockSpec(memory_space=pltpu.SMEM)
ANY = pl.BlockSpec(memory_space=pl.ANY)
BIG = pltpu.CompilerParams(vmem_limit_bytes=56 * 1024 * 1024)


def prepare_kernel(parts, after_ref, wide_ref, tall_ref, out_ref):
    del after_ref
    arrays = [ref[:, 0, :].astype(LOW) for ref in (wide_ref, tall_ref)]
    for part in range(parts):
        pieces = []
        for array in arrays:
            size = array.shape[1] // parts
            pieces.append(array[:, part * size : (part + 1) * size])
        out_ref[part] = jnp.concatenate(pieces, axis=1)


def prepare(after, wide, tall, parts):
    rows = wide.shape[0]
    size = (wide.shape[2] + tall.shape[2]) // parts
    return pl.pallas_call(
        partial(prepare_kernel, parts),
        in_specs=[ANY, VMEM, VMEM],
        out_specs=VMEM,
        out_shape=jax.ShapeDtypeStruct((parts, rows, size), LOW),
        compiler_params=BIG,
        name="prepare",
    )(after, wide, tall)


def adam_kernel(rates, after_ref, blocks_ref, *refs):
    del after_ref
    parts = blocks_ref.shape[0]
    start = 0
    for index, rate in enumerate(rates):
        weight, first, second = refs[3 * index : 3 * index + 3]
        size = weight.shape[2] // parts
        gradient = jnp.concatenate(
            [blocks_ref[part, :, start : start + size] for part in range(parts)], axis=1
        ).astype(jnp.float32)
        start += size
        new = adam_update(weight[:, 0, :], first[:, 0, :], second[:, 0, :], gradient, rate, 0.1)
        for array, ref in zip(new, refs[3 * len(rates) + 3 * index :]):
            ref[:, 0, :] = array


def adam(after, blocks, rates, *arrays):
    return pl.pallas_call(
        partial(adam_kernel, rates),
        in_specs=[ANY] + [VMEM] * (1 + len(arrays)),
        out_specs=[VMEM] * len(arrays),
        out_shape=[jax.ShapeDtypeStruct(a.shape, jnp.float32) for a in arrays],
        compiler_params=BIG,
        name="adam",
    )(after, blocks, *arrays)


def assembled(place, parts, scratch):
    if len(parts) == 1:
        return parts[0][...]
    for step, part in enumerate(parts):
        scratch[place ^ step] = part[...]
    return scratch[...].reshape(-1, scratch.shape[2])


def part_scratch(parts):
    return pltpu.VMEM((len(parts),) + parts[0].shape, LOW)


def head_probs(queries, key_rows):
    scores = dot(queries, key_rows, 0, 0) * HEAD ** (-0.5)
    scores = jnp.where(lax.broadcasted_iota(jnp.int32, scores.shape, 1) < SEQ, scores, -1e30)
    exponent = jnp.exp(scores - jnp.max(scores, axis=1, keepdims=True))
    return exponent * (1.0 / jnp.sum(exponent, axis=1, keepdims=True))


def split_cores(core, first, second, theirs_ref, mine_ref):
    @pl.when(core == 0)
    def _():
        mine_ref[...] = first
        theirs_ref[...] = second

    @pl.when(core != 0)
    def _():
        mine_ref[...] = second
        theirs_ref[...] = first


def join_cores(core, near_ref, far_ref, ref):
    ref[core] = near_ref[...]
    ref[1 - core] = far_ref[...]


def attend_kernel(place_ref, after_ref, za_ref, bias_ref, *refs):
    del after_ref
    *parts, w_ref, qkv_ref, att_ref, theirs_ref, mine_ref, scratch = refs
    w_ref[...] = assembled(place_ref[1], parts, scratch)
    heads = qkv_ref.shape[0]
    split = heads * 3 * HEAD
    qkv = dot(w_ref[:, :split], za_ref[...], 0, 0) + bias_ref[...]
    outs = []
    for head in range(heads):
        for t in range(3):
            start = (head * 3 + t) * HEAD
            qkv_ref[head, t] = qkv[start : start + HEAD].astype(LOW)
        probs = head_probs(qkv_ref[head, 0], qkv_ref[head, 1]).astype(LOW)
        outs.append(dot(qkv_ref[head, 2], probs, 1, 1))
    attended = jnp.concatenate(outs, axis=0).T.astype(LOW)
    att_ref[...] = attended
    branch = dot(attended, w_ref[:, split:], 1, 1).astype(LOW)
    half = branch.shape[0] // 2
    split_cores(place_ref[0], branch[:half], branch[half:], theirs_ref, mine_ref)


def attend(place, after, za, qkv_bias, parts, width):
    tokens = za.shape[1]
    return pl.pallas_call(
        attend_kernel,
        in_specs=[SMEM, ANY, VMEM, VMEM] + [VMEM] * len(parts),
        out_specs=[VMEM] * 5,
        out_shape=(
            jax.ShapeDtypeStruct((D, 4 * width), LOW),
            jax.ShapeDtypeStruct((width // HEAD, 3, HEAD, tokens), LOW),
            jax.ShapeDtypeStruct((tokens, width), LOW),
            jax.ShapeDtypeStruct((tokens // 2, D), LOW),
            jax.ShapeDtypeStruct((tokens // 2, D), LOW),
        ),
        scratch_shapes=[part_scratch(parts)],
        compiler_params=BIG,
        name="attend",
    )(place, after, za, qkv_bias, *parts)


def own_tokens(place_ref, chunk, tokens):
    pick = lax.broadcasted_iota(jnp.int32, (chunk, tokens), 0) + place_ref[2] * chunk
    return (lax.broadcasted_iota(jnp.int32, (chunk, tokens), 1) == pick).astype(LOW)


def beside_kernel(n_row, place_ref, after_ref, order_ref, cot_ref, w_ref, x_ref, tokens_ref, mixed_ref, mine_ref):
    del after_ref
    group, width = cot_ref.shape[:2]
    n_col = group // n_row
    order = order_ref[...]
    cot = [cot_ref[row * n_col + core] for core in range(n_col) for row in range(n_row)]
    tokens_ref[...] = dot(jnp.concatenate(cot, axis=0), order, 0, 0).astype(LOW)
    mixed_ref[...] = dot(order, w_ref[:, : 3 * width], 1, 0).astype(LOW)
    pick = own_tokens(place_ref, mine_ref.shape[0], x_ref.shape[1])
    mine_ref[...] = dot(dot(pick, x_ref[...], 1, 1).astype(LOW), order, 1, 0)


def beside(place, after, order, cot_all, w_first, x_all, n_row, chunk):
    group, width, tokens = cot_all.shape
    return pl.pallas_call(
        partial(beside_kernel, n_row),
        in_specs=[SMEM, ANY] + [VMEM] * 4,
        out_specs=[VMEM] * 3,
        out_shape=(
            jax.ShapeDtypeStruct((tokens, D), LOW),
            jax.ShapeDtypeStruct((D, 3 * width), LOW),
            jax.ShapeDtypeStruct((chunk, D), jnp.float32),
        ),
        compiler_params=BIG,
        name="beside",
    )(place, after, order, cot_all, w_first, x_all)


def before_kernel(place_ref, near_ref, far_ref, order_ref, cot_ref, *refs):
    *parts, zb_ref, up_ref, grad_ref, mixed_ref, scratch = refs
    join_cores(place_ref[0], near_ref, far_ref, zb_ref)
    w_rest = assembled(place_ref[1], parts, scratch)
    wide = up_ref.shape[1]
    up_ref[...] = w_rest[:, :wide]
    w_down = w_rest[:, wide:]
    grad_ref[...] = dot(cot_ref[...], w_down, 1, 0)
    mixed_ref[...] = dot(order_ref[...], w_down, 1, 0).astype(LOW)


def before(place, near, far, order, cot_tokens, parts):
    wide = parts[0].shape[1] // 2
    return pl.pallas_call(
        before_kernel,
        in_specs=[SMEM] + [VMEM] * (4 + len(parts)),
        out_specs=[VMEM] * 4,
        out_shape=(
            jax.ShapeDtypeStruct((2,) + near.shape, LOW),
            jax.ShapeDtypeStruct((D, wide), LOW),
            jax.ShapeDtypeStruct((cot_tokens.shape[0], wide), jnp.float32),
            jax.ShapeDtypeStruct((D, wide), LOW),
        ),
        scratch_shapes=[part_scratch(parts)],
        compiler_params=BIG,
        name="before",
    )(place, near, far, order, cot_tokens, *parts)


def behind_kernel(
    place_ref, after_ref, zb_ref, hid_ref, cot_ref, act_ref, down_ref, mid_ref, grad_ref, theirs_ref, mine_ref
):
    del after_ref
    active = act_ref[...]
    up_grad = dot(zb_ref[...], hid_ref[...], 0, 0).astype(LOW)
    down_grad = dot(cot_ref[...], active, 0, 0).astype(LOW)
    grad_ref[...] = jnp.concatenate([up_grad, down_grad], axis=1).reshape(grad_ref.shape)
    pick = own_tokens(place_ref, mid_ref.shape[1], active.shape[0])
    result = dot(down_ref[...], active, 1, 1) + dot(mid_ref[...], pick, 1, 0)
    result = result.astype(LOW)
    half = D // 2
    split_cores(place_ref[0], result[:half], result[half:], theirs_ref, mine_ref)


def behind(place, after, zb, hidden_grad, cot_tokens, active, down_mixed, middle_mixed, n_dp):
    tokens, wide = active.shape
    return pl.pallas_call(
        behind_kernel,
        in_specs=[SMEM, ANY] + [VMEM] * 6,
        out_specs=[VMEM] * 3,
        out_shape=(
            jax.ShapeDtypeStruct((n_dp, D // n_dp, 2 * wide), LOW),
            jax.ShapeDtypeStruct((D // 2, tokens), LOW),
            jax.ShapeDtypeStruct((D // 2, tokens), LOW),
        ),
        compiler_params=BIG,
        name="behind",
    )(place, after, zb, hidden_grad, cot_tokens, active, down_mixed, middle_mixed)


def mlp_kernel(
    core_ref, zb_ref, up_ref, bias_ref, grad_ref, act_ref, hid_ref, theirs_ref, mine_ref, sum_ref
):
    step = pl.program_id(0)
    near = step >= pl.num_programs(0) // 2
    hidden = dot(zb_ref[...], up_ref[...], 1, 0) + bias_ref[...]
    square = hidden * hidden
    slope = 0.7978845608028654 * (1.0 + 0.044715 * square)
    bent = jnp.tanh(hidden * slope)
    gate = 0.5 * (1.0 + bent)
    act_ref[...] = (hidden * gate).astype(LOW)
    steep = gate + 0.5 * hidden * (1.0 - bent * bent) * (
        0.7978845608028654 * (1.0 + 3 * 0.044715 * square)
    )
    hidden_grad = (grad_ref[...] * steep).astype(LOW)
    hid_ref[...] = hidden_grad
    two_grad = dot(hidden_grad, up_ref[...], 1, 1).astype(LOW)

    @pl.when(near)
    def _():
        mine_ref[...] = two_grad

    @pl.when(jnp.logical_not(near))
    def _():
        theirs_ref[...] = two_grad

    @pl.when(step == 0)
    def _():
        sum_ref[...] = jnp.zeros(sum_ref.shape, jnp.float32)

    sum_ref[...] += jnp.sum(hidden_grad.astype(jnp.float32), axis=0, keepdims=True)


def mlp(core, zb, w_up, up_bias, active_grad):
    tokens = zb.shape[0]
    wide = w_up.shape[1]
    steps = 6
    block = tokens // steps
    turned = lambda i, c: ((i + (steps // 2) * (1 - c[0])) % steps, 0)
    whole = lambda i, c: (0, 0)
    return pl.pallas_call(
        mlp_kernel,
        grid_spec=pltpu.PrefetchScalarGridSpec(
            num_scalar_prefetch=1,
            grid=(steps,),
            in_specs=[
                pl.BlockSpec((block, D), turned),
                pl.BlockSpec((D, wide), whole),
                pl.BlockSpec((1, wide), whole),
                pl.BlockSpec((block, wide), turned),
            ],
            out_specs=[
                pl.BlockSpec((block, wide), turned),
                pl.BlockSpec((block, wide), turned),
                pl.BlockSpec((block, D), lambda i, c: (jnp.minimum(i, steps // 2 - 1), 0)),
                pl.BlockSpec((block, D), lambda i, c: (jnp.maximum(i - steps // 2, 0), 0)),
                pl.BlockSpec((1, wide), whole),
            ],
        ),
        out_shape=(
            jax.ShapeDtypeStruct((tokens, wide), LOW),
            jax.ShapeDtypeStruct((tokens, wide), LOW),
            jax.ShapeDtypeStruct((tokens // 2, D), LOW),
            jax.ShapeDtypeStruct((tokens // 2, D), LOW),
            jax.ShapeDtypeStruct((1, wide), jnp.float32),
        ),
        compiler_params=BIG,
        name="mlp",
    )(core, zb, w_up, up_bias, active_grad)


def back_kernel(
    place_ref, after_ref, near_ref, far_ref, w_ref, qkv_ref, za_ref, att_ref, all_ref, grad_ref, sum_ref, wg_ref
):
    del after_ref
    join_cores(place_ref[0], near_ref, far_ref, all_ref)
    branch_all = all_ref[...].reshape(att_ref.shape[0], D)
    heads = qkv_ref.shape[0]
    attended_grad = dot(branch_all, w_ref[:, heads * 3 * HEAD :], 1, 0).T
    scale = HEAD ** (-0.5)
    parts = []
    for head in range(heads):
        queries, key_rows, values = qkv_ref[head, 0], qkv_ref[head, 1], qkv_ref[head, 2]
        grad = attended_grad[head * HEAD : (head + 1) * HEAD].astype(LOW)
        probs = head_probs(queries, key_rows)
        probs_grad = dot(grad, values, 0, 0)
        inner = jnp.sum(probs * probs_grad, axis=1, keepdims=True)
        scores_grad = (probs * (probs_grad - inner)).astype(LOW)
        parts.append(dot(key_rows, scores_grad, 1, 1) * scale)
        parts.append(dot(queries, scores_grad, 1, 0) * scale)
        parts.append(dot(grad, probs.astype(LOW), 1, 0))
    qkv_grad = jnp.concatenate(parts, axis=0).astype(LOW)
    grad_ref[...] = qkv_grad
    sum_ref[...] = jnp.sum(qkv_grad.astype(jnp.float32), axis=1, keepdims=True)
    qkv_part = dot(za_ref[...], qkv_grad, 1, 1).astype(LOW)
    out_part = dot(branch_all, att_ref[...], 0, 0).astype(LOW)
    wg_ref[...] = jnp.concatenate([qkv_part, out_part], axis=1).reshape(wg_ref.shape)


def attend_back(place, after, near, far, w_first, qkv, za, attended, n_dp):
    tokens, width = attended.shape
    return pl.pallas_call(
        back_kernel,
        in_specs=[SMEM, ANY] + [VMEM] * 6,
        out_specs=[VMEM] * 4,
        out_shape=(
            jax.ShapeDtypeStruct((2,) + near.shape, LOW),
            jax.ShapeDtypeStruct((3 * width, tokens), LOW),
            jax.ShapeDtypeStruct((3 * width, 1), jnp.float32),
            jax.ShapeDtypeStruct((n_dp, D // n_dp, 4 * width), LOW),
        ),
        compiler_params=BIG,
        name="attend_back",
    )(place, after, near, far, w_first, qkv, za, attended)


def first_kernel(core_ref, w_ref, grad_ref, x_ref, mean_ref, inv_ref, gain_ref, theirs_ref, mine_ref, sum_ref):
    n_row, rows, tokens = theirs_ref.shape
    width = rows - 16
    first = jnp.zeros((1, tokens), jnp.float32)
    second = jnp.zeros((1, tokens), jnp.float32)
    blocks = []
    for slot in range(D // width):
        here = slice(slot * width, (slot + 1) * width)
        part = dot(w_ref[here], grad_ref[...], 1, 0)
        normed = (x_ref[here].astype(jnp.float32) - mean_ref[...]) * inv_ref[...]
        product = part * normed
        sum_ref[here, 0:1] = jnp.sum(product, axis=1, keepdims=True)
        sum_ref[here, 1:2] = jnp.sum(part, axis=1, keepdims=True)
        first += jnp.sum(part * gain_ref[here], axis=0, keepdims=True)
        second += jnp.sum(product * gain_ref[here], axis=0, keepdims=True)
        blocks.append(part.astype(LOW))
    line = lax.broadcasted_iota(jnp.int32, (16, tokens), 0)
    sums = jnp.where(line == 0, first, jnp.where(line == 1, second, 0.0)).astype(LOW)
    for near, ref in ((False, theirs_ref), (True, mine_ref)):
        for core in range(2):

            @pl.when((core_ref[0] == core) == near)
            def _(core=core, ref=ref):
                for row in range(n_row):
                    ref[row, :width] = blocks[core * n_row + row]
                    ref[row, width:] = sums


def first_back(core, w_mixed, qkv_grad, x_all, x_mean, inverse, gain, width, n_row):
    tokens = x_all.shape[1]
    return pl.pallas_call(
        first_kernel,
        in_specs=[SMEM] + [VMEM] * 6,
        out_specs=[VMEM] * 3,
        out_shape=(
            jax.ShapeDtypeStruct((n_row, width + 16, tokens), LOW),
            jax.ShapeDtypeStruct((n_row, width + 16, tokens), LOW),
            jax.ShapeDtypeStruct((D, 2), jnp.float32),
        ),
        compiler_params=BIG,
        name="first_back",
    )(core, w_mixed, qkv_grad, x_all, x_mean, inverse, gain)


def adam_update(weights, moment_one, second, gradient, step_rate, weight_decay):
    moment_one = BETA_ONE * moment_one + (1.0 - BETA_ONE) * gradient
    second = BETA_TWO * second + (1.0 - BETA_TWO) * gradient * gradient
    direction = (
        moment_one / (1.0 - BETA_ONE**STEP) / (jnp.sqrt(second / (1.0 - BETA_TWO**STEP)) + ADAM_EPS)
    )
    return (weights - step_rate * (direction + weight_decay * weights), moment_one, second)


def shards(
    inputs,
    cotangent,
    qkv_master,
    out_master,
    up_master,
    down_master,
    qkv_first,
    out_first,
    up_first,
    down_first,
    qkv_second,
    out_second,
    up_second,
    down_second,
    norm_gains,
    gain_first,
    gain_second,
    biases,
    bias_first,
    bias_second,
):
    tokens, width = inputs.shape
    n_row = lax.axis_size("row")
    n_col = lax.axis_size("col")
    n_dp = lax.axis_size("dp")
    row = lax.axis_index("row")
    core = lax.axis_index("col")
    group = n_row * n_col
    heads = width // HEAD
    hidden_width = FF // group
    own = core * n_row + row
    place = jnp.stack([core, lax.axis_index("dp"), own]).astype(jnp.int32)
    chunk = -(-tokens // (group * 16)) * 16
    padded = chunk * group
    shard_rows = qkv_master.shape[0]

    index = jnp.arange(D)
    feature = (
        ((index // width) % n_row) * n_col + index // (width * n_row)
    ) * width + index % width
    index = (feature % n_dp) * (D // n_dp) + feature // n_dp
    order = (lax.broadcasted_iota(jnp.int32, (D, D), 1) == index[:, None]).astype(LOW)
    order = lax.optimization_barrier(order)

    def mixed(vector):
        return vector.reshape(n_row, n_col, width).transpose(1, 0, 2).reshape(D)

    def dealt(vector):
        return vector.reshape(D // n_dp, n_dp).T.reshape(D)

    def returned(rows):
        return exchange_rows(rows.reshape(n_row, shard_rows, -1))

    def long(array):
        return jnp.pad(array, ((0, 0), (0, padded - tokens)))

    flat = lambda array: array.transpose(1, 2, 0)
    tall = lambda array: array.transpose(2, 0, 1)
    first_rows = prepare(place, qkv_master, flat(out_master), n_row)
    first_rows = exchange_rows(first_rows).reshape(D // n_dp, -1)
    x_own = long(inputs.T)
    x_after = x_own + zero_of(first_rows).astype(LOW)
    x_rows = lax.all_gather(x_after, "row", axis=0, tiled=True)
    first_parts = gather_parts(first_rows, "dp")
    rest = prepare(x_rows, up_master, flat(down_master), n_row)
    rest = exchange_rows(rest).reshape(D // n_dp, -1)
    rest_parts = gather_parts(rest, "dp")
    x_all = both_cores(x_rows)
    cot_own = long(cotangent.T) + zero_of(rest).astype(LOW)
    cot_all = lax.all_gather(cot_own, ("row", "col"), axis=0)

    gain_one = mixed(norm_gains[0])
    gain_two = dealt(norm_gains[1])
    shift_one = mixed(biases[:D])
    shift_two = dealt(biases[D : 2 * D])
    query_bias = lax.dynamic_slice_in_dim(biases, 2 * D + own * width, width).reshape(heads, HEAD)
    value_bias = lax.dynamic_slice_in_dim(biases, 3 * D + own * width, width).reshape(heads, HEAD)
    out_bias = dealt(biases[4 * D : 5 * D])
    feature_start = (row * n_col + core) * width
    down_bias = lax.dynamic_slice_in_dim(biases, 5 * D + feature_start, width)
    up_bias = lax.dynamic_slice_in_dim(biases, 6 * D + own * hidden_width, hidden_width)
    qkv_bias = jnp.stack([query_bias, jnp.zeros_like(query_bias), value_bias], axis=1).reshape(
        3 * width, 1
    )

    x_full = x_all.astype(jnp.float32)
    x_mean = jnp.sum(x_full, axis=0, keepdims=True) / D
    center = x_full - x_mean
    inverse_one = lax.rsqrt(jnp.sum(center * center, axis=0, keepdims=True) / D + NORM_EPS)
    za = (center * inverse_one * gain_one[:, None] + shift_one[:, None]).astype(LOW)
    za = dot(order, za, 0, 0, LOW)

    w_first, qkv, attended, theirs, mine = attend(place, rest, za, qkv_bias, first_parts, width)
    pair = (mine.astype(jnp.float32) + swap_cores(theirs).astype(jnp.float32)).astype(LOW)
    branch = sum_over_rows(pair)
    cot_tokens, qkv_mixed, x_mine = beside(
        place, pair, order, cot_all, w_first, x_all, n_row, chunk
    )
    cot_mine = take(cot_tokens, own, chunk).astype(jnp.float32)

    middle = x_mine + branch + out_bias[None, :]
    center = middle - jnp.sum(middle, axis=1, keepdims=True) / D
    inverse_two = lax.rsqrt(jnp.sum(center * center, axis=1, keepdims=True) / D + NORM_EPS)
    normed_two = center * inverse_two
    zb = (normed_two * gain_two + shift_two).astype(LOW)
    zb_rows = lax.all_gather(zb, "row", axis=0, tiled=True)
    zb, w_up, active_grad, down_mixed = before(
        place, zb_rows, swap_cores(zb_rows), order, cot_tokens, rest_parts
    )
    zb = zb.reshape(padded, D)

    core_of = core.reshape(1).astype(jnp.int32)
    active, hidden_grad, theirs, mine, up_sums = mlp(
        core_of, zb, w_up, up_bias[None, :], active_grad
    )
    pair = (mine.astype(jnp.float32) + swap_cores(theirs).astype(jnp.float32)).astype(LOW)
    two_grad = sum_over_rows(pair)

    middle_mixed = dot(order, middle.astype(LOW), 1, 1, LOW)
    rest_grad, theirs, mine = behind(
        place, pair, zb, hidden_grad, cot_tokens, active, down_mixed, middle_mixed, n_dp
    )
    result = mine.astype(jnp.float32) + swap_cores(theirs).astype(jnp.float32)

    scaled = two_grad * gain_two
    first_sum = jnp.sum(scaled, axis=1, keepdims=True) / D
    second_sum = jnp.sum(scaled * normed_two, axis=1, keepdims=True) / D
    middle_grad = cot_mine + inverse_two * (scaled - first_sum - normed_two * second_sum)
    middle_grad = middle_grad.astype(LOW)
    branch_rows = lax.all_gather(middle_grad, "row", axis=0, tiled=True)
    rest_rows = sum_blocks(rest_grad, "dp", zero_of(branch_rows))
    rest_blocks = returned(rest_rows)
    branch_all, qkv_grad, bias_sums, first_grad = attend_back(
        place, rest_rows, branch_rows, swap_cores(branch_rows), w_first, qkv, za, attended, n_dp
    )
    branch_all = branch_all.reshape(padded, D)
    theirs, mine, one_sums = first_back(
        core_of, qkv_mixed, qkv_grad, x_all, x_mean, inverse_one, gain_one[:, None], width, n_row
    )
    pair = mine.astype(jnp.float32) + zero_of(rest_blocks)
    pair = (pair + swap_cores(theirs).astype(jnp.float32)).astype(LOW)
    one_grad = sum_over_rows(pair.reshape(-1, padded))
    later = zero_of(one_grad)
    result = sum_over_rows(result + later) + down_bias[:, None]
    result = result.astype(LOW)[:, :tokens].T
    first_rows = sum_blocks(first_grad, "dp", 0.0)

    own_gain = lax.dynamic_slice_in_dim(norm_gains[0], feature_start, width)[:, None]
    own_normed = (x_own.astype(jnp.float32) - x_mean) * inverse_one
    own_order = lax.dynamic_slice_in_dim(order, own * width, width, axis=0)
    own_middle = dot(own_order, branch_all, 1, 1)
    input_grad = own_middle + inverse_one * (
        one_grad[:width] * own_gain
        - one_grad[width : width + 1] / D
        - own_normed * (one_grad[width + 1 : width + 2] / D)
    )
    input_grad = input_grad.astype(LOW)[:, :tokens].T

    bias_sums = bias_sums.reshape(heads, 3, HEAD)
    all_rows = jnp.stack(
        [
            one_sums[:, 0],
            one_sums[:, 1],
            jnp.sum(two_grad * normed_two, axis=0),
            jnp.sum(two_grad, axis=0),
            jnp.sum(middle_grad, axis=0, dtype=jnp.float32),
            jnp.sum(cot_mine, axis=0),
        ]
    )
    own_row = jnp.concatenate(
        [bias_sums[:, 0].reshape(width), bias_sums[:, 2].reshape(width), up_sums[0]]
    )
    own_row = jnp.pad(own_row, (0, D - own_row.shape[0]))
    own_rows = jnp.where(jnp.arange(group)[:, None] == own, own_row[None, :], 0.0)
    total = all_sum(jnp.concatenate([jnp.pad(all_rows, ((0, 2), (0, 0))), own_rows]) + later)
    one_rows = total[:2].reshape(2, n_col, n_row, width).transpose(0, 2, 1, 3).reshape(2, D)
    two_rows = total[2:6].reshape(4, n_dp, D // n_dp).transpose(0, 2, 1).reshape(4, D)
    own_rows = total[8:]
    gain_total = jnp.stack([one_rows[0], two_rows[0]])
    bias_total = jnp.concatenate(
        [
            one_rows[1],
            two_rows[1],
            own_rows[:, :width].reshape(D),
            own_rows[:, width : 2 * width].reshape(D),
            two_rows[2],
            two_rows[3],
            own_rows[:, 2 * width : 2 * width + hidden_width].reshape(FF),
        ]
    )

    rest_new = adam(
        pair,
        rest_blocks,
        (0.03, 0.02),
        up_master,
        up_first,
        up_second,
        flat(down_master),
        flat(down_first),
        flat(down_second),
    )
    first_new = adam(
        pair,
        returned(first_rows),
        (0.03, 0.12),
        qkv_master,
        qkv_first,
        qkv_second,
        flat(out_master),
        flat(out_first),
        flat(out_second),
    )
    g_new = adam_update(norm_gains, gain_first, gain_second, gain_total, 0.5, 0.0)
    b_new = adam_update(biases, bias_first, bias_second, bias_total, 0.5, 0.0)
    return (
        result,
        input_grad,
        *first_new[:3],
        *(tall(array) for array in first_new[3:]),
        *rest_new[:3],
        *(tall(array) for array in rest_new[3:]),
        *g_new,
        *b_new,
    )


def solution(mesh):
    token_spec = P("dp", ("row", "col"))
    wide = P("row", "dp", "col")
    tall = P("col", "row", "dp")
    return jax.shard_map(
        shards,
        mesh=mesh,
        in_specs=(token_spec,) * 2 + (wide, tall, wide, tall) * 3 + (P(),) * 6,
        out_specs=(token_spec,) * 2
        + (wide,) * 3
        + (tall,) * 3
        + (wide,) * 3
        + (tall,) * 3
        + (P(),) * 6,
        check_vma=False,
    )
```

```python
from functools import partial

import jax
import jax.numpy as jnp
from jax import lax
from jax.experimental import pallas as pl
from jax.experimental.pallas import tpu as pltpu
from jax.sharding import PartitionSpec as P

D = 1152
FF = 4304
HEAD = 72
SEQ = 729
STEP = 10

NORM_EPS = 1e-06
ADAM_EPS = 1e-08
BETA_ONE = 0.9
BETA_TWO = 0.999
LOW = jnp.bfloat16


def dot(left, right, left_dim, right_dim, out=jnp.float32, precision=None):
    return lax.dot_general(
        left,
        right,
        (((left_dim,), (right_dim,)), ((), ())),
        precision=precision,
        preferred_element_type=out,
    )


def take(array, index, size):
    return lax.dynamic_slice_in_dim(array, index * size, size, axis=0)


def swap_cores(array):
    n_col = lax.axis_size("col")
    return lax.ppermute(array, "col", [(i, (i + 1) % n_col) for i in range(n_col)])


def both_cores(rows):
    pieces = [
        lax.all_gather(piece, "col", axis=0) for piece in jnp.split(rows, 2, axis=0)
    ]
    return jnp.concatenate(pieces, axis=1).reshape(-1, rows.shape[1])


def gather_parts(block, axis):
    size = lax.axis_size(axis)
    if size > 4:
        copies = jnp.broadcast_to(block, (size,) + block.shape)
        return [lax.all_to_all(copies, axis, 0, 0).reshape(-1, block.shape[1])]
    return [block] + [
        lax.ppermute(block, axis, [(i, i ^ step) for i in range(size)]) for step in range(1, size)
    ]


def zero_of(array):
    first = lax.slice(array, (0,) * array.ndim, (1,) * array.ndim)
    return first.reshape(()).astype(jnp.float32) * 0.0


def exchange_rows(blocks):
    return lax.all_to_all(blocks, "row", 0, 0)


def sum_blocks(blocks, axis, later):
    blocks = lax.all_to_all(blocks, axis, 0, 0)
    return jnp.sum(blocks.astype(jnp.float32) + later, axis=0).astype(LOW)


def sum_over_rows(half):
    summed = lax.psum_scatter(half.astype(LOW), "row", scatter_dimension=0, tiled=True)
    return summed.astype(jnp.float32)


def all_sum(vector):
    for axis in ("col", "row", "dp"):
        size = lax.axis_size(axis)
        if size & (size - 1) or size > 4:
            vector = lax.psum(vector, axis)
            continue
        step = 1
        while step < size:
            vector = vector + lax.ppermute(vector, axis, [(i, i ^ step) for i in range(size)])
            step *= 2
    return vector


VMEM = pl.BlockSpec(memory_space=pltpu.VMEM)
SMEM = pl.BlockSpec(memory_space=pltpu.SMEM)
ANY = pl.BlockSpec(memory_space=pl.ANY)
BIG = pltpu.CompilerParams(vmem_limit_bytes=56 * 1024 * 1024)


def prepare_kernel(parts, after_ref, wide_ref, tall_ref, out_ref):
    del after_ref
    arrays = [ref[:, 0, :].astype(LOW) for ref in (wide_ref, tall_ref)]
    for part in range(parts):
        pieces = []
        for array in arrays:
            size = array.shape[1] // parts
            pieces.append(array[:, part * size : (part + 1) * size])
        out_ref[part] = jnp.concatenate(pieces, axis=1)


def prepare(after, wide, tall, parts):
    rows = wide.shape[0]
    size = (wide.shape[2] + tall.shape[2]) // parts
    return pl.pallas_call(
        partial(prepare_kernel, parts),
        in_specs=[ANY, VMEM, VMEM],
        out_specs=VMEM,
        out_shape=jax.ShapeDtypeStruct((parts, rows, size), LOW),
        compiler_params=BIG,
        name="prepare",
    )(after, wide, tall)


def adam_kernel(rates, after_ref, blocks_ref, *refs):
    del after_ref
    parts = blocks_ref.shape[0]
    start = 0
    for index, rate in enumerate(rates):
        weight, first, second = refs[3 * index : 3 * index + 3]
        size = weight.shape[2] // parts
        gradient = jnp.concatenate(
            [blocks_ref[part, :, start : start + size] for part in range(parts)], axis=1
        ).astype(jnp.float32)
        start += size
        new = adam_update(weight[:, 0, :], first[:, 0, :], second[:, 0, :], gradient, rate, 0.1)
        for array, ref in zip(new, refs[3 * len(rates) + 3 * index :]):
            ref[:, 0, :] = array


def adam(after, blocks, rates, *arrays):
    return pl.pallas_call(
        partial(adam_kernel, rates),
        in_specs=[ANY] + [VMEM] * (1 + len(arrays)),
        out_specs=[VMEM] * len(arrays),
        out_shape=[jax.ShapeDtypeStruct(a.shape, jnp.float32) for a in arrays],
        compiler_params=BIG,
        name="adam",
    )(after, blocks, *arrays)


def assembled(place, parts, scratch):
    if len(parts) == 1:
        return parts[0][...]
    for step, part in enumerate(parts):
        scratch[place ^ step] = part[...]
    return scratch[...].reshape(-1, scratch.shape[2])


def part_scratch(parts):
    return pltpu.VMEM((len(parts),) + parts[0].shape, LOW)


def head_probs(queries, key_rows):
    scores = dot(queries, key_rows, 0, 0) * HEAD ** (-0.5)
    scores = jnp.where(lax.broadcasted_iota(jnp.int32, scores.shape, 1) < SEQ, scores, -1e30)
    exponent = jnp.exp(scores - jnp.max(scores, axis=1, keepdims=True))
    return exponent * (1.0 / jnp.sum(exponent, axis=1, keepdims=True))


def split_cores(core, first, second, theirs_ref, mine_ref):
    @pl.when(core == 0)
    def _():
        mine_ref[...] = first
        theirs_ref[...] = second

    @pl.when(core != 0)
    def _():
        mine_ref[...] = second
        theirs_ref[...] = first


def join_cores(core, near_ref, far_ref, ref):
    ref[core] = near_ref[...]
    ref[1 - core] = far_ref[...]


def attend_kernel(place_ref, after_ref, za_ref, bias_ref, *refs):
    del after_ref
    *parts, w_ref, qkv_ref, att_ref, theirs_ref, mine_ref, scratch = refs
    w_ref[...] = assembled(place_ref[1], parts, scratch)
    heads = qkv_ref.shape[0]
    split = heads * 3 * HEAD
    qkv = dot(w_ref[:, :split], za_ref[...], 0, 0) + bias_ref[...]
    outs = []
    for head in range(heads):
        for t in range(3):
            start = (head * 3 + t) * HEAD
            qkv_ref[head, t] = qkv[start : start + HEAD].astype(LOW)
        probs = head_probs(qkv_ref[head, 0], qkv_ref[head, 1]).astype(LOW)
        outs.append(dot(qkv_ref[head, 2], probs, 1, 1))
    attended = jnp.concatenate(outs, axis=0).T.astype(LOW)
    att_ref[...] = attended
    branch = dot(attended, w_ref[:, split:], 1, 1).astype(LOW)
    half = branch.shape[0] // 2
    split_cores(place_ref[0], branch[:half], branch[half:], theirs_ref, mine_ref)


def attend(place, after, za, qkv_bias, parts, width):
    tokens = za.shape[1]
    return pl.pallas_call(
        attend_kernel,
        in_specs=[SMEM, ANY, VMEM, VMEM] + [VMEM] * len(parts),
        out_specs=[VMEM] * 5,
        out_shape=(
            jax.ShapeDtypeStruct((D, 4 * width), LOW),
            jax.ShapeDtypeStruct((width // HEAD, 3, HEAD, tokens), LOW),
            jax.ShapeDtypeStruct((tokens, width), LOW),
            jax.ShapeDtypeStruct((tokens // 2, D), LOW),
            jax.ShapeDtypeStruct((tokens // 2, D), LOW),
        ),
        scratch_shapes=[part_scratch(parts)],
        compiler_params=BIG,
        name="attend",
    )(place, after, za, qkv_bias, *parts)


def own_tokens(place_ref, chunk, tokens):
    pick = lax.broadcasted_iota(jnp.int32, (chunk, tokens), 0) + place_ref[2] * chunk
    return (lax.broadcasted_iota(jnp.int32, (chunk, tokens), 1) == pick).astype(LOW)


def beside_kernel(n_row, place_ref, after_ref, order_ref, cot_ref, w_ref, x_ref, tokens_ref, mixed_ref, mine_ref):
    del after_ref
    group, width = cot_ref.shape[:2]
    n_col = group // n_row
    order = order_ref[...]
    cot = [cot_ref[row * n_col + core] for core in range(n_col) for row in range(n_row)]
    tokens_ref[...] = dot(jnp.concatenate(cot, axis=0), order, 0, 0).astype(LOW)
    mixed_ref[...] = dot(order, w_ref[:, : 3 * width], 1, 0).astype(LOW)
    pick = own_tokens(place_ref, mine_ref.shape[0], x_ref.shape[1])
    mine_ref[...] = dot(dot(pick, x_ref[...], 1, 1).astype(LOW), order, 1, 0)


def beside(place, after, order, cot_all, w_first, x_all, n_row, chunk):
    group, width, tokens = cot_all.shape
    return pl.pallas_call(
        partial(beside_kernel, n_row),
        in_specs=[SMEM, ANY] + [VMEM] * 4,
        out_specs=[VMEM] * 3,
        out_shape=(
            jax.ShapeDtypeStruct((tokens, D), LOW),
            jax.ShapeDtypeStruct((D, 3 * width), LOW),
            jax.ShapeDtypeStruct((chunk, D), jnp.float32),
        ),
        compiler_params=BIG,
        name="beside",
    )(place, after, order, cot_all, w_first, x_all)


def before_kernel(place_ref, near_ref, far_ref, order_ref, cot_ref, *refs):
    *parts, zb_ref, up_ref, grad_ref, mixed_ref, scratch = refs
    join_cores(place_ref[0], near_ref, far_ref, zb_ref)
    w_rest = assembled(place_ref[1], parts, scratch)
    wide = up_ref.shape[1]
    up_ref[...] = w_rest[:, :wide]
    w_down = w_rest[:, wide:]
    grad_ref[...] = dot(cot_ref[...], w_down, 1, 0)
    mixed_ref[...] = dot(order_ref[...], w_down, 1, 0).astype(LOW)


def before(place, near, far, order, cot_tokens, parts):
    wide = parts[0].shape[1] // 2
    return pl.pallas_call(
        before_kernel,
        in_specs=[SMEM] + [VMEM] * (4 + len(parts)),
        out_specs=[VMEM] * 4,
        out_shape=(
            jax.ShapeDtypeStruct((2,) + near.shape, LOW),
            jax.ShapeDtypeStruct((D, wide), LOW),
            jax.ShapeDtypeStruct((cot_tokens.shape[0], wide), jnp.float32),
            jax.ShapeDtypeStruct((D, wide), LOW),
        ),
        scratch_shapes=[part_scratch(parts)],
        compiler_params=BIG,
        name="before",
    )(place, near, far, order, cot_tokens, *parts)


def behind_kernel(
    place_ref, after_ref, zb_ref, hid_ref, cot_ref, act_ref, down_ref, mid_ref, grad_ref, theirs_ref, mine_ref
):
    del after_ref
    active = act_ref[...]
    up_grad = dot(zb_ref[...], hid_ref[...], 0, 0).astype(LOW)
    down_grad = dot(cot_ref[...], active, 0, 0).astype(LOW)
    grad_ref[...] = jnp.concatenate([up_grad, down_grad], axis=1).reshape(grad_ref.shape)
    pick = own_tokens(place_ref, mid_ref.shape[1], active.shape[0])
    result = dot(down_ref[...], active, 1, 1) + dot(mid_ref[...], pick, 1, 0)
    result = result.astype(LOW)
    half = D // 2
    split_cores(place_ref[0], result[:half], result[half:], theirs_ref, mine_ref)


def behind(place, after, zb, hidden_grad, cot_tokens, active, down_mixed, middle_mixed, n_dp):
    tokens, wide = active.shape
    return pl.pallas_call(
        behind_kernel,
        in_specs=[SMEM, ANY] + [VMEM] * 6,
        out_specs=[VMEM] * 3,
        out_shape=(
            jax.ShapeDtypeStruct((n_dp, D // n_dp, 2 * wide), LOW),
            jax.ShapeDtypeStruct((D // 2, tokens), LOW),
            jax.ShapeDtypeStruct((D // 2, tokens), LOW),
        ),
        compiler_params=BIG,
        name="behind",
    )(place, after, zb, hidden_grad, cot_tokens, active, down_mixed, middle_mixed)


def mlp_kernel(
    core_ref, zb_ref, up_ref, bias_ref, grad_ref, act_ref, hid_ref, theirs_ref, mine_ref, sum_ref
):
    step = pl.program_id(0)
    near = step >= pl.num_programs(0) // 2
    hidden = dot(zb_ref[...], up_ref[...], 1, 0) + bias_ref[...]
    square = hidden * hidden
    slope = 0.7978845608028654 * (1.0 + 0.044715 * square)
    bent = jnp.tanh(hidden * slope)
    gate = 0.5 * (1.0 + bent)
    act_ref[...] = (hidden * gate).astype(LOW)
    steep = gate + 0.5 * hidden * (1.0 - bent * bent) * (
        0.7978845608028654 * (1.0 + 3 * 0.044715 * square)
    )
    hidden_grad = (grad_ref[...] * steep).astype(LOW)
    hid_ref[...] = hidden_grad
    two_grad = dot(hidden_grad, up_ref[...], 1, 1).astype(LOW)

    @pl.when(near)
    def _():
        mine_ref[...] = two_grad

    @pl.when(jnp.logical_not(near))
    def _():
        theirs_ref[...] = two_grad

    @pl.when(step == 0)
    def _():
        sum_ref[...] = jnp.zeros(sum_ref.shape, jnp.float32)

    sum_ref[...] += jnp.sum(hidden_grad.astype(jnp.float32), axis=0, keepdims=True)


def mlp(core, zb, w_up, up_bias, active_grad):
    tokens = zb.shape[0]
    wide = w_up.shape[1]
    steps = 6
    block = tokens // steps
    turned = lambda i, c: ((i + (steps // 2) * (1 - c[0])) % steps, 0)
    whole = lambda i, c: (0, 0)
    return pl.pallas_call(
        mlp_kernel,
        grid_spec=pltpu.PrefetchScalarGridSpec(
            num_scalar_prefetch=1,
            grid=(steps,),
            in_specs=[
                pl.BlockSpec((block, D), turned),
                pl.BlockSpec((D, wide), whole),
                pl.BlockSpec((1, wide), whole),
                pl.BlockSpec((block, wide), turned),
            ],
            out_specs=[
                pl.BlockSpec((block, wide), turned),
                pl.BlockSpec((block, wide), turned),
                pl.BlockSpec((block, D), lambda i, c: (jnp.minimum(i, steps // 2 - 1), 0)),
                pl.BlockSpec((block, D), lambda i, c: (jnp.maximum(i - steps // 2, 0), 0)),
                pl.BlockSpec((1, wide), whole),
            ],
        ),
        out_shape=(
            jax.ShapeDtypeStruct((tokens, wide), LOW),
            jax.ShapeDtypeStruct((tokens, wide), LOW),
            jax.ShapeDtypeStruct((tokens // 2, D), LOW),
            jax.ShapeDtypeStruct((tokens // 2, D), LOW),
            jax.ShapeDtypeStruct((1, wide), jnp.float32),
        ),
        compiler_params=BIG,
        name="mlp",
    )(core, zb, w_up, up_bias, active_grad)


def back_kernel(
    place_ref, after_ref, near_ref, far_ref, w_ref, qkv_ref, za_ref, att_ref, all_ref, grad_ref, sum_ref, wg_ref
):
    del after_ref
    join_cores(place_ref[0], near_ref, far_ref, all_ref)
    branch_all = all_ref[...].reshape(att_ref.shape[0], D)
    heads = qkv_ref.shape[0]
    attended_grad = dot(branch_all, w_ref[:, heads * 3 * HEAD :], 1, 0).T
    scale = HEAD ** (-0.5)
    parts = []
    for head in range(heads):
        queries, key_rows, values = qkv_ref[head, 0], qkv_ref[head, 1], qkv_ref[head, 2]
        grad = attended_grad[head * HEAD : (head + 1) * HEAD].astype(LOW)
        probs = head_probs(queries, key_rows)
        probs_grad = dot(grad, values, 0, 0)
        inner = jnp.sum(probs * probs_grad, axis=1, keepdims=True)
        scores_grad = (probs * (probs_grad - inner)).astype(LOW)
        parts.append(dot(key_rows, scores_grad, 1, 1) * scale)
        parts.append(dot(queries, scores_grad, 1, 0) * scale)
        parts.append(dot(grad, probs.astype(LOW), 1, 0))
    qkv_grad = jnp.concatenate(parts, axis=0).astype(LOW)
    grad_ref[...] = qkv_grad
    sum_ref[...] = jnp.sum(qkv_grad.astype(jnp.float32), axis=1, keepdims=True)
    qkv_part = dot(za_ref[...], qkv_grad, 1, 1).astype(LOW)
    out_part = dot(branch_all, att_ref[...], 0, 0).astype(LOW)
    wg_ref[...] = jnp.concatenate([qkv_part, out_part], axis=1).reshape(wg_ref.shape)


def attend_back(place, after, near, far, w_first, qkv, za, attended, n_dp):
    tokens, width = attended.shape
    return pl.pallas_call(
        back_kernel,
        in_specs=[SMEM, ANY] + [VMEM] * 6,
        out_specs=[VMEM] * 4,
        out_shape=(
            jax.ShapeDtypeStruct((2,) + near.shape, LOW),
            jax.ShapeDtypeStruct((3 * width, tokens), LOW),
            jax.ShapeDtypeStruct((3 * width, 1), jnp.float32),
            jax.ShapeDtypeStruct((n_dp, D // n_dp, 4 * width), LOW),
        ),
        compiler_params=BIG,
        name="attend_back",
    )(place, after, near, far, w_first, qkv, za, attended)


def first_kernel(core_ref, w_ref, grad_ref, x_ref, mean_ref, inv_ref, gain_ref, theirs_ref, mine_ref, sum_ref):
    n_row, rows, tokens = theirs_ref.shape
    width = rows - 16
    first = jnp.zeros((1, tokens), jnp.float32)
    second = jnp.zeros((1, tokens), jnp.float32)
    blocks = []
    for slot in range(D // width):
        here = slice(slot * width, (slot + 1) * width)
        part = dot(w_ref[here], grad_ref[...], 1, 0)
        normed = (x_ref[here].astype(jnp.float32) - mean_ref[...]) * inv_ref[...]
        product = part * normed
        sum_ref[here, 0:1] = jnp.sum(product, axis=1, keepdims=True)
        sum_ref[here, 1:2] = jnp.sum(part, axis=1, keepdims=True)
        first += jnp.sum(part * gain_ref[here], axis=0, keepdims=True)
        second += jnp.sum(product * gain_ref[here], axis=0, keepdims=True)
        blocks.append(part.astype(LOW))
    line = lax.broadcasted_iota(jnp.int32, (16, tokens), 0)
    sums = jnp.where(line == 0, first, jnp.where(line == 1, second, 0.0)).astype(LOW)
    for near, ref in ((False, theirs_ref), (True, mine_ref)):
        for core in range(2):

            @pl.when((core_ref[0] == core) == near)
            def _(core=core, ref=ref):
                for row in range(n_row):
                    ref[row, :width] = blocks[core * n_row + row]
                    ref[row, width:] = sums


def first_back(core, w_mixed, qkv_grad, x_all, x_mean, inverse, gain, width, n_row):
    tokens = x_all.shape[1]
    return pl.pallas_call(
        first_kernel,
        in_specs=[SMEM] + [VMEM] * 6,
        out_specs=[VMEM] * 3,
        out_shape=(
            jax.ShapeDtypeStruct((n_row, width + 16, tokens), LOW),
            jax.ShapeDtypeStruct((n_row, width + 16, tokens), LOW),
            jax.ShapeDtypeStruct((D, 2), jnp.float32),
        ),
        compiler_params=BIG,
        name="first_back",
    )(core, w_mixed, qkv_grad, x_all, x_mean, inverse, gain)


def adam_update(weights, moment_one, second, gradient, step_rate, weight_decay):
    moment_one = BETA_ONE * moment_one + (1.0 - BETA_ONE) * gradient
    second = BETA_TWO * second + (1.0 - BETA_TWO) * gradient * gradient
    direction = (
        moment_one / (1.0 - BETA_ONE**STEP) / (jnp.sqrt(second / (1.0 - BETA_TWO**STEP)) + ADAM_EPS)
    )
    return (weights - step_rate * (direction + weight_decay * weights), moment_one, second)


def shards(
    inputs,
    cotangent,
    qkv_master,
    out_master,
    up_master,
    down_master,
    qkv_first,
    out_first,
    up_first,
    down_first,
    qkv_second,
    out_second,
    up_second,
    down_second,
    norm_gains,
    gain_first,
    gain_second,
    biases,
    bias_first,
    bias_second,
):
    tokens, width = inputs.shape
    n_row = lax.axis_size("row")
    n_col = lax.axis_size("col")
    n_dp = lax.axis_size("dp")
    row = lax.axis_index("row")
    core = lax.axis_index("col")
    group = n_row * n_col
    heads = width // HEAD
    hidden_width = FF // group
    own = core * n_row + row
    place = jnp.stack([core, lax.axis_index("dp"), own]).astype(jnp.int32)
    chunk = -(-tokens // (group * 16)) * 16
    padded = chunk * group
    shard_rows = qkv_master.shape[0]

    index = jnp.arange(D)
    feature = (
        ((index // width) % n_row) * n_col + index // (width * n_row)
    ) * width + index % width
    index = (feature % n_dp) * (D // n_dp) + feature // n_dp
    order = (lax.broadcasted_iota(jnp.int32, (D, D), 1) == index[:, None]).astype(LOW)
    order = lax.optimization_barrier(order)

    def mixed(vector):
        return vector.reshape(n_row, n_col, width).transpose(1, 0, 2).reshape(D)

    def dealt(vector):
        return vector.reshape(D // n_dp, n_dp).T.reshape(D)

    def returned(rows):
        return exchange_rows(rows.reshape(n_row, shard_rows, -1))

    def long(array):
        return jnp.pad(array, ((0, 0), (0, padded - tokens)))

    flat = lambda array: array.transpose(1, 2, 0)
    tall = lambda array: array.transpose(2, 0, 1)
    first_rows = prepare(place, qkv_master, flat(out_master), n_row)
    first_rows = exchange_rows(first_rows).reshape(D // n_dp, -1)
    x_own = long(inputs.T)
    x_after = x_own + zero_of(first_rows).astype(LOW)
    x_rows = lax.all_gather(x_after, "row", axis=0, tiled=True)
    first_parts = gather_parts(first_rows, "dp")
    rest = prepare(x_rows, up_master, flat(down_master), n_row)
    rest = exchange_rows(rest).reshape(D // n_dp, -1)
    rest_parts = gather_parts(rest, "dp")
    x_all = both_cores(x_rows)
    cot_own = long(cotangent.T) + zero_of(rest).astype(LOW)
    cot_all = lax.all_gather(cot_own, ("row", "col"), axis=0)

    gain_one = mixed(norm_gains[0])
    gain_two = dealt(norm_gains[1])
    shift_one = mixed(biases[:D])
    shift_two = dealt(biases[D : 2 * D])
    query_bias = lax.dynamic_slice_in_dim(biases, 2 * D + own * width, width).reshape(heads, HEAD)
    value_bias = lax.dynamic_slice_in_dim(biases, 3 * D + own * width, width).reshape(heads, HEAD)
    out_bias = dealt(biases[4 * D : 5 * D])
    feature_start = (row * n_col + core) * width
    down_bias = lax.dynamic_slice_in_dim(biases, 5 * D + feature_start, width)
    up_bias = lax.dynamic_slice_in_dim(biases, 6 * D + own * hidden_width, hidden_width)
    qkv_bias = jnp.stack([query_bias, jnp.zeros_like(query_bias), value_bias], axis=1).reshape(
        3 * width, 1
    )

    x_full = x_all.astype(jnp.float32)
    x_mean = jnp.sum(x_full, axis=0, keepdims=True) / D
    center = x_full - x_mean
    inverse_one = lax.rsqrt(jnp.sum(center * center, axis=0, keepdims=True) / D + NORM_EPS)
    za = (center * inverse_one * gain_one[:, None] + shift_one[:, None]).astype(LOW)
    za = dot(order, za, 0, 0, LOW)

    w_first, qkv, attended, theirs, mine = attend(place, rest, za, qkv_bias, first_parts, width)
    pair = (mine.astype(jnp.float32) + swap_cores(theirs).astype(jnp.float32)).astype(LOW)
    branch = sum_over_rows(pair)
    cot_tokens, qkv_mixed, x_mine = beside(
        place, pair, order, cot_all, w_first, x_all, n_row, chunk
    )
    cot_mine = take(cot_tokens, own, chunk).astype(jnp.float32)

    flown = sum(zero_of(part) for part in rest_parts[1:]) if len(rest_parts) > 1 else 0.0
    middle = x_mine + branch + (out_bias + flown)[None, :]
    center = middle - jnp.sum(middle, axis=1, keepdims=True) / D
    inverse_two = lax.rsqrt(jnp.sum(center * center, axis=1, keepdims=True) / D + NORM_EPS)
    normed_two = center * inverse_two
    zb = (normed_two * gain_two + shift_two).astype(LOW)
    zb_rows = lax.all_gather(zb, "row", axis=0, tiled=True)
    zb, w_up, active_grad, down_mixed = before(
        place, zb_rows, swap_cores(zb_rows), order, cot_tokens, rest_parts
    )
    zb = zb.reshape(padded, D)

    core_of = core.reshape(1).astype(jnp.int32)
    active, hidden_grad, theirs, mine, up_sums = mlp(
        core_of, zb, w_up, up_bias[None, :], active_grad
    )
    pair = (mine.astype(jnp.float32) + swap_cores(theirs).astype(jnp.float32)).astype(LOW)
    two_grad = sum_over_rows(pair)

    middle_mixed = dot(order, middle.astype(LOW), 1, 1, LOW)
    rest_grad, theirs, mine = behind(
        place, pair, zb, hidden_grad, cot_tokens, active, down_mixed, middle_mixed, n_dp
    )
    result = mine.astype(jnp.float32) + swap_cores(theirs).astype(jnp.float32)

    scaled = two_grad * gain_two
    first_sum = jnp.sum(scaled, axis=1, keepdims=True) / D
    second_sum = jnp.sum(scaled * normed_two, axis=1, keepdims=True) / D
    middle_grad = cot_mine + inverse_two * (scaled - first_sum - normed_two * second_sum)
    middle_grad = middle_grad.astype(LOW)
    branch_rows = lax.all_gather(middle_grad, "row", axis=0, tiled=True)
    rest_rows = sum_blocks(rest_grad, "dp", zero_of(branch_rows))
    rest_blocks = returned(rest_rows)
    branch_all, qkv_grad, bias_sums, first_grad = attend_back(
        place, branch_rows, branch_rows, swap_cores(branch_rows), w_first, qkv, za, attended, n_dp
    )
    branch_all = branch_all.reshape(padded, D)
    theirs, mine, one_sums = first_back(
        core_of, qkv_mixed, qkv_grad, x_all, x_mean, inverse_one, gain_one[:, None], width, n_row
    )
    pair = (mine.astype(jnp.float32) + swap_cores(theirs).astype(jnp.float32)).astype(LOW)
    one_grad = sum_over_rows(pair.reshape(-1, padded))
    later = zero_of(one_grad)
    result = sum_over_rows(result + later) + down_bias[:, None]
    result = result.astype(LOW)[:, :tokens].T
    first_rows = sum_blocks(first_grad, "dp", 0.0)

    own_gain = lax.dynamic_slice_in_dim(norm_gains[0], feature_start, width)[:, None]
    own_normed = (x_own.astype(jnp.float32) - x_mean) * inverse_one
    own_order = lax.dynamic_slice_in_dim(order, own * width, width, axis=0)
    own_middle = dot(own_order, branch_all, 1, 1)
    input_grad = own_middle + inverse_one * (
        one_grad[:width] * own_gain
        - one_grad[width : width + 1] / D
        - own_normed * (one_grad[width + 1 : width + 2] / D)
    )
    input_grad = input_grad.astype(LOW)[:, :tokens].T

    bias_sums = bias_sums.reshape(heads, 3, HEAD)
    all_rows = jnp.stack(
        [
            one_sums[:, 0],
            one_sums[:, 1],
            jnp.sum(two_grad * normed_two, axis=0),
            jnp.sum(two_grad, axis=0),
            jnp.sum(middle_grad, axis=0, dtype=jnp.float32),
            jnp.sum(cot_mine, axis=0),
        ]
    )
    own_row = jnp.concatenate(
        [bias_sums[:, 0].reshape(width), bias_sums[:, 2].reshape(width), up_sums[0]]
    )
    own_row = jnp.pad(own_row, (0, D - own_row.shape[0]))
    own_rows = jnp.where(jnp.arange(group)[:, None] == own, own_row[None, :], 0.0)
    total = all_sum(jnp.concatenate([jnp.pad(all_rows, ((0, 2), (0, 0))), own_rows]) + later)
    one_rows = total[:2].reshape(2, n_col, n_row, width).transpose(0, 2, 1, 3).reshape(2, D)
    two_rows = total[2:6].reshape(4, n_dp, D // n_dp).transpose(0, 2, 1).reshape(4, D)
    own_rows = total[8:]
    gain_total = jnp.stack([one_rows[0], two_rows[0]])
    bias_total = jnp.concatenate(
        [
            one_rows[1],
            two_rows[1],
            own_rows[:, :width].reshape(D),
            own_rows[:, width : 2 * width].reshape(D),
            two_rows[2],
            two_rows[3],
            own_rows[:, 2 * width : 2 * width + hidden_width].reshape(FF),
        ]
    )

    rest_new = adam(
        pair,
        rest_blocks,
        (0.03, 0.02),
        up_master,
        up_first,
        up_second,
        flat(down_master),
        flat(down_first),
        flat(down_second),
    )
    first_new = adam(
        pair,
        returned(first_rows),
        (0.03, 0.12),
        qkv_master,
        qkv_first,
        qkv_second,
        flat(out_master),
        flat(out_first),
        flat(out_second),
    )
    g_new = adam_update(norm_gains, gain_first, gain_second, gain_total, 0.5, 0.0)
    b_new = adam_update(biases, bias_first, bias_second, bias_total, 0.5, 0.0)
    return (
        result,
        input_grad,
        *first_new[:3],
        *(tall(array) for array in first_new[3:]),
        *rest_new[:3],
        *(tall(array) for array in rest_new[3:]),
        *g_new,
        *b_new,
    )


def solution(mesh):
    token_spec = P("dp", ("row", "col"))
    wide = P("row", "dp", "col")
    tall = P("col", "row", "dp")
    return jax.shard_map(
        shards,
        mesh=mesh,
        in_specs=(token_spec,) * 2 + (wide, tall, wide, tall) * 3 + (P(),) * 6,
        out_specs=(token_spec,) * 2
        + (wide,) * 3
        + (tall,) * 3
        + (wide,) * 3
        + (tall,) * 3
        + (P(),) * 6,
        check_vma=False,
    )
```

```python
from functools import partial

import jax
import jax.numpy as jnp
from jax import lax
from jax.experimental import pallas as pl
from jax.experimental.pallas import tpu as pltpu
from jax.sharding import PartitionSpec as P

D = 1152
FF = 4304
HEAD = 72
SEQ = 729
STEP = 10

NORM_EPS = 1e-06
ADAM_EPS = 1e-08
BETA_ONE = 0.9
BETA_TWO = 0.999
LOW = jnp.bfloat16


def dot(left, right, left_dim, right_dim, out=jnp.float32, precision=None):
    return lax.dot_general(
        left,
        right,
        (((left_dim,), (right_dim,)), ((), ())),
        precision=precision,
        preferred_element_type=out,
    )


def take(array, index, size):
    return lax.dynamic_slice_in_dim(array, index * size, size, axis=0)


def swap_cores(array):
    n_col = lax.axis_size("col")
    return lax.ppermute(array, "col", [(i, (i + 1) % n_col) for i in range(n_col)])


def both_cores(rows):
    pieces = [
        lax.all_gather(piece, "col", axis=0) for piece in jnp.split(rows, 2, axis=0)
    ]
    return jnp.concatenate(pieces, axis=1).reshape(-1, rows.shape[1])


def gather_parts(block, axis):
    size = lax.axis_size(axis)
    if size > 4:
        copies = jnp.broadcast_to(block, (size,) + block.shape)
        return [lax.all_to_all(copies, axis, 0, 0).reshape(-1, block.shape[1])]
    return [block] + [
        lax.ppermute(block, axis, [(i, i ^ step) for i in range(size)]) for step in range(1, size)
    ]


def zero_of(array):
    first = lax.slice(array, (0,) * array.ndim, (1,) * array.ndim)
    return first.reshape(()).astype(jnp.float32) * 0.0


def exchange_rows(blocks):
    return lax.all_to_all(blocks, "row", 0, 0)


def sum_blocks(blocks, axis, later):
    blocks = lax.all_to_all(blocks, axis, 0, 0)
    return jnp.sum(blocks.astype(jnp.float32) + later, axis=0).astype(LOW)


def sum_over_rows(half):
    summed = lax.psum_scatter(half.astype(LOW), "row", scatter_dimension=0, tiled=True)
    return summed.astype(jnp.float32)


def all_sum(vector):
    for axis in ("col", "row", "dp"):
        size = lax.axis_size(axis)
        if size & (size - 1) or size > 4:
            vector = lax.psum(vector, axis)
            continue
        step = 1
        while step < size:
            vector = vector + lax.ppermute(vector, axis, [(i, i ^ step) for i in range(size)])
            step *= 2
    return vector


VMEM = pl.BlockSpec(memory_space=pltpu.VMEM)
SMEM = pl.BlockSpec(memory_space=pltpu.SMEM)
ANY = pl.BlockSpec(memory_space=pl.ANY)
BIG = pltpu.CompilerParams(vmem_limit_bytes=56 * 1024 * 1024)


def prepare_kernel(parts, after_ref, wide_ref, tall_ref, out_ref):
    del after_ref
    arrays = [ref[:, 0, :].astype(LOW) for ref in (wide_ref, tall_ref)]
    for part in range(parts):
        pieces = []
        for array in arrays:
            size = array.shape[1] // parts
            pieces.append(array[:, part * size : (part + 1) * size])
        out_ref[part] = jnp.concatenate(pieces, axis=1)


def prepare(after, wide, tall, parts):
    rows = wide.shape[0]
    size = (wide.shape[2] + tall.shape[2]) // parts
    return pl.pallas_call(
        partial(prepare_kernel, parts),
        in_specs=[ANY, VMEM, VMEM],
        out_specs=VMEM,
        out_shape=jax.ShapeDtypeStruct((parts, rows, size), LOW),
        compiler_params=BIG,
        name="prepare",
    )(after, wide, tall)


def adam_kernel(rates, after_ref, blocks_ref, *refs):
    del after_ref
    parts = blocks_ref.shape[0]
    start = 0
    for index, rate in enumerate(rates):
        weight, first, second = refs[3 * index : 3 * index + 3]
        size = weight.shape[2] // parts
        gradient = jnp.concatenate(
            [blocks_ref[part, :, start : start + size] for part in range(parts)], axis=1
        ).astype(jnp.float32)
        start += size
        new = adam_update(weight[:, 0, :], first[:, 0, :], second[:, 0, :], gradient, rate, 0.1)
        for array, ref in zip(new, refs[3 * len(rates) + 3 * index :]):
            ref[:, 0, :] = array


def adam(after, blocks, rates, *arrays):
    return pl.pallas_call(
        partial(adam_kernel, rates),
        in_specs=[ANY] + [VMEM] * (1 + len(arrays)),
        out_specs=[VMEM] * len(arrays),
        out_shape=[jax.ShapeDtypeStruct(a.shape, jnp.float32) for a in arrays],
        compiler_params=BIG,
        name="adam",
    )(after, blocks, *arrays)


def assembled(place, parts, scratch):
    if len(parts) == 1:
        return parts[0][...]
    for step, part in enumerate(parts):
        scratch[place ^ step] = part[...]
    return scratch[...].reshape(-1, scratch.shape[2])


def part_scratch(parts):
    return pltpu.VMEM((len(parts),) + parts[0].shape, LOW)


def head_probs(queries, key_rows):
    scores = dot(queries, key_rows, 0, 0) * HEAD ** (-0.5)
    scores = jnp.where(lax.broadcasted_iota(jnp.int32, scores.shape, 1) < SEQ, scores, -1e30)
    exponent = jnp.exp(scores - jnp.max(scores, axis=1, keepdims=True))
    return exponent * (1.0 / jnp.sum(exponent, axis=1, keepdims=True))


def split_cores(core, first, second, theirs_ref, mine_ref):
    @pl.when(core == 0)
    def _():
        mine_ref[...] = first
        theirs_ref[...] = second

    @pl.when(core != 0)
    def _():
        mine_ref[...] = second
        theirs_ref[...] = first


def attend_kernel(place_ref, after_ref, za_ref, bias_ref, *refs):
    del after_ref
    *parts, w_ref, qkv_ref, att_ref, theirs_ref, mine_ref, scratch = refs
    w_ref[...] = assembled(place_ref[1], parts, scratch)
    heads = qkv_ref.shape[0]
    split = heads * 3 * HEAD
    qkv = dot(w_ref[:, :split], za_ref[...], 0, 0) + bias_ref[...]
    outs = []
    for head in range(heads):
        for t in range(3):
            start = (head * 3 + t) * HEAD
            qkv_ref[head, t] = qkv[start : start + HEAD].astype(LOW)
        probs = head_probs(qkv_ref[head, 0], qkv_ref[head, 1]).astype(LOW)
        outs.append(dot(qkv_ref[head, 2], probs, 1, 1))
    attended = jnp.concatenate(outs, axis=0).T.astype(LOW)
    att_ref[...] = attended
    branch = dot(attended, w_ref[:, split:], 1, 1).astype(LOW)
    half = branch.shape[0] // 2
    split_cores(place_ref[0], branch[:half], branch[half:], theirs_ref, mine_ref)


def attend(place, after, za, qkv_bias, parts, width):
    tokens = za.shape[1]
    return pl.pallas_call(
        attend_kernel,
        in_specs=[SMEM, ANY, VMEM, VMEM] + [VMEM] * len(parts),
        out_specs=[VMEM] * 5,
        out_shape=(
            jax.ShapeDtypeStruct((D, 4 * width), LOW),
            jax.ShapeDtypeStruct((width // HEAD, 3, HEAD, tokens), LOW),
            jax.ShapeDtypeStruct((tokens, width), LOW),
            jax.ShapeDtypeStruct((tokens // 2, D), LOW),
            jax.ShapeDtypeStruct((tokens // 2, D), LOW),
        ),
        scratch_shapes=[part_scratch(parts)],
        compiler_params=BIG,
        name="attend",
    )(place, after, za, qkv_bias, *parts)


def own_tokens(place_ref, chunk, tokens):
    pick = lax.broadcasted_iota(jnp.int32, (chunk, tokens), 0) + place_ref[2] * chunk
    return (lax.broadcasted_iota(jnp.int32, (chunk, tokens), 1) == pick).astype(LOW)


def beside_kernel(n_row, place_ref, after_ref, order_ref, cot_ref, w_ref, x_ref, tokens_ref, mixed_ref, mine_ref):
    del after_ref
    group, width = cot_ref.shape[:2]
    n_col = group // n_row
    order = order_ref[...]
    cot = [cot_ref[row * n_col + core] for core in range(n_col) for row in range(n_row)]
    tokens_ref[...] = dot(jnp.concatenate(cot, axis=0), order, 0, 0).astype(LOW)
    mixed_ref[...] = dot(order, w_ref[:, : 3 * width], 1, 0).astype(LOW)
    pick = own_tokens(place_ref, mine_ref.shape[0], x_ref.shape[1])
    mine_ref[...] = dot(dot(pick, x_ref[...], 1, 1).astype(LOW), order, 1, 0)


def beside(place, after, order, cot_all, w_first, x_all, n_row, chunk):
    group, width, tokens = cot_all.shape
    return pl.pallas_call(
        partial(beside_kernel, n_row),
        in_specs=[SMEM, ANY] + [VMEM] * 4,
        out_specs=[VMEM] * 3,
        out_shape=(
            jax.ShapeDtypeStruct((tokens, D), LOW),
            jax.ShapeDtypeStruct((D, 3 * width), LOW),
            jax.ShapeDtypeStruct((chunk, D), jnp.float32),
        ),
        compiler_params=BIG,
        name="beside",
    )(place, after, order, cot_all, w_first, x_all)


def before_kernel(place_ref, after_ref, order_ref, cot_ref, *refs):
    del after_ref
    *parts, up_ref, grad_ref, mixed_ref, scratch = refs
    w_rest = assembled(place_ref[1], parts, scratch)
    wide = up_ref.shape[1]
    up_ref[...] = w_rest[:, :wide]
    w_down = w_rest[:, wide:]
    grad_ref[...] = dot(cot_ref[...], w_down, 1, 0)
    mixed_ref[...] = dot(order_ref[...], w_down, 1, 0).astype(LOW)


def before(place, after, order, cot_tokens, parts):
    wide = parts[0].shape[1] // 2
    return pl.pallas_call(
        before_kernel,
        in_specs=[SMEM, ANY, VMEM, VMEM] + [VMEM] * len(parts),
        out_specs=[VMEM] * 3,
        out_shape=(
            jax.ShapeDtypeStruct((D, wide), LOW),
            jax.ShapeDtypeStruct((cot_tokens.shape[0], wide), jnp.float32),
            jax.ShapeDtypeStruct((D, wide), LOW),
        ),
        scratch_shapes=[part_scratch(parts)],
        compiler_params=BIG,
        name="before",
    )(place, after, order, cot_tokens, *parts)


def behind_kernel(
    place_ref, after_ref, zb_ref, hid_ref, cot_ref, act_ref, down_ref, mid_ref, grad_ref, theirs_ref, mine_ref
):
    del after_ref
    active = act_ref[...]
    up_grad = dot(zb_ref[...], hid_ref[...], 0, 0).astype(LOW)
    down_grad = dot(cot_ref[...], active, 0, 0).astype(LOW)
    grad_ref[...] = jnp.concatenate([up_grad, down_grad], axis=1).reshape(grad_ref.shape)
    pick = own_tokens(place_ref, mid_ref.shape[1], active.shape[0])
    result = dot(down_ref[...], active, 1, 1) + dot(mid_ref[...], pick, 1, 0)
    result = result.astype(LOW)
    half = D // 2
    split_cores(place_ref[0], result[:half], result[half:], theirs_ref, mine_ref)


def behind(place, after, zb, hidden_grad, cot_tokens, active, down_mixed, middle_mixed, n_dp):
    tokens, wide = active.shape
    return pl.pallas_call(
        behind_kernel,
        in_specs=[SMEM, ANY] + [VMEM] * 6,
        out_specs=[VMEM] * 3,
        out_shape=(
            jax.ShapeDtypeStruct((n_dp, D // n_dp, 2 * wide), LOW),
            jax.ShapeDtypeStruct((D // 2, tokens), LOW),
            jax.ShapeDtypeStruct((D // 2, tokens), LOW),
        ),
        compiler_params=BIG,
        name="behind",
    )(place, after, zb, hidden_grad, cot_tokens, active, down_mixed, middle_mixed)


def mlp_kernel(
    core_ref, zb_ref, up_ref, bias_ref, grad_ref, act_ref, hid_ref, theirs_ref, mine_ref, sum_ref
):
    step = pl.program_id(0)
    near = step >= pl.num_programs(0) // 2
    hidden = dot(zb_ref[...], up_ref[...], 1, 0) + bias_ref[...]
    square = hidden * hidden
    slope = 0.7978845608028654 * (1.0 + 0.044715 * square)
    bent = jnp.tanh(hidden * slope)
    gate = 0.5 * (1.0 + bent)
    act_ref[...] = (hidden * gate).astype(LOW)
    steep = gate + 0.5 * hidden * (1.0 - bent * bent) * (
        0.7978845608028654 * (1.0 + 3 * 0.044715 * square)
    )
    hidden_grad = (grad_ref[...] * steep).astype(LOW)
    hid_ref[...] = hidden_grad
    two_grad = dot(hidden_grad, up_ref[...], 1, 1).astype(LOW)

    @pl.when(near)
    def _():
        mine_ref[...] = two_grad

    @pl.when(jnp.logical_not(near))
    def _():
        theirs_ref[...] = two_grad

    @pl.when(step == 0)
    def _():
        sum_ref[...] = jnp.zeros(sum_ref.shape, jnp.float32)

    sum_ref[...] += jnp.sum(hidden_grad.astype(jnp.float32), axis=0, keepdims=True)


def mlp(core, zb, w_up, up_bias, active_grad):
    tokens = zb.shape[0]
    wide = w_up.shape[1]
    steps = 6
    block = tokens // steps
    turned = lambda i, c: ((i + (steps // 2) * (1 - c[0])) % steps, 0)
    whole = lambda i, c: (0, 0)
    return pl.pallas_call(
        mlp_kernel,
        grid_spec=pltpu.PrefetchScalarGridSpec(
            num_scalar_prefetch=1,
            grid=(steps,),
            in_specs=[
                pl.BlockSpec((block, D), turned),
                pl.BlockSpec((D, wide), whole),
                pl.BlockSpec((1, wide), whole),
                pl.BlockSpec((block, wide), turned),
            ],
            out_specs=[
                pl.BlockSpec((block, wide), turned),
                pl.BlockSpec((block, wide), turned),
                pl.BlockSpec((block, D), lambda i, c: (jnp.minimum(i, steps // 2 - 1), 0)),
                pl.BlockSpec((block, D), lambda i, c: (jnp.maximum(i - steps // 2, 0), 0)),
                pl.BlockSpec((1, wide), whole),
            ],
        ),
        out_shape=(
            jax.ShapeDtypeStruct((tokens, wide), LOW),
            jax.ShapeDtypeStruct((tokens, wide), LOW),
            jax.ShapeDtypeStruct((tokens // 2, D), LOW),
            jax.ShapeDtypeStruct((tokens // 2, D), LOW),
            jax.ShapeDtypeStruct((1, wide), jnp.float32),
        ),
        compiler_params=BIG,
        name="mlp",
    )(core, zb, w_up, up_bias, active_grad)


def back_kernel(bg_ref, w_ref, qkv_ref, za_ref, att_ref, grad_ref, sum_ref, wg_ref):
    heads = qkv_ref.shape[0]
    attended_grad = dot(bg_ref[...], w_ref[:, heads * 3 * HEAD :], 1, 0).T
    scale = HEAD ** (-0.5)
    parts = []
    for head in range(heads):
        queries, key_rows, values = qkv_ref[head, 0], qkv_ref[head, 1], qkv_ref[head, 2]
        grad = attended_grad[head * HEAD : (head + 1) * HEAD].astype(LOW)
        probs = head_probs(queries, key_rows)
        probs_grad = dot(grad, values, 0, 0)
        inner = jnp.sum(probs * probs_grad, axis=1, keepdims=True)
        scores_grad = (probs * (probs_grad - inner)).astype(LOW)
        parts.append(dot(key_rows, scores_grad, 1, 1) * scale)
        parts.append(dot(queries, scores_grad, 1, 0) * scale)
        parts.append(dot(grad, probs.astype(LOW), 1, 0))
    qkv_grad = jnp.concatenate(parts, axis=0).astype(LOW)
    grad_ref[...] = qkv_grad
    sum_ref[...] = jnp.sum(qkv_grad.astype(jnp.float32), axis=1, keepdims=True)
    qkv_part = dot(za_ref[...], qkv_grad, 1, 1).astype(LOW)
    out_part = dot(bg_ref[...], att_ref[...], 0, 0).astype(LOW)
    wg_ref[...] = jnp.concatenate([qkv_part, out_part], axis=1).reshape(wg_ref.shape)


def attend_back(branch_all, w_first, qkv, za, attended, n_dp):
    tokens, width = attended.shape
    return pl.pallas_call(
        back_kernel,
        in_specs=[VMEM] * 5,
        out_specs=[VMEM] * 3,
        out_shape=(
            jax.ShapeDtypeStruct((3 * width, tokens), LOW),
            jax.ShapeDtypeStruct((3 * width, 1), jnp.float32),
            jax.ShapeDtypeStruct((n_dp, D // n_dp, 4 * width), LOW),
        ),
        compiler_params=BIG,
        name="attend_back",
    )(branch_all, w_first, qkv, za, attended)


def first_kernel(
    core_ref, w_ref, grad_ref, x_ref, mean_ref, inv_ref, gain_ref, far_ref, near_ref, theirs_ref, mine_ref, sum_ref
):
    n_row, width, tokens = far_ref.shape
    theirs_ref[:, width + 16 :] = far_ref[...]
    mine_ref[:, width + 16 :] = near_ref[...]
    first = jnp.zeros((1, tokens), jnp.float32)
    second = jnp.zeros((1, tokens), jnp.float32)
    blocks = []
    for slot in range(D // width):
        here = slice(slot * width, (slot + 1) * width)
        part = dot(w_ref[here], grad_ref[...], 1, 0)
        normed = (x_ref[here].astype(jnp.float32) - mean_ref[...]) * inv_ref[...]
        product = part * normed
        sum_ref[here, 0:1] = jnp.sum(product, axis=1, keepdims=True)
        sum_ref[here, 1:2] = jnp.sum(part, axis=1, keepdims=True)
        first += jnp.sum(part * gain_ref[here], axis=0, keepdims=True)
        second += jnp.sum(product * gain_ref[here], axis=0, keepdims=True)
        blocks.append(part.astype(LOW))
    line = lax.broadcasted_iota(jnp.int32, (16, tokens), 0)
    sums = jnp.where(line == 0, first, jnp.where(line == 1, second, 0.0)).astype(LOW)
    for near, ref in ((False, theirs_ref), (True, mine_ref)):
        for core in range(2):

            @pl.when((core_ref[0] == core) == near)
            def _(core=core, ref=ref):
                for row in range(n_row):
                    ref[row, :width] = blocks[core * n_row + row]
                    ref[row, width : width + 16] = sums


def first_back(core, w_mixed, qkv_grad, x_all, x_mean, inverse, gain, far, near):
    n_row, width, tokens = far.shape
    return pl.pallas_call(
        first_kernel,
        in_specs=[SMEM] + [VMEM] * 8,
        out_specs=[VMEM] * 3,
        out_shape=(
            jax.ShapeDtypeStruct((n_row, 2 * width + 16, tokens), LOW),
            jax.ShapeDtypeStruct((n_row, 2 * width + 16, tokens), LOW),
            jax.ShapeDtypeStruct((D, 2), jnp.float32),
        ),
        compiler_params=BIG,
        name="first_back",
    )(core, w_mixed, qkv_grad, x_all, x_mean, inverse, gain, far, near)


def adam_update(weights, moment_one, second, gradient, step_rate, weight_decay):
    moment_one = BETA_ONE * moment_one + (1.0 - BETA_ONE) * gradient
    second = BETA_TWO * second + (1.0 - BETA_TWO) * gradient * gradient
    direction = (
        moment_one / (1.0 - BETA_ONE**STEP) / (jnp.sqrt(second / (1.0 - BETA_TWO**STEP)) + ADAM_EPS)
    )
    return (weights - step_rate * (direction + weight_decay * weights), moment_one, second)


def shards(
    inputs,
    cotangent,
    qkv_master,
    out_master,
    up_master,
    down_master,
    qkv_first,
    out_first,
    up_first,
    down_first,
    qkv_second,
    out_second,
    up_second,
    down_second,
    norm_gains,
    gain_first,
    gain_second,
    biases,
    bias_first,
    bias_second,
):
    tokens, width = inputs.shape
    n_row = lax.axis_size("row")
    n_col = lax.axis_size("col")
    n_dp = lax.axis_size("dp")
    row = lax.axis_index("row")
    core = lax.axis_index("col")
    group = n_row * n_col
    heads = width // HEAD
    hidden_width = FF // group
    own = core * n_row + row
    place = jnp.stack([core, lax.axis_index("dp"), own]).astype(jnp.int32)
    chunk = -(-tokens // (group * 16)) * 16
    padded = chunk * group
    shard_rows = qkv_master.shape[0]

    index = jnp.arange(D)
    feature = (
        ((index // width) % n_row) * n_col + index // (width * n_row)
    ) * width + index % width
    index = (feature % n_dp) * (D // n_dp) + feature // n_dp
    order = (lax.broadcasted_iota(jnp.int32, (D, D), 1) == index[:, None]).astype(LOW)
    order = lax.optimization_barrier(order)

    def mixed(vector):
        return vector.reshape(n_row, n_col, width).transpose(1, 0, 2).reshape(D)

    def dealt(vector):
        return vector.reshape(D // n_dp, n_dp).T.reshape(D)

    def returned(rows):
        return exchange_rows(rows.reshape(n_row, shard_rows, -1))

    def long(array):
        return jnp.pad(array, ((0, 0), (0, padded - tokens)))

    flat = lambda array: array.transpose(1, 2, 0)
    tall = lambda array: array.transpose(2, 0, 1)
    first_rows = prepare(place, qkv_master, flat(out_master), n_row)
    first_rows = exchange_rows(first_rows).reshape(D // n_dp, -1)
    x_own = long(inputs.T)
    x_after = x_own + zero_of(first_rows).astype(LOW)
    x_rows = lax.all_gather(x_after, "row", axis=0, tiled=True)
    first_parts = gather_parts(first_rows, "dp")
    rest = prepare(x_rows, up_master, flat(down_master), n_row)
    rest = exchange_rows(rest).reshape(D // n_dp, -1)
    rest_parts = gather_parts(rest, "dp")
    x_all = both_cores(x_rows)
    cot_own = long(cotangent.T) + zero_of(rest).astype(LOW)
    cot_all = lax.all_gather(cot_own, ("row", "col"), axis=0)

    gain_one = mixed(norm_gains[0])
    gain_two = dealt(norm_gains[1])
    shift_one = mixed(biases[:D])
    shift_two = dealt(biases[D : 2 * D])
    query_bias = lax.dynamic_slice_in_dim(biases, 2 * D + own * width, width).reshape(heads, HEAD)
    value_bias = lax.dynamic_slice_in_dim(biases, 3 * D + own * width, width).reshape(heads, HEAD)
    out_bias = dealt(biases[4 * D : 5 * D])
    feature_start = (row * n_col + core) * width
    down_bias = lax.dynamic_slice_in_dim(biases, 5 * D + feature_start, width)
    up_bias = lax.dynamic_slice_in_dim(biases, 6 * D + own * hidden_width, hidden_width)
    qkv_bias = jnp.stack([query_bias, jnp.zeros_like(query_bias), value_bias], axis=1).reshape(
        3 * width, 1
    )

    x_full = x_all.astype(jnp.float32)
    x_mean = jnp.sum(x_full, axis=0, keepdims=True) / D
    center = x_full - x_mean
    inverse_one = lax.rsqrt(jnp.sum(center * center, axis=0, keepdims=True) / D + NORM_EPS)
    za = (center * inverse_one * gain_one[:, None] + shift_one[:, None]).astype(LOW)
    za = dot(order, za, 0, 0, LOW)

    w_first, qkv, attended, theirs, mine = attend(place, rest, za, qkv_bias, first_parts, width)
    pair = (mine.astype(jnp.float32) + swap_cores(theirs).astype(jnp.float32)).astype(LOW)
    branch = sum_over_rows(pair)
    cot_tokens, qkv_mixed, x_mine = beside(
        place, pair, order, cot_all, w_first, x_all, n_row, chunk
    )
    cot_mine = take(cot_tokens, own, chunk).astype(jnp.float32)

    middle = x_mine + branch + out_bias[None, :]
    center = middle - jnp.sum(middle, axis=1, keepdims=True) / D
    inverse_two = lax.rsqrt(jnp.sum(center * center, axis=1, keepdims=True) / D + NORM_EPS)
    normed_two = center * inverse_two
    zb = (normed_two * gain_two + shift_two).astype(LOW)
    zb_rows = lax.all_gather(zb, "row", axis=0, tiled=True)
    w_up, active_grad, down_mixed = before(place, zb_rows, order, cot_tokens, rest_parts)
    zb = both_cores(zb_rows)

    core_of = core.reshape(1).astype(jnp.int32)
    active, hidden_grad, theirs, mine, up_sums = mlp(
        core_of, zb, w_up, up_bias[None, :], active_grad
    )
    pair = (mine.astype(jnp.float32) + swap_cores(theirs).astype(jnp.float32)).astype(LOW)
    two_grad = sum_over_rows(pair)

    middle_mixed = dot(order, middle.astype(LOW), 1, 1, LOW)
    rest_grad, far, near = behind(
        place, pair, zb, hidden_grad, cot_tokens, active, down_mixed, middle_mixed, n_dp
    )

    scaled = two_grad * gain_two
    first_sum = jnp.sum(scaled, axis=1, keepdims=True) / D
    second_sum = jnp.sum(scaled * normed_two, axis=1, keepdims=True) / D
    middle_grad = cot_mine + zero_of(far) + inverse_two * (scaled - first_sum - normed_two * second_sum)
    middle_grad = middle_grad.astype(LOW)
    branch_rows = lax.all_gather(middle_grad, "row", axis=0, tiled=True)
    later = zero_of(branch_rows)
    branch_all = both_cores(branch_rows)

    qkv_grad, bias_sums, first_grad = attend_back(
        branch_all, w_first, qkv, za, attended, n_dp
    )
    theirs, mine, one_sums = first_back(
        core_of, qkv_mixed, qkv_grad, x_all, x_mean, inverse_one, gain_one[:, None],
        far.reshape(n_row, width, padded), near.reshape(n_row, width, padded),
    )
    pair = (mine.astype(jnp.float32) + swap_cores(theirs).astype(jnp.float32)).astype(LOW)
    one_grad = sum_over_rows(pair.reshape(-1, padded))
    result = one_grad[width + 16 :] + down_bias[:, None]
    result = result.astype(LOW)[:, :tokens].T
    first_rows = sum_blocks(first_grad, "dp", 0.0)
    rest_rows = sum_blocks(rest_grad, "dp", later)

    own_gain = lax.dynamic_slice_in_dim(norm_gains[0], feature_start, width)[:, None]
    own_normed = (x_own.astype(jnp.float32) - x_mean) * inverse_one
    own_order = lax.dynamic_slice_in_dim(order, own * width, width, axis=0)
    own_middle = dot(own_order, branch_all, 1, 1)
    input_grad = own_middle + inverse_one * (
        one_grad[:width] * own_gain
        - one_grad[width : width + 1] / D
        - own_normed * (one_grad[width + 1 : width + 2] / D)
    )
    input_grad = input_grad.astype(LOW)[:, :tokens].T

    later = zero_of(pair)
    bias_sums = bias_sums.reshape(heads, 3, HEAD)
    all_rows = jnp.stack(
        [
            one_sums[:, 0],
            one_sums[:, 1],
            jnp.sum(two_grad * normed_two, axis=0),
            jnp.sum(two_grad, axis=0),
            jnp.sum(middle_grad, axis=0, dtype=jnp.float32),
            jnp.sum(cot_mine, axis=0),
        ]
    )
    own_row = jnp.concatenate(
        [bias_sums[:, 0].reshape(width), bias_sums[:, 2].reshape(width), up_sums[0]]
    )
    own_row = jnp.pad(own_row, (0, D - own_row.shape[0]))
    own_rows = jnp.where(jnp.arange(group)[:, None] == own, own_row[None, :], 0.0)
    total = all_sum(jnp.concatenate([jnp.pad(all_rows, ((0, 2), (0, 0))), own_rows]) + later)
    one_rows = total[:2].reshape(2, n_col, n_row, width).transpose(0, 2, 1, 3).reshape(2, D)
    two_rows = total[2:6].reshape(4, n_dp, D // n_dp).transpose(0, 2, 1).reshape(4, D)
    own_rows = total[8:]
    gain_total = jnp.stack([one_rows[0], two_rows[0]])
    bias_total = jnp.concatenate(
        [
            one_rows[1],
            two_rows[1],
            own_rows[:, :width].reshape(D),
            own_rows[:, width : 2 * width].reshape(D),
            two_rows[2],
            two_rows[3],
            own_rows[:, 2 * width : 2 * width + hidden_width].reshape(FF),
        ]
    )

    first_new = adam(
        pair,
        returned(jnp.concatenate([first_rows, rest_rows], axis=1)),
        (0.03, 0.12, 0.03, 0.02),
        qkv_master,
        qkv_first,
        qkv_second,
        flat(out_master),
        flat(out_first),
        flat(out_second),
        up_master,
        up_first,
        up_second,
        flat(down_master),
        flat(down_first),
        flat(down_second),
    )
    first_new, rest_new = first_new[:6], first_new[6:]
    g_new = adam_update(norm_gains, gain_first, gain_second, gain_total, 0.5, 0.0)
    b_new = adam_update(biases, bias_first, bias_second, bias_total, 0.5, 0.0)
    return (
        result,
        input_grad,
        *first_new[:3],
        *(tall(array) for array in first_new[3:]),
        *rest_new[:3],
        *(tall(array) for array in rest_new[3:]),
        *g_new,
        *b_new,
    )


def solution(mesh):
    token_spec = P("dp", ("row", "col"))
    wide = P("row", "dp", "col")
    tall = P("col", "row", "dp")
    return jax.shard_map(
        shards,
        mesh=mesh,
        in_specs=(token_spec,) * 2 + (wide, tall, wide, tall) * 3 + (P(),) * 6,
        out_specs=(token_spec,) * 2
        + (wide,) * 3
        + (tall,) * 3
        + (wide,) * 3
        + (tall,) * 3
        + (P(),) * 6,
        check_vma=False,
    )
```

```python
from functools import partial

import jax
import jax.numpy as jnp
from jax import lax
from jax.experimental import pallas as pl
from jax.experimental.pallas import tpu as pltpu
from jax.sharding import PartitionSpec as P

D = 1152
FF = 4304
HEAD = 72
SEQ = 729
STEP = 10

NORM_EPS = 1e-06
ADAM_EPS = 1e-08
BETA_ONE = 0.9
BETA_TWO = 0.999
LOW = jnp.bfloat16


def dot(left, right, left_dim, right_dim, out=jnp.float32, precision=None):
    return lax.dot_general(
        left,
        right,
        (((left_dim,), (right_dim,)), ((), ())),
        precision=precision,
        preferred_element_type=out,
    )


def take(array, index, size):
    return lax.dynamic_slice_in_dim(array, index * size, size, axis=0)


def swap_cores(array):
    n_col = lax.axis_size("col")
    return lax.ppermute(array, "col", [(i, (i + 1) % n_col) for i in range(n_col)])


def both_cores(rows):
    pieces = [
        lax.all_gather(piece, "col", axis=0) for piece in jnp.split(rows, 2, axis=0)
    ]
    return jnp.concatenate(pieces, axis=1).reshape(-1, rows.shape[1])


def gather_parts(block, axis):
    size = lax.axis_size(axis)
    if size > 4:
        copies = jnp.broadcast_to(block, (size,) + block.shape)
        return [lax.all_to_all(copies, axis, 0, 0).reshape(-1, block.shape[1])]
    return [block] + [
        lax.ppermute(block, axis, [(i, i ^ step) for i in range(size)]) for step in range(1, size)
    ]


def zero_of(array):
    first = lax.slice(array, (0,) * array.ndim, (1,) * array.ndim)
    return first.reshape(()).astype(jnp.float32) * 0.0


def exchange_rows(blocks):
    return lax.all_to_all(blocks, "row", 0, 0)


def sum_blocks(blocks, axis, later):
    blocks = lax.all_to_all(blocks, axis, 0, 0)
    return jnp.sum(blocks.astype(jnp.float32) + later, axis=0).astype(LOW)


def sum_over_rows(half):
    summed = lax.psum_scatter(half.astype(LOW), "row", scatter_dimension=0, tiled=True)
    return summed.astype(jnp.float32)


def all_sum(vector):
    for axis in ("col", "row", "dp"):
        size = lax.axis_size(axis)
        if size & (size - 1) or size > 4:
            vector = lax.psum(vector, axis)
            continue
        step = 1
        while step < size:
            vector = vector + lax.ppermute(vector, axis, [(i, i ^ step) for i in range(size)])
            step *= 2
    return vector


VMEM = pl.BlockSpec(memory_space=pltpu.VMEM)
SMEM = pl.BlockSpec(memory_space=pltpu.SMEM)
ANY = pl.BlockSpec(memory_space=pl.ANY)
BIG = pltpu.CompilerParams(vmem_limit_bytes=56 * 1024 * 1024)


def prepare_kernel(parts, after_ref, wide_ref, tall_ref, out_ref):
    del after_ref
    arrays = [ref[:, 0, :].astype(LOW) for ref in (wide_ref, tall_ref)]
    for part in range(parts):
        pieces = []
        for array in arrays:
            size = array.shape[1] // parts
            pieces.append(array[:, part * size : (part + 1) * size])
        out_ref[part] = jnp.concatenate(pieces, axis=1)


def prepare(after, wide, tall, parts):
    rows = wide.shape[0]
    size = (wide.shape[2] + tall.shape[2]) // parts
    return pl.pallas_call(
        partial(prepare_kernel, parts),
        in_specs=[ANY, VMEM, VMEM],
        out_specs=VMEM,
        out_shape=jax.ShapeDtypeStruct((parts, rows, size), LOW),
        compiler_params=BIG,
        name="prepare",
    )(after, wide, tall)


def adam_kernel(rates, after_ref, blocks_ref, *refs):
    del after_ref
    parts = blocks_ref.shape[0]
    start = 0
    for index, rate in enumerate(rates):
        weight, first, second = refs[3 * index : 3 * index + 3]
        size = weight.shape[2] // parts
        gradient = jnp.concatenate(
            [blocks_ref[part, :, start : start + size] for part in range(parts)], axis=1
        ).astype(jnp.float32)
        start += size
        new = adam_update(weight[:, 0, :], first[:, 0, :], second[:, 0, :], gradient, rate, 0.1)
        for array, ref in zip(new, refs[3 * len(rates) + 3 * index :]):
            ref[:, 0, :] = array


def adam(after, blocks, rates, *arrays):
    return pl.pallas_call(
        partial(adam_kernel, rates),
        in_specs=[ANY] + [VMEM] * (1 + len(arrays)),
        out_specs=[VMEM] * len(arrays),
        out_shape=[jax.ShapeDtypeStruct(a.shape, jnp.float32) for a in arrays],
        compiler_params=BIG,
        name="adam",
    )(after, blocks, *arrays)


def assembled(place, parts, scratch):
    if len(parts) == 1:
        return parts[0][...]
    for step, part in enumerate(parts):
        scratch[place ^ step] = part[...]
    return scratch[...].reshape(-1, scratch.shape[2])


def part_scratch(parts):
    return pltpu.VMEM((len(parts),) + parts[0].shape, LOW)


def head_probs(queries, key_rows):
    scores = dot(queries, key_rows, 0, 0) * HEAD ** (-0.5)
    scores = jnp.where(lax.broadcasted_iota(jnp.int32, scores.shape, 1) < SEQ, scores, -1e30)
    exponent = jnp.exp(scores - jnp.max(scores, axis=1, keepdims=True))
    return exponent * (1.0 / jnp.sum(exponent, axis=1, keepdims=True))


def split_cores(core, first, second, theirs_ref, mine_ref):
    @pl.when(core == 0)
    def _():
        mine_ref[...] = first
        theirs_ref[...] = second

    @pl.when(core != 0)
    def _():
        mine_ref[...] = second
        theirs_ref[...] = first


def attend_kernel(place_ref, after_ref, za_ref, bias_ref, *refs):
    del after_ref
    *parts, w_ref, qkv_ref, att_ref, theirs_ref, mine_ref, scratch = refs
    w_ref[...] = assembled(place_ref[1], parts, scratch)
    heads = qkv_ref.shape[0]
    split = heads * 3 * HEAD
    qkv = dot(w_ref[:, :split], za_ref[...], 0, 0) + bias_ref[...]
    outs = []
    for head in range(heads):
        for t in range(3):
            start = (head * 3 + t) * HEAD
            qkv_ref[head, t] = qkv[start : start + HEAD].astype(LOW)
        probs = head_probs(qkv_ref[head, 0], qkv_ref[head, 1]).astype(LOW)
        outs.append(dot(qkv_ref[head, 2], probs, 1, 1))
    attended = jnp.concatenate(outs, axis=0).T.astype(LOW)
    att_ref[...] = attended
    branch = dot(attended, w_ref[:, split:], 1, 1).astype(LOW)
    half = branch.shape[0] // 2
    split_cores(place_ref[0], branch[:half], branch[half:], theirs_ref, mine_ref)


def attend(place, after, za, qkv_bias, parts, width):
    tokens = za.shape[1]
    return pl.pallas_call(
        attend_kernel,
        in_specs=[SMEM, ANY, VMEM, VMEM] + [VMEM] * len(parts),
        out_specs=[VMEM] * 5,
        out_shape=(
            jax.ShapeDtypeStruct((D, 4 * width), LOW),
            jax.ShapeDtypeStruct((width // HEAD, 3, HEAD, tokens), LOW),
            jax.ShapeDtypeStruct((tokens, width), LOW),
            jax.ShapeDtypeStruct((tokens // 2, D), LOW),
            jax.ShapeDtypeStruct((tokens // 2, D), LOW),
        ),
        scratch_shapes=[part_scratch(parts)],
        compiler_params=BIG,
        name="attend",
    )(place, after, za, qkv_bias, *parts)


def own_tokens(place_ref, chunk, tokens):
    pick = lax.broadcasted_iota(jnp.int32, (chunk, tokens), 0) + place_ref[2] * chunk
    return (lax.broadcasted_iota(jnp.int32, (chunk, tokens), 1) == pick).astype(LOW)


def beside_kernel(n_row, place_ref, after_ref, order_ref, cot_ref, w_ref, x_ref, tokens_ref, mixed_ref, mine_ref):
    del after_ref
    group, width = cot_ref.shape[:2]
    n_col = group // n_row
    order = order_ref[...]
    cot = [cot_ref[row * n_col + core] for core in range(n_col) for row in range(n_row)]
    tokens_ref[...] = dot(jnp.concatenate(cot, axis=0), order, 0, 0).astype(LOW)
    mixed_ref[...] = dot(order, w_ref[:, : 3 * width], 1, 0).astype(LOW)
    pick = own_tokens(place_ref, mine_ref.shape[0], x_ref.shape[1])
    mine_ref[...] = dot(dot(pick, x_ref[...], 1, 1).astype(LOW), order, 1, 0)


def beside(place, after, order, cot_all, w_first, x_all, n_row, chunk):
    group, width, tokens = cot_all.shape
    return pl.pallas_call(
        partial(beside_kernel, n_row),
        in_specs=[SMEM, ANY] + [VMEM] * 4,
        out_specs=[VMEM] * 3,
        out_shape=(
            jax.ShapeDtypeStruct((tokens, D), LOW),
            jax.ShapeDtypeStruct((D, 3 * width), LOW),
            jax.ShapeDtypeStruct((chunk, D), jnp.float32),
        ),
        compiler_params=BIG,
        name="beside",
    )(place, after, order, cot_all, w_first, x_all)


def before_kernel(place_ref, after_ref, order_ref, cot_ref, *refs):
    del after_ref
    *parts, up_ref, grad_ref, mixed_ref, scratch = refs
    w_rest = assembled(place_ref[1], parts, scratch)
    wide = up_ref.shape[1]
    up_ref[...] = w_rest[:, :wide]
    w_down = w_rest[:, wide:]
    grad_ref[...] = dot(cot_ref[...], w_down, 1, 0)
    mixed_ref[...] = dot(order_ref[...], w_down, 1, 0).astype(LOW)


def before(place, after, order, cot_tokens, parts):
    wide = parts[0].shape[1] // 2
    return pl.pallas_call(
        before_kernel,
        in_specs=[SMEM, ANY, VMEM, VMEM] + [VMEM] * len(parts),
        out_specs=[VMEM] * 3,
        out_shape=(
            jax.ShapeDtypeStruct((D, wide), LOW),
            jax.ShapeDtypeStruct((cot_tokens.shape[0], wide), jnp.float32),
            jax.ShapeDtypeStruct((D, wide), LOW),
        ),
        scratch_shapes=[part_scratch(parts)],
        compiler_params=BIG,
        name="before",
    )(place, after, order, cot_tokens, *parts)


def behind_kernel(
    place_ref, after_ref, zb_ref, hid_ref, cot_ref, act_ref, down_ref, mid_ref, grad_ref, theirs_ref, mine_ref
):
    del after_ref
    active = act_ref[...]
    up_grad = dot(zb_ref[...], hid_ref[...], 0, 0).astype(LOW)
    down_grad = dot(cot_ref[...], active, 0, 0).astype(LOW)
    grad_ref[...] = jnp.concatenate([up_grad, down_grad], axis=1).reshape(grad_ref.shape)
    pick = own_tokens(place_ref, mid_ref.shape[1], active.shape[0])
    result = dot(down_ref[...], active, 1, 1) + dot(mid_ref[...], pick, 1, 0)
    result = result.astype(LOW)
    half = D // 2
    split_cores(place_ref[0], result[:half], result[half:], theirs_ref, mine_ref)


def behind(place, after, zb, hidden_grad, cot_tokens, active, down_mixed, middle_mixed, n_dp):
    tokens, wide = active.shape
    return pl.pallas_call(
        behind_kernel,
        in_specs=[SMEM, ANY] + [VMEM] * 6,
        out_specs=[VMEM] * 3,
        out_shape=(
            jax.ShapeDtypeStruct((n_dp, D // n_dp, 2 * wide), LOW),
            jax.ShapeDtypeStruct((D // 2, tokens), LOW),
            jax.ShapeDtypeStruct((D // 2, tokens), LOW),
        ),
        compiler_params=BIG,
        name="behind",
    )(place, after, zb, hidden_grad, cot_tokens, active, down_mixed, middle_mixed)


def mlp_kernel(
    core_ref, zb_ref, up_ref, bias_ref, grad_ref, act_ref, hid_ref, theirs_ref, mine_ref, sum_ref
):
    step = pl.program_id(0)
    near = step >= pl.num_programs(0) // 2
    hidden = dot(zb_ref[...], up_ref[...], 1, 0) + bias_ref[...]
    square = hidden * hidden
    slope = 0.7978845608028654 * (1.0 + 0.044715 * square)
    bent = jnp.tanh(hidden * slope)
    gate = 0.5 * (1.0 + bent)
    act_ref[...] = (hidden * gate).astype(LOW)
    steep = gate + 0.5 * hidden * (1.0 - bent * bent) * (
        0.7978845608028654 * (1.0 + 3 * 0.044715 * square)
    )
    hidden_grad = (grad_ref[...] * steep).astype(LOW)
    hid_ref[...] = hidden_grad
    two_grad = dot(hidden_grad, up_ref[...], 1, 1).astype(LOW)

    @pl.when(near)
    def _():
        mine_ref[...] = two_grad

    @pl.when(jnp.logical_not(near))
    def _():
        theirs_ref[...] = two_grad

    @pl.when(step == 0)
    def _():
        sum_ref[...] = jnp.zeros(sum_ref.shape, jnp.float32)

    sum_ref[...] += jnp.sum(hidden_grad.astype(jnp.float32), axis=0, keepdims=True)


def mlp(core, zb, w_up, up_bias, active_grad):
    tokens = zb.shape[0]
    wide = w_up.shape[1]
    steps = 6
    block = tokens // steps
    turned = lambda i, c: ((i + (steps // 2) * (1 - c[0])) % steps, 0)
    whole = lambda i, c: (0, 0)
    return pl.pallas_call(
        mlp_kernel,
        grid_spec=pltpu.PrefetchScalarGridSpec(
            num_scalar_prefetch=1,
            grid=(steps,),
            in_specs=[
                pl.BlockSpec((block, D), turned),
                pl.BlockSpec((D, wide), whole),
                pl.BlockSpec((1, wide), whole),
                pl.BlockSpec((block, wide), turned),
            ],
            out_specs=[
                pl.BlockSpec((block, wide), turned),
                pl.BlockSpec((block, wide), turned),
                pl.BlockSpec((block, D), lambda i, c: (jnp.minimum(i, steps // 2 - 1), 0)),
                pl.BlockSpec((block, D), lambda i, c: (jnp.maximum(i - steps // 2, 0), 0)),
                pl.BlockSpec((1, wide), whole),
            ],
        ),
        out_shape=(
            jax.ShapeDtypeStruct((tokens, wide), LOW),
            jax.ShapeDtypeStruct((tokens, wide), LOW),
            jax.ShapeDtypeStruct((tokens // 2, D), LOW),
            jax.ShapeDtypeStruct((tokens // 2, D), LOW),
            jax.ShapeDtypeStruct((1, wide), jnp.float32),
        ),
        compiler_params=BIG,
        name="mlp",
    )(core, zb, w_up, up_bias, active_grad)


def back_kernel(after_ref, bg_ref, w_ref, qkv_ref, za_ref, att_ref, grad_ref, sum_ref, wg_ref):
    del after_ref
    heads = qkv_ref.shape[0]
    attended_grad = dot(bg_ref[...], w_ref[:, heads * 3 * HEAD :], 1, 0).T
    scale = HEAD ** (-0.5)
    parts = []
    for head in range(heads):
        queries, key_rows, values = qkv_ref[head, 0], qkv_ref[head, 1], qkv_ref[head, 2]
        grad = attended_grad[head * HEAD : (head + 1) * HEAD].astype(LOW)
        probs = head_probs(queries, key_rows)
        probs_grad = dot(grad, values, 0, 0)
        inner = jnp.sum(probs * probs_grad, axis=1, keepdims=True)
        scores_grad = (probs * (probs_grad - inner)).astype(LOW)
        parts.append(dot(key_rows, scores_grad, 1, 1) * scale)
        parts.append(dot(queries, scores_grad, 1, 0) * scale)
        parts.append(dot(grad, probs.astype(LOW), 1, 0))
    qkv_grad = jnp.concatenate(parts, axis=0).astype(LOW)
    grad_ref[...] = qkv_grad
    sum_ref[...] = jnp.sum(qkv_grad.astype(jnp.float32), axis=1, keepdims=True)
    qkv_part = dot(za_ref[...], qkv_grad, 1, 1).astype(LOW)
    out_part = dot(bg_ref[...], att_ref[...], 0, 0).astype(LOW)
    wg_ref[...] = jnp.concatenate([qkv_part, out_part], axis=1).reshape(wg_ref.shape)


def attend_back(after, branch_all, w_first, qkv, za, attended, n_dp):
    tokens, width = attended.shape
    return pl.pallas_call(
        back_kernel,
        in_specs=[ANY] + [VMEM] * 5,
        out_specs=[VMEM] * 3,
        out_shape=(
            jax.ShapeDtypeStruct((3 * width, tokens), LOW),
            jax.ShapeDtypeStruct((3 * width, 1), jnp.float32),
            jax.ShapeDtypeStruct((n_dp, D // n_dp, 4 * width), LOW),
        ),
        compiler_params=BIG,
        name="attend_back",
    )(after, branch_all, w_first, qkv, za, attended)


def first_kernel(
    core_ref, w_ref, grad_ref, x_ref, mean_ref, inv_ref, gain_ref, far_ref, near_ref, theirs_ref, mine_ref, sum_ref
):
    n_row, width, tokens = far_ref.shape
    theirs_ref[:, width + 16 :] = far_ref[...]
    mine_ref[:, width + 16 :] = near_ref[...]
    first = jnp.zeros((1, tokens), jnp.float32)
    second = jnp.zeros((1, tokens), jnp.float32)
    blocks = []
    for slot in range(D // width):
        here = slice(slot * width, (slot + 1) * width)
        part = dot(w_ref[here], grad_ref[...], 1, 0)
        normed = (x_ref[here].astype(jnp.float32) - mean_ref[...]) * inv_ref[...]
        product = part * normed
        sum_ref[here, 0:1] = jnp.sum(product, axis=1, keepdims=True)
        sum_ref[here, 1:2] = jnp.sum(part, axis=1, keepdims=True)
        first += jnp.sum(part * gain_ref[here], axis=0, keepdims=True)
        second += jnp.sum(product * gain_ref[here], axis=0, keepdims=True)
        blocks.append(part.astype(LOW))
    line = lax.broadcasted_iota(jnp.int32, (16, tokens), 0)
    sums = jnp.where(line == 0, first, jnp.where(line == 1, second, 0.0)).astype(LOW)
    for near, ref in ((False, theirs_ref), (True, mine_ref)):
        for core in range(2):

            @pl.when((core_ref[0] == core) == near)
            def _(core=core, ref=ref):
                for row in range(n_row):
                    ref[row, :width] = blocks[core * n_row + row]
                    ref[row, width : width + 16] = sums


def first_back(core, w_mixed, qkv_grad, x_all, x_mean, inverse, gain, far, near):
    n_row, width, tokens = far.shape
    return pl.pallas_call(
        first_kernel,
        in_specs=[SMEM] + [VMEM] * 8,
        out_specs=[VMEM] * 3,
        out_shape=(
            jax.ShapeDtypeStruct((n_row, 2 * width + 16, tokens), LOW),
            jax.ShapeDtypeStruct((n_row, 2 * width + 16, tokens), LOW),
            jax.ShapeDtypeStruct((D, 2), jnp.float32),
        ),
        compiler_params=BIG,
        name="first_back",
    )(core, w_mixed, qkv_grad, x_all, x_mean, inverse, gain, far, near)


def adam_update(weights, moment_one, second, gradient, step_rate, weight_decay):
    moment_one = BETA_ONE * moment_one + (1.0 - BETA_ONE) * gradient
    second = BETA_TWO * second + (1.0 - BETA_TWO) * gradient * gradient
    direction = (
        moment_one / (1.0 - BETA_ONE**STEP) / (jnp.sqrt(second / (1.0 - BETA_TWO**STEP)) + ADAM_EPS)
    )
    return (weights - step_rate * (direction + weight_decay * weights), moment_one, second)


def shards(
    inputs,
    cotangent,
    qkv_master,
    out_master,
    up_master,
    down_master,
    qkv_first,
    out_first,
    up_first,
    down_first,
    qkv_second,
    out_second,
    up_second,
    down_second,
    norm_gains,
    gain_first,
    gain_second,
    biases,
    bias_first,
    bias_second,
):
    tokens, width = inputs.shape
    n_row = lax.axis_size("row")
    n_col = lax.axis_size("col")
    n_dp = lax.axis_size("dp")
    row = lax.axis_index("row")
    core = lax.axis_index("col")
    group = n_row * n_col
    heads = width // HEAD
    hidden_width = FF // group
    own = core * n_row + row
    place = jnp.stack([core, lax.axis_index("dp"), own]).astype(jnp.int32)
    chunk = -(-tokens // (group * 16)) * 16
    padded = chunk * group
    shard_rows = qkv_master.shape[0]

    index = jnp.arange(D)
    feature = (
        ((index // width) % n_row) * n_col + index // (width * n_row)
    ) * width + index % width
    index = (feature % n_dp) * (D // n_dp) + feature // n_dp
    order = (lax.broadcasted_iota(jnp.int32, (D, D), 1) == index[:, None]).astype(LOW)
    order = lax.optimization_barrier(order)

    def mixed(vector):
        return vector.reshape(n_row, n_col, width).transpose(1, 0, 2).reshape(D)

    def dealt(vector):
        return vector.reshape(D // n_dp, n_dp).T.reshape(D)

    def returned(rows):
        return exchange_rows(rows.reshape(n_row, shard_rows, -1))

    def long(array):
        return jnp.pad(array, ((0, 0), (0, padded - tokens)))

    flat = lambda array: array.transpose(1, 2, 0)
    tall = lambda array: array.transpose(2, 0, 1)
    first_rows = prepare(place, qkv_master, flat(out_master), n_row)
    first_rows = exchange_rows(first_rows).reshape(D // n_dp, -1)
    x_own = long(inputs.T)
    x_after = x_own + zero_of(first_rows).astype(LOW)
    x_rows = lax.all_gather(x_after, "row", axis=0, tiled=True)
    first_parts = gather_parts(first_rows, "dp")
    rest = prepare(x_rows, up_master, flat(down_master), n_row)
    rest = exchange_rows(rest).reshape(D // n_dp, -1)
    rest_parts = gather_parts(rest, "dp")
    x_all = both_cores(x_rows)
    cot_own = long(cotangent.T) + zero_of(rest).astype(LOW)
    cot_all = lax.all_gather(cot_own, ("row", "col"), axis=0)

    gain_one = mixed(norm_gains[0])
    gain_two = dealt(norm_gains[1])
    shift_one = mixed(biases[:D])
    shift_two = dealt(biases[D : 2 * D])
    query_bias = lax.dynamic_slice_in_dim(biases, 2 * D + own * width, width).reshape(heads, HEAD)
    value_bias = lax.dynamic_slice_in_dim(biases, 3 * D + own * width, width).reshape(heads, HEAD)
    out_bias = dealt(biases[4 * D : 5 * D])
    feature_start = (row * n_col + core) * width
    down_bias = lax.dynamic_slice_in_dim(biases, 5 * D + feature_start, width)
    up_bias = lax.dynamic_slice_in_dim(biases, 6 * D + own * hidden_width, hidden_width)
    qkv_bias = jnp.stack([query_bias, jnp.zeros_like(query_bias), value_bias], axis=1).reshape(
        3 * width, 1
    )

    x_full = x_all.astype(jnp.float32)
    x_mean = jnp.sum(x_full, axis=0, keepdims=True) / D
    center = x_full - x_mean
    inverse_one = lax.rsqrt(jnp.sum(center * center, axis=0, keepdims=True) / D + NORM_EPS)
    za = (center * inverse_one * gain_one[:, None] + shift_one[:, None]).astype(LOW)
    za = dot(order, za, 0, 0, LOW)

    w_first, qkv, attended, theirs, mine = attend(place, rest, za, qkv_bias, first_parts, width)
    pair = (mine.astype(jnp.float32) + swap_cores(theirs).astype(jnp.float32)).astype(LOW)
    branch = sum_over_rows(pair)
    cot_tokens, qkv_mixed, x_mine = beside(
        place, pair, order, cot_all, w_first, x_all, n_row, chunk
    )
    cot_mine = take(cot_tokens, own, chunk).astype(jnp.float32)

    middle = x_mine + branch + out_bias[None, :]
    center = middle - jnp.sum(middle, axis=1, keepdims=True) / D
    inverse_two = lax.rsqrt(jnp.sum(center * center, axis=1, keepdims=True) / D + NORM_EPS)
    normed_two = center * inverse_two
    zb = (normed_two * gain_two + shift_two).astype(LOW)
    zb_rows = lax.all_gather(zb, "row", axis=0, tiled=True)
    w_up, active_grad, down_mixed = before(place, zb_rows, order, cot_tokens, rest_parts)
    zb = both_cores(zb_rows)

    core_of = core.reshape(1).astype(jnp.int32)
    active, hidden_grad, theirs, mine, up_sums = mlp(
        core_of, zb, w_up, up_bias[None, :], active_grad
    )
    pair = (mine.astype(jnp.float32) + swap_cores(theirs).astype(jnp.float32)).astype(LOW)
    two_grad = sum_over_rows(pair)

    middle_mixed = dot(order, middle.astype(LOW), 1, 1, LOW)
    rest_grad, far, near = behind(
        place, pair, zb, hidden_grad, cot_tokens, active, down_mixed, middle_mixed, n_dp
    )

    scaled = two_grad * gain_two
    first_sum = jnp.sum(scaled, axis=1, keepdims=True) / D
    second_sum = jnp.sum(scaled * normed_two, axis=1, keepdims=True) / D
    middle_grad = cot_mine + zero_of(far) + inverse_two * (scaled - first_sum - normed_two * second_sum)
    middle_grad = middle_grad.astype(LOW)
    branch_rows = lax.all_gather(middle_grad, "row", axis=0, tiled=True)
    later = zero_of(branch_rows)
    branch_all = both_cores(branch_rows)
    rest_rows = sum_blocks(rest_grad, "dp", later)

    qkv_grad, bias_sums, first_grad = attend_back(
        rest_rows, branch_all, w_first, qkv, za, attended, n_dp
    )
    theirs, mine, one_sums = first_back(
        core_of, qkv_mixed, qkv_grad, x_all, x_mean, inverse_one, gain_one[:, None],
        far.reshape(n_row, width, padded), near.reshape(n_row, width, padded),
    )
    pair = (mine.astype(jnp.float32) + swap_cores(theirs).astype(jnp.float32)).astype(LOW)
    one_grad = sum_over_rows(pair.reshape(-1, padded))
    result = one_grad[width + 16 :] + down_bias[:, None]
    result = result.astype(LOW)[:, :tokens].T
    first_rows = sum_blocks(first_grad, "dp", 0.0)

    own_gain = lax.dynamic_slice_in_dim(norm_gains[0], feature_start, width)[:, None]
    own_normed = (x_own.astype(jnp.float32) - x_mean) * inverse_one
    own_order = lax.dynamic_slice_in_dim(order, own * width, width, axis=0)
    own_middle = dot(own_order, branch_all, 1, 1)
    input_grad = own_middle + inverse_one * (
        one_grad[:width] * own_gain
        - one_grad[width : width + 1] / D
        - own_normed * (one_grad[width + 1 : width + 2] / D)
    )
    input_grad = input_grad.astype(LOW)[:, :tokens].T

    later = zero_of(pair)
    bias_sums = (bias_sums + later).reshape(heads, 3, HEAD)
    all_rows = jnp.stack(
        [
            one_sums[:, 0] + later,
            one_sums[:, 1] + later,
            jnp.sum(two_grad * normed_two + later, axis=0),
            jnp.sum(two_grad + later, axis=0),
            jnp.sum(middle_grad.astype(jnp.float32) + later, axis=0),
            jnp.sum(cot_mine + later, axis=0),
        ]
    )
    own_row = jnp.concatenate(
        [bias_sums[:, 0].reshape(width), bias_sums[:, 2].reshape(width), up_sums[0] + later]
    )
    own_row = jnp.pad(own_row, (0, D - own_row.shape[0]))
    own_rows = jnp.where(jnp.arange(group)[:, None] == own, own_row[None, :], 0.0)
    total = all_sum(jnp.concatenate([jnp.pad(all_rows, ((0, 2), (0, 0))), own_rows]) + later)
    one_rows = total[:2].reshape(2, n_col, n_row, width).transpose(0, 2, 1, 3).reshape(2, D)
    two_rows = total[2:6].reshape(4, n_dp, D // n_dp).transpose(0, 2, 1).reshape(4, D)
    own_rows = total[8:]
    gain_total = jnp.stack([one_rows[0], two_rows[0]])
    bias_total = jnp.concatenate(
        [
            one_rows[1],
            two_rows[1],
            own_rows[:, :width].reshape(D),
            own_rows[:, width : 2 * width].reshape(D),
            two_rows[2],
            two_rows[3],
            own_rows[:, 2 * width : 2 * width + hidden_width].reshape(FF),
        ]
    )

    first_new = adam(
        pair,
        returned(jnp.concatenate([first_rows, rest_rows], axis=1)),
        (0.03, 0.12, 0.03, 0.02),
        qkv_master,
        qkv_first,
        qkv_second,
        flat(out_master),
        flat(out_first),
        flat(out_second),
        up_master,
        up_first,
        up_second,
        flat(down_master),
        flat(down_first),
        flat(down_second),
    )
    first_new, rest_new = first_new[:6], first_new[6:]
    g_new = adam_update(norm_gains, gain_first, gain_second, gain_total, 0.5, 0.0)
    b_new = adam_update(biases, bias_first, bias_second, bias_total, 0.5, 0.0)
    return (
        result,
        input_grad,
        *first_new[:3],
        *(tall(array) for array in first_new[3:]),
        *rest_new[:3],
        *(tall(array) for array in rest_new[3:]),
        *g_new,
        *b_new,
    )


def solution(mesh):
    token_spec = P("dp", ("row", "col"))
    wide = P("row", "dp", "col")
    tall = P("col", "row", "dp")
    return jax.shard_map(
        shards,
        mesh=mesh,
        in_specs=(token_spec,) * 2 + (wide, tall, wide, tall) * 3 + (P(),) * 6,
        out_specs=(token_spec,) * 2
        + (wide,) * 3
        + (tall,) * 3
        + (wide,) * 3
        + (tall,) * 3
        + (P(),) * 6,
        check_vma=False,
    )
```

```python
from functools import partial

import jax
import jax.numpy as jnp
from jax import lax
from jax.experimental import pallas as pl
from jax.experimental.pallas import tpu as pltpu
from jax.sharding import PartitionSpec as P

D = 1152
FF = 4304
HEAD = 72
SEQ = 729
STEP = 10

NORM_EPS = 1e-06
ADAM_EPS = 1e-08
BETA_ONE = 0.9
BETA_TWO = 0.999
LOW = jnp.bfloat16


def dot(left, right, left_dim, right_dim, out=jnp.float32, precision=None):
    return lax.dot_general(
        left,
        right,
        (((left_dim,), (right_dim,)), ((), ())),
        precision=precision,
        preferred_element_type=out,
    )


def take(array, index, size):
    return lax.dynamic_slice_in_dim(array, index * size, size, axis=0)


def swap_cores(array):
    n_col = lax.axis_size("col")
    return lax.ppermute(array, "col", [(i, (i + 1) % n_col) for i in range(n_col)])


def both_cores(rows):
    pieces = [
        lax.all_gather(piece, "col", axis=0) for piece in jnp.split(rows, 2, axis=0)
    ]
    return jnp.concatenate(pieces, axis=1).reshape(-1, rows.shape[1])


def gather_parts(block, axis):
    size = lax.axis_size(axis)
    if size > 4:
        copies = jnp.broadcast_to(block, (size,) + block.shape)
        return [lax.all_to_all(copies, axis, 0, 0).reshape(-1, block.shape[1])]
    return [block] + [
        lax.ppermute(block, axis, [(i, i ^ step) for i in range(size)]) for step in range(1, size)
    ]


def zero_of(array):
    first = lax.slice(array, (0,) * array.ndim, (1,) * array.ndim)
    return first.reshape(()).astype(jnp.float32) * 0.0


def exchange_rows(blocks):
    return lax.all_to_all(blocks, "row", 0, 0)


def sum_blocks(blocks, axis, later):
    blocks = lax.all_to_all(blocks, axis, 0, 0)
    return jnp.sum(blocks.astype(jnp.float32) + later, axis=0).astype(LOW)


def sum_over_rows(half):
    summed = lax.psum_scatter(half.astype(LOW), "row", scatter_dimension=0, tiled=True)
    return summed.astype(jnp.float32)


def all_sum(vector):
    for axis in ("col", "row", "dp"):
        size = lax.axis_size(axis)
        if size & (size - 1) or size > 4:
            vector = lax.psum(vector, axis)
            continue
        step = 1
        while step < size:
            vector = vector + lax.ppermute(vector, axis, [(i, i ^ step) for i in range(size)])
            step *= 2
    return vector


VMEM = pl.BlockSpec(memory_space=pltpu.VMEM)
SMEM = pl.BlockSpec(memory_space=pltpu.SMEM)
ANY = pl.BlockSpec(memory_space=pl.ANY)
BIG = pltpu.CompilerParams(vmem_limit_bytes=56 * 1024 * 1024)


def prepare_kernel(parts, after_ref, wide_ref, tall_ref, out_ref):
    del after_ref
    arrays = [ref[:, 0, :].astype(LOW) for ref in (wide_ref, tall_ref)]
    for part in range(parts):
        pieces = []
        for array in arrays:
            size = array.shape[1] // parts
            pieces.append(array[:, part * size : (part + 1) * size])
        out_ref[part] = jnp.concatenate(pieces, axis=1)


def prepare(after, wide, tall, parts):
    rows = wide.shape[0]
    size = (wide.shape[2] + tall.shape[2]) // parts
    return pl.pallas_call(
        partial(prepare_kernel, parts),
        in_specs=[ANY, VMEM, VMEM],
        out_specs=VMEM,
        out_shape=jax.ShapeDtypeStruct((parts, rows, size), LOW),
        compiler_params=BIG,
        name="prepare",
    )(after, wide, tall)


def adam_kernel(rates, after_ref, blocks_ref, *refs):
    del after_ref
    parts = blocks_ref.shape[0]
    start = 0
    for index, rate in enumerate(rates):
        weight, first, second = refs[3 * index : 3 * index + 3]
        size = weight.shape[2] // parts
        gradient = jnp.concatenate(
            [blocks_ref[part, :, start : start + size] for part in range(parts)], axis=1
        ).astype(jnp.float32)
        start += size
        new = adam_update(weight[:, 0, :], first[:, 0, :], second[:, 0, :], gradient, rate, 0.1)
        for array, ref in zip(new, refs[3 * len(rates) + 3 * index :]):
            ref[:, 0, :] = array


def adam(after, blocks, rates, *arrays):
    return pl.pallas_call(
        partial(adam_kernel, rates),
        in_specs=[ANY] + [VMEM] * (1 + len(arrays)),
        out_specs=[VMEM] * len(arrays),
        out_shape=[jax.ShapeDtypeStruct(a.shape, jnp.float32) for a in arrays],
        compiler_params=BIG,
        name="adam",
    )(after, blocks, *arrays)


def assembled(place, parts, scratch):
    if len(parts) == 1:
        return parts[0][...]
    for step, part in enumerate(parts):
        scratch[place ^ step] = part[...]
    return scratch[...].reshape(-1, scratch.shape[2])


def part_scratch(parts):
    return pltpu.VMEM((len(parts),) + parts[0].shape, LOW)


def head_probs(queries, key_rows):
    scores = dot(queries, key_rows, 0, 0) * HEAD ** (-0.5)
    scores = jnp.where(lax.broadcasted_iota(jnp.int32, scores.shape, 1) < SEQ, scores, -1e30)
    exponent = jnp.exp(scores - jnp.max(scores, axis=1, keepdims=True))
    return exponent * (1.0 / jnp.sum(exponent, axis=1, keepdims=True))


def split_cores(core, first, second, theirs_ref, mine_ref):
    @pl.when(core == 0)
    def _():
        mine_ref[...] = first
        theirs_ref[...] = second

    @pl.when(core != 0)
    def _():
        mine_ref[...] = second
        theirs_ref[...] = first


def attend_kernel(place_ref, after_ref, za_ref, bias_ref, *refs):
    del after_ref
    *parts, w_ref, qkv_ref, att_ref, theirs_ref, mine_ref, scratch = refs
    w_ref[...] = assembled(place_ref[1], parts, scratch)
    heads = qkv_ref.shape[0]
    split = heads * 3 * HEAD
    qkv = dot(w_ref[:, :split], za_ref[...], 0, 0) + bias_ref[...]
    outs = []
    for head in range(heads):
        for t in range(3):
            start = (head * 3 + t) * HEAD
            qkv_ref[head, t] = qkv[start : start + HEAD].astype(LOW)
        probs = head_probs(qkv_ref[head, 0], qkv_ref[head, 1]).astype(LOW)
        outs.append(dot(qkv_ref[head, 2], probs, 1, 1))
    attended = jnp.concatenate(outs, axis=0).T.astype(LOW)
    att_ref[...] = attended
    branch = dot(attended, w_ref[:, split:], 1, 1).astype(LOW)
    half = branch.shape[0] // 2
    split_cores(place_ref[0], branch[:half], branch[half:], theirs_ref, mine_ref)


def attend(place, after, za, qkv_bias, parts, width):
    tokens = za.shape[1]
    return pl.pallas_call(
        attend_kernel,
        in_specs=[SMEM, ANY, VMEM, VMEM] + [VMEM] * len(parts),
        out_specs=[VMEM] * 5,
        out_shape=(
            jax.ShapeDtypeStruct((D, 4 * width), LOW),
            jax.ShapeDtypeStruct((width // HEAD, 3, HEAD, tokens), LOW),
            jax.ShapeDtypeStruct((tokens, width), LOW),
            jax.ShapeDtypeStruct((tokens // 2, D), LOW),
            jax.ShapeDtypeStruct((tokens // 2, D), LOW),
        ),
        scratch_shapes=[part_scratch(parts)],
        compiler_params=BIG,
        name="attend",
    )(place, after, za, qkv_bias, *parts)


def own_tokens(place_ref, chunk, tokens):
    pick = lax.broadcasted_iota(jnp.int32, (chunk, tokens), 0) + place_ref[2] * chunk
    return (lax.broadcasted_iota(jnp.int32, (chunk, tokens), 1) == pick).astype(LOW)


def beside_kernel(n_row, place_ref, after_ref, order_ref, cot_ref, w_ref, x_ref, tokens_ref, mixed_ref, mine_ref):
    del after_ref
    group, width = cot_ref.shape[:2]
    n_col = group // n_row
    order = order_ref[...]
    cot = [cot_ref[row * n_col + core] for core in range(n_col) for row in range(n_row)]
    tokens_ref[...] = dot(jnp.concatenate(cot, axis=0), order, 0, 0).astype(LOW)
    mixed_ref[...] = dot(order, w_ref[:, : 3 * width], 1, 0).astype(LOW)
    pick = own_tokens(place_ref, mine_ref.shape[0], x_ref.shape[1])
    mine_ref[...] = dot(dot(pick, x_ref[...], 1, 1).astype(LOW), order, 1, 0)


def beside(place, after, order, cot_all, w_first, x_all, n_row, chunk):
    group, width, tokens = cot_all.shape
    return pl.pallas_call(
        partial(beside_kernel, n_row),
        in_specs=[SMEM, ANY] + [VMEM] * 4,
        out_specs=[VMEM] * 3,
        out_shape=(
            jax.ShapeDtypeStruct((tokens, D), LOW),
            jax.ShapeDtypeStruct((D, 3 * width), LOW),
            jax.ShapeDtypeStruct((chunk, D), jnp.float32),
        ),
        compiler_params=BIG,
        name="beside",
    )(place, after, order, cot_all, w_first, x_all)


def before_kernel(place_ref, after_ref, order_ref, cot_ref, *refs):
    del after_ref
    *parts, up_ref, grad_ref, mixed_ref, scratch = refs
    w_rest = assembled(place_ref[1], parts, scratch)
    wide = up_ref.shape[1]
    up_ref[...] = w_rest[:, :wide]
    w_down = w_rest[:, wide:]
    grad_ref[...] = dot(cot_ref[...], w_down, 1, 0)
    mixed_ref[...] = dot(order_ref[...], w_down, 1, 0).astype(LOW)


def before(place, after, order, cot_tokens, parts):
    wide = parts[0].shape[1] // 2
    return pl.pallas_call(
        before_kernel,
        in_specs=[SMEM, ANY, VMEM, VMEM] + [VMEM] * len(parts),
        out_specs=[VMEM] * 3,
        out_shape=(
            jax.ShapeDtypeStruct((D, wide), LOW),
            jax.ShapeDtypeStruct((cot_tokens.shape[0], wide), jnp.float32),
            jax.ShapeDtypeStruct((D, wide), LOW),
        ),
        scratch_shapes=[part_scratch(parts)],
        compiler_params=BIG,
        name="before",
    )(place, after, order, cot_tokens, *parts)


def behind_kernel(
    place_ref, after_ref, zb_ref, hid_ref, cot_ref, act_ref, down_ref, mid_ref, grad_ref, theirs_ref, mine_ref
):
    del after_ref
    active = act_ref[...]
    up_grad = dot(zb_ref[...], hid_ref[...], 0, 0).astype(LOW)
    down_grad = dot(cot_ref[...], active, 0, 0).astype(LOW)
    grad_ref[...] = jnp.concatenate([up_grad, down_grad], axis=1).reshape(grad_ref.shape)
    pick = own_tokens(place_ref, mid_ref.shape[1], active.shape[0])
    result = dot(down_ref[...], active, 1, 1) + dot(mid_ref[...], pick, 1, 0)
    result = result.astype(LOW)
    half = D // 2
    split_cores(place_ref[0], result[:half], result[half:], theirs_ref, mine_ref)


def behind(place, after, zb, hidden_grad, cot_tokens, active, down_mixed, middle_mixed, n_dp):
    tokens, wide = active.shape
    return pl.pallas_call(
        behind_kernel,
        in_specs=[SMEM, ANY] + [VMEM] * 6,
        out_specs=[VMEM] * 3,
        out_shape=(
            jax.ShapeDtypeStruct((n_dp, D // n_dp, 2 * wide), LOW),
            jax.ShapeDtypeStruct((D // 2, tokens), LOW),
            jax.ShapeDtypeStruct((D // 2, tokens), LOW),
        ),
        compiler_params=BIG,
        name="behind",
    )(place, after, zb, hidden_grad, cot_tokens, active, down_mixed, middle_mixed)


def mlp_kernel(
    core_ref, zb_ref, up_ref, bias_ref, grad_ref, act_ref, hid_ref, theirs_ref, mine_ref, sum_ref
):
    step = pl.program_id(0)
    near = step >= pl.num_programs(0) // 2
    hidden = dot(zb_ref[...], up_ref[...], 1, 0) + bias_ref[...]
    square = hidden * hidden
    slope = 0.7978845608028654 * (1.0 + 0.044715 * square)
    bent = jnp.tanh(hidden * slope)
    gate = 0.5 * (1.0 + bent)
    act_ref[...] = (hidden * gate).astype(LOW)
    steep = gate + 0.5 * hidden * (1.0 - bent * bent) * (
        0.7978845608028654 * (1.0 + 3 * 0.044715 * square)
    )
    hidden_grad = (grad_ref[...] * steep).astype(LOW)
    hid_ref[...] = hidden_grad
    two_grad = dot(hidden_grad, up_ref[...], 1, 1).astype(LOW)

    @pl.when(near)
    def _():
        mine_ref[...] = two_grad

    @pl.when(jnp.logical_not(near))
    def _():
        theirs_ref[...] = two_grad

    @pl.when(step == 0)
    def _():
        sum_ref[...] = jnp.zeros(sum_ref.shape, jnp.float32)

    sum_ref[...] += jnp.sum(hidden_grad.astype(jnp.float32), axis=0, keepdims=True)


def mlp(core, zb, w_up, up_bias, active_grad):
    tokens = zb.shape[0]
    wide = w_up.shape[1]
    steps = 6
    block = tokens // steps
    turned = lambda i, c: ((i + (steps // 2) * (1 - c[0])) % steps, 0)
    whole = lambda i, c: (0, 0)
    return pl.pallas_call(
        mlp_kernel,
        grid_spec=pltpu.PrefetchScalarGridSpec(
            num_scalar_prefetch=1,
            grid=(steps,),
            in_specs=[
                pl.BlockSpec((block, D), turned),
                pl.BlockSpec((D, wide), whole),
                pl.BlockSpec((1, wide), whole),
                pl.BlockSpec((block, wide), turned),
            ],
            out_specs=[
                pl.BlockSpec((block, wide), turned),
                pl.BlockSpec((block, wide), turned),
                pl.BlockSpec((block, D), lambda i, c: (jnp.minimum(i, steps // 2 - 1), 0)),
                pl.BlockSpec((block, D), lambda i, c: (jnp.maximum(i - steps // 2, 0), 0)),
                pl.BlockSpec((1, wide), whole),
            ],
        ),
        out_shape=(
            jax.ShapeDtypeStruct((tokens, wide), LOW),
            jax.ShapeDtypeStruct((tokens, wide), LOW),
            jax.ShapeDtypeStruct((tokens // 2, D), LOW),
            jax.ShapeDtypeStruct((tokens // 2, D), LOW),
            jax.ShapeDtypeStruct((1, wide), jnp.float32),
        ),
        compiler_params=BIG,
        name="mlp",
    )(core, zb, w_up, up_bias, active_grad)


def back_kernel(after_ref, bg_ref, w_ref, qkv_ref, za_ref, att_ref, grad_ref, sum_ref, wg_ref):
    del after_ref
    heads = qkv_ref.shape[0]
    attended_grad = dot(bg_ref[...], w_ref[:, heads * 3 * HEAD :], 1, 0).T
    scale = HEAD ** (-0.5)
    parts = []
    for head in range(heads):
        queries, key_rows, values = qkv_ref[head, 0], qkv_ref[head, 1], qkv_ref[head, 2]
        grad = attended_grad[head * HEAD : (head + 1) * HEAD].astype(LOW)
        probs = head_probs(queries, key_rows)
        probs_grad = dot(grad, values, 0, 0)
        inner = jnp.sum(probs * probs_grad, axis=1, keepdims=True)
        scores_grad = (probs * (probs_grad - inner)).astype(LOW)
        parts.append(dot(key_rows, scores_grad, 1, 1) * scale)
        parts.append(dot(queries, scores_grad, 1, 0) * scale)
        parts.append(dot(grad, probs.astype(LOW), 1, 0))
    qkv_grad = jnp.concatenate(parts, axis=0).astype(LOW)
    grad_ref[...] = qkv_grad
    sum_ref[...] = jnp.sum(qkv_grad.astype(jnp.float32), axis=1, keepdims=True)
    qkv_part = dot(za_ref[...], qkv_grad, 1, 1).astype(LOW)
    out_part = dot(bg_ref[...], att_ref[...], 0, 0).astype(LOW)
    wg_ref[...] = jnp.concatenate([qkv_part, out_part], axis=1).reshape(wg_ref.shape)


def attend_back(after, branch_all, w_first, qkv, za, attended, n_dp):
    tokens, width = attended.shape
    return pl.pallas_call(
        back_kernel,
        in_specs=[ANY] + [VMEM] * 5,
        out_specs=[VMEM] * 3,
        out_shape=(
            jax.ShapeDtypeStruct((3 * width, tokens), LOW),
            jax.ShapeDtypeStruct((3 * width, 1), jnp.float32),
            jax.ShapeDtypeStruct((n_dp, D // n_dp, 4 * width), LOW),
        ),
        compiler_params=BIG,
        name="attend_back",
    )(after, branch_all, w_first, qkv, za, attended)


def first_kernel(
    core_ref, w_ref, grad_ref, x_ref, mean_ref, inv_ref, gain_ref, far_ref, near_ref, theirs_ref, mine_ref, sum_ref
):
    n_row, width, tokens = far_ref.shape
    theirs_ref[:, width + 16 :] = far_ref[...]
    mine_ref[:, width + 16 :] = near_ref[...]
    first = jnp.zeros((1, tokens), jnp.float32)
    second = jnp.zeros((1, tokens), jnp.float32)
    blocks = []
    for slot in range(D // width):
        here = slice(slot * width, (slot + 1) * width)
        part = dot(w_ref[here], grad_ref[...], 1, 0)
        normed = (x_ref[here].astype(jnp.float32) - mean_ref[...]) * inv_ref[...]
        product = part * normed
        sum_ref[here, 0:1] = jnp.sum(product, axis=1, keepdims=True)
        sum_ref[here, 1:2] = jnp.sum(part, axis=1, keepdims=True)
        first += jnp.sum(part * gain_ref[here], axis=0, keepdims=True)
        second += jnp.sum(product * gain_ref[here], axis=0, keepdims=True)
        blocks.append(part.astype(LOW))
    line = lax.broadcasted_iota(jnp.int32, (16, tokens), 0)
    sums = jnp.where(line == 0, first, jnp.where(line == 1, second, 0.0)).astype(LOW)
    for near, ref in ((False, theirs_ref), (True, mine_ref)):
        for core in range(2):

            @pl.when((core_ref[0] == core) == near)
            def _(core=core, ref=ref):
                for row in range(n_row):
                    ref[row, :width] = blocks[core * n_row + row]
                    ref[row, width : width + 16] = sums


def first_back(core, w_mixed, qkv_grad, x_all, x_mean, inverse, gain, far, near):
    n_row, width, tokens = far.shape
    return pl.pallas_call(
        first_kernel,
        in_specs=[SMEM] + [VMEM] * 8,
        out_specs=[VMEM] * 3,
        out_shape=(
            jax.ShapeDtypeStruct((n_row, 2 * width + 16, tokens), LOW),
            jax.ShapeDtypeStruct((n_row, 2 * width + 16, tokens), LOW),
            jax.ShapeDtypeStruct((D, 2), jnp.float32),
        ),
        compiler_params=BIG,
        name="first_back",
    )(core, w_mixed, qkv_grad, x_all, x_mean, inverse, gain, far, near)


def adam_update(weights, moment_one, second, gradient, step_rate, weight_decay):
    moment_one = BETA_ONE * moment_one + (1.0 - BETA_ONE) * gradient
    second = BETA_TWO * second + (1.0 - BETA_TWO) * gradient * gradient
    direction = (
        moment_one / (1.0 - BETA_ONE**STEP) / (jnp.sqrt(second / (1.0 - BETA_TWO**STEP)) + ADAM_EPS)
    )
    return (weights - step_rate * (direction + weight_decay * weights), moment_one, second)


def shards(
    inputs,
    cotangent,
    qkv_master,
    out_master,
    up_master,
    down_master,
    qkv_first,
    out_first,
    up_first,
    down_first,
    qkv_second,
    out_second,
    up_second,
    down_second,
    norm_gains,
    gain_first,
    gain_second,
    biases,
    bias_first,
    bias_second,
):
    tokens, width = inputs.shape
    n_row = lax.axis_size("row")
    n_col = lax.axis_size("col")
    n_dp = lax.axis_size("dp")
    row = lax.axis_index("row")
    core = lax.axis_index("col")
    group = n_row * n_col
    heads = width // HEAD
    hidden_width = FF // group
    own = core * n_row + row
    place = jnp.stack([core, lax.axis_index("dp"), own]).astype(jnp.int32)
    chunk = -(-tokens // (group * 16)) * 16
    padded = chunk * group
    shard_rows = qkv_master.shape[0]

    index = jnp.arange(D)
    feature = (
        ((index // width) % n_row) * n_col + index // (width * n_row)
    ) * width + index % width
    index = (feature % n_dp) * (D // n_dp) + feature // n_dp
    order = (lax.broadcasted_iota(jnp.int32, (D, D), 1) == index[:, None]).astype(LOW)
    order = lax.optimization_barrier(order)

    def mixed(vector):
        return vector.reshape(n_row, n_col, width).transpose(1, 0, 2).reshape(D)

    def dealt(vector):
        return vector.reshape(D // n_dp, n_dp).T.reshape(D)

    def returned(rows):
        return exchange_rows(rows.reshape(n_row, shard_rows, -1))

    def long(array):
        return jnp.pad(array, ((0, 0), (0, padded - tokens)))

    flat = lambda array: array.transpose(1, 2, 0)
    tall = lambda array: array.transpose(2, 0, 1)
    first_rows = prepare(place, qkv_master, flat(out_master), n_row)
    first_rows = exchange_rows(first_rows).reshape(D // n_dp, -1)
    x_own = long(inputs.T)
    x_after = x_own + zero_of(first_rows).astype(LOW)
    x_rows = lax.all_gather(x_after, "row", axis=0, tiled=True)
    first_parts = gather_parts(first_rows, "dp")
    rest = prepare(x_rows, up_master, flat(down_master), n_row)
    rest = exchange_rows(rest).reshape(D // n_dp, -1)
    rest_parts = gather_parts(rest, "dp")
    x_all = both_cores(x_rows)
    cot_own = long(cotangent.T) + zero_of(rest).astype(LOW)
    cot_all = lax.all_gather(cot_own, ("row", "col"), axis=0)

    gain_one = mixed(norm_gains[0])
    gain_two = dealt(norm_gains[1])
    shift_one = mixed(biases[:D])
    shift_two = dealt(biases[D : 2 * D])
    query_bias = lax.dynamic_slice_in_dim(biases, 2 * D + own * width, width).reshape(heads, HEAD)
    value_bias = lax.dynamic_slice_in_dim(biases, 3 * D + own * width, width).reshape(heads, HEAD)
    out_bias = dealt(biases[4 * D : 5 * D])
    feature_start = (row * n_col + core) * width
    down_bias = lax.dynamic_slice_in_dim(biases, 5 * D + feature_start, width)
    up_bias = lax.dynamic_slice_in_dim(biases, 6 * D + own * hidden_width, hidden_width)
    qkv_bias = jnp.stack([query_bias, jnp.zeros_like(query_bias), value_bias], axis=1).reshape(
        3 * width, 1
    )

    x_full = x_all.astype(jnp.float32)
    x_mean = jnp.sum(x_full, axis=0, keepdims=True) / D
    center = x_full - x_mean
    inverse_one = lax.rsqrt(jnp.sum(center * center, axis=0, keepdims=True) / D + NORM_EPS)
    za = (center * inverse_one * gain_one[:, None] + shift_one[:, None]).astype(LOW)
    za = dot(order, za, 0, 0, LOW)

    w_first, qkv, attended, theirs, mine = attend(place, rest, za, qkv_bias, first_parts, width)
    pair = (mine.astype(jnp.float32) + swap_cores(theirs).astype(jnp.float32)).astype(LOW)
    branch = sum_over_rows(pair)
    cot_tokens, qkv_mixed, x_mine = beside(
        place, pair, order, cot_all, w_first, x_all, n_row, chunk
    )
    cot_mine = take(cot_tokens, own, chunk).astype(jnp.float32)

    middle = x_mine + branch + out_bias[None, :]
    center = middle - jnp.sum(middle, axis=1, keepdims=True) / D
    inverse_two = lax.rsqrt(jnp.sum(center * center, axis=1, keepdims=True) / D + NORM_EPS)
    normed_two = center * inverse_two
    zb = (normed_two * gain_two + shift_two).astype(LOW)
    zb_rows = lax.all_gather(zb, "row", axis=0, tiled=True)
    w_up, active_grad, down_mixed = before(place, zb_rows, order, cot_tokens, rest_parts)
    zb = both_cores(zb_rows)

    core_of = core.reshape(1).astype(jnp.int32)
    active, hidden_grad, theirs, mine, up_sums = mlp(
        core_of, zb, w_up, up_bias[None, :], active_grad
    )
    pair = (mine.astype(jnp.float32) + swap_cores(theirs).astype(jnp.float32)).astype(LOW)
    two_grad = sum_over_rows(pair)

    middle_mixed = dot(order, middle.astype(LOW), 1, 1, LOW)
    rest_grad, far, near = behind(
        place, pair, zb, hidden_grad, cot_tokens, active, down_mixed, middle_mixed, n_dp
    )

    scaled = two_grad * gain_two
    first_sum = jnp.sum(scaled, axis=1, keepdims=True) / D
    second_sum = jnp.sum(scaled * normed_two, axis=1, keepdims=True) / D
    middle_grad = cot_mine + zero_of(far) + inverse_two * (scaled - first_sum - normed_two * second_sum)
    middle_grad = middle_grad.astype(LOW)
    branch_rows = lax.all_gather(middle_grad, "row", axis=0, tiled=True)
    later = zero_of(branch_rows)
    branch_all = both_cores(branch_rows)
    rest_rows = sum_blocks(rest_grad, "dp", later)

    qkv_grad, bias_sums, first_grad = attend_back(
        rest_rows, branch_all, w_first, qkv, za, attended, n_dp
    )
    theirs, mine, one_sums = first_back(
        core_of, qkv_mixed, qkv_grad, x_all, x_mean, inverse_one, gain_one[:, None],
        far.reshape(n_row, width, padded), near.reshape(n_row, width, padded),
    )
    pair = (mine.astype(jnp.float32) + swap_cores(theirs).astype(jnp.float32)).astype(LOW)
    one_grad = sum_over_rows(pair.reshape(-1, padded))
    result = one_grad[width + 16 :] + down_bias[:, None]
    result = result.astype(LOW)[:, :tokens].T
    first_rows = sum_blocks(first_grad, "dp", 0.0)

    own_gain = lax.dynamic_slice_in_dim(norm_gains[0], feature_start, width)[:, None]
    own_normed = (x_own.astype(jnp.float32) - x_mean) * inverse_one
    own_order = lax.dynamic_slice_in_dim(order, own * width, width, axis=0)
    own_middle = dot(own_order, branch_all, 1, 1)
    input_grad = own_middle + inverse_one * (
        one_grad[:width] * own_gain
        - one_grad[width : width + 1] / D
        - own_normed * (one_grad[width + 1 : width + 2] / D)
    )
    input_grad = input_grad.astype(LOW)[:, :tokens].T

    later = zero_of(pair)
    bias_sums = (bias_sums + later).reshape(heads, 3, HEAD)
    all_rows = jnp.stack(
        [
            one_sums[:, 0] + later,
            one_sums[:, 1] + later,
            jnp.sum(two_grad * normed_two + later, axis=0),
            jnp.sum(two_grad + later, axis=0),
            jnp.sum(middle_grad.astype(jnp.float32) + later, axis=0),
            jnp.sum(cot_mine + later, axis=0),
        ]
    )
    own_row = jnp.concatenate(
        [bias_sums[:, 0].reshape(width), bias_sums[:, 2].reshape(width), up_sums[0] + later]
    )
    own_row = jnp.pad(own_row, (0, D - own_row.shape[0]))
    own_rows = jnp.where(jnp.arange(group)[:, None] == own, own_row[None, :], 0.0)
    total = all_sum(jnp.concatenate([jnp.pad(all_rows, ((0, 2), (0, 0))), own_rows]) + zero_of(first_rows))
    one_rows = total[:2].reshape(2, n_col, n_row, width).transpose(0, 2, 1, 3).reshape(2, D)
    two_rows = total[2:6].reshape(4, n_dp, D // n_dp).transpose(0, 2, 1).reshape(4, D)
    own_rows = total[8:]
    gain_total = jnp.stack([one_rows[0], two_rows[0]])
    bias_total = jnp.concatenate(
        [
            one_rows[1],
            two_rows[1],
            own_rows[:, :width].reshape(D),
            own_rows[:, width : 2 * width].reshape(D),
            two_rows[2],
            two_rows[3],
            own_rows[:, 2 * width : 2 * width + hidden_width].reshape(FF),
        ]
    )

    first_new = adam(
        pair,
        returned(jnp.concatenate([first_rows, rest_rows], axis=1)),
        (0.03, 0.12, 0.03, 0.02),
        qkv_master,
        qkv_first,
        qkv_second,
        flat(out_master),
        flat(out_first),
        flat(out_second),
        up_master,
        up_first,
        up_second,
        flat(down_master),
        flat(down_first),
        flat(down_second),
    )
    first_new, rest_new = first_new[:6], first_new[6:]
    g_new = adam_update(norm_gains, gain_first, gain_second, gain_total, 0.5, 0.0)
    b_new = adam_update(biases, bias_first, bias_second, bias_total, 0.5, 0.0)
    return (
        result,
        input_grad,
        *first_new[:3],
        *(tall(array) for array in first_new[3:]),
        *rest_new[:3],
        *(tall(array) for array in rest_new[3:]),
        *g_new,
        *b_new,
    )


def solution(mesh):
    token_spec = P("dp", ("row", "col"))
    wide = P("row", "dp", "col")
    tall = P("col", "row", "dp")
    return jax.shard_map(
        shards,
        mesh=mesh,
        in_specs=(token_spec,) * 2 + (wide, tall, wide, tall) * 3 + (P(),) * 6,
        out_specs=(token_spec,) * 2
        + (wide,) * 3
        + (tall,) * 3
        + (wide,) * 3
        + (tall,) * 3
        + (P(),) * 6,
        check_vma=False,
    )
```
